128 devices in a mesh: dp: 16 (over x, y), ep: 8 (over z, core).
Axes of the slice: x: 4, y: 4, z: 4, core: 2. Of those that a mesh axis runs over, the one named last changes fastest.
Arguments:
- tokens: bfloat16 [32, 1024, 1024], P('dp', 'ep'), may hold values from -6 to 6
- cotangent: bfloat16 [32, 1024, 1024], P('dp', 'ep'), may hold values from -6 to 6
- block_ids: int32 [32, 1024], P('dp'), may hold values from 0 to 7, never falling along the last dimension, each value on 1 to 256 neighbouring positions
- routes: int32 [32, 1024, 8], P('dp', 'ep'), may hold values from 0 to 31, all different within a row
- w_query: bfloat16 [1024, 1024], P(('dp', 'ep')), may hold values from -0.75 to 0.75
- w_key: bfloat16 [1024, 512], P(('dp', 'ep')), may hold values from -0.75 to 0.75
- w_value: bfloat16 [1024, 512], P(('dp', 'ep')), may hold values from -0.1875 to 0.1875
- w_output: bfloat16 [1024, 1024], P(('dp', 'ep')), may hold values from -3 to 3
- w_router: bfloat16 [1024, 32], P(('dp', 'ep')), may hold values from -0.09375 to 0.09375
- gain_attn: bfloat16 [1024], P(('dp', 'ep')), may hold values from 0.5 to 1.5
- gain_moe: bfloat16 [1024], P(('dp', 'ep')), may hold values from 0.5 to 1.5
- expert_gate: bfloat16 [32, 1024, 512], P('ep'), may hold values from -0.1875 to 0.1875
- expert_up: bfloat16 [32, 1024, 512], P('ep'), may hold values from -0.1875 to 0.1875
- expert_down: bfloat16 [32, 512, 1024], P('ep'), may hold values from -2 to 2
Outputs:
- output: bfloat16 [32, 1024, 1024], P('dp', 'ep')
- grad_tokens: bfloat16 [32, 1024, 1024], P('dp', 'ep')
- grad_query: float32 [1024, 1024], P(('dp', 'ep'))
- grad_key: float32 [1024, 512], P(('dp', 'ep'))
- grad_value: float32 [1024, 512], P(('dp', 'ep'))
- grad_output: float32 [1024, 1024], P(('dp', 'ep'))
- grad_router: float32 [1024, 32], P(('dp', 'ep'))
- grad_gain_attn: float32 [1024], P(('dp', 'ep'))
- grad_gain_moe: float32 [1024], P(('dp', 'ep'))
- grad_expert_gate: float32 [32, 1024, 512], P('ep')
- grad_expert_up: float32 [32, 1024, 512], P('ep')
- grad_expert_down: float32 [32, 512, 1024], P('ep')
The draws below stay inside these ranges and needn't reach their ends.
Inputs may be any that keep to these rules, and one draw needn't show every extreme that they name: `block_ids`: along each sequence the ids never fall; every id up to the largest occurs on 1 to 256 consecutive tokens, one block has exactly 256. `routes`: each token names 8 different experts; every expert is named by some token.
All inputs are finite; a program needn't handle non-finite values.
Results may differ from the reference program's by a relative error of at most 0.018.
Values may be sent and summed in bfloat16 or wider, within the bound.
A program may use at most 256 MiB of HBM per device.

```python
import math
from functools import partial
import jax
import jax.numpy as jnp
import numpy as np
from jax import lax

D = 1024
HEADS = 16
KV_HEADS = 8
HD = 64
F = 512
TOPK = 8
SEQS = 2
LEN = 1024
BLOCK = 256
DKV = 512
EXPERTS = 32
B = 32
CAP = 80
N_DP = 16
N_EP = 8


def levels(rng, extent, cuts, least, top_value):
    loudness = 1.0
    for position, blocks in cuts:
        draws = jax.random.uniform(jax.random.fold_in(jax.random.fold_in(rng, 6), position), (blocks,), jnp.float32, least / len(cuts), top_value / len(cuts))
        loudness = loudness * jnp.repeat(jnp.exp(draws), extent[position] // blocks).reshape((-1,) + (1,) * (len(extent) - 1 - position))
    return loudness


def different_ones(rng, rows, number_of, top, lift):
    order = jax.random.permutation(jax.random.fold_in(rng, 1), number_of)
    favour = order
    for power in range(3):
        favour = favour * favour // number_of
    favour = favour * lift // number_of
    chance = jax.random.randint(jax.random.fold_in(rng, 2), (rows, number_of), 0, 4096) + favour
    fixed_rows = jax.random.permutation(jax.random.fold_in(rng, 3), rows)[jnp.arange(number_of) % rows]
    chance = jnp.where(jnp.arange(rows)[:, None] == fixed_rows[None, :], 1 << 14, chance)
    score = chance * number_of + jnp.arange(number_of)
    return lax.top_k(score.astype(jnp.int32), top)[1].astype(jnp.int32)


def profile(count, total, bound, skew):
    weights = [(1 << 20) // math.isqrt(rank ** skew) + 1 for rank in range(2, count + 1)]
    spare, counts = total - bound - (count - 1), [1] * (count - 1)
    while spare > 0:
        free = [i for i in range(count - 1) if counts[i] < bound]
        pool, left = sum([weights[i] for i in free]), spare
        for i in free:
            more = min(bound - counts[i], max(1, left * weights[i] // pool), spare)
            counts[i] = counts[i] + more
            spare = spare - more
    return np.array([bound] + counts)


def ragged_sizes(stream_key, count, total, reach, skew):
    if count == 2:
        one = jax.random.randint(stream_key, (), max(1, total - reach), min(reach, total - 1) + 1)
        return jnp.stack([one, total - one])
    lengths = jnp.asarray(profile(count, total, reach, skew), jnp.int32)
    twos = (count - 1) // 2
    donor, receiver = lengths[1:1 + 2 * twos:2], lengths[2:2 + 2 * twos:2]
    slack = jnp.minimum(donor - 1, reach - receiver)
    moved = jax.random.randint(jax.random.fold_in(stream_key, 1), (twos,), 0, 1 << 20) % (slack + 1)
    lengths = lengths.at[1:1 + 2 * twos:2].set(donor - moved).at[2:2 + 2 * twos:2].set(receiver + moved)
    return lengths[jax.random.permutation(jax.random.fold_in(stream_key, 2), count)]


def noise(own_key, shape, deviation, reach, split=(), kind=jnp.bfloat16):
    array = jax.random.normal(own_key, shape, jnp.float32) * deviation
    if len(split) > 0:
        array = levels(own_key, shape, split, -0.22, 0.18) * array
    return jnp.clip(array, min=-reach, max=reach).astype(kind)


def setup_inputs(seed: int = 0) -> dict:
    key_list = jax.random.split(jax.random.key(seed), 15)
    return {
        "tokens": noise(key_list[0], (B, LEN, D), 1.0, 6.0, ((0, 16), (1, 8))),
        "cotangent": noise(key_list[1], (B, LEN, D), 1.0, 6.0, ((0, 16), (1, 8))),
        "block_ids": jax.vmap(lambda own: jnp.searchsorted(jnp.cumsum(ragged_sizes(own, 2 * LEN // BLOCK, LEN, BLOCK, 0)), jnp.arange(LEN), side="right"))(jax.random.split(key_list[2], B)).reshape((B, LEN)).astype(jnp.int32),
        "routes": different_ones(key_list[3], B * LEN, EXPERTS, TOPK, 2048).reshape((B, LEN, TOPK)),
        "w_query": noise(key_list[4], (D, D), (D // 16) ** -0.5, 0.75, ((0, 128),)),
        "w_key": noise(key_list[5], (D, DKV), (D // 16) ** -0.5, 0.75, ((0, 128),)),
        "w_value": noise(key_list[6], (D, DKV), D ** -0.5, 0.1875, ((0, 128),)),
        "w_output": noise(key_list[7], (D, D), (max(D // 256, 2)) ** -0.5, 3.0, ((0, 128),)),
        "w_router": noise(key_list[8], (D, EXPERTS), (4 * D) ** -0.5, 0.09375, ((0, 128),)),
        "gain_attn": jnp.clip(1.0 + 0.1 * jax.random.normal(key_list[9], (D,), jnp.float32), 0.5, 1.5).astype(jnp.bfloat16),
        "gain_moe": jnp.clip(1.0 + 0.1 * jax.random.normal(key_list[10], (D,), jnp.float32), 0.5, 1.5).astype(jnp.bfloat16),
        "expert_gate": noise(key_list[11], (EXPERTS, D, F), D ** -0.5, 0.1875, ((0, 8),)),
        "expert_up": noise(key_list[12], (EXPERTS, D, F), D ** -0.5, 0.1875, ((0, 8),)),
        "expert_down": noise(key_list[13], (EXPERTS, F, D), (max(F // 64, 1)) ** -0.5, 2.0, ((0, 8),)),
    }


highest = lax.Precision.HIGHEST
epsilon = 1e-06
residual_scale = 0.22
score_scale = 0.015625
rope_base = 10000.0
masked_value = -1e+30

@jax.custom_vjp
def low(v):
    return lax.optimization_barrier(v.astype(jnp.bfloat16)).astype(jnp.float32)

@jax.custom_vjp
def low_back(v):
    return v

def low_keep(v):
    return (low(v), None)

def low_pass(kept, grad):
    return (grad,)

def back_keep(v):
    return (v, None)

def back_low(kept, grad):
    return (low(grad),)
low.defvjp(low_keep, low_pass)
low_back.defvjp(back_keep, back_low)

def rms_scale(values, gain):
    return values * lax.rsqrt(lax.optimization_barrier(jnp.mean(values * values, axis=-1, keepdims=True)) + epsilon) * gain

def angles(positions, head_size):
    even_index = jnp.arange(0, head_size, 2).astype(positions.dtype)
    frequency = rope_base ** (-even_index / head_size)
    angle_grid = positions[:, None] * frequency[None, :]
    angle_grid = jnp.concatenate([angle_grid, angle_grid], axis=-1)
    return (jnp.cos(angle_grid), jnp.sin(angle_grid))

def rotate(values, cosine_table, sine_table):
    half_size = values.shape[-1] // 2
    turned = jnp.concatenate([-values[..., half_size:], values[..., :half_size]], axis=-1)
    return values * cosine_table + turned * sine_table

def attend(weights, packed):
    w_query, w_key, w_value, w_output, gain_attn = weights
    inputs, blocks = packed
    length = inputs.shape[0]
    normed = low(rms_scale(inputs, gain_attn))
    query_rows = low_back(jnp.dot(normed, w_query, precision=highest))
    key_rows = low_back(jnp.dot(normed, w_key, precision=highest))
    valued = low(low_back(jnp.dot(normed, w_value, precision=highest)))
    cosine_table, sine_table = angles(jnp.arange(length).astype(jnp.float32), HD)
    cosine_table = cosine_table[:, None, :]
    sine_table = sine_table[:, None, :]
    query_rot = low(rotate(query_rows.reshape(length, HEADS, HD), cosine_table, sine_table))
    key_rot = low(rotate(key_rows.reshape(length, KV_HEADS, HD), cosine_table, sine_table))
    grouped = query_rot.reshape(length, KV_HEADS, HEADS // KV_HEADS, HD)
    scores = low_back(score_scale * jnp.einsum('qgrd,kgd->grqk', grouped, key_rot, precision=highest))
    allowed = blocks[None, :] <= blocks[:, None]
    scores = jnp.where(allowed, scores, masked_value)
    probabilities = low(jax.nn.softmax(scores, axis=-1))
    attended = jnp.einsum('grqk,kgd->qgrd', probabilities, valued.reshape(length, KV_HEADS, HD), precision=highest)
    attended = low(low_back(attended.reshape(length, HEADS * HD)))
    branch = low_back(jnp.dot(attended, w_output, precision=highest))
    return inputs + residual_scale * branch

def dispatch_experts(weights, packed):
    expert_gate, expert_up, expert_down = weights
    moe_in, chosen_routes, gate_weights = packed
    row_count = moe_in.shape[0]
    top_count = chosen_routes.shape[1]
    flat_routes = chosen_routes.reshape(-1).astype(jnp.int32)
    one_hot = (flat_routes[:, None] == jnp.arange(EXPERTS)[None, :]).astype(jnp.int32)
    slot_index = lax.optimization_barrier(jnp.sum((jnp.cumsum(one_hot, axis=0) - one_hot) * one_hot, axis=1)).astype(jnp.int32)
    destination = jnp.where(slot_index < CAP, flat_routes * CAP + slot_index, EXPERTS * CAP).astype(jnp.int32)
    owner_token = (jnp.arange(row_count * top_count) // top_count).astype(jnp.int32)
    source = jnp.full((EXPERTS * CAP + 1,), row_count, jnp.int32).at[destination].set(owner_token)[:EXPERTS * CAP]
    zero_row = jnp.zeros((1, moe_in.shape[1]), moe_in.dtype)
    sent_rows = low_back(jnp.concatenate([moe_in, zero_row])[source]).reshape(EXPERTS, CAP, moe_in.shape[1])
    gate_pre = low_back(jnp.einsum('ecd,edf->ecf', sent_rows, expert_gate, precision=highest))
    up_pre = low_back(jnp.einsum('ecd,edf->ecf', sent_rows, expert_up, precision=highest))
    hidden = low(jax.nn.silu(gate_pre) * up_pre)
    returned = low_back(low(jnp.einsum('ecf,efd->ecd', hidden, expert_down, precision=highest)))
    padded = jnp.concatenate([returned.reshape(EXPERTS * CAP, moe_in.shape[1]), zero_row])
    picked = padded[destination].reshape(row_count, top_count, moe_in.shape[1])
    return lax.optimization_barrier(jnp.sum(gate_weights[:, :, None] * picked, axis=1))

def arrange(values):
    trailing = values.shape[2:]
    blocked = values.reshape((N_DP, SEQS, N_EP, LEN // N_EP) + trailing)
    return jnp.swapaxes(blocked, 1, 2).reshape((N_DP * N_EP, SEQS * (LEN // N_EP)) + trailing)

def restore(values):
    trailing = values.shape[2:]
    blocked = values.reshape((N_DP, N_EP, SEQS, LEN // N_EP) + trailing)
    return jnp.swapaxes(blocked, 1, 2).reshape((N_DP * SEQS, LEN) + trailing)

def forward(block_ids, routes, tokens, w_query, w_key, w_value, w_output, w_router, gain_attn, gain_moe, expert_gate, expert_up, expert_down):
    attend_one = jax.checkpoint(partial(attend, (w_query, w_key, w_value, w_output, gain_attn)))
    middle = lax.map(attend_one, (tokens, block_ids))
    flat_mid = middle.reshape(-1, middle.shape[-1])
    moe_in = low(rms_scale(flat_mid, gain_moe))
    logits = low_back(jnp.dot(moe_in, w_router, precision=highest))
    chosen_routes = routes.reshape(-1, TOPK)
    one_hot = (chosen_routes[:, :, None] == jnp.arange(EXPERTS)[None, None, :]).astype(logits.dtype)
    chosen = lax.optimization_barrier(jnp.sum(one_hot * logits[:, None, :], axis=-1))
    gate_weights = jax.nn.softmax(chosen, axis=-1)
    run_one = jax.checkpoint(partial(dispatch_experts, (expert_gate, expert_up, expert_down)))
    mixture = lax.map(run_one, (arrange(moe_in.reshape(middle.shape)), arrange(routes), arrange(gate_weights.reshape(routes.shape))))
    return middle + residual_scale * restore(mixture)

def reference(tokens, cotangent, block_ids, routes, w_query, w_key, w_value, w_output, w_router, gain_attn, gain_moe, expert_gate, expert_up, expert_down):
    output, pullback = jax.vjp(partial(forward, block_ids, routes), tokens.astype(jnp.float32), w_query.astype(jnp.float32), w_key.astype(jnp.float32), w_value.astype(jnp.float32), w_output.astype(jnp.float32), w_router.astype(jnp.float32), gain_attn.astype(jnp.float32), gain_moe.astype(jnp.float32), expert_gate.astype(jnp.float32), expert_up.astype(jnp.float32), expert_down.astype(jnp.float32))
    grads = pullback(cotangent.astype(jnp.float32))
    return (output.astype(jnp.bfloat16), grads[0].astype(jnp.bfloat16), grads[1], grads[2], grads[3], grads[4], grads[5], grads[6], grads[7], grads[8], grads[9], grads[10])
```

```python
import math

import jax
import jax.numpy as jnp
import numpy as np
from jax import lax
from jax.experimental import pallas as pl
from jax.experimental.pallas import tpu as pltpu
from jax.sharding import PartitionSpec as P

MESH = pl.DeviceIdType.MESH
BF = jnp.bfloat16
F32 = jnp.float32
ANY = pl.BlockSpec(memory_space=pl.ANY)
VM = pl.BlockSpec(memory_space=pltpu.VMEM)

DP, EP, CHIPS = 16, 8, 4
D, HD, F = 1024, 64, 512
ROWS, HALF, LEN, SEQS = 256, 128, 1024, 2
EXPERTS, OWN, CAP = 32, 4, 80
SLOTS = EP * CAP
EPS = 1e-6
RES = 0.22
SCORE = 0.015625
LOG2E = 1.4426950408889634
MASKED = -1e30
MIB = 2**20


def nt(a, b):
    return lax.dot_general(a, b, (((1,), (1,)), ((), ())), preferred_element_type=F32)


def nn(a, b):
    return jnp.dot(a, b, preferred_element_type=F32)


def tn(a, b):
    return lax.dot_general(a, b, (((0,), (0,)), ((), ())), preferred_element_type=F32)


def place():
    e = lax.axis_index("ep")
    return lax.axis_index("dp"), e, e // 2, lax.rem(e, 2)


def greet(peers):
    b = pltpu.get_barrier_semaphore()
    for p in peers:
        pl.semaphore_signal(b, inc=1, device_id=p, device_id_type=MESH)
    return lambda: pl.semaphore_wait(b, len(peers))


def ep_peers(d, e):
    return [(d, lax.rem(e + k, EP)) for k in range(1, EP)]


def dp_peers(d, e):
    return [(lax.rem(d + k, DP), e) for k in range(1, DP)]


class Sender:
    def __init__(self, ss, rs):
        self.ss, self.rs, self.n = ss, rs, 0

    def __call__(self, src, dst, dev):
        i = self.n
        self.n += 1
        cp = pltpu.make_async_remote_copy(
            src, dst, self.ss.at[i], self.rs.at[i], device_id=dev, device_id_type=MESH
        )
        cp.start()
        return cp


def ring(out, d, e, z, c, send):
    right, left = (d, lax.rem(z + 1, CHIPS) * 2 + c), (d, lax.rem(z + 3, CHIPS) * 2 + c)
    part = (d, z * 2 + 1 - c)
    er, el, eo = right[1], left[1], lax.rem(z + 2, CHIPS) * 2 + c

    def start(src0, src1, half):
        if half == 0:
            return [
                send(src0, out.at[e, 0], right),
                send(src0, out.at[e, 0], left),
                send(src0, out.at[e, 0], part),
            ]
        return [
            send(src1, out.at[e, 1], left),
            send(src1, out.at[e, 1], right),
            send(src1, out.at[e, 1], part),
        ]

    def finish(a, b):
        (r0, l0, p0), (l1, r1, p1) = a, b
        f = []
        r0.wait_recv()
        fr = send(out.at[el, 0], out.at[el, 0], right)
        f.append(send(out.at[el, 0], out.at[el, 0], part))
        l1.wait_recv()
        fl = send(out.at[er, 1], out.at[er, 1], left)
        f.append(send(out.at[er, 1], out.at[er, 1], part))
        r1.wait_recv()
        f.append(send(out.at[el, 1], out.at[el, 1], part))
        l0.wait_recv()
        f.append(send(out.at[er, 0], out.at[er, 0], part))
        fr.wait_recv()
        f.append(send(out.at[eo, 0], out.at[eo, 0], part))
        fl.wait_recv()
        f.append(send(out.at[eo, 1], out.at[eo, 1], part))
        for cp in (r0, l0, l1, r1, fr, fl):
            cp.wait_send()
        for cp in [p0, p1] + f:
            cp.wait()

    return start, finish


def remote_call(body, cid, outs, ins, specs, scratch, sems, out_specs=None, vmem=48, flops=0):
    return pl.pallas_call(
        body,
        name=body.__name__,
        out_shape=outs,
        in_specs=specs,
        out_specs=out_specs if out_specs is not None else [ANY] * len(outs),
        scratch_shapes=[
            *scratch,
            pltpu.SemaphoreType.DMA((4,)),
            pltpu.SemaphoreType.DMA((sems,)),
            pltpu.SemaphoreType.DMA((sems,)),
        ],
        compiler_params=pltpu.CompilerParams(
            collective_id=cid, has_side_effects=True, vmem_limit_bytes=vmem * MIB
        ),
        cost_estimate=pl.CostEstimate(flops=flops, bytes_accessed=20 * MIB, transcendentals=0),
    )(*ins)


def sds(shape, dtype):
    return jax.ShapeDtypeStruct(shape, dtype)


def gather_inputs(x, rt, wq, wk, wv, wo, sm, xall, rall, wsl, wof, wp, wop, ls, ss, rs):
    d, e, z, c = place()
    wait = greet(ep_peers(d, e) + dp_peers(d, e))
    q, k, v = wq[...].astype(F32), wk[...].astype(F32), wv[...].astype(F32)
    small = sm[...].astype(F32)
    for t in range(EP):
        row = jnp.concatenate(
            [
                q[:, 128 * t : 128 * t + 128],
                k[:, 64 * t : 64 * t + 64],
                v[:, 64 * t : 64 * t + 64],
            ],
            axis=1,
        )
        wp[t] = jnp.concatenate([row, small], axis=0).astype(BF)
    o = wo[...].astype(F32)
    wop[...] = jnp.concatenate([o[:, :512], o[:, 512:]], axis=0).astype(BF)
    wait()
    send = Sender(ss, rs)
    own = [
        pltpu.make_async_copy(x, xall.at[e], ls.at[0]),
        pltpu.make_async_copy(wp.at[e], wsl.at[d, e], ls.at[1]),
        pltpu.make_async_copy(wop, wof.at[d, e], ls.at[2]),
        pltpu.make_async_copy(rt, rall.at[e], ls.at[3]),
    ]
    for cp in own:
        cp.start()
    first = []
    for k in range(1, EP):
        t = lax.rem(e + k, EP)
        first.append(send(wp.at[t], wsl.at[d, e], (d, t)))
    for k in range(1, EP):
        t = lax.rem(e + k, EP)
        first.append(send(wop, wof.at[d, e], (d, t)))
    start, finish = ring(xall, d, e, z, c, send)
    a = start(x.at[0], x.at[1], 0)
    b = start(x.at[0], x.at[1], 1)
    routes = [send(rt, rall.at[e], p) for p in ep_peers(d, e)]
    own[1].wait()
    for cp in first[: EP - 1]:
        cp.wait_recv()
    second = [send(wsl.at[d], wsl.at[d], p) for p in dp_peers(d, e)]
    own[2].wait()
    for cp in first[EP - 1 :]:
        cp.wait_recv()
    mine = pl.ds(c * 4, 4)
    third = [send(wof.at[d, mine], wof.at[d, mine], p) for p in dp_peers(d, e)]
    finish(a, b)
    part = (d, z * 2 + 1 - c)
    last = []
    for k, cp in enumerate(third):
        cp.wait_recv()
        s = lax.rem(d + DP - 1 - k, DP)
        last.append(send(wof.at[s, mine], wof.at[s, mine], part))
    for cp in first + third:
        cp.wait_send()
    for cp in routes + second + last:
        cp.wait()
    own[0].wait()
    own[3].wait()


def lanes(shape):
    return lax.broadcasted_iota(jnp.int32, shape, 1)


def turn(v):
    first = lax.rem(lanes(v.shape), HD) < HD // 2
    return jnp.where(first, -pltpu.roll(v, 128 - HD // 2, 1), pltpu.roll(v, HD // 2, 1))


def both(kv):
    low = lanes(kv.shape) < HD
    other = pltpu.roll(kv, HD, 1)
    return jnp.where(low, kv, other).astype(BF), jnp.where(low, other, kv).astype(BF)


def two_heads(v):
    low = lanes(v.shape) < HD
    zero = jnp.zeros_like(v)
    return jnp.concatenate([jnp.where(low, v, zero), jnp.where(low, zero, v)], axis=0)


def spans(i):
    return i * ROWS, min(LEN, i * ROWS + 2 * ROWS)


def project_attend(
    x, wsl, wof, cs, sn, ids, q_o, kv_o, nrm_o, att_o, lse_o, gt_o, wo_o, w_s, kk_s, vv_s
):
    @pl.when(pl.program_id(0) == 0)
    def _():
        w = wsl[...].astype(F32).reshape(D // 8, 16, 256)
        w_s[...] = w[:, :8].reshape(D, 256).astype(BF)
        gt_o[...] = w[:, 8:].reshape(D, 256)[:, :128].T
        for i in range(4):
            o = wof[4 * i : 4 * i + 4].astype(F32).reshape(32, 16, 512)
            wo_o[256 * i : 256 * i + 256, :512] = o[:, :8].reshape(256, 512).astype(BF)
            wo_o[256 * i : 256 * i + 256, 512:] = o[:, 8:].reshape(256, 512).astype(BF)

    gain = gt_o[32:33, :]
    for r in range(4):
        rows = slice(256 * r, 256 * r + 256)
        v = x[2 * r : 2 * r + 2, 0].astype(F32).reshape(256, D)
        factor = lax.rsqrt(jnp.mean(v * v, axis=1, keepdims=True) + EPS)
        n = (v * factor * gain).astype(BF)
        nrm_o[0, rows] = n
        pre = nn(n, w_s[...])
        co, si = cs[rows], sn[rows]
        q, kv = pre[:, :128], pre[:, 128:]
        q_o[0, rows] = (q * co + turn(q) * si).astype(BF)
        kv = jnp.where(lanes(kv.shape) < HD, kv * co + turn(kv) * si, kv).astype(BF)
        kv_o[0, rows] = kv
        kk_s[rows], vv_s[rows] = both(kv.astype(F32))
    ids_k = ids[0]
    ids_q = jnp.broadcast_to(ids_k, (128, LEN)).T[:, :1]
    for i in range(4):
        q2 = two_heads(q_o[0, ROWS * i : ROWS * i + ROWS].astype(F32)).astype(BF)
        own = ids_q[ROWS * i : ROWS * i + ROWS]
        own = jnp.concatenate([own, own], axis=0)
        at, end = spans(i)
        parts = []
        if at:
            parts.append((nt(q2, kk_s[:at]) * (SCORE * LOG2E), slice(0, at)))
        t = nt(q2, kk_s[at:end]) * (SCORE * LOG2E)
        parts.append((jnp.where(ids_k[:, at:end] <= own, t, MASKED), slice(at, end)))
        peak = parts[0][0].max(axis=1, keepdims=True)
        for t, _ in parts[1:]:
            peak = jnp.maximum(peak, t.max(axis=1, keepdims=True))
        total, out = 0.0, 0.0
        for t, span in parts:
            p = jnp.exp2(t - peak)
            total = total + p.sum(axis=1, keepdims=True)
            out = out + nn(p.astype(BF), vv_s[span])
        out = out * (1.0 / total)
        lse = jnp.broadcast_to(peak + jnp.log2(total), (2 * ROWS, 128))
        low = lanes((ROWS, 128)) < HD
        att = jnp.where(low, out[:ROWS], out[ROWS:]).astype(BF)
        att_o[2 * i : 2 * i + 2, 0] = att.reshape(2, HALF, 128)
        lse_o[0, ROWS * i : ROWS * i + ROWS] = jnp.where(low, lse[:ROWS], lse[ROWS:])


def attended_to_moe(att, x, wo, gt, moe, mid_o, own_o, at_o, arr, mo, ls, ss, rs):
    d, e, z, c = place()
    greet(ep_peers(d, e))()
    send = Sender(ss, rs)
    lc = pltpu.make_async_copy(att.at[e], arr.at[e], ls.at[0])
    lc.start()
    cps = []
    for k in (4, 3, 5, 2, 6, 1, 7):
        t = lax.rem(e + k, EP)
        cps.append(send(att.at[t], arr.at[e], (d, t)))
    lc.wait()
    for cp in cps:
        cp.wait_recv()
    start, finish = ring(moe, d, e, z, c, send)
    gain = gt[33:34, :]
    begun, own = [], []
    for h in range(2):
        rows = slice(HALF * h, HALF * h + HALF)
        a = jnp.concatenate([arr[s, rows] for s in range(EP)], axis=1)
        at_o[rows] = a
        m = x[rows].astype(F32) + RES * nn(a, wo[...])
        mid_o[rows] = m
        factor = lax.rsqrt(jnp.mean(m * m, axis=1, keepdims=True) + EPS)
        n = (m * factor * gain).astype(BF)
        mo[h] = n
        own_o[rows] = n
        own.append(pltpu.make_async_copy(mo.at[h], moe.at[e, h], ls.at[1 + h]))
        own[h].start()
        begun.append(start(mo.at[0], mo.at[1], h))
    finish(*begun)
    for cp in cps:
        cp.wait_send()
    for cp in own:
        cp.wait()


def routing(rt, logits_t):
    ids = lax.broadcasted_iota(jnp.int32, (EXPERTS, ROWS), 0)
    hit = rt[0:1] == ids
    for k in range(1, 8):
        hit = hit | (rt[k : k + 1] == ids)
    w = jnp.where(hit, logits_t, MASKED)
    w = jnp.where(hit, jnp.exp(w - w.max(axis=0, keepdims=True)), 0.0)
    gates = w / w.sum(axis=0, keepdims=True)
    earlier = lax.broadcasted_iota(jnp.int32, (ROWS, ROWS), 0) < lax.broadcasted_iota(
        jnp.int32, (ROWS, ROWS), 1
    )
    slot = nn(jnp.where(hit, 1.0, 0.0).astype(BF), jnp.where(earlier, 1.0, 0.0).astype(BF))
    return gates, jnp.where(hit, slot, -1.0)


def experts_weights(moe, cot, rall, gt, wg, wu, wd, dw_o, hs_o, dg_o, du_o, gg_o, p_o, x_s, y_s, g_s):
    j = pl.program_id(0)
    first = lax.axis_index("ep") * OWN

    @pl.when(j == 0)
    def _():
        router_t = gt[:EXPERTS].astype(BF)
        row = lax.broadcasted_iota(jnp.int32, (EXPERTS, ROWS), 0)
        place_in = lax.broadcasted_iota(jnp.int32, (CAP, ROWS), 0).astype(F32)

        def source(s, carry):
            m = moe[s]
            gates, slot = routing(rall[s], nt(router_t, m))
            picks = []
            for i in range(OWN):
                sel = row == first + i
                pick = jnp.sum(jnp.where(sel, slot, 0.0), axis=0, keepdims=True) == place_in
                gate = jnp.sum(jnp.where(sel, gates, 0.0), axis=0, keepdims=True)
                g = jnp.sum(jnp.where(pick, gate, 0.0), axis=1, keepdims=True)
                g_s[i, pl.ds(pl.multiple_of(s * CAP, 16), CAP)] = jnp.broadcast_to(g, (CAP, 128))
                picks.append(jnp.where(pick, 1.0, 0.0).astype(BF))
            pick = jnp.concatenate(picks, axis=0)
            p_o[s] = pick
            xs = nn(pick, m).astype(BF)
            ys = nn(pick, cot[s]).astype(BF)
            for i in range(OWN):
                at = pl.ds(pl.multiple_of(s * CAP, 16), CAP)
                x_s[i, at] = xs[CAP * i : CAP * i + CAP]
                y_s[i, at] = ys[CAP * i : CAP * i + CAP]
            return carry

        lax.fori_loop(0, EP, source, 0)

    x, y = x_s[j], y_s[j]
    gate = g_s[j][:, :1] * RES
    g = nn(x, wg[0])
    u = nn(x, wu[0])
    dh = nt(y, wd[0])
    s = 1.0 / (1.0 + jnp.exp(-g))
    silu = g * s
    h = silu * u
    gg_o[0] = jnp.broadcast_to(RES * jnp.sum(h * dh, axis=1, keepdims=True), (SLOTS, 128))
    dh = dh * gate
    hs = (h * gate).astype(BF)
    dg = (dh * u * s * (1.0 + g * (1.0 - s))).astype(BF)
    du = (dh * silu).astype(BF)
    hs_o[0], dg_o[0], du_o[0] = hs, dg, du
    w = tn(x, jnp.concatenate([dg, du], axis=1))
    dw_o[0, :D] = w[:, :F].astype(BF)
    dw_o[0, D : 2 * D] = w[:, F:].astype(BF)
    w = tn(hs, y)
    dw_o[0, 2 * D : 2 * D + F] = w[:, :F].astype(BF)
    dw_o[0, 2 * D + F :] = w[:, F:].astype(BF)


def experts_back(hs, dg, du, gg, picks, wg, wu, wd, part_o, gg_o, eo_s, dx_s):
    j = pl.program_id(0)
    eo = nn(hs[0], wd[0]).astype(BF)
    dx = (nt(dg[0], wg[0]) + nt(du[0], wu[0])).astype(BF)
    for s in range(EP):
        eo_s[s, pl.ds(pl.multiple_of(j * CAP, 16), CAP)] = eo[CAP * s : CAP * s + CAP]
        dx_s[s, pl.ds(pl.multiple_of(j * CAP, 16), CAP)] = dx[CAP * s : CAP * s + CAP]

    @pl.when(j == OWN - 1)
    def _():
        def back(s, carry):
            p = picks[s]
            part_o[s, :, :D] = tn(p, eo_s[s]).astype(BF)
            part_o[s, :, D:] = tn(p, dx_s[s]).astype(BF)
            at = pl.ds(pl.multiple_of(s * CAP, 16), CAP)
            rows = [
                jnp.sum(
                    p[CAP * i : CAP * i + CAP].astype(F32) * gg[i, at][:, :1],
                    axis=0,
                    keepdims=True,
                )
                for i in range(OWN)
            ]
            gg_o[s] = jnp.concatenate(rows + [jnp.zeros((8 - OWN, ROWS), F32)], axis=0)
            return carry

        lax.fori_loop(0, EP, back, 0)


def combine(part, gg, mg_o, gt_o, mine, buf, acc, m1, m2, m3, m3s, ls, ss, rs):
    d, e, z, c = place()
    greet(ep_peers(d, e))()
    send = Sender(ss, rs)
    right, left = (d, lax.rem(z + 1, CHIPS) * 2 + c), (d, lax.rem(z + 3, CHIPS) * 2 + c)
    other = (d, z * 2 + 1 - c)
    order = (2, 1, 3, 0)
    mates, locs = [], []
    for i, k in enumerate(order):
        t = lax.rem(z + k, CHIPS) * 2
        mates.append(send(part.at[t + 1 - c], buf.at[i], other))
        locs.append(pltpu.make_async_copy(part.at[t + c], mine.at[i], ls.at[i]))
        locs[i].start()
    rows = [send(gg.at[lax.rem(e + k, EP)], gt_o.at[e], (d, lax.rem(e + k, EP))) for k in range(1, EP)]

    def add(i):
        locs[i].wait()
        mates[i].wait_recv()
        for h in range(2):
            for q in range(2):
                r = slice(64 * q, 64 * q + 64)
                acc[i, h, r] = (
                    mine[i, pl.ds(128 * h + 64 * q, 64)].astype(F32)
                    + buf[i, pl.ds(128 * h + 64 * q, 64)].astype(F32)
                ).astype(BF)

    add(0)
    a = send(acc.at[0, 0], m1.at[0], right)
    b = send(acc.at[0, 1], m1.at[1], left)
    add(1)
    a2 = send(acc.at[1, 1], m2.at[0], right)
    add(2)
    b2 = send(acc.at[2, 0], m2.at[1], left)

    def pass_on(cp, i, h, slot, dev):
        cp.wait_recv()
        m3s[slot] = (acc[i, h].astype(F32) + m1[slot].astype(F32)).astype(BF)
        return send(m3s.at[slot], m3.at[slot], dev)

    a3 = pass_on(a, 1, 0, 0, right)
    b3 = pass_on(b, 2, 1, 1, left)
    add(3)
    own = pltpu.make_async_copy(gg.at[e], gt_o.at[e], ls.at[0])
    own.start()
    b2.wait_recv()
    a3.wait_recv()
    mg_o[:HALF] = acc[3, 0].astype(F32) + m2[1].astype(F32) + m3[0].astype(F32)
    a2.wait_recv()
    b3.wait_recv()
    mg_o[HALF:] = acc[3, 1].astype(F32) + m2[0].astype(F32) + m3[1].astype(F32)
    for cp in mates + [a, b, a2, b2, a3, b3]:
        cp.wait_send()
    for cp in rows:
        cp.wait()
    own.wait()


def norm_back(grad, values, factor, gain):
    scaled = grad * gain
    grad_gain = jnp.sum(grad * values * factor, axis=0, keepdims=True)
    mean = jnp.mean(scaled * values, axis=1, keepdims=True)
    return factor * (scaled - values * (factor * factor * mean)), grad_gain


def after_experts(mg, gg, rt, moe, mid, cot, gt, wo, out_o, gm_o, gb_o, da_o, st_o):
    m = mid[...]
    out_o[...] = (m + mg[:, :D]).astype(BF)
    router_t = gt[:EXPERTS].astype(BF)
    gates, _ = routing(rt, nt(router_t, moe[...]))
    back = gg[...][:, :OWN].reshape(EXPERTS, ROWS)
    both_ = gates * back
    gl = (both_ - gates * jnp.sum(both_, axis=0, keepdims=True)).astype(BF)
    st_o[...] = jnp.zeros_like(st_o)
    st_o[:EXPERTS] = nn(gl, moe[...])
    grad = mg[:, D:] + tn(gl, router_t)
    factor = lax.rsqrt(jnp.mean(m * m, axis=1, keepdims=True) + EPS)
    gm, gain = norm_back(grad, m, factor, gt[33:34])
    st_o[33:34] = gain
    gm = cot[...].astype(F32) + gm
    gm_o[...] = gm
    gb = (RES * gm).astype(BF)
    ga = nt(gb, wo[...]).astype(BF)
    for t in range(EP):
        gb_o[t] = gb[:, 128 * t : 128 * t + 128]
        da_o[t] = ga[:, 128 * t : 128 * t + 128]


def to_heads(da, gb, at, da_o, gb_o, at_o, ls, ss, rs):
    d, e, z, c = place()
    greet(ep_peers(d, e))()
    send = Sender(ss, rs)
    own = [
        pltpu.make_async_copy(da.at[e], da_o.at[e], ls.at[0]),
        pltpu.make_async_copy(gb.at[e], gb_o.at[e], ls.at[1]),
        pltpu.make_async_copy(at, at_o.at[e], ls.at[2]),
    ]
    for cp in own:
        cp.start()
    cps = []
    for k in (4, 3, 5, 2, 6, 1, 7):
        t = lax.rem(e + k, EP)
        cps.append(send(da.at[t], da_o.at[e], (d, t)))
        cps.append(send(gb.at[t], gb_o.at[e], (d, t)))
    start, finish = ring(at_o, d, e, z, c, send)
    a = start(at.at[0], at.at[1], 0)
    finish(a, start(at.at[0], at.at[1], 1))
    for cp in cps:
        cp.wait()
    for cp in own:
        cp.wait()


def attend_back(q, kv, nrm, att, lse, da, gb, at, cs, sn, ids, dq_o, dw_o, kk_s, vv_s, dk_s, dv_s):
    s = pl.program_id(0)
    kk_s[...], vv_s[...] = both(kv[0].astype(F32))
    dk_s[...] = jnp.zeros_like(dk_s)
    dv_s[...] = jnp.zeros_like(dv_s)
    ids_k = ids[0]
    ids_q = jnp.broadcast_to(ids_k, (128, LEN)).T[:, :1]
    low = lanes((ROWS, 128)) < HD

    def unturn(v, rows):
        return v * cs[rows] - turn(v) * sn[rows]

    dqs = []
    for i in range(4):
        rows = slice(ROWS * i, ROWS * i + ROWS)
        q2 = two_heads(q[0, rows].astype(F32)).astype(BF)
        o = da[2 * i : 2 * i + 2, 0].reshape(ROWS, 128).astype(F32)
        o2f = two_heads(o)
        o2 = o2f.astype(BF)
        a = att[2 * i : 2 * i + 2, 0].reshape(ROWS, 128).astype(F32)
        delta = jnp.sum(o2f * jnp.concatenate([a, a], axis=0), axis=1, keepdims=True)
        l2 = jnp.concatenate([lse[0, rows][:, :1], lse[0, rows][:, HD : HD + 1]], axis=0)
        own = ids_q[rows]
        own = jnp.concatenate([own, own], axis=0)
        at_, end = spans(i)
        dq = 0.0
        for span in ([slice(0, at_)] if at_ else []) + [slice(at_, end)]:
            t = nt(q2, kk_s[span]) * (SCORE * LOG2E) - l2
            if span.start == at_:
                t = jnp.where(ids_k[:, span] <= own, t, MASKED)
            p = jnp.exp2(t)
            gp = nt(o2, vv_s[span])
            ds = (p * (gp - delta)).astype(BF)
            dq = dq + nn(ds, kk_s[span])
            dk_s[span] += tn(ds, q2)
            dv_s[span] += tn(p.astype(BF), o2)
        dq = SCORE * jnp.where(low, dq[:ROWS], dq[ROWS:])
        dqs.append(unturn(dq, rows).astype(BF))
    w = []
    for i in range(4):
        rows = slice(ROWS * i, ROWS * i + ROWS)
        dk, dv = dk_s[rows], dv_s[rows]
        dk = unturn(SCORE * (dk + pltpu.roll(dk, HD, 1)), rows)
        dv = dv + pltpu.roll(dv, HD, 1)
        dkv = jnp.where(low, dk, dv).astype(BF)
        dqkv = jnp.concatenate([dqs[i], dkv], axis=1)
        dq_o[2 * i : 2 * i + 2, 0] = dqkv.reshape(2, HALF, 256)
        w.append(dqkv)
    wqkv = tn(nrm[0], jnp.concatenate(w, axis=0))
    wout = tn(at[:, 0].reshape(LEN, D), gb[:, 0].reshape(LEN, 128))
    w = jnp.concatenate([wqkv, wout], axis=1)

    @pl.when(s == 0)
    def _():
        dw_o[...] = w

    @pl.when(s == 1)
    def _():
        dw_o[...] += w


def to_tokens(dq, dq_o, ls, ss, rs):
    d, e, z, c = place()
    greet(ep_peers(d, e))()
    send = Sender(ss, rs)
    own = pltpu.make_async_copy(dq.at[e], dq_o.at[e], ls.at[0])
    own.start()
    cps = []
    for k in (4, 3, 5, 2, 6, 1, 7):
        t = lax.rem(e + k, EP)
        cps.append(send(dq.at[t], dq_o.at[e], (d, t)))
    for cp in cps:
        cp.wait()
    own.wait()


def first_norm_back(dq, wf, x, gm, gt, st, dw, gx_o, pk_o):
    grad = 0.0
    for s in range(EP):
        w = wf[s].astype(F32).reshape(D // 8, 16, 256)[:, :8].reshape(D, 256).astype(BF)
        grad = grad + nt(dq[s], w)
    v = x[...].astype(F32)
    factor = lax.rsqrt(jnp.mean(v * v, axis=1, keepdims=True) + EPS)
    g, gain = norm_back(grad, v, factor, gt[32:33])
    gx_o[...] = (gm[...] + g).astype(BF)
    row = lax.broadcasted_iota(jnp.int32, (128, D), 0)
    small = jnp.where(row == 32, gain, st[...]).T
    w = jnp.concatenate([dw[...], small], axis=1).astype(BF)
    pk_o[...] = w.reshape(DP, D // DP, 512)


def sum_weights(pk, wq_o, wk_o, wv_o, wo_o, sm_o, r1, s1, r2, ls, ss, rs):
    d, e, z, c = place()
    greet(ep_peers(d, e) + dp_peers(d, e))()
    send = Sender(ss, rs)
    own = pltpu.make_async_copy(pk.at[d], r1.at[d], ls.at[0])
    own.start()
    cps = [send(pk.at[p[0]], r1.at[d], p) for p in dp_peers(d, e)]
    own.wait()
    for cp in cps:
        cp.wait_recv()
    t = r1[0].astype(F32)
    for i in range(1, DP):
        t = t + r1[i].astype(F32)
    s1[...] = t.reshape(EP, 8, 512)
    own = pltpu.make_async_copy(s1.at[e], r2.at[e], ls.at[1])
    own.start()
    more = [send(s1.at[p[1]], r2.at[e], p) for p in ep_peers(d, e)]
    own.wait()
    for cp in more:
        cp.wait_recv()
    small = r2[0, :, 384:]
    for s in range(1, EP):
        small = small + r2[s, :, 384:]
    sm_o[...] = small
    wq_o[...] = jnp.concatenate([r2[s, :, :128] for s in range(EP)], axis=1)
    wk_o[...] = jnp.concatenate([r2[s, :, 128:192] for s in range(EP)], axis=1)
    wv_o[...] = jnp.concatenate([r2[s, :, 192:256] for s in range(EP)], axis=1)
    wo_o[...] = jnp.concatenate([r2[s, :, 256:384] for s in range(EP)], axis=1)
    for cp in cps + more:
        cp.wait_send()


def tables():
    even = np.arange(0, HD, 2).astype(np.float32)
    frequency = (np.float32(10000.0) ** (-even / np.float32(HD))).astype(np.float32)
    angle = np.arange(LEN, dtype=np.float32)[:, None] * frequency[None, :]
    angle = np.concatenate([angle] * 4, axis=1).astype(np.float64)
    return np.cos(angle).astype(np.float32), np.sin(angle).astype(np.float32)


def per_device(
    tokens, cotangent, block_ids, routes, w_query, w_key, w_value, w_output, w_router,
    gain_attn, gain_moe, expert_gate, expert_up, expert_down,
):
    x = tokens.reshape(ROWS, D)
    cot = cotangent.reshape(ROWS, D)
    rt = routes.reshape(ROWS, 8).T
    ids = block_ids.reshape(SEQS, 1, LEN)
    small = jnp.concatenate(
        [w_router, gain_attn[:, None], gain_moe[:, None], jnp.zeros((8, 222), BF)], axis=1
    )
    cos, sin = tables()
    cos, sin = jnp.asarray(cos), jnp.asarray(sin)
    params = pltpu.CompilerParams(vmem_limit_bytes=60 * MIB)
    once = pl.Buffered(1)

    def whole(shape):
        return pl.BlockSpec(shape, lambda s: (0,) * len(shape), pipeline_mode=once)

    xall, rall, wsl, wof = remote_call(
        gather_inputs, 1,
        [sds((EP, 2, HALF, D), BF), sds((EP, 8, ROWS), jnp.int32), sds((DP, EP, 16, 256), BF),
         sds((DP, EP, 16, 512), BF)],
        [tokens.reshape(2, HALF, D), rt, w_query, w_key, w_value, w_output, small],
        [ANY] + [VM] * 6,
        [pltpu.VMEM((EP, 16, 256), BF), pltpu.VMEM((16, 512), BF)],
        96,
    )
    cot_late, _ = lax.optimization_barrier((cot, xall))
    cot_all = lax.all_gather(cot_late, "ep", axis=0)

    seq = lambda *shape: pl.BlockSpec((1, *shape), lambda s: (s,) + (0,) * len(shape))
    cut = lambda n: pl.BlockSpec((EP, 1, HALF, n), lambda s: (0, s, 0, 0))
    q, kv, nrm, att, lse, gt, wo = pl.pallas_call(
        project_attend,
        name="project_attend",
        grid=(SEQS,),
        out_shape=[
            sds((SEQS, LEN, 128), BF), sds((SEQS, LEN, 128), BF), sds((SEQS, LEN, D), BF),
            sds((EP, 2, HALF, 128), BF), sds((SEQS, LEN, 128), F32), sds((128, D), F32),
            sds((D, D), BF),
        ],
        in_specs=[
            cut(D), whole((DP, EP, 16, 256)), whole((DP, EP, 16, 512)), whole((LEN, 128)),
            whole((LEN, 128)), seq(1, LEN),
        ],
        out_specs=[
            seq(LEN, 128), seq(LEN, 128), seq(LEN, D), cut(128), seq(LEN, 128), whole((128, D)),
            whole((D, D)),
        ],
        scratch_shapes=[
            pltpu.VMEM((D, 256), BF), pltpu.VMEM((LEN, 128), BF), pltpu.VMEM((LEN, 128), BF),
        ],
        compiler_params=params,
    )(xall, wsl, wof, cos, sin, ids)

    moe, mid, moe_own, at_own = remote_call(
        attended_to_moe, 2,
        [sds((EP, 2, HALF, D), BF), sds((ROWS, D), F32), sds((ROWS, D), BF), sds((ROWS, D), BF)],
        [att.reshape(EP, ROWS, 128), x, wo, gt],
        [ANY, VM, VM, VM],
        [pltpu.VMEM((EP, ROWS, 128), BF), pltpu.VMEM((2, HALF, D), BF)],
        24,
        [ANY, VM, VM, VM],
    )
    w_late, moe = lax.optimization_barrier((wsl, moe))
    w_full = lax.all_gather(w_late.reshape(D // 8, 16, 256), "ep", axis=0)

    each = lambda *shape: pl.BlockSpec((1, *shape), lambda j: (j,) + (0,) * len(shape))
    dw, hs, dg, du, gg, picks = pl.pallas_call(
        experts_weights,
        name="experts_weights",
        grid=(OWN,),
        out_shape=[
            sds((OWN, 3 * D, F), BF), sds((OWN, SLOTS, F), BF), sds((OWN, SLOTS, F), BF),
            sds((OWN, SLOTS, F), BF), sds((OWN, SLOTS, 128), F32), sds((EP, OWN * CAP, ROWS), BF),
        ],
        in_specs=[
            whole((EP, ROWS, D)), whole((EP, ROWS, D)), whole((EP, 8, ROWS)), whole((128, D)),
            each(D, F), each(D, F), each(F, D),
        ],
        out_specs=[
            each(3 * D, F), each(SLOTS, F), each(SLOTS, F), each(SLOTS, F), each(SLOTS, 128),
            whole((EP, OWN * CAP, ROWS)),
        ],
        scratch_shapes=[
            pltpu.VMEM((OWN, SLOTS, D), BF), pltpu.VMEM((OWN, SLOTS, D), BF),
            pltpu.VMEM((OWN, SLOTS, 128), F32),
        ],
        compiler_params=params,
    )(moe.reshape(EP, ROWS, D), cot_all, rall, gt, expert_gate, expert_up, expert_down)

    dw_sum = lax.psum(dw.reshape(OWN * 3 * D, F), "dp").reshape(OWN, 3 * D, F)

    part, gg_part = pl.pallas_call(
        experts_back,
        name="experts_back",
        grid=(OWN,),
        out_shape=[sds((EP, ROWS, 2 * D), BF), sds((EP, 8, ROWS), F32)],
        in_specs=[
            each(SLOTS, F), each(SLOTS, F), each(SLOTS, F), whole((OWN, SLOTS, 128)),
            whole((EP, OWN * CAP, ROWS)), each(D, F), each(D, F), each(F, D),
        ],
        out_specs=[whole((EP, ROWS, 2 * D)), whole((EP, 8, ROWS))],
        scratch_shapes=[pltpu.VMEM((EP, OWN * CAP, D), BF), pltpu.VMEM((EP, OWN * CAP, D), BF)],
        compiler_params=params,
    )(hs, dg, du, gg, picks, expert_gate, expert_up, expert_down)

    mg, gg_all = remote_call(
        combine, 3,
        [sds((ROWS, 2 * D), F32), sds((EP, 8, ROWS), F32)],
        [part, gg_part],
        [ANY, ANY],
        [
            pltpu.VMEM((4, ROWS, 2 * D), BF), pltpu.VMEM((4, ROWS, 2 * D), BF),
            pltpu.VMEM((4, 2, HALF, 2 * D), BF), pltpu.VMEM((2, HALF, 2 * D), BF),
            pltpu.VMEM((2, HALF, 2 * D), BF), pltpu.VMEM((2, HALF, 2 * D), BF),
            pltpu.VMEM((2, HALF, 2 * D), BF),
        ],
        20,
        [VM, ANY],
    )

    output, gm, gb, da, st = pl.pallas_call(
        after_experts,
        name="after_experts",
        out_shape=[
            sds((ROWS, D), BF), sds((ROWS, D), F32), sds((EP, ROWS, 128), BF),
            sds((EP, ROWS, 128), BF), sds((128, D), F32),
        ],
        in_specs=[VM] * 8,
        out_specs=[VM] * 5,
        compiler_params=params,
    )(mg, gg_all, rt, moe_own, mid, cot, gt, wo)

    da_all, gb_all, at_all = remote_call(
        to_heads, 4,
        [sds((EP, ROWS, 128), BF), sds((EP, ROWS, 128), BF), sds((EP, 2, HALF, D), BF)],
        [da, gb, at_own.reshape(2, HALF, D)],
        [ANY] * 3,
        [],
        32,
    )

    dq, dw_attn = pl.pallas_call(
        attend_back,
        name="attend_back",
        grid=(SEQS,),
        out_shape=[sds((EP, 2, HALF, 256), BF), sds((D, 384), F32)],
        in_specs=[
            seq(LEN, 128), seq(LEN, 128), seq(LEN, D), cut(128), seq(LEN, 128), cut(128),
            cut(128), cut(D), whole((LEN, 128)), whole((LEN, 128)), seq(1, LEN),
        ],
        out_specs=[cut(256), whole((D, 384))],
        scratch_shapes=[
            pltpu.VMEM((LEN, 128), BF), pltpu.VMEM((LEN, 128), BF),
            pltpu.VMEM((LEN, 128), F32), pltpu.VMEM((LEN, 128), F32),
        ],
        compiler_params=params,
    )(
        q, kv, nrm, att, lse, da_all.reshape(EP, 2, HALF, 128), gb_all.reshape(EP, 2, HALF, 128),
        at_all, cos, sin, ids,
    )

    (dq_all,) = remote_call(
        to_tokens, 5, [sds((EP, ROWS, 256), BF)], [dq.reshape(EP, ROWS, 256)], [ANY], [], 8
    )

    grad_x, packed = pl.pallas_call(
        first_norm_back,
        name="first_norm_back",
        out_shape=[sds((ROWS, D), BF), sds((DP, D // DP, 512), BF)],
        in_specs=[VM] * 7,
        out_specs=[VM] * 2,
        compiler_params=params,
    )(dq_all, w_full, x, gm, gt, st, dw_attn)

    gq, gk, gv, go, gs = remote_call(
        sum_weights, 6,
        [sds((8, D), F32), sds((8, 512), F32), sds((8, 512), F32), sds((8, D), F32), sds((8, 128), F32)],
        [packed],
        [ANY],
        [
            pltpu.VMEM((DP, D // DP, 512), BF), pltpu.VMEM((EP, 8, 512), F32),
            pltpu.VMEM((EP, 8, 512), F32),
        ],
        24,
        [VM] * 5,
    )

    f = dw_sum.astype(F32)
    down = jnp.concatenate([f[:, 2 * D : 2 * D + F], f[:, 2 * D + F :]], axis=2)
    return (
        output.reshape(tokens.shape),
        grad_x.reshape(tokens.shape),
        gq,
        gk,
        gv,
        go,
        gs[:, :EXPERTS],
        gs[:, 32],
        gs[:, 33],
        f[:, :D],
        f[:, D : 2 * D],
        down,
    )


def solution(mesh):
    rows, own, both_axes = P("dp", "ep", None), P("ep", None, None), P(("dp", "ep"), None)
    line = P(("dp", "ep"))
    return jax.shard_map(
        per_device,
        mesh=mesh,
        in_specs=(
            rows, rows, P("dp", None), rows, both_axes, both_axes, both_axes, both_axes, both_axes,
            line, line, own, own, own,
        ),
        out_specs=(
            rows, rows, both_axes, both_axes, both_axes, both_axes, both_axes, line, line, own,
            own, own,
        ),
        check_vma=False,
    )
```

```python
import math

import jax
import jax.numpy as jnp
import numpy as np
from jax import lax
from jax.experimental import pallas as pl
from jax.experimental.pallas import tpu as pltpu
from jax.sharding import PartitionSpec as P

MESH = pl.DeviceIdType.MESH
BF = jnp.bfloat16
F32 = jnp.float32
ANY = pl.BlockSpec(memory_space=pl.ANY)
VM = pl.BlockSpec(memory_space=pltpu.VMEM)

DP, EP, CHIPS = 16, 8, 4
D, HD, F = 1024, 64, 512
ROWS, HALF, LEN, SEQS = 256, 128, 1024, 2
EXPERTS, OWN, CAP = 32, 4, 80
SLOTS = EP * CAP
EPS = 1e-6
RES = 0.22
SCORE = 0.015625
LOG2E = 1.4426950408889634
MASKED = -1e30
MIB = 2**20


def nt(a, b):
    return lax.dot_general(a, b, (((1,), (1,)), ((), ())), preferred_element_type=F32)


def nn(a, b):
    return jnp.dot(a, b, preferred_element_type=F32)


def tn(a, b):
    return lax.dot_general(a, b, (((0,), (0,)), ((), ())), preferred_element_type=F32)


def place():
    e = lax.axis_index("ep")
    return lax.axis_index("dp"), e, e // 2, lax.rem(e, 2)


def greet(peers):
    b = pltpu.get_barrier_semaphore()
    for p in peers:
        pl.semaphore_signal(b, inc=1, device_id=p, device_id_type=MESH)
    return lambda: pl.semaphore_wait(b, len(peers))


def ep_peers(d, e):
    return [(d, lax.rem(e + k, EP)) for k in range(1, EP)]


def dp_peers(d, e):
    return [(lax.rem(d + k, DP), e) for k in range(1, DP)]


class Sender:
    def __init__(self, ss, rs):
        self.ss, self.rs, self.n = ss, rs, 0

    def __call__(self, src, dst, dev):
        i = self.n
        self.n += 1
        return pltpu.make_async_remote_copy(
            src, dst, self.ss.at[i], self.rs.at[i], device_id=dev, device_id_type=MESH
        )

    def now(self, src, dst, dev):
        cp = self(src, dst, dev)
        cp.start()
        return cp


class Ring:
    def __init__(self, out, src0, src1, d, e, z, c, make):
        right, left = (d, lax.rem(z + 1, CHIPS) * 2 + c), (d, lax.rem(z + 3, CHIPS) * 2 + c)
        part = (d, z * 2 + 1 - c)
        er, el, eo = right[1], left[1], lax.rem(z + 2, CHIPS) * 2 + c
        self.near = [
            [make(src0, out.at[e, 0], right), make(src0, out.at[e, 0], left)],
            [make(src1, out.at[e, 1], left), make(src1, out.at[e, 1], right)],
        ]
        self.mate = [make(src0, out.at[e, 0], part), make(src1, out.at[e, 1], part)]
        self.far = [
            make(out.at[el, 0], out.at[el, 0], right),
            make(out.at[er, 1], out.at[er, 1], left),
        ]
        self.share = [make(out.at[s, h], out.at[s, h], part) for s, h in
                      ((el, 0), (er, 1), (el, 1), (er, 0), (eo, 0), (eo, 1))]

    def start(self, h):
        for cp in self.near[h]:
            cp.start()
        self.mate[h].start()

    def forward(self):
        for h in range(2):
            self.near[h][0].wait_recv()
            self.far[h].start()
            self.share[h].start()
        for h in range(2):
            self.near[1 - h][1].wait_recv()
            self.share[2 + h].start()

    def finish(self):
        for h in range(2):
            self.far[h].wait_recv()
            self.share[4 + h].start()
        for cp in self.near[0] + self.near[1] + self.far:
            cp.wait_send()
        for cp in self.mate + self.share:
            cp.wait()


def remote_call(body, cid, outs, ins, specs, scratch, sems, out_specs=None, vmem=48, flops=0):
    return pl.pallas_call(
        body,
        name=body.__name__,
        out_shape=outs,
        in_specs=specs,
        out_specs=out_specs if out_specs is not None else [ANY] * len(outs),
        scratch_shapes=[
            *scratch,
            pltpu.SemaphoreType.DMA((4,)),
            pltpu.SemaphoreType.DMA((sems,)),
            pltpu.SemaphoreType.DMA((sems,)),
        ],
        compiler_params=pltpu.CompilerParams(
            collective_id=cid, has_side_effects=True, vmem_limit_bytes=vmem * MIB
        ),
        cost_estimate=pl.CostEstimate(flops=flops, bytes_accessed=20 * MIB, transcendentals=0),
    )(*ins)


def sds(shape, dtype):
    return jax.ShapeDtypeStruct(shape, dtype)


def gather_inputs(x, rt, wq, wo, sm, xall, rall, wsl, wof, wp, wop, ls, ss, rs):
    d, e, z, c = place()
    u, v = d // 4, lax.rem(d, 4)
    across = [(lax.rem(u + k, 4) * 4 + v, e) for k in (1, 3, 2)]
    along = [(u * 4 + lax.rem(v + k, 4), e) for k in (1, 3, 2)]
    wait = greet(ep_peers(d, e) + across + along)
    q = wq[...].astype(F32)
    small = sm[...].astype(F32)
    for t in range(EP):
        wp[t] = jnp.concatenate([q[:, 256 * t : 256 * t + 256], small], axis=0).astype(BF)
    o = wo[...].astype(F32)
    wop[...] = jnp.concatenate([o[:, :512], o[:, 512:]], axis=0).astype(BF)
    wait()
    make = Sender(ss, rs)
    send = make.now
    own = [
        pltpu.make_async_copy(x, xall.at[e], ls.at[0]),
        pltpu.make_async_copy(wp.at[e], wsl.at[v, u, e], ls.at[1]),
        pltpu.make_async_copy(wop, wof.at[u, v, e], ls.at[2]),
        pltpu.make_async_copy(rt, rall.at[e], ls.at[3]),
    ]
    for cp in own:
        cp.start()
    first = [send(wp.at[p[1]], wsl.at[v, u, e], p) for p in ep_peers(d, e)]
    first += [send(wop, wof.at[u, v, e], p) for p in ep_peers(d, e)]
    ring = Ring(xall, x.at[0], x.at[1], d, e, z, c, make)
    ring.start(0)
    ring.start(1)
    routes = [send(rt, rall.at[e], p) for p in ep_peers(d, e)]
    own[1].wait()
    for cp in first[: EP - 1]:
        cp.wait_recv()
    w1 = [send(wsl.at[v, u], wsl.at[v, u], p) for p in across]
    own[2].wait()
    for cp in first[EP - 1 :]:
        cp.wait_recv()
    mine = pl.ds(c * 4, 4)
    part = (d, z * 2 + 1 - c)
    o1 = [send(wof.at[u, v, mine], wof.at[u, v, mine], p) for p in along]
    for cp in w1:
        cp.wait_recv()
    w2 = [send(wsl.at[v], wsl.at[v], p) for p in along]
    for cp in o1:
        cp.wait_recv()
    o2 = [send(wof.at[u, :, mine], wof.at[u, :, mine], p) for p in across]
    ring.forward()
    ring.finish()
    last = []
    for k, cp in zip((1, 3, 2), o1):
        t = lax.rem(v + 4 - k, 4)
        last.append(send(wof.at[u, t, mine], wof.at[u, t, mine], part))
    for k, cp in zip((1, 3, 2), o2):
        cp.wait_recv()
        t = lax.rem(u + 4 - k, 4)
        last.append(send(wof.at[t, :, mine], wof.at[t, :, mine], part))
    for cp in first + w1 + o1 + o2:
        cp.wait_send()
    for cp in routes + w2 + last:
        cp.wait()
    own[0].wait()
    own[3].wait()


def lanes(shape):
    return lax.broadcasted_iota(jnp.int32, shape, 1)


def turn(v):
    first = lax.rem(lanes(v.shape), HD) < HD // 2
    return jnp.where(first, -pltpu.roll(v, 128 - HD // 2, 1), pltpu.roll(v, HD // 2, 1))


def both(kv):
    low = lanes(kv.shape) < HD
    other = pltpu.roll(kv, HD, 1)
    return jnp.where(low, kv, other).astype(BF), jnp.where(low, other, kv).astype(BF)


def two_heads(v):
    low = lanes(v.shape) < HD
    zero = jnp.zeros_like(v)
    return jnp.concatenate([jnp.where(low, v, zero), jnp.where(low, zero, v)], axis=0)


def spans(i):
    return i * ROWS, min(LEN, i * ROWS + 2 * ROWS)


def project_attend(
    x, wsl, wof, cs, sn, ids, q_o, kv_o, nrm_o, att_o, lse_o, gt_o, wo_o, w_s, sm_s, kk_s, vv_s
):
    @pl.when(pl.program_id(0) == 0)
    def _():
        for i in range(DP):
            w = wsl[i % 4, i // 4].astype(F32)
            rows = slice(64 * i, 64 * i + 64)
            w_s[rows] = w[:, :8].reshape(64, 256).astype(BF)
            sm_s[rows] = w[:, 8:, :128].reshape(64, 128)
        gt_o[...] = sm_s[...].T
        for i in range(4):
            o = wof[i].astype(F32).reshape(32, 16, 512)
            wo_o[256 * i : 256 * i + 256, :512] = o[:, :8].reshape(256, 512).astype(BF)
            wo_o[256 * i : 256 * i + 256, 512:] = o[:, 8:].reshape(256, 512).astype(BF)

    gain = gt_o[32:33, :]
    for r in range(4):
        rows = slice(256 * r, 256 * r + 256)
        v = x[2 * r : 2 * r + 2, 0].astype(F32).reshape(256, D)
        factor = lax.rsqrt(jnp.mean(v * v, axis=1, keepdims=True) + EPS)
        n = (v * factor * gain).astype(BF)
        nrm_o[0, rows] = n
        pre = nn(n, w_s[...])
        co, si = cs[rows], sn[rows]
        q, kv = pre[:, :128], pre[:, 128:]
        q_o[0, rows] = (q * co + turn(q) * si).astype(BF)
        kv = jnp.where(lanes(kv.shape) < HD, kv * co + turn(kv) * si, kv).astype(BF)
        kv_o[0, rows] = kv
        kk_s[rows], vv_s[rows] = both(kv.astype(F32))
    ids_k = ids[0]
    ids_q = jnp.broadcast_to(ids_k, (128, LEN)).T[:, :1]
    for i in range(4):
        q2 = two_heads(q_o[0, ROWS * i : ROWS * i + ROWS].astype(F32)).astype(BF)
        own = ids_q[ROWS * i : ROWS * i + ROWS]
        own = jnp.concatenate([own, own], axis=0)
        at, end = spans(i)
        parts = []
        if at:
            parts.append((nt(q2, kk_s[:at]) * (SCORE * LOG2E), slice(0, at)))
        t = nt(q2, kk_s[at:end]) * (SCORE * LOG2E)
        parts.append((jnp.where(ids_k[:, at:end] <= own, t, MASKED), slice(at, end)))
        peak = parts[0][0].max(axis=1, keepdims=True)
        for t, _ in parts[1:]:
            peak = jnp.maximum(peak, t.max(axis=1, keepdims=True))
        total, out = 0.0, 0.0
        for t, span in parts:
            p = jnp.exp2(t - peak)
            total = total + p.sum(axis=1, keepdims=True)
            out = out + nn(p.astype(BF), vv_s[span])
        out = out * (1.0 / total)
        lse = jnp.broadcast_to(peak + jnp.log2(total), (2 * ROWS, 128))
        low = lanes((ROWS, 128)) < HD
        att = jnp.where(low, out[:ROWS], out[ROWS:]).astype(BF)
        att_o[2 * i : 2 * i + 2, 0] = att.reshape(2, HALF, 128)
        lse_o[0, ROWS * i : ROWS * i + ROWS] = jnp.where(low, lse[:ROWS], lse[ROWS:])


def attended_to_moe(att, x, wo, gt, moe, mid_o, own_o, at_o, arr, mo, ls, ss, rs):
    d, e, z, c = place()
    greet(ep_peers(d, e))()
    make = Sender(ss, rs)
    send = make.now
    lc = pltpu.make_async_copy(att.at[e], arr.at[e], ls.at[0])
    lc.start()
    cps = []
    for k in (4, 3, 5, 2, 6, 1, 7):
        t = lax.rem(e + k, EP)
        cps.append(send(att.at[t], arr.at[e], (d, t)))
    lc.wait()
    for cp in cps:
        cp.wait_recv()
    ring = Ring(moe, mo.at[0], mo.at[1], d, e, z, c, make)
    gain = gt[33:34, :]
    own = []
    for h in range(2):
        rows = slice(HALF * h, HALF * h + HALF)
        a = jnp.concatenate([arr[s, rows] for s in range(EP)], axis=1)
        at_o[rows] = a
        m = x[rows].astype(F32) + RES * nn(a, wo[...])
        mid_o[rows] = m
        factor = lax.rsqrt(jnp.mean(m * m, axis=1, keepdims=True) + EPS)
        n = (m * factor * gain).astype(BF)
        mo[h] = n
        own_o[rows] = n
        own.append(pltpu.make_async_copy(mo.at[h], moe.at[e, h], ls.at[1 + h]))
        own[h].start()
        ring.start(h)
    ring.forward()
    ring.finish()
    for cp in cps:
        cp.wait_send()
    for cp in own:
        cp.wait()


def routing(rt, logits_t):
    ids = lax.broadcasted_iota(jnp.int32, (EXPERTS, ROWS), 0)
    hit = rt[0:1] == ids
    for k in range(1, 8):
        hit = hit | (rt[k : k + 1] == ids)
    w = jnp.where(hit, logits_t, MASKED)
    w = jnp.where(hit, jnp.exp(w - w.max(axis=0, keepdims=True)), 0.0)
    gates = w / w.sum(axis=0, keepdims=True)
    earlier = lax.broadcasted_iota(jnp.int32, (ROWS, ROWS), 0) < lax.broadcasted_iota(
        jnp.int32, (ROWS, ROWS), 1
    )
    slot = nn(jnp.where(hit, 1.0, 0.0).astype(BF), jnp.where(earlier, 1.0, 0.0).astype(BF))
    return gates, jnp.where(hit, slot, -1.0)


def experts_weights(moe, cot, rall, gt, wg, wu, wd, dw_o, hs_o, dg_o, du_o, gg_o, p_o, x_s, y_s, g_s):
    j = pl.program_id(0)
    first = lax.axis_index("ep") * OWN

    @pl.when(j == 0)
    def _():
        router_t = gt[:EXPERTS].astype(BF)
        row = lax.broadcasted_iota(jnp.int32, (EXPERTS, ROWS), 0)
        place_in = lax.broadcasted_iota(jnp.int32, (CAP, ROWS), 0).astype(F32)

        def source(s, carry):
            m = moe[s]
            gates, slot = routing(rall[s], nt(router_t, m))
            picks = []
            for i in range(OWN):
                sel = row == first + i
                pick = jnp.sum(jnp.where(sel, slot, 0.0), axis=0, keepdims=True) == place_in
                gate = jnp.sum(jnp.where(sel, gates, 0.0), axis=0, keepdims=True)
                g = jnp.sum(jnp.where(pick, gate, 0.0), axis=1, keepdims=True)
                g_s[i, pl.ds(pl.multiple_of(s * CAP, 16), CAP)] = jnp.broadcast_to(g, (CAP, 128))
                picks.append(jnp.where(pick, 1.0, 0.0).astype(BF))
            pick = jnp.concatenate(picks, axis=0)
            p_o[s] = pick
            xs = nn(pick, m).astype(BF)
            ys = nn(pick, cot[s]).astype(BF)
            for i in range(OWN):
                at = pl.ds(pl.multiple_of(s * CAP, 16), CAP)
                x_s[i, at] = xs[CAP * i : CAP * i + CAP]
                y_s[i, at] = ys[CAP * i : CAP * i + CAP]
            return carry

        lax.fori_loop(0, EP, source, 0)

    x, y = x_s[j], y_s[j]
    gate = g_s[j][:, :1] * RES
    g = nn(x, wg[0])
    u = nn(x, wu[0])
    dh = nt(y, wd[0])
    s = 1.0 / (1.0 + jnp.exp(-g))
    silu = g * s
    h = silu * u
    gg_o[0] = jnp.broadcast_to(RES * jnp.sum(h * dh, axis=1, keepdims=True), (SLOTS, 128))
    dh = dh * gate
    hs = (h * gate).astype(BF)
    dg = (dh * u * s * (1.0 + g * (1.0 - s))).astype(BF)
    du = (dh * silu).astype(BF)
    hs_o[0], dg_o[0], du_o[0] = hs, dg, du
    w = tn(x, jnp.concatenate([dg, du], axis=1))
    dw_o[0, :D] = w[:, :F].astype(BF)
    dw_o[0, D : 2 * D] = w[:, F:].astype(BF)
    w = tn(hs, y)
    dw_o[0, 2 * D : 2 * D + F] = w[:, :F].astype(BF)
    dw_o[0, 2 * D + F :] = w[:, F:].astype(BF)


class Reduce:
    def __init__(self, chunk, me, ahead, behind, one, two, three, make):
        at = lambda k: lax.rem(me + k, 4)
        self.one, self.two, self.three = one, two, three
        self.first = [
            make(chunk(at(2), 0), one.at[0], ahead),
            make(chunk(at(2), 1), one.at[1], behind),
        ]
        self.second = [
            make(chunk(at(1), 1), two.at[0], ahead),
            make(chunk(at(3), 0), two.at[1], behind),
        ]
        self.third = [make(one.at[0], three.at[0], ahead), make(one.at[1], three.at[1], behind)]

    def start(self):
        for cp in self.first + self.second:
            cp.start()

    def go_on(self, k, mine, pieces):
        self.first[k].wait_recv()

        def add(i, carry):
            self.one[k, i] = self.one[k, i] + mine[i]
            return carry

        lax.fori_loop(0, pieces, add, 0)
        self.third[k].start()

    def arrived(self, k):
        self.second[1 - k].wait_recv()
        self.third[k].wait_recv()

    def sent(self):
        for cp in self.first + self.second + self.third:
            cp.wait_send()


def experts_combine(
    hs, dg, du, gg, picks, wg, wu, wd, dw, at, mg_o, gt_o, at_o, sh_o,
    eo_s, dx_s, gg_s, stage, buf, m1, m2, m3,
    a1, a2, a3, amine, ac, b1, b2, b3, bmine, bc, a4, a5, a6, b4, b5, b6, ls, ss, rs,
):
    j = pl.program_id(0)
    d, e, z, c = place()
    u, v = d // 4, lax.rem(d, 4)
    near = lambda k, n: lax.rem(k + n, 4)
    up, down = (near(u, 1) * 4 + v, e), (near(u, 3) * 4 + v, e)
    ahead, behind = (u * 4 + near(v, 1), e), (u * 4 + near(v, 3), e)
    right, left = (d, near(z, 1) * 2 + c), (d, near(z, 3) * 2 + c)
    other = (d, z * 2 + 1 - c)
    make = Sender(ss, rs)
    ring = Ring(at_o, at.at[0], at.at[1], d, e, z, c, make)
    half = lambda h: pl.ds(2 * h, 2)
    deep = lambda h: pl.ds(48 * h, 48)
    ra = Reduce(lambda i, h: dw.at[:, i, half(h), 0], u, up, down, a1, a2, a3, make)
    rb = Reduce(lambda i, h: dw.at[:, half(h), i, 1], v, ahead, behind, b1, b2, b3, make)
    qa = Reduce(lambda i, h: ac.at[:, i, deep(h)], v, ahead, behind, a4, a5, a6, make)
    qb = Reduce(lambda i, h: bc.at[:, i, deep(h)], u, up, down, b4, b5, b6, make)
    load = pltpu.make_async_copy
    own = [
        load(dw.at[:, near(u, 1), half(0), 0], amine.at[0], ls.at[0]),
        load(dw.at[:, near(u, 3), half(1), 0], amine.at[1], ls.at[1]),
        load(dw.at[:, half(0), near(v, 1), 1], bmine.at[0], ls.at[2]),
        load(dw.at[:, half(1), near(v, 3), 1], bmine.at[1], ls.at[3]),
        load(dw.at[:, u, :, 0], ac, ls.at[4]),
        load(dw.at[:, :, v, 1], bc, ls.at[5]),
        load(at, at_o.at[e], ls.at[6]),
    ]

    @pl.when(j == 0)
    def _():
        greet(ep_peers(d, e) + [up, down, ahead, behind])()
        ra.start()
        rb.start()
        ring.start(0)
        ring.start(1)
        for cp in own:
            cp.start()

    eo = nn(hs[0], wd[0]).astype(BF)
    dx = (nt(dg[0], wg[0]) + nt(du[0], wu[0])).astype(BF)
    for s in range(EP):
        row = pl.ds(pl.multiple_of(j * CAP, 16), CAP)
        eo_s[s, row] = eo[CAP * s : CAP * s + CAP]
        dx_s[s, row] = dx[CAP * s : CAP * s + CAP]

    @pl.when(j == 2)
    def _():
        ring.forward()

    @pl.when(j == OWN - 1)
    def _():
        for cp in own:
            cp.wait()
        for k in range(2):
            ra.go_on(k, amine.at[k], OWN)
            rb.go_on(k, bmine.at[k], OWN)

        def gate_rows(s):
            p = picks[s]
            row = pl.ds(pl.multiple_of(s * CAP, 16), CAP)
            rows = [
                jnp.sum(
                    p[CAP * i : CAP * i + CAP].astype(F32) * gg[i, row][:, :1], axis=0, keepdims=True
                )
                for i in range(OWN)
            ]
            gg_s[s] = jnp.concatenate(rows + [jnp.zeros((8 - OWN, ROWS), F32)], axis=0)

        turns = [near(z, k) * 2 for k in (2, 1, 3, 0)]
        mates = []
        for i, t in enumerate(turns):
            s = t + 1 - c
            stage[i, :, :D] = tn(picks[s], eo_s[s]).astype(BF)
            stage[i, :, D:] = tn(picks[s], dx_s[s]).astype(BF)
            mates.append(make.now(stage.at[i], buf.at[i], other))
        ring.finish()

        def add(i):
            s = turns[i] + c
            left_, right_ = tn(picks[s], eo_s[s]), tn(picks[s], dx_s[s])
            mates[i].wait_recv()
            buf[i, :, :D] = (buf[i, :, :D].astype(F32) + left_).astype(BF)
            buf[i, :, D:] = (buf[i, :, D:].astype(F32) + right_).astype(BF)

        lo, hi = slice(0, HALF), slice(HALF, ROWS)
        add(0)
        s1 = [make.now(buf.at[0, pl.ds(0, HALF)], m1.at[0], right)]
        s1.append(make.now(buf.at[0, pl.ds(HALF, HALF)], m1.at[1], left))
        add(1)
        s2 = [make.now(buf.at[1, pl.ds(HALF, HALF)], m2.at[0], right)]
        add(2)
        s2.append(make.now(buf.at[2, pl.ds(0, HALF)], m2.at[1], left))
        for s in range(EP):
            gate_rows(s)
        rows = [make.now(gg_s.at[p[1]], gt_o.at[e], p) for p in ep_peers(d, e)]
        gt_own = load(gg_s.at[e], gt_o.at[e], ls.at[7])
        gt_own.start()
        s1[0].wait_recv()
        m1[0] = m1[0] + buf[1, lo]
        s3 = [make.now(m1.at[0], m3.at[0], right)]
        s1[1].wait_recv()
        m1[1] = m1[1] + buf[2, hi]
        s3.append(make.now(m1.at[1], m3.at[1], left))
        add(3)

        def close(r, chunk):
            for k in range(2):
                r.arrived(k)

                def body(i, carry):
                    for q in range(2):
                        piece = r.two[1 - k, i, q].astype(F32) + r.three[k, i, q].astype(F32)
                        chunk[i, 2 * k + q] = (chunk[i, 2 * k + q].astype(F32) + piece).astype(BF)
                    return carry

                lax.fori_loop(0, OWN, body, 0)

        close(ra, ac)
        qa.start()
        close(rb, bc)
        qb.start()
        s2[1].wait_recv()
        s3[0].wait_recv()
        mg_o[lo] = buf[3, lo].astype(F32) + m2[1].astype(F32) + m3[0].astype(F32)
        s2[0].wait_recv()
        s3[1].wait_recv()
        mg_o[hi] = buf[3, hi].astype(F32) + m2[0].astype(F32) + m3[1].astype(F32)
        for q, chunk, me in ((qa, ac, v), (qb, bc, u)):
            for k in range(2):
                t = near(me, 1 + 2 * k)
                q.first[k].wait_recv()
                q.one[k] = q.one[k] + chunk[:, t, 48 * k : 48 * k + 48]
                q.third[k].start()
        for h, q, chunk, me in ((0, qa, ac, v), (1, qb, bc, u)):
            for k in range(2):
                q.arrived(k)
                mine = chunk[:, me, 48 * k : 48 * k + 48].astype(F32)
                total = mine + q.two[1 - k].astype(F32) + q.three[k].astype(F32)
                sh_o[:, h, 48 * k : 48 * k + 48] = total.astype(BF)
        for r in (ra, rb, qa, qb):
            r.sent()
        for cp in mates + s1 + s2 + s3:
            cp.wait_send()
        for cp in rows:
            cp.wait()
        gt_own.wait()


def norm_back(grad, values, factor, gain):
    scaled = grad * gain
    grad_gain = jnp.sum(grad * values * factor, axis=0, keepdims=True)
    mean = jnp.mean(scaled * values, axis=1, keepdims=True)
    return factor * (scaled - values * (factor * factor * mean)), grad_gain


def after_experts(mg, gg, rt, moe, mid, cot, gt, wo, out_o, gm_o, gb_o, da_o, st_o):
    m = mid[...]
    out_o[...] = (m + mg[:, :D]).astype(BF)
    router_t = gt[:EXPERTS].astype(BF)
    gates, _ = routing(rt, nt(router_t, moe[...]))
    back = gg[...][:, :OWN].reshape(EXPERTS, ROWS)
    both_ = gates * back
    gl = (both_ - gates * jnp.sum(both_, axis=0, keepdims=True)).astype(BF)
    st_o[...] = jnp.zeros_like(st_o)
    st_o[:EXPERTS] = nn(gl, moe[...])
    grad = mg[:, D:] + tn(gl, router_t)
    factor = lax.rsqrt(jnp.mean(m * m, axis=1, keepdims=True) + EPS)
    gm, gain = norm_back(grad, m, factor, gt[33:34])
    st_o[33:34] = gain
    gm = cot[...].astype(F32) + gm
    gm_o[...] = gm
    gb = (RES * gm).astype(BF)
    ga = nt(gb, wo[...]).astype(BF)
    for t in range(EP):
        gb_o[t] = gb[:, 128 * t : 128 * t + 128]
        da_o[t] = ga[:, 128 * t : 128 * t + 128]


def to_heads(da, gb, da_o, gb_o, ls, ss, rs):
    d, e, z, c = place()
    greet(ep_peers(d, e))()
    make = Sender(ss, rs)
    send = make.now
    own = [
        pltpu.make_async_copy(da.at[e], da_o.at[e], ls.at[0]),
        pltpu.make_async_copy(gb.at[e], gb_o.at[e], ls.at[1]),
    ]
    for cp in own:
        cp.start()
    cps = []
    for k in (4, 3, 5, 2, 6, 1, 7):
        t = lax.rem(e + k, EP)
        cps.append(send(da.at[t], da_o.at[e], (d, t)))
        cps.append(send(gb.at[t], gb_o.at[e], (d, t)))
    for cp in cps:
        cp.wait()
    for cp in own:
        cp.wait()


def attend_back(q, kv, nrm, att, lse, da, gb, at, cs, sn, ids, dq_o, dw_o, kk_s, vv_s, dk_s, dv_s):
    s = pl.program_id(0)
    kk_s[...], vv_s[...] = both(kv[0].astype(F32))
    dk_s[...] = jnp.zeros_like(dk_s)
    dv_s[...] = jnp.zeros_like(dv_s)
    ids_k = ids[0]
    ids_q = jnp.broadcast_to(ids_k, (128, LEN)).T[:, :1]
    low = lanes((ROWS, 128)) < HD

    def unturn(v, rows):
        return v * cs[rows] - turn(v) * sn[rows]

    dqs = []
    for i in range(4):
        rows = slice(ROWS * i, ROWS * i + ROWS)
        q2 = two_heads(q[0, rows].astype(F32)).astype(BF)
        o = da[2 * i : 2 * i + 2, 0].reshape(ROWS, 128).astype(F32)
        o2f = two_heads(o)
        o2 = o2f.astype(BF)
        a = att[2 * i : 2 * i + 2, 0].reshape(ROWS, 128).astype(F32)
        delta = jnp.sum(o2f * jnp.concatenate([a, a], axis=0), axis=1, keepdims=True)
        l2 = jnp.concatenate([lse[0, rows][:, :1], lse[0, rows][:, HD : HD + 1]], axis=0)
        own = ids_q[rows]
        own = jnp.concatenate([own, own], axis=0)
        at_, end = spans(i)
        dq = 0.0
        for span in ([slice(0, at_)] if at_ else []) + [slice(at_, end)]:
            t = nt(q2, kk_s[span]) * (SCORE * LOG2E) - l2
            if span.start == at_:
                t = jnp.where(ids_k[:, span] <= own, t, MASKED)
            p = jnp.exp2(t)
            gp = nt(o2, vv_s[span])
            ds = (p * (gp - delta)).astype(BF)
            dq = dq + nn(ds, kk_s[span])
            dk_s[span] += tn(ds, q2)
            dv_s[span] += tn(p.astype(BF), o2)
        dq = SCORE * jnp.where(low, dq[:ROWS], dq[ROWS:])
        dqs.append(unturn(dq, rows).astype(BF))
    w = []
    for i in range(4):
        rows = slice(ROWS * i, ROWS * i + ROWS)
        dk, dv = dk_s[rows], dv_s[rows]
        dk = unturn(SCORE * (dk + pltpu.roll(dk, HD, 1)), rows)
        dv = dv + pltpu.roll(dv, HD, 1)
        dkv = jnp.where(low, dk, dv).astype(BF)
        dqkv = jnp.concatenate([dqs[i], dkv], axis=1)
        dq_o[2 * i : 2 * i + 2, 0] = dqkv.reshape(2, HALF, 256)
        w.append(dqkv)
    wqkv = tn(nrm[0], jnp.concatenate(w, axis=0))
    wout = tn(at[:, 0].reshape(LEN, D), gb[:, 0].reshape(LEN, 128))
    w = jnp.concatenate([wqkv, wout], axis=1)

    @pl.when(s == 0)
    def _():
        dw_o[...] = w

    @pl.when(s == 1)
    def _():
        dw_o[...] += w


def to_tokens(dq, dq_o, ls, ss, rs):
    d, e, z, c = place()
    greet(ep_peers(d, e))()
    make = Sender(ss, rs)
    send = make.now
    own = pltpu.make_async_copy(dq.at[e], dq_o.at[e], ls.at[0])
    own.start()
    cps = []
    for k in (4, 3, 5, 2, 6, 1, 7):
        t = lax.rem(e + k, EP)
        cps.append(send(dq.at[t], dq_o.at[e], (d, t)))
    for cp in cps:
        cp.wait()
    own.wait()


def first_norm_back(dq, wf, x, gm, gt, st, dw, gx_o, pk_o):
    grad = 0.0
    for s in range(EP):
        grad = grad + nt(dq[s], wf[:, 256 * s : 256 * s + 256])
    v = x[...].astype(F32)
    factor = lax.rsqrt(jnp.mean(v * v, axis=1, keepdims=True) + EPS)
    g, gain = norm_back(grad, v, factor, gt[32:33])
    gx_o[...] = (gm[...] + g).astype(BF)
    row = lax.broadcasted_iota(jnp.int32, (128, D), 0)
    small = jnp.where(row == 32, gain, st[...]).T
    pk_o[0] = dw[:, :256].astype(BF).reshape(4, 4, 64, 256)
    w = jnp.concatenate([dw[:, 256:], small], axis=1).astype(BF)
    pk_o[1] = w.reshape(4, 4, 64, 256)


def sum_weights(pk, wq_o, wk_o, wv_o, wo_o, sm_o, ra, rb, ta, tb, qa, qb, s1, r2, ls, ss, rs):
    d, e, z, c = place()
    u, v = d // 4, lax.rem(d, 4)
    across = [(lax.rem(u + k, 4) * 4 + v, e) for k in (1, 3, 2)]
    along = [(u * 4 + lax.rem(v + k, 4), e) for k in (1, 3, 2)]
    greet(ep_peers(d, e) + across + along)()
    make = Sender(ss, rs)
    send = make.now
    own = [
        pltpu.make_async_copy(pk.at[0, u], ra.at[0], ls.at[0]),
        pltpu.make_async_copy(pk.at[1, :, v], rb.at[0], ls.at[1]),
    ]
    for cp in own:
        cp.start()
    a1, b1 = [], []
    for i, k in enumerate((1, 3, 2)):
        a1.append(send(pk.at[0, lax.rem(u + k, 4)], ra.at[1 + i], across[i]))
        b1.append(send(pk.at[1, :, lax.rem(v + k, 4)], rb.at[1 + i], along[i]))
    for cp in own:
        cp.wait()

    def total(r):
        return (r[0].astype(F32) + r[1].astype(F32)) + (r[2].astype(F32) + r[3].astype(F32))

    for cp in a1:
        cp.wait_recv()
    ta[...] = total(ra).astype(BF)
    a2 = [send(ta.at[lax.rem(v + k, 4)], qa.at[1 + i], along[i]) for i, k in enumerate((1, 3, 2))]
    qa[0] = ta[v]
    for cp in b1:
        cp.wait_recv()
    tb[...] = total(rb).astype(BF)
    b2 = [send(tb.at[lax.rem(u + k, 4)], qb.at[1 + i], across[i]) for i, k in enumerate((1, 3, 2))]
    qb[0] = tb[u]
    for cp in a2:
        cp.wait_recv()
    s1[:, :, :256] = total(qa).reshape(EP, 8, 256)
    for cp in b2:
        cp.wait_recv()
    s1[:, :, 256:] = total(qb).reshape(EP, 8, 256)
    r2[e] = s1[e]
    more = [send(s1.at[p[1]], r2.at[e], p) for p in ep_peers(d, e)]
    for cp in more:
        cp.wait_recv()
    small = r2[0, :, 384:]
    for s in range(1, EP):
        small = small + r2[s, :, 384:]
    sm_o[...] = small
    wq_o[...] = jnp.concatenate([r2[s, :, :128] for s in range(EP)], axis=1)
    wk_o[...] = jnp.concatenate([r2[s, :, 128:192] for s in range(EP)], axis=1)
    wv_o[...] = jnp.concatenate([r2[s, :, 192:256] for s in range(EP)], axis=1)
    wo_o[...] = jnp.concatenate([r2[s, :, 256:384] for s in range(EP)], axis=1)
    for cp in a1 + b1 + a2 + b2 + more:
        cp.wait_send()


def widen(dw, g_o, u_o, d_o):
    w = dw[...].reshape(3 * D, F).astype(F32)
    g_o[0] = w[:D]
    u_o[0] = w[D : 2 * D]
    d_o[0, :, :F] = w[2 * D : 2 * D + F]
    d_o[0, :, F:] = w[2 * D + F :]


def tables():
    even = np.arange(0, HD, 2).astype(np.float32)
    frequency = (np.float32(10000.0) ** (-even / np.float32(HD))).astype(np.float32)
    angle = np.arange(LEN, dtype=np.float32)[:, None] * frequency[None, :]
    angle = np.concatenate([angle] * 4, axis=1).astype(np.float64)
    return np.cos(angle).astype(np.float32), np.sin(angle).astype(np.float32)


def per_device(
    tokens, cotangent, block_ids, routes, w_query, w_key, w_value, w_output, w_router,
    gain_attn, gain_moe, expert_gate, expert_up, expert_down,
):
    x = tokens.reshape(ROWS, D)
    cot = cotangent.reshape(ROWS, D)
    rt = routes.reshape(ROWS, 8).T
    ids = block_ids.reshape(SEQS, 1, LEN)
    small = jnp.concatenate(
        [w_router, gain_attn[:, None], gain_moe[:, None], jnp.zeros((8, 222), BF)], axis=1
    )
    w_qkv = jnp.concatenate(
        [w_query.reshape(8, EP, 128), w_key.reshape(8, EP, HD), w_value.reshape(8, EP, HD)], axis=2
    ).reshape(8, 2 * D)
    cos, sin = tables()
    cos, sin = jnp.asarray(cos), jnp.asarray(sin)
    params = pltpu.CompilerParams(vmem_limit_bytes=60 * MIB)
    once = pl.Buffered(1)

    def whole(shape):
        return pl.BlockSpec(shape, lambda s: (0,) * len(shape), pipeline_mode=once)

    xall, rall, wsl, wof = remote_call(
        gather_inputs, 1,
        [
            sds((EP, 2, HALF, D), BF), sds((EP, 8, ROWS), jnp.int32),
            sds((4, 4, EP, 16, 256), BF), sds((4, 4, EP, 16, 512), BF),
        ],
        [tokens.reshape(2, HALF, D), rt, w_qkv, w_output, small],
        [ANY] + [VM] * 4,
        [pltpu.VMEM((EP, 16, 256), BF), pltpu.VMEM((16, 512), BF)],
        64,
    )
    cot_all = lax.all_gather(cot, "ep", axis=0)
    w_late, xall = lax.optimization_barrier((w_qkv, xall))
    w_full = lax.all_gather(w_late, ("dp", "ep"), axis=0, tiled=True)

    seq = lambda *shape: pl.BlockSpec((1, *shape), lambda s: (s,) + (0,) * len(shape))
    cut = lambda n: pl.BlockSpec((EP, 1, HALF, n), lambda s: (0, s, 0, 0))
    q, kv, nrm, att, lse, gt, wo = pl.pallas_call(
        project_attend,
        name="project_attend",
        grid=(SEQS,),
        out_shape=[
            sds((SEQS, LEN, 128), BF), sds((SEQS, LEN, 128), BF), sds((SEQS, LEN, D), BF),
            sds((EP, 2, HALF, 128), BF), sds((SEQS, LEN, 128), F32), sds((128, D), F32),
            sds((D, D), BF),
        ],
        in_specs=[
            cut(D), whole((4, 4, EP, 16, 256)), whole((4, 4, EP, 16, 512)), whole((LEN, 128)),
            whole((LEN, 128)), seq(1, LEN),
        ],
        out_specs=[
            seq(LEN, 128), seq(LEN, 128), seq(LEN, D), cut(128), seq(LEN, 128), whole((128, D)),
            whole((D, D)),
        ],
        scratch_shapes=[
            pltpu.VMEM((D, 256), BF), pltpu.VMEM((D, 128), F32), pltpu.VMEM((LEN, 128), BF),
            pltpu.VMEM((LEN, 128), BF),
        ],
        compiler_params=params,
    )(xall, wsl, wof, cos, sin, ids)

    moe, mid, moe_own, at_own = remote_call(
        attended_to_moe, 2,
        [sds((EP, 2, HALF, D), BF), sds((ROWS, D), F32), sds((ROWS, D), BF), sds((ROWS, D), BF)],
        [att.reshape(EP, ROWS, 128), x, wo, gt],
        [ANY, VM, VM, VM],
        [pltpu.VMEM((EP, ROWS, 128), BF), pltpu.VMEM((2, HALF, D), BF)],
        24,
        [ANY, VM, VM, VM],
    )

    each = lambda *shape: pl.BlockSpec((1, *shape), lambda j: (j,) + (0,) * len(shape))
    dw, hs, dg, du, gg, picks = pl.pallas_call(
        experts_weights,
        name="experts_weights",
        grid=(OWN,),
        out_shape=[
            sds((OWN, 3 * D, F), BF), sds((OWN, SLOTS, F), BF), sds((OWN, SLOTS, F), BF),
            sds((OWN, SLOTS, F), BF), sds((OWN, SLOTS, 128), F32), sds((EP, OWN * CAP, ROWS), BF),
        ],
        in_specs=[
            whole((EP, ROWS, D)), whole((EP, ROWS, D)), whole((EP, 8, ROWS)), whole((128, D)),
            each(D, F), each(D, F), each(F, D),
        ],
        out_specs=[
            each(3 * D, F), each(SLOTS, F), each(SLOTS, F), each(SLOTS, F), each(SLOTS, 128),
            whole((EP, OWN * CAP, ROWS)),
        ],
        scratch_shapes=[
            pltpu.VMEM((OWN, SLOTS, D), BF), pltpu.VMEM((OWN, SLOTS, D), BF),
            pltpu.VMEM((OWN, SLOTS, 128), F32),
        ],
        compiler_params=params,
    )(moe.reshape(EP, ROWS, D), cot_all, rall, gt, expert_gate, expert_up, expert_down)

    mg, gg_all, at_all, shard = pl.pallas_call(
        experts_combine,
        name="experts_combine",
        grid=(OWN,),
        out_shape=[
            sds((ROWS, 2 * D), F32), sds((EP, 8, ROWS), F32), sds((EP, 2, HALF, D), BF),
            sds((OWN, 2, 96, F), BF),
        ],
        in_specs=[
            each(SLOTS, F), each(SLOTS, F), each(SLOTS, F), whole((OWN, SLOTS, 128)),
            whole((EP, OWN * CAP, ROWS)), each(D, F), each(D, F), each(F, D), ANY, ANY,
        ],
        out_specs=[whole((ROWS, 2 * D)), ANY, ANY, whole((OWN, 2, 96, F))],
        scratch_shapes=[
            pltpu.VMEM((EP, OWN * CAP, D), BF), pltpu.VMEM((EP, OWN * CAP, D), BF),
            pltpu.VMEM((EP, 8, ROWS), F32),
            pltpu.VMEM((4, ROWS, 2 * D), BF), pltpu.VMEM((4, ROWS, 2 * D), BF),
            *[pltpu.VMEM((2, HALF, 2 * D), BF)] * 3,
            *([pltpu.VMEM((2, OWN, 2, 96, F), BF)] * 4 + [pltpu.VMEM((OWN, 4, 96, F), BF)]) * 2,
            *[pltpu.VMEM((2, OWN, 48, F), BF)] * 6,
            pltpu.SemaphoreType.DMA((8,)),
            pltpu.SemaphoreType.DMA((64,)),
            pltpu.SemaphoreType.DMA((64,)),
        ],
        compiler_params=pltpu.CompilerParams(
            collective_id=3, has_side_effects=True, vmem_limit_bytes=62 * MIB
        ),
    )(
        hs, dg, du, gg, picks, expert_gate, expert_up, expert_down,
        dw.reshape(OWN, 4, 4, 2, 96, F), at_own.reshape(2, HALF, D),
    )
    dw_sum = lax.all_gather(shard.reshape(OWN, 192, F), "dp", axis=0)

    output, gm, gb, da, st = pl.pallas_call(
        after_experts,
        name="after_experts",
        out_shape=[
            sds((ROWS, D), BF), sds((ROWS, D), F32), sds((EP, ROWS, 128), BF),
            sds((EP, ROWS, 128), BF), sds((128, D), F32),
        ],
        in_specs=[VM] * 8,
        out_specs=[VM] * 5,
        compiler_params=params,
    )(mg, gg_all, rt, moe_own, mid, cot, gt, wo)

    da_all, gb_all = remote_call(
        to_heads, 4, [sds((EP, ROWS, 128), BF)] * 2, [da, gb], [ANY] * 2, [], 16
    )

    dq, dw_attn = pl.pallas_call(
        attend_back,
        name="attend_back",
        grid=(SEQS,),
        out_shape=[sds((EP, 2, HALF, 256), BF), sds((D, 384), F32)],
        in_specs=[
            seq(LEN, 128), seq(LEN, 128), seq(LEN, D), cut(128), seq(LEN, 128), cut(128),
            cut(128), cut(D), whole((LEN, 128)), whole((LEN, 128)), seq(1, LEN),
        ],
        out_specs=[cut(256), whole((D, 384))],
        scratch_shapes=[
            pltpu.VMEM((LEN, 128), BF), pltpu.VMEM((LEN, 128), BF),
            pltpu.VMEM((LEN, 128), F32), pltpu.VMEM((LEN, 128), F32),
        ],
        compiler_params=params,
    )(
        q, kv, nrm, att, lse, da_all.reshape(EP, 2, HALF, 128), gb_all.reshape(EP, 2, HALF, 128),
        at_all, cos, sin, ids,
    )

    (dq_all,) = remote_call(
        to_tokens, 5, [sds((EP, ROWS, 256), BF)], [dq.reshape(EP, ROWS, 256)], [ANY], [], 8
    )

    grad_x, packed = pl.pallas_call(
        first_norm_back,
        name="first_norm_back",
        out_shape=[sds((ROWS, D), BF), sds((2, 4, 4, 64, 256), BF)],
        in_specs=[VM] * 7,
        out_specs=[VM] * 2,
        compiler_params=params,
    )(dq_all, w_full, x, gm, gt, st, dw_attn)

    gq, gk, gv, go, gs = remote_call(
        sum_weights, 6,
        [sds((8, D), F32), sds((8, 512), F32), sds((8, 512), F32), sds((8, D), F32), sds((8, 128), F32)],
        [packed],
        [ANY],
        [
            pltpu.VMEM((4, 4, 64, 256), BF), pltpu.VMEM((4, 4, 64, 256), BF),
            pltpu.VMEM((4, 64, 256), BF), pltpu.VMEM((4, 64, 256), BF),
            pltpu.VMEM((4, 64, 256), BF), pltpu.VMEM((4, 64, 256), BF),
            pltpu.VMEM((EP, 8, 512), F32), pltpu.VMEM((EP, 8, 512), F32),
        ],
        24,
        [VM] * 5,
    )

    g_gate, g_up, g_down = pl.pallas_call(
        widen,
        name="widen",
        grid=(OWN,),
        out_shape=[sds((OWN, D, F), F32), sds((OWN, D, F), F32), sds((OWN, F, D), F32)],
        in_specs=[pl.BlockSpec((DP, 1, 192, F), lambda j: (0, j, 0, 0))],
        out_specs=[each(D, F), each(D, F), each(F, D)],
        compiler_params=params,
    )(dw_sum)
    return (
        output.reshape(tokens.shape),
        grad_x.reshape(tokens.shape),
        gq,
        gk,
        gv,
        go,
        gs[:, :EXPERTS],
        gs[:, 32],
        gs[:, 33],
        g_gate,
        g_up,
        g_down,
    )


def solution(mesh):
    rows, own, both_axes = P("dp", "ep", None), P("ep", None, None), P(("dp", "ep"), None)
    line = P(("dp", "ep"))
    return jax.shard_map(
        per_device,
        mesh=mesh,
        in_specs=(
            rows, rows, P("dp", None), rows, both_axes, both_axes, both_axes, both_axes, both_axes,
            line, line, own, own, own,
        ),
        out_specs=(
            rows, rows, both_axes, both_axes, both_axes, both_axes, both_axes, line, line, own,
            own, own,
        ),
        check_vma=False,
    )
```

```python
import math

import jax
import jax.numpy as jnp
import numpy as np
from jax import lax
from jax.experimental import pallas as pl
from jax.experimental.pallas import tpu as pltpu
from jax.sharding import PartitionSpec as P

MESH = pl.DeviceIdType.MESH
BF = jnp.bfloat16
F32 = jnp.float32
ANY = pl.BlockSpec(memory_space=pl.ANY)
VM = pl.BlockSpec(memory_space=pltpu.VMEM)

DP, EP, CHIPS = 16, 8, 4
D, HD, F = 1024, 64, 512
ROWS, HALF, LEN, SEQS = 256, 128, 1024, 2
EXPERTS, OWN, CAP = 32, 4, 80
SLOTS = EP * CAP
EPS = 1e-6
RES = 0.22
SCORE = 0.015625
LOG2E = 1.4426950408889634
MASKED = -1e30
MIB = 2**20


def nt(a, b):
    return lax.dot_general(a, b, (((1,), (1,)), ((), ())), preferred_element_type=F32)


def nn(a, b):
    return jnp.dot(a, b, preferred_element_type=F32)


def tn(a, b):
    return lax.dot_general(a, b, (((0,), (0,)), ((), ())), preferred_element_type=F32)


def place():
    e = lax.axis_index("ep")
    return lax.axis_index("dp"), e, e // 2, lax.rem(e, 2)


def near(k, n):
    return lax.rem(k + n, 4)


def plane(d, e):
    u, v = d // 4, lax.rem(d, 4)
    up, down = (near(u, 1) * 4 + v, e), (near(u, 3) * 4 + v, e)
    return u, v, up, down, (u * 4 + near(v, 1), e), (u * 4 + near(v, 3), e)


def pair(h):
    return pl.ds(2 * h, 2)


def greet(peers):
    b = pltpu.get_barrier_semaphore()
    for p in peers:
        pl.semaphore_signal(b, inc=1, device_id=p, device_id_type=MESH)
    return lambda: pl.semaphore_wait(b, len(peers))


def ep_peers(d, e):
    return [(d, lax.rem(e + k, EP)) for k in range(1, EP)]


def dp_peers(d, e):
    return [(lax.rem(d + k, DP), e) for k in range(1, DP)]


class Sender:
    def __init__(self, ss, rs):
        self.ss, self.rs, self.n = ss, rs, 0

    def __call__(self, src, dst, dev):
        i = self.n
        self.n += 1
        return pltpu.make_async_remote_copy(
            src, dst, self.ss.at[i], self.rs.at[i], device_id=dev, device_id_type=MESH
        )

    def now(self, src, dst, dev):
        cp = self(src, dst, dev)
        cp.start()
        return cp


class Ring:
    def __init__(self, out, src, d, e, z, c, make):
        right, left = (d, lax.rem(z + 1, CHIPS) * 2 + c), (d, lax.rem(z + 3, CHIPS) * 2 + c)
        part = (d, z * 2 + 1 - c)
        er, el, eo = right[1], left[1], lax.rem(z + 2, CHIPS) * 2 + c
        self.near = [
            [make(src(0), out(e, 0), right), make(src(0), out(e, 0), left)],
            [make(src(1), out(e, 1), left), make(src(1), out(e, 1), right)],
        ]
        self.mate = [make(src(0), out(e, 0), part), make(src(1), out(e, 1), part)]
        self.far = [make(out(el, 0), out(el, 0), right), make(out(er, 1), out(er, 1), left)]
        self.share = [
            make(out(s, h), out(s, h), part)
            for s, h in ((el, 0), (er, 1), (el, 1), (er, 0), (eo, 0), (eo, 1))
        ]

    def start(self, h):
        for cp in self.near[h]:
            cp.start()
        self.mate[h].start()

    def forward(self):
        for h in range(2):
            self.near[h][0].wait_recv()
            self.far[h].start()
            self.share[h].start()
        for h in range(2):
            self.near[1 - h][1].wait_recv()
            self.share[2 + h].start()

    def finish(self):
        for h in range(2):
            self.far[h].wait_recv()
            self.share[4 + h].start()
        for cp in self.near[0] + self.near[1] + self.far:
            cp.wait_send()
        for cp in self.mate + self.share:
            cp.wait()


class Quad:
    def __init__(self, out, me, ahead, behind, make):
        after, before = lax.rem(me + 1, 4), lax.rem(me + 3, 4)
        mine = lambda h, dev: make(out(me, h), out(me, h), dev)
        self.near = [
            [mine(0, ahead), mine(0, behind)],
            [mine(1, behind), mine(1, ahead)],
        ]
        self.far = [
            make(out(before, 0), out(before, 0), ahead),
            make(out(after, 1), out(after, 1), behind),
        ]

    def start(self):
        for h in range(2):
            for cp in self.near[h]:
                cp.start()

    def forward(self):
        for h in range(2):
            self.near[h][0].wait_recv()
            self.far[h].start()

    def arrived(self):
        for h in range(2):
            self.near[h][1].wait_recv()
        for h in range(2):
            self.far[h].wait_recv()

    def sent(self):
        for cp in self.near[0] + self.near[1] + self.far:
            cp.wait_send()


def remote_call(body, cid, outs, ins, specs, scratch, sems, out_specs=None, vmem=48, flops=0):
    return pl.pallas_call(
        body,
        name=body.__name__,
        out_shape=outs,
        in_specs=specs,
        out_specs=out_specs if out_specs is not None else [ANY] * len(outs),
        scratch_shapes=[
            *scratch,
            pltpu.SemaphoreType.DMA((9,)),
            pltpu.SemaphoreType.DMA((sems,)),
            pltpu.SemaphoreType.DMA((sems,)),
        ],
        compiler_params=pltpu.CompilerParams(
            collective_id=cid, has_side_effects=True, vmem_limit_bytes=vmem * MIB
        ),
        cost_estimate=pl.CostEstimate(flops=flops, bytes_accessed=20 * MIB, transcendentals=0),
    )(*ins)


def sds(shape, dtype):
    return jax.ShapeDtypeStruct(shape, dtype)


def lanes(shape):
    return lax.broadcasted_iota(jnp.int32, shape, 1)


def turn(v):
    first = lax.rem(lanes(v.shape), HD) < HD // 2
    return jnp.where(first, -pltpu.roll(v, 128 - HD // 2, 1), pltpu.roll(v, HD // 2, 1))


def both(kv):
    low = lanes(kv.shape) < HD
    other = pltpu.roll(kv, HD, 1)
    return jnp.where(low, kv, other).astype(BF), jnp.where(low, other, kv).astype(BF)


def two_heads(v):
    low = lanes(v.shape) < HD
    zero = jnp.zeros_like(v)
    return jnp.concatenate([jnp.where(low, v, zero), jnp.where(low, zero, v)], axis=0)


def spans(i):
    return i * ROWS, min(LEN, i * ROWS + 2 * ROWS)


def before_experts(
    x, rt, w_q, w_k, w_v, wo, wr, ga, gm, cs, sn, ids,
    rall, q_o, kv_o, nrm_o, att_o, lse_o, gt_o, wo_o, moe, mid_o, own_o, at_o,
    xall, wsl, wof, wp, wop, gp, gb, gs, w_s, sm_s, kk_s, vv_s, arr, mo, ls, ss, rs,
):
    d, e, z, c = place()
    u, v, up, down, ahead, behind = plane(d, e)
    across = [up, down, (near(u, 2) * 4 + v, e)]
    along = [ahead, behind, (u * 4 + near(v, 2), e)]
    wait = greet(ep_peers(d, e) + across + along)
    q, k, w = w_q[...].astype(F32), w_k[...].astype(F32), w_v[...].astype(F32)
    diagonal = lax.broadcasted_iota(jnp.int32, (8, 8), 0) == lanes((8, 8))
    column = lambda g: jnp.sum(jnp.where(diagonal, g[...].astype(F32), 0.0), axis=1, keepdims=True)
    for t in range(EP):
        kv = [k[:, 64 * t : 64 * t + 64], w[:, 64 * t : 64 * t + 64]]
        row = jnp.concatenate([q[:, 128 * t : 128 * t + 128], jnp.concatenate(kv, axis=1)], axis=0)
        wp[t] = row.astype(BF)
    w, r = wo[...].astype(F32), wr[...].astype(F32)
    left = jnp.concatenate([w[:, :512], r, jnp.zeros((8, 96), F32)], axis=1)
    right = jnp.concatenate([w[:, 512:], column(ga), column(gm), jnp.zeros((8, 126), F32)], axis=1)
    wop[...] = jnp.concatenate([left, right], axis=0).astype(BF)
    spread = lax.broadcasted_iota(jnp.int32, (8, 128), 1) - 8 * e
    spread = spread == lax.broadcasted_iota(jnp.int32, (8, 128), 0)
    line = jnp.sum(jnp.where(spread, column(ga), 0.0), axis=0, keepdims=True)
    gp[...] = jnp.broadcast_to(line, (8, 128))
    wait()
    make = Sender(ss, rs)
    send = make.now
    own = [
        pltpu.make_async_copy(x, xall.at[e], ls.at[0]),
        pltpu.make_async_copy(wp.at[e], wsl.at[v, u, e], ls.at[1]),
        pltpu.make_async_copy(wop, wof.at[u, v, e], ls.at[2]),
        pltpu.make_async_copy(rt, rall.at[e], ls.at[3]),
        pltpu.make_async_copy(gp, gb.at[e], ls.at[8]),
    ]
    for cp in own:
        cp.start()
    tokens = [
        Ring(lambda s, k: xall.at[s, h, k], lambda k: x.at[h, k], d, e, z, c, make) for h in range(2)
    ]
    moes = [
        Ring(lambda s, k: moe.at[s, h, k], lambda k: mo.at[h, k], d, e, z, c, make) for h in range(2)
    ]
    gains = [send(gp, gb.at[e], p) for p in ep_peers(d, e)]
    first = [send(wp.at[p[1]], wsl.at[v, u, e], p) for p in ep_peers(d, e)]
    first += [send(wop, wof.at[u, v, e], p) for p in ep_peers(d, e)]
    tokens[0].start(0)
    tokens[0].start(1)
    own[1].wait()
    for cp in first[: EP - 1]:
        cp.wait_recv()
    w1 = [send(wsl.at[v, u], wsl.at[v, u], p) for p in across]
    own[4].wait()
    for cp in gains:
        cp.wait_recv()
    line = gb[0]
    for s in range(1, EP):
        line = line + gb[s]
    gs[v, u] = line
    g1 = [send(gs.at[v, u], gs.at[v, u], p) for p in across]
    own[2].wait()
    for cp in first[EP - 1 :]:
        cp.wait_recv()
    mine = pl.ds(c * 4, 4)
    part = (d, z * 2 + 1 - c)
    o1 = [send(wof.at[u, v, mine], wof.at[u, v, mine], p) for p in along]
    tokens[0].forward()
    for cp in w1:
        cp.wait_recv()
    w2 = Quad(lambda i, h: wsl.at[i, pair(h)], v, ahead, behind, make)
    w2.start()
    for cp in g1:
        cp.wait_recv()
    g2 = [send(gs.at[v], gs.at[v], p) for p in along]
    last = []
    for k, cp in zip((1, 3, 2), o1):
        cp.wait_recv()
        t = lax.rem(v + 4 - k, 4)
        last.append(send(wof.at[u, t, mine], wof.at[u, t, mine], part))
    o2 = Quad(lambda i, h: wof.at[i, :, pl.ds(c * 4 + 2 * h, 2)], u, up, down, make)
    o2.start()
    tokens[1].start(0)
    tokens[1].start(1)
    w2.forward()
    tokens[0].finish()
    own[0].wait()
    w2.arrived()
    for cp in g2:
        cp.wait_recv()
    for i in range(DP):
        w = wsl[i % 4, i // 4].astype(F32)
        w = jnp.concatenate([w[:, :8].reshape(64, 128), w[:, 8:].reshape(64, 128)], axis=1)
        w_s[64 * i : 64 * i + 64] = w.astype(BF)
    gain_a = jnp.concatenate([gs[i % 4, i // 4][:1, :64] for i in range(DP)], axis=1)

    def project(h):
        for r in range(4):
            rows = slice(256 * r, 256 * r + 256)
            t = xall[2 * r : 2 * r + 2, h].astype(F32).reshape(256, D)
            factor = lax.rsqrt(jnp.mean(t * t, axis=1, keepdims=True) + EPS)
            n = (t * factor * gain_a).astype(BF)
            nrm_o[h, rows] = n
            pre = nn(n, w_s[...])
            co, si = cs[rows], sn[rows]
            q, kv = pre[:, :128], pre[:, 128:]
            q_o[h, rows] = (q * co + turn(q) * si).astype(BF)
            kv = jnp.where(lanes(kv.shape) < HD, kv * co + turn(kv) * si, kv).astype(BF)
            kv_o[h, rows] = kv
            kk_s[rows], vv_s[rows] = both(kv.astype(F32))

    def attend(h, i):
        ids_k = ids[h : h + 1]
        ids_q = jnp.broadcast_to(ids_k[:, ROWS * i : ROWS * i + ROWS], (128, ROWS)).T[:, :1]
        q2 = two_heads(q_o[h, ROWS * i : ROWS * i + ROWS].astype(F32)).astype(BF)
        own_ids = jnp.concatenate([ids_q, ids_q], axis=0)
        at, end = spans(i)
        parts = []
        if at:
            parts.append((nt(q2, kk_s[:at]) * (SCORE * LOG2E), slice(0, at)))
        t = nt(q2, kk_s[at:end]) * (SCORE * LOG2E)
        parts.append((jnp.where(ids_k[:, at:end] <= own_ids, t, MASKED), slice(at, end)))
        peak = parts[0][0].max(axis=1, keepdims=True)
        for t, _ in parts[1:]:
            peak = jnp.maximum(peak, t.max(axis=1, keepdims=True))
        total, out = 0.0, 0.0
        for t, span in parts:
            p = jnp.exp2(t - peak)
            total = total + p.sum(axis=1, keepdims=True)
            out = out + nn(p.astype(BF), vv_s[span])
        out = out * (1.0 / total)
        lse = jnp.broadcast_to(peak + jnp.log2(total), (2 * ROWS, 128))
        low = lanes((ROWS, 128)) < HD
        att = jnp.where(low, out[:ROWS], out[ROWS:]).astype(BF)
        att_o[2 * i : 2 * i + 2, h] = att.reshape(2, HALF, 128)
        lse_o[h, ROWS * i : ROWS * i + ROWS] = jnp.where(low, lse[:ROWS], lse[ROWS:])

    att_own = [pltpu.make_async_copy(att_o.at[e, h], arr.at[e, h], ls.at[4 + h]) for h in range(2)]
    moe_own = [pltpu.make_async_copy(mo.at[h], moe.at[e, h], ls.at[6 + h]) for h in range(2)]

    def exchange(h):
        att_own[h].start()
        cps = []
        for k in (4, 3, 5, 2, 6, 1, 7):
            t = lax.rem(e + k, EP)
            cps.append(send(att_o.at[t, h], arr.at[e, h], (d, t)))
        return cps

    def branch(h, cps):
        att_own[h].wait()
        for cp in cps:
            cp.wait_recv()
        a = jnp.concatenate([arr[s, h] for s in range(EP)], axis=1)
        at_o[h] = a
        m = xall[e, h].astype(F32).reshape(HALF, D) + RES * nn(a, wo_o[...])
        mid_o[h] = m
        factor = lax.rsqrt(jnp.mean(m * m, axis=1, keepdims=True) + EPS)
        n = (m * factor * gt_o[33:34, :]).astype(BF)
        own_o[h] = n
        mo[h] = n.reshape(2, HALF // 2, D)
        moe_own[h].start()
        moes[h].start(0)
        moes[h].start(1)

    project(0)
    tokens[1].forward()
    attend(0, 0)
    attend(0, 1)
    o2.forward()
    attend(0, 2)
    attend(0, 3)
    x0 = exchange(0)
    tokens[1].finish()
    project(1)
    attend(1, 0)
    attend(1, 1)
    attend(1, 2)
    attend(1, 3)
    x1 = exchange(1)
    o2.arrived()
    for k in (1, 3, 2):
        t = near(u, k)
        last.append(send(wof.at[t, :, mine], wof.at[t, :, mine], part))
    routes = [send(rt, rall.at[e], p) for p in ep_peers(d, e)]
    for cp in last:
        cp.wait_recv()
    for i in range(4):
        rows = slice(256 * i, 256 * i + 256)
        o = wof[i].astype(F32).reshape(32, 16, 640)
        left, right = o[:, :8].reshape(256, 640), o[:, 8:].reshape(256, 640)
        wo_o[rows, :512] = left[:, :512].astype(BF)
        wo_o[rows, 512:] = right[:, :512].astype(BF)
        sm_s[rows] = jnp.where(lanes((256, 128)) < 32, left[:, 512:], pltpu.roll(right[:, 512:], 32, 1))
    gt_o[...] = sm_s[...].T
    branch(0, x0)
    branch(1, x1)
    moes[0].forward()
    moes[1].forward()
    moes[0].finish()
    moes[1].finish()
    w2.sent()
    o2.sent()
    for cp in gains + first + w1 + g1 + g2 + o1 + last + x0 + x1:
        cp.wait_send()
    for cp in routes:
        cp.wait()
    own[3].wait()
    for cp in moe_own:
        cp.wait()


def routing(rt, logits_t):
    ids = lax.broadcasted_iota(jnp.int32, (EXPERTS, ROWS), 0)
    hit = rt[0:1] == ids
    for k in range(1, 8):
        hit = hit | (rt[k : k + 1] == ids)
    w = jnp.where(hit, logits_t, MASKED)
    w = jnp.where(hit, jnp.exp(w - w.max(axis=0, keepdims=True)), 0.0)
    gates = w / w.sum(axis=0, keepdims=True)
    earlier = lax.broadcasted_iota(jnp.int32, (ROWS, ROWS), 0) < lax.broadcasted_iota(
        jnp.int32, (ROWS, ROWS), 1
    )
    slot = nn(jnp.where(hit, 1.0, 0.0).astype(BF), jnp.where(earlier, 1.0, 0.0).astype(BF))
    return gates, jnp.where(hit, slot, -1.0)


class Reduce:
    def __init__(self, chunk, me, ahead, behind, one, two, three, make):
        at = lambda k: lax.rem(me + k, 4)
        self.one, self.two, self.three = one, two, three
        self.first = [
            make(chunk(at(2), 0), one.at[0], ahead),
            make(chunk(at(2), 1), one.at[1], behind),
        ]
        self.second = [
            make(chunk(at(1), 1), two.at[0], ahead),
            make(chunk(at(3), 0), two.at[1], behind),
        ]
        self.third = [make(one.at[0], three.at[0], ahead), make(one.at[1], three.at[1], behind)]

    def start(self):
        for cp in self.first + self.second:
            cp.start()

    def go_on(self, k, mine, pieces):
        self.first[k].wait_recv()

        def add(i, carry):
            self.one[k, i] = self.one[k, i] + (mine[i] if pieces > 1 else mine[...])
            return carry

        lax.fori_loop(0, pieces, add, 0)
        self.third[k].start()

    def arrived(self, k):
        self.second[1 - k].wait_recv()
        self.third[k].wait_recv()

    def sent(self):
        for cp in self.first + self.second + self.third:
            cp.wait_send()


def close(r, chunk, pieces):
    for k in range(2):
        r.arrived(k)

        def body(i, carry):
            for q in range(2):
                piece = r.two[1 - k, i, q].astype(F32) + r.three[k, i, q].astype(F32)
                chunk[i, 2 * k + q] = (chunk[i, 2 * k + q].astype(F32) + piece).astype(BF)
            return carry

        lax.fori_loop(0, pieces, body, 0)


def experts_weights(
    moe, cot, at, rall, gt, wg, wu, wd, dw_o, eo_o, dg_o, du_o, gg_o, p_o, ca_o, cb_o, at_o,
    cot_s, x_s, y_s, gate_s, a_s, b_s, h_s, dw_s, a1, a2, a3, b1, b2, b3, ls, ss, rs,
):
    step = pl.program_id(0)
    d, e, z, c = place()
    u, v, up, down, ahead, behind = plane(d, e)
    first = e * OWN
    make = Sender(ss, rs)
    cots = Ring(lambda s, k: cot_s.at[s, k], lambda k: cot.at[k], d, e, z, c, make)
    ats = Ring(lambda s, k: at_o.at[s, k], lambda k: at.at[k], d, e, z, c, make)
    ra = Reduce(lambda i, h: dw_s.at[:, i, pair(h), 0], u, up, down, a1, a2, a3, make)
    rb = Reduce(lambda i, h: dw_s.at[:, pair(h), i, 1], v, ahead, behind, b1, b2, b3, make)
    own = pltpu.make_async_copy(cot, cot_s.at[e], ls.at[0])
    own_at = pltpu.make_async_copy(at, at_o.at[e], ls.at[2])
    rows_of = lambda s: pl.ds(pl.multiple_of(s * CAP, 16), CAP)

    @pl.when(step == 0)
    def _():
        load = pltpu.make_async_copy(moe, y_s.at[pl.ds(0, EP * ROWS)], ls.at[1])
        load.start()
        greet(ep_peers(d, e) + [up, down, ahead, behind])()
        cots.start(0)
        cots.start(1)
        own.start()
        own_at.start()
        load.wait()
        router_t = gt[:EXPERTS].astype(BF)
        row = lax.broadcasted_iota(jnp.int32, (EXPERTS, ROWS), 0)
        place_in = lax.broadcasted_iota(jnp.int32, (CAP, ROWS), 0).astype(F32)

        def source(s, carry):
            m = y_s[pl.ds(pl.multiple_of(s * ROWS, ROWS), ROWS)]
            gates, slot = routing(rall[s], nt(router_t, m))
            picks = []
            for i in range(OWN):
                sel = row == first + i
                pick = jnp.sum(jnp.where(sel, slot, 0.0), axis=0, keepdims=True) == place_in
                gate = jnp.sum(jnp.where(sel, gates, 0.0), axis=0, keepdims=True)
                g = jnp.sum(jnp.where(pick, gate, 0.0), axis=1, keepdims=True)
                gate_s[i, rows_of(s)] = jnp.broadcast_to(g, (CAP, 128))
                picks.append(jnp.where(pick, 1.0, 0.0).astype(BF))
            pick = jnp.concatenate(picks, axis=0)
            p_o[s] = pick
            xs = nn(pick, m).astype(BF)
            for i in range(OWN):
                x_s[i, rows_of(s)] = xs[CAP * i : CAP * i + CAP]
            return carry

        lax.fori_loop(0, EP, source, 0)

    @pl.when(step < OWN)
    def _():
        x = x_s[step]
        gate = gate_s[step][:, :1] * RES
        g = nn(x, wg[0])
        u = nn(x, wu[0])
        s = 1.0 / (1.0 + jnp.exp(-g))
        silu = g * s
        a_s[step] = (u * s * (1.0 + g * (1.0 - s))).astype(BF)
        b_s[step] = silu.astype(BF)
        h = silu * u
        h_s[step] = h.astype(BF)
        eo = nn((h * gate).astype(BF), wd[0]).astype(BF)
        for i in range(EP):
            eo_o[i, rows_of(step)] = eo[CAP * i : CAP * i + CAP]

    @pl.when(step == 2)
    def _():
        cots.forward()
        ats.start(0)
        ats.start(1)

    @pl.when(step == OWN)
    def _():
        cots.finish()
        own.wait()

        def source(s, carry):
            ys = nn(p_o[s], cot_s[s].reshape(ROWS, D)).astype(BF)
            for i in range(OWN):
                at = pl.ds(pl.multiple_of(i * SLOTS + s * CAP, 16), CAP)
                y_s[at] = ys[CAP * i : CAP * i + CAP]
            return carry

        lax.fori_loop(0, EP, source, 0)

    def back(j, store):
        x, y = x_s[j], y_s[pl.ds(pl.multiple_of(j * SLOTS, SLOTS), SLOTS)]
        gate = gate_s[j][:, :1] * RES
        dh = nt(y, wd[0])
        h = h_s[j].astype(F32)
        gg_o[0] = jnp.broadcast_to(RES * jnp.sum(h * dh, axis=1, keepdims=True), (SLOTS, 128))
        dh = dh * gate
        dg = (dh * a_s[j].astype(F32)).astype(BF)
        du = (dh * b_s[j].astype(F32)).astype(BF)
        dg_o[0], du_o[0] = dg, du
        w = tn(x, jnp.concatenate([dg, du], axis=1))
        store(0, w[:, :F].astype(BF))
        store(1, w[:, F:].astype(BF))
        w = tn((h * gate).astype(BF), y)
        store(2, jnp.concatenate([w[:, :F], w[:, F:]], axis=0).astype(BF))

    @pl.when(step == OWN)
    def _():
        whole_w = [None] * 3

        def store(i, w):
            whole_w[i] = w

        back(0, store)
        dw_s[0] = jnp.concatenate(whole_w, axis=0).reshape(4, 4, 2, 96, F)
        ra.start()
        rb.start()

    @pl.when(step > OWN)
    def _():
        def store(i, w):
            dw_o[0, D * i : D * i + D] = w

        back(step - OWN, store)

    @pl.when(step == OWN + 1)
    def _():
        ats.forward()
        for k in range(2):
            ra.go_on(k, dw_s.at[0, near(u, 1 + 2 * k), pair(k), 0], 1)
            rb.go_on(k, dw_s.at[0, pair(k), near(v, 1 + 2 * k), 1], 1)

    @pl.when(step == 2 * OWN - 1)
    def _():
        ats.finish()
        own_at.wait()
        ca_o[0] = dw_s[0, u, :, 0]
        cb_o[0] = dw_s[0, :, v, 1]
        close(ra, ca_o, 1)
        close(rb, cb_o, 1)
        ra.sent()
        rb.sent()


class Combine:
    def __init__(self, term, stage, buf, m1, m2, m3, d, z, c, make):
        right, left = (d, near(z, 1) * 2 + c), (d, near(z, 3) * 2 + c)
        self.term, self.stage, self.buf, self.m1, self.m2, self.m3, self.c = term, stage, buf, m1, m2, m3, c
        self.turns = [near(z, k) * 2 for k in (2, 1, 3, 0)]
        self.mates = [make(stage.at[i], buf.at[i], (d, z * 2 + 1 - c)) for i in range(4)]
        lo, hi = pl.ds(0, HALF), pl.ds(HALF, HALF)
        self.s1 = [make(buf.at[0, lo], m1.at[0], right), make(buf.at[0, hi], m1.at[1], left)]
        self.s2 = [make(buf.at[1, hi], m2.at[0], right), make(buf.at[2, lo], m2.at[1], left)]
        self.s3 = [make(m1.at[0], m3.at[0], right), make(m1.at[1], m3.at[1], left)]

    def begin(self):
        for i, t in enumerate(self.turns):
            self.stage[i] = self.term(t + 1 - self.c).astype(BF)
            self.mates[i].start()

    def add(self, i):
        own = self.term(self.turns[i] + self.c)
        self.mates[i].wait_recv()
        self.buf[i] = (self.buf[i].astype(F32) + own).astype(BF)

    def send(self):
        self.add(0)
        for cp in self.s1:
            cp.start()
        self.add(1)
        self.s2[0].start()
        self.add(2)
        self.s2[1].start()

    def go_on(self):
        for k, i in ((0, 1), (1, 2)):
            self.s1[k].wait_recv()
            self.m1[k] = self.m1[k] + self.buf[i, HALF * k : HALF * k + HALF]
            self.s3[k].start()

    def finish(self, out, columns):
        for k in range(2):
            rows = slice(HALF * k, HALF * k + HALF)
            self.s2[1 - k].wait_recv()
            self.s3[k].wait_recv()
            arrived = self.m2[1 - k].astype(F32) + self.m3[k].astype(F32)
            out[rows, columns] = self.buf[3, rows].astype(F32) + arrived

    def sent(self):
        for cp in self.mates + self.s1 + self.s2 + self.s3:
            cp.wait_send()


def experts_combine(
    eo, dg, du, gg, picks, wg, wu, dw, ca, cb, mg_o, gt_o, sh_o,
    dx_s, gg_s, stage, buf, m1, m2, m3, stage_, buf_, m1_, m2_, m3_,
    a1, a2, a3, amine, ac, b1, b2, b3, bmine, bc, a4, a5, a6, b4, b5, b6, ls, ss, rs,
):
    j = pl.program_id(0)
    d, e, z, c = place()
    u, v, up, down, ahead, behind = plane(d, e)
    make = Sender(ss, rs)
    later = pl.ds(1, OWN - 1)
    deep = lambda h: pl.ds(48 * h, 48)
    ra = Reduce(lambda i, h: dw.at[:, i, pair(h), 0], u, up, down, a1, a2, a3, make)
    rb = Reduce(lambda i, h: dw.at[:, pair(h), i, 1], v, ahead, behind, b1, b2, b3, make)
    qa = Reduce(lambda i, h: ac.at[:, i, deep(h)], v, ahead, behind, a4, a5, a6, make)
    qb = Reduce(lambda i, h: bc.at[:, i, deep(h)], u, up, down, b4, b5, b6, make)
    mix = Combine(lambda s: tn(picks[s], eo[s]), stage, buf, m1, m2, m3, d, z, c, make)
    back = Combine(lambda s: tn(picks[s], dx_s[s]), stage_, buf_, m1_, m2_, m3_, d, z, c, make)
    load = pltpu.make_async_copy
    own = [
        load(dw.at[:, near(u, 1), pair(0), 0], amine.at[0], ls.at[0]),
        load(dw.at[:, near(u, 3), pair(1), 0], amine.at[1], ls.at[1]),
        load(dw.at[:, pair(0), near(v, 1), 1], bmine.at[0], ls.at[2]),
        load(dw.at[:, pair(1), near(v, 3), 1], bmine.at[1], ls.at[3]),
        load(dw.at[:, u, :, 0], ac.at[later], ls.at[4]),
        load(dw.at[:, :, v, 1], bc.at[later], ls.at[5]),
        load(ca, ac.at[pl.ds(0, 1)], ls.at[6]),
        load(cb, bc.at[pl.ds(0, 1)], ls.at[7]),
    ]
    gt_own = load(gg_s.at[e], gt_o.at[e], ls.at[8])
    rows = [make(gg_s.at[p[1]], gt_o.at[e], p) for p in ep_peers(d, e)]

    @pl.when(j == 0)
    def _():
        greet(ep_peers(d, e) + [up, down, ahead, behind])()
        ra.start()
        rb.start()
        for cp in own:
            cp.start()
        mix.begin()

    @pl.when(j == 1)
    def _():
        mix.send()

    dx = (nt(dg[0], wg[0]) + nt(du[0], wu[0])).astype(BF)
    for s in range(EP):
        dx_s[s, pl.ds(pl.multiple_of(j * CAP, 16), CAP)] = dx[CAP * s : CAP * s + CAP]

    @pl.when(j == OWN - 1)
    def _():
        back.begin()
        mix.go_on()
        back.send()
        for cp in own:
            cp.wait()
        for k in range(2):
            ra.go_on(k, amine.at[k], OWN - 1)
            rb.go_on(k, bmine.at[k], OWN - 1)
        mix.add(3)
        for s in range(EP):
            p = picks[s]
            at = pl.ds(pl.multiple_of(s * CAP, 16), CAP)
            lines = [
                jnp.sum(
                    p[CAP * i : CAP * i + CAP].astype(F32) * gg[i, at][:, :1], axis=0, keepdims=True
                )
                for i in range(OWN)
            ]
            gg_s[s] = jnp.concatenate(lines + [jnp.zeros((8 - OWN, ROWS), F32)], axis=0)
        for cp in rows:
            cp.start()
        gt_own.start()
        back.add(3)
        back.go_on()
        mix.finish(mg_o, slice(0, D))
        close(ra, ac.at[later], OWN - 1)
        qa.start()
        close(rb, bc.at[later], OWN - 1)
        qb.start()
        back.finish(mg_o, slice(D, 2 * D))
        for q, chunk, me in ((qa, ac, v), (qb, bc, u)):
            for k in range(2):
                t = near(me, 1 + 2 * k)
                q.first[k].wait_recv()
                q.one[k] = q.one[k] + chunk[:, t, 48 * k : 48 * k + 48]
                q.third[k].start()
        for h, q, chunk, me in ((0, qa, ac, v), (1, qb, bc, u)):
            for k in range(2):
                q.arrived(k)
                mine = chunk[:, me, 48 * k : 48 * k + 48].astype(F32)
                total = mine + q.two[1 - k].astype(F32) + q.three[k].astype(F32)
                sh_o[:, h, 48 * k : 48 * k + 48] = total.astype(BF)
        for r in (ra, rb, qa, qb, mix, back):
            r.sent()
        for cp in rows:
            cp.wait()
        gt_own.wait()


def norm_back(grad, values, factor, gain):
    scaled = grad * gain
    grad_gain = jnp.sum(grad * values * factor, axis=0, keepdims=True)
    mean = jnp.mean(scaled * values, axis=1, keepdims=True)
    return factor * (scaled - values * (factor * factor * mean)), grad_gain


def after_experts(mg, gg, rt, moe, mid, cot, gt, wo, out_o, gm_o, gb_o, da_o, st_o):
    m = mid[...]
    out_o[...] = (m + mg[:, :D]).astype(BF)
    router_t = gt[:EXPERTS].astype(BF)
    gates, _ = routing(rt, nt(router_t, moe[...]))
    back = gg[...][:, :OWN].reshape(EXPERTS, ROWS)
    both_ = gates * back
    gl = (both_ - gates * jnp.sum(both_, axis=0, keepdims=True)).astype(BF)
    st_o[...] = jnp.zeros_like(st_o)
    st_o[:EXPERTS] = nn(gl, moe[...])
    grad = mg[:, D:] + tn(gl, router_t)
    factor = lax.rsqrt(jnp.mean(m * m, axis=1, keepdims=True) + EPS)
    gm, gain = norm_back(grad, m, factor, gt[33:34])
    st_o[33:34] = gain
    gm = cot[...].astype(F32) + gm
    gm_o[...] = gm
    gb = (RES * gm).astype(BF)
    ga = nt(gb, wo[...]).astype(BF)
    for t in range(EP):
        gb_o[t] = gb[:, 128 * t : 128 * t + 128]
        da_o[t] = ga[:, 128 * t : 128 * t + 128]


def to_heads(da, gb, da_o, gb_o, ls, ss, rs):
    d, e, z, c = place()
    greet(ep_peers(d, e))()
    make = Sender(ss, rs)
    send = make.now
    own = [
        pltpu.make_async_copy(da.at[e], da_o.at[e], ls.at[0]),
        pltpu.make_async_copy(gb.at[e], gb_o.at[e], ls.at[1]),
    ]
    for cp in own:
        cp.start()
    cps = []
    for k in (4, 3, 5, 2, 6, 1, 7):
        t = lax.rem(e + k, EP)
        cps.append(send(da.at[t], da_o.at[e], (d, t)))
        cps.append(send(gb.at[t], gb_o.at[e], (d, t)))
    for cp in cps:
        cp.wait()
    for cp in own:
        cp.wait()


def attend_back(q, kv, nrm, att, lse, da, gb, at, cs, sn, ids, dq_o, dw_o, kk_s, vv_s, dk_s, dv_s):
    s = pl.program_id(0)
    kk_s[...], vv_s[...] = both(kv[0].astype(F32))
    dk_s[...] = jnp.zeros_like(dk_s)
    dv_s[...] = jnp.zeros_like(dv_s)
    ids_k = ids[0]
    ids_q = jnp.broadcast_to(ids_k, (128, LEN)).T[:, :1]
    low = lanes((ROWS, 128)) < HD

    def unturn(v, rows):
        return v * cs[rows] - turn(v) * sn[rows]

    dqs = []
    for i in range(4):
        rows = slice(ROWS * i, ROWS * i + ROWS)
        q2 = two_heads(q[0, rows].astype(F32)).astype(BF)
        o = da[2 * i : 2 * i + 2, 0].reshape(ROWS, 128).astype(F32)
        o2f = two_heads(o)
        o2 = o2f.astype(BF)
        a = att[2 * i : 2 * i + 2, 0].reshape(ROWS, 128).astype(F32)
        delta = jnp.sum(o2f * jnp.concatenate([a, a], axis=0), axis=1, keepdims=True)
        l2 = jnp.concatenate([lse[0, rows][:, :1], lse[0, rows][:, HD : HD + 1]], axis=0)
        own = ids_q[rows]
        own = jnp.concatenate([own, own], axis=0)
        at_, end = spans(i)
        dq = 0.0
        for span in ([slice(0, at_)] if at_ else []) + [slice(at_, end)]:
            t = nt(q2, kk_s[span]) * (SCORE * LOG2E) - l2
            if span.start == at_:
                t = jnp.where(ids_k[:, span] <= own, t, MASKED)
            p = jnp.exp2(t)
            gp = nt(o2, vv_s[span])
            ds = (p * (gp - delta)).astype(BF)
            dq = dq + nn(ds, kk_s[span])
            dk_s[span] += tn(ds, q2)
            dv_s[span] += tn(p.astype(BF), o2)
        dq = SCORE * jnp.where(low, dq[:ROWS], dq[ROWS:])
        dqs.append(unturn(dq, rows).astype(BF))
    w = []
    for i in range(4):
        rows = slice(ROWS * i, ROWS * i + ROWS)
        dk, dv = dk_s[rows], dv_s[rows]
        dk = unturn(SCORE * (dk + pltpu.roll(dk, HD, 1)), rows)
        dv = dv + pltpu.roll(dv, HD, 1)
        dkv = jnp.where(low, dk, dv).astype(BF)
        dqkv = jnp.concatenate([dqs[i], dkv], axis=1)
        dq_o[2 * i : 2 * i + 2, 0] = dqkv.reshape(2, HALF, 256)
        w.append(dqkv)
    wqkv = tn(nrm[0], jnp.concatenate(w, axis=0))
    wout = tn(at[:, 0].reshape(LEN, D), gb[:, 0].reshape(LEN, 128))
    w = jnp.concatenate([wqkv, wout], axis=1)

    @pl.when(s == 0)
    def _():
        dw_o[...] = w

    @pl.when(s == 1)
    def _():
        dw_o[...] += w


def to_tokens(dq, dq_o, ls, ss, rs):
    d, e, z, c = place()
    greet(ep_peers(d, e))()
    make = Sender(ss, rs)
    send = make.now
    own = pltpu.make_async_copy(dq.at[e], dq_o.at[e], ls.at[0])
    own.start()
    cps = []
    for k in (4, 3, 5, 2, 6, 1, 7):
        t = lax.rem(e + k, EP)
        cps.append(send(dq.at[t], dq_o.at[e], (d, t)))
    for cp in cps:
        cp.wait()
    own.wait()


def first_norm_back(dq, wf, x, gm, gt, st, dw, gx_o, pk_o):
    grad = 0.0
    for s in range(EP):
        grad = grad + nt(dq[s], wf[:, 256 * s : 256 * s + 256])
    v = x[...].astype(F32)
    factor = lax.rsqrt(jnp.mean(v * v, axis=1, keepdims=True) + EPS)
    g, gain = norm_back(grad, v, factor, gt[32:33])
    gx_o[...] = (gm[...] + g).astype(BF)
    row = lax.broadcasted_iota(jnp.int32, (128, D), 0)
    small = jnp.where(row == 32, gain, st[...]).T
    pk_o[0] = dw[:, :256].astype(BF).reshape(4, 4, 64, 256)
    w = jnp.concatenate([dw[:, 256:], small], axis=1).astype(BF)
    pk_o[1] = w.reshape(4, 4, 64, 256)


def sum_weights(pk, wq_o, wk_o, wv_o, wo_o, sm_o, ra, rb, ta, tb, qa, qb, s1, r2, ls, ss, rs):
    d, e, z, c = place()
    u, v = d // 4, lax.rem(d, 4)
    across = [(lax.rem(u + k, 4) * 4 + v, e) for k in (1, 3, 2)]
    along = [(u * 4 + lax.rem(v + k, 4), e) for k in (1, 3, 2)]
    greet(ep_peers(d, e) + across + along)()
    make = Sender(ss, rs)
    send = make.now
    own = [
        pltpu.make_async_copy(pk.at[0, u], ra.at[0], ls.at[0]),
        pltpu.make_async_copy(pk.at[1, :, v], rb.at[0], ls.at[1]),
    ]
    for cp in own:
        cp.start()
    a1, b1 = [], []
    for i, k in enumerate((1, 3, 2)):
        a1.append(send(pk.at[0, lax.rem(u + k, 4)], ra.at[1 + i], across[i]))
        b1.append(send(pk.at[1, :, lax.rem(v + k, 4)], rb.at[1 + i], along[i]))
    for cp in own:
        cp.wait()

    def total(r):
        return (r[0].astype(F32) + r[1].astype(F32)) + (r[2].astype(F32) + r[3].astype(F32))

    for cp in a1:
        cp.wait_recv()
    ta[...] = total(ra).astype(BF)
    a2 = [send(ta.at[lax.rem(v + k, 4)], qa.at[1 + i], along[i]) for i, k in enumerate((1, 3, 2))]
    qa[0] = ta[v]
    for cp in b1:
        cp.wait_recv()
    tb[...] = total(rb).astype(BF)
    b2 = [send(tb.at[lax.rem(u + k, 4)], qb.at[1 + i], across[i]) for i, k in enumerate((1, 3, 2))]
    qb[0] = tb[u]
    for cp in a2:
        cp.wait_recv()
    s1[:, :, :256] = total(qa).reshape(EP, 8, 256)
    for cp in b2:
        cp.wait_recv()
    s1[:, :, 256:] = total(qb).reshape(EP, 8, 256)
    r2[e] = s1[e]
    more = [send(s1.at[p[1]], r2.at[e], p) for p in ep_peers(d, e)]
    for cp in more:
        cp.wait_recv()
    small = r2[0, :, 384:]
    for s in range(1, EP):
        small = small + r2[s, :, 384:]
    sm_o[...] = small
    wq_o[...] = jnp.concatenate([r2[s, :, :128] for s in range(EP)], axis=1)
    wk_o[...] = jnp.concatenate([r2[s, :, 128:192] for s in range(EP)], axis=1)
    wv_o[...] = jnp.concatenate([r2[s, :, 192:256] for s in range(EP)], axis=1)
    wo_o[...] = jnp.concatenate([r2[s, :, 256:384] for s in range(EP)], axis=1)
    for cp in a1 + b1 + a2 + b2 + more:
        cp.wait_send()


def widen(dw, q, k, v, o, sm, g_o, u_o, d_o, q_o, k_o, v_o, o_o, r_o):
    w = dw[...].reshape(3 * D, F).astype(F32)
    g_o[0] = w[:D]
    u_o[0] = w[D : 2 * D]
    d_o[0, :, :F] = w[2 * D : 2 * D + F]
    d_o[0, :, F:] = w[2 * D + F :]

    @pl.when(pl.program_id(0) == 0)
    def _():
        q_o[...], k_o[...], v_o[...], o_o[...] = q[...], k[...], v[...], o[...]
        r_o[...] = sm[:, :EXPERTS]


def tables():
    even = np.arange(0, HD, 2).astype(np.float32)
    frequency = (np.float32(10000.0) ** (-even / np.float32(HD))).astype(np.float32)
    angle = np.arange(LEN, dtype=np.float32)[:, None] * frequency[None, :]
    angle = np.concatenate([angle] * 4, axis=1).astype(np.float64)
    return np.cos(angle).astype(np.float32), np.sin(angle).astype(np.float32)


def per_device(
    tokens, cotangent, block_ids, routes, w_query, w_key, w_value, w_output, w_router,
    gain_attn, gain_moe, expert_gate, expert_up, expert_down,
):
    x = tokens.reshape(ROWS, D)
    cot = cotangent.reshape(ROWS, D)
    rt = routes.reshape(ROWS, 8).T
    cos, sin = tables()
    cos, sin = jnp.asarray(cos), jnp.asarray(sin)
    params = pltpu.CompilerParams(vmem_limit_bytes=60 * MIB)
    once = pl.Buffered(1)

    def whole(shape):
        return pl.BlockSpec(shape, lambda s: (0,) * len(shape), pipeline_mode=once)

    rall, q, kv, nrm, att, lse, gt, wo, moe, mid, moe_own, at_own = remote_call(
        before_experts, 1,
        [
            sds((EP, 8, ROWS), jnp.int32), sds((SEQS, LEN, 128), BF), sds((SEQS, LEN, 128), BF),
            sds((SEQS, LEN, D), BF), sds((EP, 2, HALF, 128), BF), sds((SEQS, LEN, 128), F32),
            sds((128, D), F32), sds((D, D), BF), sds((EP, 2, 2, HALF // 2, D), BF),
            sds((2, HALF, D), F32), sds((2, HALF, D), BF), sds((2, HALF, D), BF),
        ],
        [
            tokens.reshape(2, 2, HALF // 2, D), rt, w_query, w_key, w_value, w_output, w_router,
            gain_attn.reshape(1, 8), gain_moe.reshape(1, 8), cos, sin, block_ids,
        ],
        [ANY] + [VM] * 11,
        [
            pltpu.VMEM((EP, 2, 2, HALF // 2, D), BF), pltpu.VMEM((4, 4, EP, 16, 128), BF),
            pltpu.VMEM((4, 4, EP, 16, 640), BF), pltpu.VMEM((EP, 16, 128), BF),
            pltpu.VMEM((16, 640), BF), pltpu.VMEM((8, 128), F32), pltpu.VMEM((EP, 8, 128), F32),
            pltpu.VMEM((4, 4, 8, 128), F32), pltpu.VMEM((D, 256), BF), pltpu.VMEM((D, 128), F32),
            pltpu.VMEM((LEN, 128), BF), pltpu.VMEM((LEN, 128), BF),
            pltpu.VMEM((EP, 2, HALF, 128), BF), pltpu.VMEM((2, 2, HALF // 2, D), BF),
        ],
        128,
        [ANY] + [VM] * 7 + [ANY] + [VM] * 3,
        vmem=60,
    )
    w_q, w_k, w_v, moe = lax.optimization_barrier((w_query, w_key, w_value, moe))
    w_qkv = jnp.concatenate(
        [w_q.reshape(8, EP, 128), w_k.reshape(8, EP, HD), w_v.reshape(8, EP, HD)], axis=2
    ).reshape(8, 2 * D)
    w_full = lax.all_gather(w_qkv, ("dp", "ep"), axis=0, tiled=True)

    seq = lambda *shape: pl.BlockSpec((1, *shape), lambda s: (s,) + (0,) * len(shape))
    cut = lambda n: pl.BlockSpec((EP, 1, HALF, n), lambda s: (0, s, 0, 0))
    each = lambda *shape: pl.BlockSpec((1, *shape), lambda j: (j,) + (0,) * len(shape))
    fwd = lambda *shape: pl.BlockSpec(
        (1, *shape), lambda j: (jnp.minimum(j, OWN - 1),) + (0,) * len(shape)
    )
    bwd = lambda *shape: pl.BlockSpec(
        (1, *shape), lambda j: (jnp.maximum(j - OWN, 0),) + (0,) * len(shape)
    )
    slots = lambda dtype, n: pltpu.VMEM((OWN, SLOTS, n), dtype)
    rest = pl.BlockSpec((1, 3 * D, F), lambda j: (jnp.maximum(j - OWN - 1, 0), 0, 0))
    both_ways = pl.BlockSpec((1, F, D), lambda j: (lax.rem(j, OWN), 0, 0))
    moved = pltpu.VMEM((2, 1, 2, 96, F), BF)
    dw, eo, dg, du, gg, picks, ca, cb, at_all = pl.pallas_call(
        experts_weights,
        name="experts_weights",
        grid=(2 * OWN,),
        out_shape=[
            sds((OWN - 1, 3 * D, F), BF), sds((EP, OWN * CAP, D), BF), sds((OWN, SLOTS, F), BF),
            sds((OWN, SLOTS, F), BF), sds((OWN, SLOTS, 128), F32), sds((EP, OWN * CAP, ROWS), BF),
            sds((1, 4, 96, F), BF), sds((1, 4, 96, F), BF), sds((EP, 2, HALF, D), BF),
        ],
        in_specs=[
            ANY, ANY, ANY, whole((EP, 8, ROWS)), whole((128, D)), fwd(D, F), fwd(D, F), both_ways,
        ],
        out_specs=[
            rest, whole((EP, OWN * CAP, D)), bwd(SLOTS, F), bwd(SLOTS, F), bwd(SLOTS, 128),
            whole((EP, OWN * CAP, ROWS)), whole((1, 4, 96, F)), whole((1, 4, 96, F)), ANY,
        ],
        scratch_shapes=[
            pltpu.VMEM((EP, 2, HALF, D), BF), slots(BF, D), pltpu.VMEM((OWN * SLOTS, D), BF),
            slots(F32, 128), slots(BF, F), slots(BF, F), slots(BF, F),
            pltpu.VMEM((1, 4, 4, 2, 96, F), BF), *[moved] * 6, pltpu.SemaphoreType.DMA((3,)),
            pltpu.SemaphoreType.DMA((48,)), pltpu.SemaphoreType.DMA((48,)),
        ],
        compiler_params=pltpu.CompilerParams(
            collective_id=2, has_side_effects=True, vmem_limit_bytes=62 * MIB
        ),
    )(
        moe.reshape(EP * ROWS, D), cotangent.reshape(2, HALF, D), at_own, rall, gt, expert_gate, expert_up,
        expert_down,
    )

    mg, gg_all, shard = pl.pallas_call(
        experts_combine,
        name="experts_combine",
        grid=(OWN,),
        out_shape=[
            sds((ROWS, 2 * D), F32), sds((EP, 8, ROWS), F32), sds((OWN, 2, 96, F), BF),
        ],
        in_specs=[
            whole((EP, OWN * CAP, D)), each(SLOTS, F), each(SLOTS, F), whole((OWN, SLOTS, 128)),
            whole((EP, OWN * CAP, ROWS)), each(D, F), each(D, F), ANY, ANY, ANY,
        ],
        out_specs=[whole((ROWS, 2 * D)), ANY, whole((OWN, 2, 96, F))],
        scratch_shapes=[
            pltpu.VMEM((EP, OWN * CAP, D), BF), pltpu.VMEM((EP, 8, ROWS), F32),
            *([pltpu.VMEM((4, ROWS, D), BF)] * 2 + [pltpu.VMEM((2, HALF, D), BF)] * 3) * 2,
            *([pltpu.VMEM((2, OWN - 1, 2, 96, F), BF)] * 4 + [pltpu.VMEM((OWN, 4, 96, F), BF)]) * 2,
            *[pltpu.VMEM((2, OWN, 48, F), BF)] * 6,
            pltpu.SemaphoreType.DMA((10,)),
            pltpu.SemaphoreType.DMA((64,)),
            pltpu.SemaphoreType.DMA((64,)),
        ],
        compiler_params=pltpu.CompilerParams(
            collective_id=3, has_side_effects=True, vmem_limit_bytes=62 * MIB
        ),
    )(
        eo, dg, du, gg, picks, expert_gate, expert_up, dw.reshape(OWN - 1, 4, 4, 2, 96, F), ca, cb,
    )
    dw_sum = lax.all_gather(shard.reshape(OWN, 192, F), "dp", axis=0)

    output, gm, gb, da, st = pl.pallas_call(
        after_experts,
        name="after_experts",
        out_shape=[
            sds((ROWS, D), BF), sds((ROWS, D), F32), sds((EP, ROWS, 128), BF),
            sds((EP, ROWS, 128), BF), sds((128, D), F32),
        ],
        in_specs=[VM] * 8,
        out_specs=[VM] * 5,
        compiler_params=params,
    )(mg, gg_all, rt, moe_own.reshape(ROWS, D), mid.reshape(ROWS, D), cot, gt, wo)

    da_all, gb_all = remote_call(
        to_heads, 4, [sds((EP, ROWS, 128), BF)] * 2, [da, gb], [ANY] * 2, [], 16
    )

    dq, dw_attn = pl.pallas_call(
        attend_back,
        name="attend_back",
        grid=(SEQS,),
        out_shape=[sds((EP, 2, HALF, 256), BF), sds((D, 384), F32)],
        in_specs=[
            seq(LEN, 128), seq(LEN, 128), seq(LEN, D), cut(128), seq(LEN, 128), cut(128),
            cut(128), cut(D), whole((LEN, 128)), whole((LEN, 128)), seq(1, LEN),
        ],
        out_specs=[cut(256), whole((D, 384))],
        scratch_shapes=[
            pltpu.VMEM((LEN, 128), BF), pltpu.VMEM((LEN, 128), BF),
            pltpu.VMEM((LEN, 128), F32), pltpu.VMEM((LEN, 128), F32),
        ],
        compiler_params=params,
    )(
        q, kv, nrm, att, lse, da_all.reshape(EP, 2, HALF, 128), gb_all.reshape(EP, 2, HALF, 128),
        at_all, cos, sin, block_ids.reshape(SEQS, 1, LEN),
    )

    (dq_all,) = remote_call(
        to_tokens, 5, [sds((EP, ROWS, 256), BF)], [dq.reshape(EP, ROWS, 256)], [ANY], [], 8
    )

    grad_x, packed = pl.pallas_call(
        first_norm_back,
        name="first_norm_back",
        out_shape=[sds((ROWS, D), BF), sds((2, 4, 4, 64, 256), BF)],
        in_specs=[VM] * 7,
        out_specs=[VM] * 2,
        compiler_params=params,
    )(dq_all, w_full, x, gm, gt, st, dw_attn)

    gq, gk, gv, go, gs = remote_call(
        sum_weights, 6,
        [sds((8, D), F32), sds((8, 512), F32), sds((8, 512), F32), sds((8, D), F32), sds((8, 128), F32)],
        [packed],
        [ANY],
        [
            pltpu.VMEM((4, 4, 64, 256), BF), pltpu.VMEM((4, 4, 64, 256), BF),
            pltpu.VMEM((4, 64, 256), BF), pltpu.VMEM((4, 64, 256), BF),
            pltpu.VMEM((4, 64, 256), BF), pltpu.VMEM((4, 64, 256), BF),
            pltpu.VMEM((EP, 8, 512), F32), pltpu.VMEM((EP, 8, 512), F32),
        ],
        24,
        [VM] * 5,
    )

    small = [(8, D), (8, 512), (8, 512), (8, D)]
    g_gate, g_up, g_down, gq, gk, gv, go, gr = pl.pallas_call(
        widen,
        name="widen",
        grid=(OWN,),
        out_shape=[
            sds((OWN, D, F), F32), sds((OWN, D, F), F32), sds((OWN, F, D), F32),
            *[sds(n, F32) for n in small], sds((8, EXPERTS), F32),
        ],
        in_specs=[
            pl.BlockSpec((DP, 1, 192, F), lambda j: (0, j, 0, 0)), *[whole(n) for n in small],
            whole((8, 128)),
        ],
        out_specs=[
            each(D, F), each(D, F), each(F, D), *[whole(n) for n in small], whole((8, EXPERTS)),
        ],
        compiler_params=params,
    )(dw_sum, gq, gk, gv, go, gs)
    return (
        output.reshape(tokens.shape),
        grad_x.reshape(tokens.shape),
        gq,
        gk,
        gv,
        go,
        gr,
        gs[:, 32],
        gs[:, 33],
        g_gate,
        g_up,
        g_down,
    )


def solution(mesh):
    rows, own, both_axes = P("dp", "ep", None), P("ep", None, None), P(("dp", "ep"), None)
    line = P(("dp", "ep"))
    return jax.shard_map(
        per_device,
        mesh=mesh,
        in_specs=(
            rows, rows, P("dp", None), rows, both_axes, both_axes, both_axes, both_axes, both_axes,
            line, line, own, own, own,
        ),
        out_specs=(
            rows, rows, both_axes, both_axes, both_axes, both_axes, both_axes, line, line, own,
            own, own,
        ),
        check_vma=False,
    )
```

```python
import math

import jax
import jax.numpy as jnp
import numpy as np
from jax import lax
from jax.experimental import pallas as pl
from jax.experimental.pallas import tpu as pltpu
from jax.sharding import PartitionSpec as P

MESH = pl.DeviceIdType.MESH
BF = jnp.bfloat16
F32 = jnp.float32
ANY = pl.BlockSpec(memory_space=pl.ANY)
VM = pl.BlockSpec(memory_space=pltpu.VMEM)

DP, EP, CHIPS = 16, 8, 4
D, HD, F = 1024, 64, 512
ROWS, HALF, LEN, SEQS = 256, 128, 1024, 2
EXPERTS, OWN, CAP = 32, 4, 80
SLOTS = EP * CAP
EPS = 1e-6
RES = 0.22
SCORE = 0.015625
LOG2E = 1.4426950408889634
MASKED = -1e30
MIB = 2**20


def nt(a, b):
    return lax.dot_general(a, b, (((1,), (1,)), ((), ())), preferred_element_type=F32)


def nn(a, b):
    return jnp.dot(a, b, preferred_element_type=F32)


def tn(a, b):
    return lax.dot_general(a, b, (((0,), (0,)), ((), ())), preferred_element_type=F32)


def place():
    e = lax.axis_index("ep")
    return lax.axis_index("dp"), e, e // 2, lax.rem(e, 2)


def near(k, n):
    return lax.rem(k + n, 4)


def plane(d, e):
    u, v = d // 4, lax.rem(d, 4)
    up, down = (near(u, 1) * 4 + v, e), (near(u, 3) * 4 + v, e)
    return u, v, up, down, (u * 4 + near(v, 1), e), (u * 4 + near(v, 3), e)


def pair(h):
    return pl.ds(2 * h, 2)


def greet(peers):
    b = pltpu.get_barrier_semaphore()
    for p in peers:
        pl.semaphore_signal(b, inc=1, device_id=p, device_id_type=MESH)
    return lambda: pl.semaphore_wait(b, len(peers))


def ep_peers(d, e):
    return [(d, lax.rem(e + k, EP)) for k in range(1, EP)]


def dp_peers(d, e):
    return [(lax.rem(d + k, DP), e) for k in range(1, DP)]


class Sender:
    def __init__(self, ss, rs):
        self.ss, self.rs, self.n = ss, rs, 0

    def __call__(self, src, dst, dev):
        i = self.n
        self.n += 1
        return pltpu.make_async_remote_copy(
            src, dst, self.ss.at[i], self.rs.at[i], device_id=dev, device_id_type=MESH
        )

    def now(self, src, dst, dev):
        cp = self(src, dst, dev)
        cp.start()
        return cp


class Ring:
    def __init__(self, out, src, d, e, z, c, make):
        right, left = (d, lax.rem(z + 1, CHIPS) * 2 + c), (d, lax.rem(z + 3, CHIPS) * 2 + c)
        part = (d, z * 2 + 1 - c)
        er, el, eo = right[1], left[1], lax.rem(z + 2, CHIPS) * 2 + c
        self.near = [
            [make(src(0), out(e, 0), right), make(src(0), out(e, 0), left)],
            [make(src(1), out(e, 1), left), make(src(1), out(e, 1), right)],
        ]
        self.mate = [make(src(0), out(e, 0), part), make(src(1), out(e, 1), part)]
        self.far = [make(out(el, 0), out(el, 0), right), make(out(er, 1), out(er, 1), left)]
        self.share = [
            make(out(s, h), out(s, h), part)
            for s, h in ((el, 0), (er, 1), (el, 1), (er, 0), (eo, 0), (eo, 1))
        ]

    def start(self, h):
        for cp in self.near[h]:
            cp.start()
        self.mate[h].start()

    def forward(self):
        for h in range(2):
            self.near[h][0].wait_recv()
            self.far[h].start()
            self.share[h].start()
        for h in range(2):
            self.near[1 - h][1].wait_recv()
            self.share[2 + h].start()

    def finish(self):
        for h in range(2):
            self.far[h].wait_recv()
            self.share[4 + h].start()
        for cp in self.near[0] + self.near[1] + self.far:
            cp.wait_send()
        for cp in self.mate + self.share:
            cp.wait()


class Quad:
    def __init__(self, out, me, ahead, behind, make, src=None):
        after, before = lax.rem(me + 1, 4), lax.rem(me + 3, 4)
        mine = lambda h, dev: make(src(h) if src else out(me, h), out(me, h), dev)
        self.near = [
            [mine(0, ahead), mine(0, behind)],
            [mine(1, behind), mine(1, ahead)],
        ]
        self.far = [
            make(out(before, 0), out(before, 0), ahead),
            make(out(after, 1), out(after, 1), behind),
        ]

    def start(self):
        for h in range(2):
            for cp in self.near[h]:
                cp.start()

    def forward(self):
        for h in range(2):
            self.near[h][0].wait_recv()
            self.far[h].start()

    def arrived(self):
        for h in range(2):
            self.near[h][1].wait_recv()
        for h in range(2):
            self.far[h].wait_recv()

    def sent(self):
        for cp in self.near[0] + self.near[1] + self.far:
            cp.wait_send()


def remote_call(body, cid, outs, ins, specs, scratch, sems, out_specs=None, vmem=48, flops=0):
    return pl.pallas_call(
        body,
        name=body.__name__,
        out_shape=outs,
        in_specs=specs,
        out_specs=out_specs if out_specs is not None else [ANY] * len(outs),
        scratch_shapes=[
            *scratch,
            pltpu.SemaphoreType.DMA((9,)),
            pltpu.SemaphoreType.DMA((sems,)),
            pltpu.SemaphoreType.DMA((sems,)),
        ],
        compiler_params=pltpu.CompilerParams(
            collective_id=cid, has_side_effects=True, vmem_limit_bytes=vmem * MIB
        ),
        cost_estimate=pl.CostEstimate(flops=flops, bytes_accessed=20 * MIB, transcendentals=0),
    )(*ins)


def sds(shape, dtype):
    return jax.ShapeDtypeStruct(shape, dtype)


def lanes(shape):
    return lax.broadcasted_iota(jnp.int32, shape, 1)


def turn(v):
    first = lax.rem(lanes(v.shape), HD) < HD // 2
    return jnp.where(first, -pltpu.roll(v, 128 - HD // 2, 1), pltpu.roll(v, HD // 2, 1))


def both(kv):
    low = lanes(kv.shape) < HD
    other = pltpu.roll(kv, HD, 1)
    return jnp.where(low, kv, other).astype(BF), jnp.where(low, other, kv).astype(BF)


def two_heads(v):
    low = lanes(v.shape) < HD
    zero = jnp.zeros_like(v)
    return jnp.concatenate([jnp.where(low, v, zero), jnp.where(low, zero, v)], axis=0)


def spans(i):
    return i * ROWS, min(LEN, i * ROWS + 2 * ROWS)


def before_experts(
    x, rt, w_q, w_k, w_v, wo, wr, ga, gm, cs, sn, ids,
    rall, q_o, kv_o, nrm_o, att_o, lse_o, gt_o, wo_o, moe, mid_o, own_o, at_o, wqkv_o,
    xall, wsl, wof, wp, wop, gp, gb, gs, w_s, sm_s, kk_s, vv_s, arr, mo, ls, ss, rs,
):
    d, e, z, c = place()
    u, v, up, down, ahead, behind = plane(d, e)
    across = [up, down, (near(u, 2) * 4 + v, e)]
    along = [ahead, behind, (u * 4 + near(v, 2), e)]
    wait = greet(ep_peers(d, e) + across + along)
    q, k, w = w_q[...].astype(F32), w_k[...].astype(F32), w_v[...].astype(F32)
    diagonal = lax.broadcasted_iota(jnp.int32, (8, 8), 0) == lanes((8, 8))
    column = lambda g: jnp.sum(jnp.where(diagonal, g[...].astype(F32), 0.0), axis=1, keepdims=True)
    for t in range(EP):
        kv = [k[:, 64 * t : 64 * t + 64], w[:, 64 * t : 64 * t + 64]]
        row = [q[:, 128 * t : 128 * t + 128], jnp.concatenate(kv, axis=1)]
        wp[t] = jnp.concatenate(row, axis=0).astype(BF)
        wqkv_o[:, 256 * t : 256 * t + 256] = jnp.concatenate(row, axis=1).astype(BF)
    w, r = wo[...].astype(F32), wr[...].astype(F32)
    left = jnp.concatenate([w[:, :512], r, jnp.zeros((8, 96), F32)], axis=1)
    right = jnp.concatenate([w[:, 512:], column(ga), column(gm), jnp.zeros((8, 126), F32)], axis=1)
    wop[...] = jnp.concatenate([left, right], axis=0).astype(BF)
    spread = lax.broadcasted_iota(jnp.int32, (8, 128), 1) - 8 * e
    spread = spread == lax.broadcasted_iota(jnp.int32, (8, 128), 0)
    line = jnp.sum(jnp.where(spread, column(ga), 0.0), axis=0, keepdims=True)
    gp[...] = jnp.broadcast_to(line, (8, 128))
    wait()
    make = Sender(ss, rs)
    send = make.now
    own = [
        pltpu.make_async_copy(x, xall.at[e], ls.at[0]),
        pltpu.make_async_copy(wp.at[e], wsl.at[v, u, e], ls.at[1]),
        pltpu.make_async_copy(wop, wof.at[u, v, e], ls.at[2]),
        pltpu.make_async_copy(rt, rall.at[e], ls.at[3]),
        pltpu.make_async_copy(gp, gb.at[e], ls.at[8]),
    ]
    for cp in own:
        cp.start()
    tokens = [
        Ring(lambda s, k: xall.at[s, h, k], lambda k: x.at[h, k], d, e, z, c, make) for h in range(2)
    ]
    moes = [
        Ring(lambda s, k: moe.at[s, h, k], lambda k: mo.at[h, k], d, e, z, c, make) for h in range(2)
    ]
    gains = [send(gp, gb.at[e], p) for p in ep_peers(d, e)]
    first = [send(wp.at[p[1]], wsl.at[v, u, e], p) for p in ep_peers(d, e)]
    first += [send(wop, wof.at[u, v, e], p) for p in ep_peers(d, e)]
    tokens[0].start(0)
    tokens[0].start(1)
    own[1].wait()
    for cp in first[: EP - 1]:
        cp.wait_recv()
    w1 = [send(wsl.at[v, u], wsl.at[v, u], p) for p in across]
    own[4].wait()
    for cp in gains:
        cp.wait_recv()
    line = gb[0]
    for s in range(1, EP):
        line = line + gb[s]
    gs[v, u] = line
    g1 = [send(gs.at[v, u], gs.at[v, u], p) for p in across]
    own[2].wait()
    for cp in first[EP - 1 :]:
        cp.wait_recv()
    mine = pl.ds(c * 4, 4)
    part = (d, z * 2 + 1 - c)
    o1 = [send(wof.at[u, v, mine], wof.at[u, v, mine], p) for p in along]
    tokens[0].forward()
    for cp in w1:
        cp.wait_recv()
    w2 = Quad(lambda i, h: wsl.at[i, pair(h)], v, ahead, behind, make)
    w2.start()
    for cp in g1:
        cp.wait_recv()
    g2 = [send(gs.at[v], gs.at[v], p) for p in along]
    last = []
    for k, cp in zip((1, 3, 2), o1):
        cp.wait_recv()
        t = lax.rem(v + 4 - k, 4)
        last.append(send(wof.at[u, t, mine], wof.at[u, t, mine], part))
    o2 = Quad(lambda i, h: wof.at[i, :, pl.ds(c * 4 + 2 * h, 2)], u, up, down, make)
    o2.start()
    tokens[1].start(0)
    tokens[1].start(1)
    w2.forward()
    tokens[0].finish()
    own[0].wait()
    w2.arrived()
    for cp in g2:
        cp.wait_recv()
    for i in range(DP):
        w = wsl[i % 4, i // 4].astype(F32)
        w = jnp.concatenate([w[:, :8].reshape(64, 128), w[:, 8:].reshape(64, 128)], axis=1)
        w_s[64 * i : 64 * i + 64] = w.astype(BF)
    gain_a = jnp.concatenate([gs[i % 4, i // 4][:1, :64] for i in range(DP)], axis=1)

    def project(h):
        for r in range(4):
            rows = slice(256 * r, 256 * r + 256)
            t = xall[2 * r : 2 * r + 2, h].astype(F32).reshape(256, D)
            factor = lax.rsqrt(jnp.mean(t * t, axis=1, keepdims=True) + EPS)
            n = (t * factor * gain_a).astype(BF)
            nrm_o[h, rows] = n
            pre = nn(n, w_s[...])
            co, si = cs[rows], sn[rows]
            q, kv = pre[:, :128], pre[:, 128:]
            q_o[h, rows] = (q * co + turn(q) * si).astype(BF)
            kv = jnp.where(lanes(kv.shape) < HD, kv * co + turn(kv) * si, kv).astype(BF)
            kv_o[h, rows] = kv
            kk_s[rows], vv_s[rows] = both(kv.astype(F32))

    def attend(h, i):
        ids_k = ids[h : h + 1]
        ids_q = jnp.broadcast_to(ids_k[:, ROWS * i : ROWS * i + ROWS], (128, ROWS)).T[:, :1]
        q2 = two_heads(q_o[h, ROWS * i : ROWS * i + ROWS].astype(F32)).astype(BF)
        own_ids = jnp.concatenate([ids_q, ids_q], axis=0)
        at, end = spans(i)
        parts = []
        if at:
            parts.append((nt(q2, kk_s[:at]) * (SCORE * LOG2E), slice(0, at)))
        t = nt(q2, kk_s[at:end]) * (SCORE * LOG2E)
        parts.append((jnp.where(ids_k[:, at:end] <= own_ids, t, MASKED), slice(at, end)))
        peak = parts[0][0].max(axis=1, keepdims=True)
        for t, _ in parts[1:]:
            peak = jnp.maximum(peak, t.max(axis=1, keepdims=True))
        total, out = 0.0, 0.0
        for t, span in parts:
            p = jnp.exp2(t - peak)
            total = total + p.sum(axis=1, keepdims=True)
            out = out + nn(p.astype(BF), vv_s[span])
        out = out * (1.0 / total)
        lse = jnp.broadcast_to(peak + jnp.log2(total), (2 * ROWS, 128))
        low = lanes((ROWS, 128)) < HD
        att = jnp.where(low, out[:ROWS], out[ROWS:]).astype(BF)
        att_o[2 * i : 2 * i + 2, h] = att.reshape(2, HALF, 128)
        lse_o[h, ROWS * i : ROWS * i + ROWS] = jnp.where(low, lse[:ROWS], lse[ROWS:])

    att_own = [pltpu.make_async_copy(att_o.at[e, h], arr.at[e, h], ls.at[4 + h]) for h in range(2)]
    moe_own = [pltpu.make_async_copy(mo.at[h], moe.at[e, h], ls.at[6 + h]) for h in range(2)]

    def exchange(h):
        att_own[h].start()
        cps = []
        for k in (4, 3, 5, 2, 6, 1, 7):
            t = lax.rem(e + k, EP)
            cps.append(send(att_o.at[t, h], arr.at[e, h], (d, t)))
        return cps

    def branch(h, cps):
        att_own[h].wait()
        for cp in cps:
            cp.wait_recv()
        a = jnp.concatenate([arr[s, h] for s in range(EP)], axis=1)
        at_o[h] = a
        m = xall[e, h].astype(F32).reshape(HALF, D) + RES * nn(a, wo_o[...])
        mid_o[h] = m
        factor = lax.rsqrt(jnp.mean(m * m, axis=1, keepdims=True) + EPS)
        n = (m * factor * gt_o[33:34, :]).astype(BF)
        own_o[h] = n
        mo[h] = n.reshape(2, HALF // 2, D)
        moe_own[h].start()
        moes[h].start(0)
        moes[h].start(1)

    project(0)
    tokens[1].forward()
    attend(0, 0)
    attend(0, 1)
    o2.forward()
    attend(0, 2)
    attend(0, 3)
    x0 = exchange(0)
    tokens[1].finish()
    project(1)
    attend(1, 0)
    attend(1, 1)
    attend(1, 2)
    attend(1, 3)
    x1 = exchange(1)
    o2.arrived()
    for k in (1, 3, 2):
        t = near(u, k)
        last.append(send(wof.at[t, :, mine], wof.at[t, :, mine], part))
    routes = [send(rt, rall.at[e], p) for p in ep_peers(d, e)]
    for cp in last:
        cp.wait_recv()
    for i in range(4):
        rows = slice(256 * i, 256 * i + 256)
        o = wof[i].astype(F32).reshape(32, 16, 640)
        left, right = o[:, :8].reshape(256, 640), o[:, 8:].reshape(256, 640)
        wo_o[rows, :512] = left[:, :512].astype(BF)
        wo_o[rows, 512:] = right[:, :512].astype(BF)
        sm_s[rows] = jnp.where(lanes((256, 128)) < 32, left[:, 512:], pltpu.roll(right[:, 512:], 32, 1))
    gt_o[...] = sm_s[...].T
    branch(0, x0)
    branch(1, x1)
    moes[0].forward()
    moes[1].forward()
    moes[0].finish()
    moes[1].finish()
    w2.sent()
    o2.sent()
    for cp in gains + first + w1 + g1 + g2 + o1 + last + x0 + x1:
        cp.wait_send()
    for cp in routes:
        cp.wait()
    own[3].wait()
    for cp in moe_own:
        cp.wait()


def routing(rt, logits_t):
    ids = lax.broadcasted_iota(jnp.int32, (EXPERTS, ROWS), 0)
    hit = rt[0:1] == ids
    for k in range(1, 8):
        hit = hit | (rt[k : k + 1] == ids)
    w = jnp.where(hit, logits_t, MASKED)
    w = jnp.where(hit, jnp.exp(w - w.max(axis=0, keepdims=True)), 0.0)
    gates = w / w.sum(axis=0, keepdims=True)
    earlier = lax.broadcasted_iota(jnp.int32, (ROWS, ROWS), 0) < lax.broadcasted_iota(
        jnp.int32, (ROWS, ROWS), 1
    )
    slot = nn(jnp.where(hit, 1.0, 0.0).astype(BF), jnp.where(earlier, 1.0, 0.0).astype(BF))
    return gates, jnp.where(hit, slot, -1.0)


class Reduce:
    def __init__(self, chunk, me, ahead, behind, one, two, three, make):
        at = lambda k: lax.rem(me + k, 4)
        self.one, self.two, self.three = one, two, three
        self.first = [
            make(chunk(at(2), 0), one.at[0], ahead),
            make(chunk(at(2), 1), one.at[1], behind),
        ]
        self.second = [
            make(chunk(at(1), 1), two.at[0], ahead),
            make(chunk(at(3), 0), two.at[1], behind),
        ]
        self.third = [make(one.at[0], three.at[0], ahead), make(one.at[1], three.at[1], behind)]

    def start(self):
        for cp in self.first + self.second:
            cp.start()

    def go_on(self, k, mine, pieces):
        self.first[k].wait_recv()

        def add(i, carry):
            self.one[k, i] = self.one[k, i] + (mine[i] if pieces > 1 else mine[...])
            return carry

        lax.fori_loop(0, pieces, add, 0)
        self.third[k].start()

    def arrived(self, k):
        self.second[1 - k].wait_recv()
        self.third[k].wait_recv()

    def sent(self):
        for cp in self.first + self.second + self.third:
            cp.wait_send()


def close(r, chunk, pieces):
    for k in range(2):
        r.arrived(k)

        def body(i, carry):
            for q in range(2):
                piece = r.two[1 - k, i, q].astype(F32) + r.three[k, i, q].astype(F32)
                chunk[i, 2 * k + q] = (chunk[i, 2 * k + q].astype(F32) + piece).astype(BF)
            return carry

        lax.fori_loop(0, pieces, body, 0)


def experts_weights(
    moe, cot, at, rall, gt, wg, wu, wd, dw_o, eo_o, dg_o, du_o, gg_o, p_o, ca_o, cb_o, at_o,
    cot_s, x_s, y_s, gate_s, a_s, b_s, h_s, dw_s, a1, a2, a3, b1, b2, b3, ls, ss, rs,
):
    step = pl.program_id(0)
    d, e, z, c = place()
    u, v, up, down, ahead, behind = plane(d, e)
    first = e * OWN
    make = Sender(ss, rs)
    cots = Ring(lambda s, k: cot_s.at[s, k], lambda k: cot.at[k], d, e, z, c, make)
    ats = Ring(lambda s, k: at_o.at[s, k], lambda k: at.at[k], d, e, z, c, make)
    ra = Reduce(lambda i, h: dw_s.at[:, i, pair(h), 0], u, up, down, a1, a2, a3, make)
    rb = Reduce(lambda i, h: dw_s.at[:, pair(h), i, 1], v, ahead, behind, b1, b2, b3, make)
    own = pltpu.make_async_copy(cot, cot_s.at[e], ls.at[0])
    own_at = pltpu.make_async_copy(at, at_o.at[e], ls.at[2])
    rows_of = lambda s: pl.ds(pl.multiple_of(s * CAP, 16), CAP)

    @pl.when(step == 0)
    def _():
        load = pltpu.make_async_copy(moe, y_s.at[pl.ds(0, EP * ROWS)], ls.at[1])
        load.start()
        greet(ep_peers(d, e) + [up, down, ahead, behind])()
        cots.start(0)
        cots.start(1)
        own.start()
        own_at.start()
        load.wait()
        router_t = gt[:EXPERTS].astype(BF)
        row = lax.broadcasted_iota(jnp.int32, (EXPERTS, ROWS), 0)
        place_in = lax.broadcasted_iota(jnp.int32, (CAP, ROWS), 0).astype(F32)

        def source(s, carry):
            m = y_s[pl.ds(pl.multiple_of(s * ROWS, ROWS), ROWS)]
            gates, slot = routing(rall[s], nt(router_t, m))
            picks = []
            for i in range(OWN):
                sel = row == first + i
                pick = jnp.sum(jnp.where(sel, slot, 0.0), axis=0, keepdims=True) == place_in
                gate = jnp.sum(jnp.where(sel, gates, 0.0), axis=0, keepdims=True)
                g = jnp.sum(jnp.where(pick, gate, 0.0), axis=1, keepdims=True)
                gate_s[i, rows_of(s)] = jnp.broadcast_to(g, (CAP, 128))
                picks.append(jnp.where(pick, 1.0, 0.0).astype(BF))
            pick = jnp.concatenate(picks, axis=0)
            p_o[s] = pick
            xs = nn(pick, m).astype(BF)
            for i in range(OWN):
                x_s[i, rows_of(s)] = xs[CAP * i : CAP * i + CAP]
            return carry

        lax.fori_loop(0, EP, source, 0)

    @pl.when(step < OWN)
    def _():
        x = x_s[step]
        gate = gate_s[step][:, :1] * RES
        g = nn(x, wg[0])
        u = nn(x, wu[0])
        s = 1.0 / (1.0 + jnp.exp(-g))
        silu = g * s
        a_s[step] = (u * s * (1.0 + g * (1.0 - s))).astype(BF)
        b_s[step] = silu.astype(BF)
        h = silu * u
        h_s[step] = h.astype(BF)
        eo = nn((h * gate).astype(BF), wd[0]).astype(BF)
        for i in range(EP):
            eo_o[i, rows_of(step)] = eo[CAP * i : CAP * i + CAP]

    @pl.when(step == 2)
    def _():
        cots.forward()
        ats.start(0)
        ats.start(1)

    @pl.when(step == OWN)
    def _():
        cots.finish()
        own.wait()

        def source(s, carry):
            ys = nn(p_o[s], cot_s[s].reshape(ROWS, D)).astype(BF)
            for i in range(OWN):
                at = pl.ds(pl.multiple_of(i * SLOTS + s * CAP, 16), CAP)
                y_s[at] = ys[CAP * i : CAP * i + CAP]
            return carry

        lax.fori_loop(0, EP, source, 0)

    def back(j, store):
        x, y = x_s[j], y_s[pl.ds(pl.multiple_of(j * SLOTS, SLOTS), SLOTS)]
        gate = gate_s[j][:, :1] * RES
        dh = nt(y, wd[0])
        h = h_s[j].astype(F32)
        gg_o[0] = jnp.broadcast_to(RES * jnp.sum(h * dh, axis=1, keepdims=True), (SLOTS, 128))
        dh = dh * gate
        dg = (dh * a_s[j].astype(F32)).astype(BF)
        du = (dh * b_s[j].astype(F32)).astype(BF)
        dg_o[0], du_o[0] = dg, du
        w = tn(x, jnp.concatenate([dg, du], axis=1))
        store(0, w[:, :F].astype(BF))
        store(1, w[:, F:].astype(BF))
        w = tn((h * gate).astype(BF), y)
        store(2, jnp.concatenate([w[:, :F], w[:, F:]], axis=0).astype(BF))

    @pl.when(step == OWN)
    def _():
        whole_w = [None] * 3

        def store(i, w):
            whole_w[i] = w

        back(0, store)
        dw_s[0] = jnp.concatenate(whole_w, axis=0).reshape(4, 4, 2, 96, F)
        ra.start()
        rb.start()

    @pl.when(step > OWN)
    def _():
        def store(i, w):
            dw_o[0, D * i : D * i + D] = w

        back(step - OWN, store)

    @pl.when(step == OWN + 1)
    def _():
        ats.forward()
        for k in range(2):
            ra.go_on(k, dw_s.at[0, near(u, 1 + 2 * k), pair(k), 0], 1)
            rb.go_on(k, dw_s.at[0, pair(k), near(v, 1 + 2 * k), 1], 1)

    @pl.when(step == 2 * OWN - 1)
    def _():
        ats.finish()
        own_at.wait()
        ca_o[0] = dw_s[0, u, :, 0]
        cb_o[0] = dw_s[0, :, v, 1]
        close(ra, ca_o, 1)
        close(rb, cb_o, 1)
        ra.sent()
        rb.sent()


class Combine:
    def __init__(self, term, stage, buf, m1, m2, m3, d, z, c, make):
        right, left = (d, near(z, 1) * 2 + c), (d, near(z, 3) * 2 + c)
        self.term, self.stage, self.buf, self.m1, self.m2, self.m3, self.c = term, stage, buf, m1, m2, m3, c
        self.turns = [near(z, k) * 2 for k in (2, 1, 3, 0)]
        self.mates = [make(stage.at[i], buf.at[i], (d, z * 2 + 1 - c)) for i in range(4)]
        lo, hi = pl.ds(0, HALF), pl.ds(HALF, HALF)
        self.s1 = [make(buf.at[0, lo], m1.at[0], right), make(buf.at[0, hi], m1.at[1], left)]
        self.s2 = [make(buf.at[1, hi], m2.at[0], right), make(buf.at[2, lo], m2.at[1], left)]
        self.s3 = [make(m1.at[0], m3.at[0], right), make(m1.at[1], m3.at[1], left)]

    def begin(self):
        for i, t in enumerate(self.turns):
            self.stage[i] = self.term(t + 1 - self.c).astype(BF)
            self.mates[i].start()

    def add(self, i):
        own = self.term(self.turns[i] + self.c)
        self.mates[i].wait_recv()
        self.buf[i] = (self.buf[i].astype(F32) + own).astype(BF)

    def send(self):
        self.add(0)
        for cp in self.s1:
            cp.start()
        self.add(1)
        self.s2[0].start()
        self.add(2)
        self.s2[1].start()

    def go_on(self):
        for k, i in ((0, 1), (1, 2)):
            self.s1[k].wait_recv()
            self.m1[k] = self.m1[k] + self.buf[i, HALF * k : HALF * k + HALF]
            self.s3[k].start()

    def finish(self, out, columns):
        for k in range(2):
            rows = slice(HALF * k, HALF * k + HALF)
            self.s2[1 - k].wait_recv()
            self.s3[k].wait_recv()
            arrived = self.m2[1 - k].astype(F32) + self.m3[k].astype(F32)
            out[rows, columns] = self.buf[3, rows].astype(F32) + arrived

    def sent(self):
        for cp in self.mates + self.s1 + self.s2 + self.s3:
            cp.wait_send()


def experts_combine(
    eo, dg, du, gg, picks, wg, wu, dw, ca, cb, mg_o, gt_o, sh_o,
    dx_s, gg_s, stage, buf, m1, m2, m3, stage_, buf_, m1_, m2_, m3_,
    a1, a2, a3, amine, ac, b1, b2, b3, bmine, bc, a4, a5, a6, b4, b5, b6, ls, ss, rs,
):
    j = pl.program_id(0)
    d, e, z, c = place()
    u, v, up, down, ahead, behind = plane(d, e)
    make = Sender(ss, rs)
    later = pl.ds(1, OWN - 1)
    deep = lambda h: pl.ds(48 * h, 48)
    ra = Reduce(lambda i, h: dw.at[:, i, pair(h), 0], u, up, down, a1, a2, a3, make)
    rb = Reduce(lambda i, h: dw.at[:, pair(h), i, 1], v, ahead, behind, b1, b2, b3, make)
    qa = Reduce(lambda i, h: ac.at[:, i, deep(h)], v, ahead, behind, a4, a5, a6, make)
    qb = Reduce(lambda i, h: bc.at[:, i, deep(h)], u, up, down, b4, b5, b6, make)
    mix = Combine(lambda s: tn(picks[s], eo[s]), stage, buf, m1, m2, m3, d, z, c, make)
    back = Combine(lambda s: tn(picks[s], dx_s[s]), stage_, buf_, m1_, m2_, m3_, d, z, c, make)
    load = pltpu.make_async_copy
    own = [
        load(dw.at[:, near(u, 1), pair(0), 0], amine.at[0], ls.at[0]),
        load(dw.at[:, near(u, 3), pair(1), 0], amine.at[1], ls.at[1]),
        load(dw.at[:, pair(0), near(v, 1), 1], bmine.at[0], ls.at[2]),
        load(dw.at[:, pair(1), near(v, 3), 1], bmine.at[1], ls.at[3]),
        load(dw.at[:, u, :, 0], ac.at[later], ls.at[4]),
        load(dw.at[:, :, v, 1], bc.at[later], ls.at[5]),
        load(ca, ac.at[pl.ds(0, 1)], ls.at[6]),
        load(cb, bc.at[pl.ds(0, 1)], ls.at[7]),
    ]
    gt_own = load(gg_s.at[e], gt_o.at[e], ls.at[8])
    rows = [make(gg_s.at[p[1]], gt_o.at[e], p) for p in ep_peers(d, e)]

    @pl.when(j == 0)
    def _():
        greet(ep_peers(d, e) + [up, down, ahead, behind])()
        ra.start()
        rb.start()
        for cp in own:
            cp.start()
        mix.begin()

    @pl.when(j == 1)
    def _():
        mix.send()

    dx = (nt(dg[0], wg[0]) + nt(du[0], wu[0])).astype(BF)
    for s in range(EP):
        dx_s[s, pl.ds(pl.multiple_of(j * CAP, 16), CAP)] = dx[CAP * s : CAP * s + CAP]

    @pl.when(j == OWN - 1)
    def _():
        back.begin()
        mix.go_on()
        back.send()
        for cp in own:
            cp.wait()
        for k in range(2):
            ra.go_on(k, amine.at[k], OWN - 1)
            rb.go_on(k, bmine.at[k], OWN - 1)
        mix.add(3)
        for s in range(EP):
            p = picks[s]
            at = pl.ds(pl.multiple_of(s * CAP, 16), CAP)
            lines = [
                jnp.sum(
                    p[CAP * i : CAP * i + CAP].astype(F32) * gg[i, at][:, :1], axis=0, keepdims=True
                )
                for i in range(OWN)
            ]
            gg_s[s] = jnp.concatenate(lines + [jnp.zeros((8 - OWN, ROWS), F32)], axis=0)
        for cp in rows:
            cp.start()
        gt_own.start()
        back.add(3)
        back.go_on()
        mix.finish(mg_o, slice(0, D))
        close(ra, ac.at[later], OWN - 1)
        qa.start()
        close(rb, bc.at[later], OWN - 1)
        qb.start()
        back.finish(mg_o, slice(D, 2 * D))
        for q, chunk, me in ((qa, ac, v), (qb, bc, u)):
            for k in range(2):
                t = near(me, 1 + 2 * k)
                q.first[k].wait_recv()
                q.one[k] = q.one[k] + chunk[:, t, 48 * k : 48 * k + 48]
                q.third[k].start()
        for h, q, chunk, me in ((0, qa, ac, v), (1, qb, bc, u)):
            for k in range(2):
                q.arrived(k)
                mine = chunk[:, me, 48 * k : 48 * k + 48].astype(F32)
                total = mine + q.two[1 - k].astype(F32) + q.three[k].astype(F32)
                sh_o[:, h, 48 * k : 48 * k + 48] = total.astype(BF)
        for r in (ra, rb, qa, qb, mix, back):
            r.sent()
        for cp in rows:
            cp.wait()
        gt_own.wait()


def norm_back(grad, values, factor, gain):
    scaled = grad * gain
    grad_gain = jnp.sum(grad * values * factor, axis=0, keepdims=True)
    mean = jnp.mean(scaled * values, axis=1, keepdims=True)
    return factor * (scaled - values * (factor * factor * mean)), grad_gain


def after_experts(
    mg, gg, rt, moe, mid, cot, gt, wo, gm_o, st_o, da_o, gb_o, da, gb, ls, ss, rs
):
    d, e, z, c = place()
    wait = greet(ep_peers(d, e))
    m = mid[...]
    router_t = gt[:EXPERTS].astype(BF)
    gates, _ = routing(rt, nt(router_t, moe[...]))
    back = gg[...][:, :OWN].reshape(EXPERTS, ROWS)
    both_ = gates * back
    gl = (both_ - gates * jnp.sum(both_, axis=0, keepdims=True)).astype(BF)
    wait()
    make = Sender(ss, rs)
    grad = mg[:, D:] + tn(gl, router_t)
    factor = lax.rsqrt(jnp.mean(m * m, axis=1, keepdims=True) + EPS)
    gm, gain = norm_back(grad, m, factor, gt[33:34])
    gm = cot[...].astype(F32) + gm
    gradient = (RES * gm).astype(BF)
    ga = nt(gradient, wo[...]).astype(BF)
    for t in range(EP):
        da[t] = ga[:, 128 * t : 128 * t + 128]
        gb[t] = gradient[:, 128 * t : 128 * t + 128]
    own = [
        pltpu.make_async_copy(da.at[e], da_o.at[e], ls.at[0]),
        pltpu.make_async_copy(gb.at[e], gb_o.at[e], ls.at[1]),
    ]
    cps = [make.now(da.at[p[1]], da_o.at[e], p) for p in ep_peers(d, e)]
    cps += [make.now(gb.at[p[1]], gb_o.at[e], p) for p in ep_peers(d, e)]
    for cp in own:
        cp.start()
    gm_o[...] = gm
    st_o[...] = jnp.zeros_like(st_o)
    st_o[:EXPERTS] = nn(gl, moe[...])
    st_o[33:34] = gain
    for cp in cps:
        cp.wait()
    for cp in own:
        cp.wait()


def attend_back(q, kv, nrm, att, lse, da, gb, at, cs, sn, ids, dq_o, dw_o, kk_s, vv_s, dk_s, dv_s):
    s = pl.program_id(0)
    kk_s[...], vv_s[...] = both(kv[0].astype(F32))
    dk_s[...] = jnp.zeros_like(dk_s)
    dv_s[...] = jnp.zeros_like(dv_s)
    ids_k = ids[0]
    ids_q = jnp.broadcast_to(ids_k, (128, LEN)).T[:, :1]
    low = lanes((ROWS, 128)) < HD

    def unturn(v, rows):
        return v * cs[rows] - turn(v) * sn[rows]

    dqs = []
    for i in range(4):
        rows = slice(ROWS * i, ROWS * i + ROWS)
        q2 = two_heads(q[0, rows].astype(F32)).astype(BF)
        o = da[2 * i : 2 * i + 2, 0].reshape(ROWS, 128).astype(F32)
        o2f = two_heads(o)
        o2 = o2f.astype(BF)
        a = att[2 * i : 2 * i + 2, 0].reshape(ROWS, 128).astype(F32)
        delta = jnp.sum(o2f * jnp.concatenate([a, a], axis=0), axis=1, keepdims=True)
        l2 = jnp.concatenate([lse[0, rows][:, :1], lse[0, rows][:, HD : HD + 1]], axis=0)
        own = ids_q[rows]
        own = jnp.concatenate([own, own], axis=0)
        at_, end = spans(i)
        dq = 0.0
        for span in ([slice(0, at_)] if at_ else []) + [slice(at_, end)]:
            t = nt(q2, kk_s[span]) * (SCORE * LOG2E) - l2
            if span.start == at_:
                t = jnp.where(ids_k[:, span] <= own, t, MASKED)
            p = jnp.exp2(t)
            gp = nt(o2, vv_s[span])
            ds = (p * (gp - delta)).astype(BF)
            dq = dq + nn(ds, kk_s[span])
            dk_s[span] += tn(ds, q2)
            dv_s[span] += tn(p.astype(BF), o2)
        dq = SCORE * jnp.where(low, dq[:ROWS], dq[ROWS:])
        dqs.append(unturn(dq, rows).astype(BF))
    w = []
    for i in range(4):
        rows = slice(ROWS * i, ROWS * i + ROWS)
        dk, dv = dk_s[rows], dv_s[rows]
        dk = unturn(SCORE * (dk + pltpu.roll(dk, HD, 1)), rows)
        dv = dv + pltpu.roll(dv, HD, 1)
        dkv = jnp.where(low, dk, dv).astype(BF)
        dqkv = jnp.concatenate([dqs[i], dkv], axis=1)
        dq_o[2 * i : 2 * i + 2, 0] = dqkv.reshape(2, HALF, 256)
        w.append(dqkv)
    wqkv = tn(nrm[0], jnp.concatenate(w, axis=0))
    wout = tn(at[:, 0].reshape(LEN, D), gb[:, 0].reshape(LEN, 128))
    w = jnp.concatenate([wqkv, wout], axis=1)

    @pl.when(s == 0)
    def _():
        dw_o[...] = w

    @pl.when(s == 1)
    def _():
        dw_o[...] += w


def finish_weights(
    dq, wf, x, gm, gt, st, dw, gx_o, wq_o, wk_o, wv_o, wo_o, sm_o,
    dq_s, wf_s, pa, pb, a1, a2, a3, b1, b2, b3, ca, cb, a4, a5, a6, b4, b5, b6, s1, r2, ls, ss, rs,
):
    d, e, z, c = place()
    u, v, up, down, ahead, behind = plane(d, e)
    wait = greet(ep_peers(d, e) + [up, down, ahead, behind])
    load = pltpu.make_async_copy
    own = [
        load(wf, wf_s, ls.at[0]),
        load(dq.at[e], dq_s.at[e], ls.at[1]),
    ]
    for cp in own:
        cp.start()
    pa[0] = dw[:, :256].astype(BF).reshape(4, 4, 64, 256)
    wait()
    make = Sender(ss, rs)
    cps = [make.now(dq.at[p[1]], dq_s.at[e], p) for p in ep_peers(d, e)]
    deep = lambda h: pl.ds(32 * h, 32)
    ra = Reduce(lambda i, h: pa.at[:, i, pair(h)], u, up, down, a1, a2, a3, make)
    rb = Reduce(lambda i, h: pb.at[:, pair(h), i], v, ahead, behind, b1, b2, b3, make)
    qa = Reduce(lambda i, h: ca.at[:, i, deep(h)], v, ahead, behind, a4, a5, a6, make)
    qb = Reduce(lambda i, h: cb.at[:, i, deep(h)], u, up, down, b4, b5, b6, make)
    ra.start()
    for k in range(2):
        ra.go_on(k, pa.at[0, near(u, 1 + 2 * k), pair(k)], 1)
    own[0].wait()
    own[1].wait()
    for cp in cps:
        cp.wait_recv()
    grad = 0.0
    for s in range(EP):
        grad = grad + nt(dq_s[s], wf_s[:, 256 * s : 256 * s + 256])
    t = x[...].astype(F32)
    factor = lax.rsqrt(jnp.mean(t * t, axis=1, keepdims=True) + EPS)
    g, gain = norm_back(grad, t, factor, gt[32:33])
    row = lax.broadcasted_iota(jnp.int32, (128, D), 0)
    small = jnp.where(row == 32, gain, st[...]).T
    pb[0] = jnp.concatenate([dw[:, 256:], small], axis=1).astype(BF).reshape(4, 4, 64, 256)
    rb.start()
    gx_o[...] = gm[...] + g
    ca[0] = pa[0, u]
    close(ra, ca, 1)
    qa.start()
    for k in range(2):
        rb.go_on(k, pb.at[0, pair(k), near(v, 1 + 2 * k)], 1)

    def second(q, chunk, me):
        for k in range(2):
            q.first[k].wait_recv()
            q.one[k] = q.one[k] + chunk[:, near(me, 1 + 2 * k), 32 * k : 32 * k + 32]
            q.third[k].start()

    def last(q, chunk, me, columns):
        for k in range(2):
            q.arrived(k)
            mine = chunk[0, me, 32 * k : 32 * k + 32].astype(F32)
            total = mine + q.two[1 - k, 0].astype(F32) + q.three[k, 0].astype(F32)
            s1[4 * k : 4 * k + 4, :, columns] = total.reshape(4, 8, 256)

    second(qa, ca, v)
    cb[0] = pb[0, :, v]
    close(rb, cb, 1)
    qb.start()
    last(qa, ca, v, slice(0, 256))
    second(qb, cb, u)
    last(qb, cb, u, slice(256, 512))
    r2[e] = s1[e]
    more = [make.now(s1.at[p[1]], r2.at[e], p) for p in ep_peers(d, e)]
    for cp in more:
        cp.wait_recv()
    small = r2[0, :, 384:]
    for s in range(1, EP):
        small = small + r2[s, :, 384:]
    sm_o[...] = small
    wq_o[...] = jnp.concatenate([r2[s, :, :128] for s in range(EP)], axis=1)
    wk_o[...] = jnp.concatenate([r2[s, :, 128:192] for s in range(EP)], axis=1)
    wv_o[...] = jnp.concatenate([r2[s, :, 192:256] for s in range(EP)], axis=1)
    wo_o[...] = jnp.concatenate([r2[s, :, 256:384] for s in range(EP)], axis=1)
    for q in (ra, rb, qa, qb):
        q.sent()
    for cp in cps + more:
        cp.wait_send()


def widen(dw, q, k, v, o, sm, g_o, u_o, d_o, q_o, k_o, v_o, o_o, r_o):
    w = dw[...].reshape(3 * D, F).astype(F32)
    g_o[0] = w[:D]
    u_o[0] = w[D : 2 * D]
    d_o[0, :, :F] = w[2 * D : 2 * D + F]
    d_o[0, :, F:] = w[2 * D + F :]

    @pl.when(pl.program_id(0) == 0)
    def _():
        q_o[...], k_o[...], v_o[...], o_o[...] = q[...], k[...], v[...], o[...]
        r_o[...] = sm[:, :EXPERTS]


def tables():
    even = np.arange(0, HD, 2).astype(np.float32)
    frequency = (np.float32(10000.0) ** (-even / np.float32(HD))).astype(np.float32)
    angle = np.arange(LEN, dtype=np.float32)[:, None] * frequency[None, :]
    angle = np.concatenate([angle] * 4, axis=1).astype(np.float64)
    return np.cos(angle).astype(np.float32), np.sin(angle).astype(np.float32)


def per_device(
    tokens, cotangent, block_ids, routes, w_query, w_key, w_value, w_output, w_router,
    gain_attn, gain_moe, expert_gate, expert_up, expert_down,
):
    x = tokens.reshape(ROWS, D)
    cot = cotangent.reshape(ROWS, D)
    rt = routes.reshape(ROWS, 8).T
    cos, sin = tables()
    cos, sin = jnp.asarray(cos), jnp.asarray(sin)
    params = pltpu.CompilerParams(vmem_limit_bytes=60 * MIB)
    once = pl.Buffered(1)

    def whole(shape):
        return pl.BlockSpec(shape, lambda s: (0,) * len(shape), pipeline_mode=once)

    rall, q, kv, nrm, att, lse, gt, wo, moe, mid, moe_own, at_own, w_qkv = remote_call(
        before_experts, 1,
        [
            sds((EP, 8, ROWS), jnp.int32), sds((SEQS, LEN, 128), BF), sds((SEQS, LEN, 128), BF),
            sds((SEQS, LEN, D), BF), sds((EP, 2, HALF, 128), BF), sds((SEQS, LEN, 128), F32),
            sds((128, D), F32), sds((D, D), BF), sds((EP, 2, 2, HALF // 2, D), BF),
            sds((2, HALF, D), F32), sds((2, HALF, D), BF), sds((2, HALF, D), BF), sds((8, 2 * D), BF),
        ],
        [
            tokens.reshape(2, 2, HALF // 2, D), rt, w_query, w_key, w_value, w_output, w_router,
            gain_attn.reshape(1, 8), gain_moe.reshape(1, 8), cos, sin, block_ids,
        ],
        [ANY] + [VM] * 11,
        [
            pltpu.VMEM((EP, 2, 2, HALF // 2, D), BF), pltpu.VMEM((4, 4, EP, 16, 128), BF),
            pltpu.VMEM((4, 4, EP, 16, 640), BF), pltpu.VMEM((EP, 16, 128), BF),
            pltpu.VMEM((16, 640), BF), pltpu.VMEM((8, 128), F32), pltpu.VMEM((EP, 8, 128), F32),
            pltpu.VMEM((4, 4, 8, 128), F32), pltpu.VMEM((D, 256), BF), pltpu.VMEM((D, 128), F32),
            pltpu.VMEM((LEN, 128), BF), pltpu.VMEM((LEN, 128), BF),
            pltpu.VMEM((EP, 2, HALF, 128), BF), pltpu.VMEM((2, 2, HALF // 2, D), BF),
        ],
        128,
        [ANY] + [VM] * 7 + [ANY] + [VM] * 4,
        vmem=60,
    )
    w_full = lax.all_gather(w_qkv, ("dp", "ep"), axis=0, tiled=True)

    seq = lambda *shape: pl.BlockSpec((1, *shape), lambda s: (s,) + (0,) * len(shape))
    cut = lambda n: pl.BlockSpec((EP, 1, HALF, n), lambda s: (0, s, 0, 0))
    each = lambda *shape: pl.BlockSpec((1, *shape), lambda j: (j,) + (0,) * len(shape))
    fwd = lambda *shape: pl.BlockSpec(
        (1, *shape), lambda j: (jnp.minimum(j, OWN - 1),) + (0,) * len(shape)
    )
    bwd = lambda *shape: pl.BlockSpec(
        (1, *shape), lambda j: (jnp.maximum(j - OWN, 0),) + (0,) * len(shape)
    )
    slots = lambda dtype, n: pltpu.VMEM((OWN, SLOTS, n), dtype)
    rest = pl.BlockSpec((1, 3 * D, F), lambda j: (jnp.maximum(j - OWN - 1, 0), 0, 0))
    both_ways = pl.BlockSpec((1, F, D), lambda j: (lax.rem(j, OWN), 0, 0))
    moved = pltpu.VMEM((2, 1, 2, 96, F), BF)
    dw, eo, dg, du, gg, picks, ca, cb, at_all = pl.pallas_call(
        experts_weights,
        name="experts_weights",
        grid=(2 * OWN,),
        out_shape=[
            sds((OWN - 1, 3 * D, F), BF), sds((EP, OWN * CAP, D), BF), sds((OWN, SLOTS, F), BF),
            sds((OWN, SLOTS, F), BF), sds((OWN, SLOTS, 128), F32), sds((EP, OWN * CAP, ROWS), BF),
            sds((1, 4, 96, F), BF), sds((1, 4, 96, F), BF), sds((EP, 2, HALF, D), BF),
        ],
        in_specs=[
            ANY, ANY, ANY, whole((EP, 8, ROWS)), whole((128, D)), fwd(D, F), fwd(D, F), both_ways,
        ],
        out_specs=[
            rest, whole((EP, OWN * CAP, D)), bwd(SLOTS, F), bwd(SLOTS, F), bwd(SLOTS, 128),
            whole((EP, OWN * CAP, ROWS)), whole((1, 4, 96, F)), whole((1, 4, 96, F)), ANY,
        ],
        scratch_shapes=[
            pltpu.VMEM((EP, 2, HALF, D), BF), slots(BF, D), pltpu.VMEM((OWN * SLOTS, D), BF),
            slots(F32, 128), slots(BF, F), slots(BF, F), slots(BF, F),
            pltpu.VMEM((1, 4, 4, 2, 96, F), BF), *[moved] * 6, pltpu.SemaphoreType.DMA((3,)),
            pltpu.SemaphoreType.DMA((48,)), pltpu.SemaphoreType.DMA((48,)),
        ],
        compiler_params=pltpu.CompilerParams(
            collective_id=2, has_side_effects=True, vmem_limit_bytes=62 * MIB
        ),
    )(
        moe.reshape(EP * ROWS, D), cotangent.reshape(2, HALF, D), at_own, rall, gt, expert_gate, expert_up,
        expert_down,
    )

    mg, gg_all, shard = pl.pallas_call(
        experts_combine,
        name="experts_combine",
        grid=(OWN,),
        out_shape=[
            sds((ROWS, 2 * D), F32), sds((EP, 8, ROWS), F32), sds((OWN, 2, 96, F), BF),
        ],
        in_specs=[
            whole((EP, OWN * CAP, D)), each(SLOTS, F), each(SLOTS, F), whole((OWN, SLOTS, 128)),
            whole((EP, OWN * CAP, ROWS)), each(D, F), each(D, F), ANY, ANY, ANY,
        ],
        out_specs=[whole((ROWS, 2 * D)), ANY, whole((OWN, 2, 96, F))],
        scratch_shapes=[
            pltpu.VMEM((EP, OWN * CAP, D), BF), pltpu.VMEM((EP, 8, ROWS), F32),
            *([pltpu.VMEM((4, ROWS, D), BF)] * 2 + [pltpu.VMEM((2, HALF, D), BF)] * 3) * 2,
            *([pltpu.VMEM((2, OWN - 1, 2, 96, F), BF)] * 4 + [pltpu.VMEM((OWN, 4, 96, F), BF)]) * 2,
            *[pltpu.VMEM((2, OWN, 48, F), BF)] * 6,
            pltpu.SemaphoreType.DMA((10,)),
            pltpu.SemaphoreType.DMA((64,)),
            pltpu.SemaphoreType.DMA((64,)),
        ],
        compiler_params=pltpu.CompilerParams(
            collective_id=3, has_side_effects=True, vmem_limit_bytes=62 * MIB
        ),
    )(
        eo, dg, du, gg, picks, expert_gate, expert_up, dw.reshape(OWN - 1, 4, 4, 2, 96, F), ca, cb,
    )
    dw_sum = lax.all_gather(shard.reshape(OWN, 192, F), "dp", axis=0)

    gm, st, da_all, gb_all = remote_call(
        after_experts, 4,
        [
            sds((ROWS, D), F32), sds((128, D), F32), sds((EP, ROWS, 128), BF),
            sds((EP, ROWS, 128), BF),
        ],
        [mg, gg_all, rt, moe_own.reshape(ROWS, D), mid.reshape(ROWS, D), cot, gt, wo],
        [VM] * 8,
        [pltpu.VMEM((EP, ROWS, 128), BF), pltpu.VMEM((EP, ROWS, 128), BF)],
        16,
        [VM] * 2 + [ANY] * 2,
    )
    output = (mid.reshape(ROWS, D) + mg[:, :D]).astype(BF)

    dq, dw_attn = pl.pallas_call(
        attend_back,
        name="attend_back",
        grid=(SEQS,),
        out_shape=[sds((EP, 2, HALF, 256), BF), sds((D, 384), F32)],
        in_specs=[
            seq(LEN, 128), seq(LEN, 128), seq(LEN, D), cut(128), seq(LEN, 128), cut(128),
            cut(128), cut(D), whole((LEN, 128)), whole((LEN, 128)), seq(1, LEN),
        ],
        out_specs=[cut(256), whole((D, 384))],
        scratch_shapes=[
            pltpu.VMEM((LEN, 128), BF), pltpu.VMEM((LEN, 128), BF),
            pltpu.VMEM((LEN, 128), F32), pltpu.VMEM((LEN, 128), F32),
        ],
        compiler_params=params,
    )(
        q, kv, nrm, att, lse, da_all.reshape(EP, 2, HALF, 128), gb_all.reshape(EP, 2, HALF, 128),
        at_all, cos, sin, block_ids.reshape(SEQS, 1, LEN),
    )

    part = lambda *n: [pltpu.VMEM((2, 1, *n), BF)] * 3
    grad_x, gq, gk, gv, go, gs = remote_call(
        finish_weights, 5,
        [
            sds((ROWS, D), F32), sds((8, D), F32), sds((8, 512), F32), sds((8, 512), F32),
            sds((8, D), F32), sds((8, 128), F32),
        ],
        [dq.reshape(EP, ROWS, 256), w_full, x, gm, gt, st, dw_attn],
        [ANY, ANY] + [VM] * 5,
        [
            pltpu.VMEM((EP, ROWS, 256), BF), pltpu.VMEM((D, 2 * D), BF),
            pltpu.VMEM((1, 4, 4, 64, 256), BF), pltpu.VMEM((1, 4, 4, 64, 256), BF),
            *part(2, 64, 256), *part(2, 64, 256), pltpu.VMEM((1, 4, 64, 256), BF),
            pltpu.VMEM((1, 4, 64, 256), BF), *part(32, 256), *part(32, 256),
            pltpu.VMEM((EP, 8, 512), F32), pltpu.VMEM((EP, 8, 512), F32),
        ],
        44,
        [VM] * 6,
    )

    small = [(8, D), (8, 512), (8, 512), (8, D)]
    g_gate, g_up, g_down, gq, gk, gv, go, gr = pl.pallas_call(
        widen,
        name="widen",
        grid=(OWN,),
        out_shape=[
            sds((OWN, D, F), F32), sds((OWN, D, F), F32), sds((OWN, F, D), F32),
            *[sds(n, F32) for n in small], sds((8, EXPERTS), F32),
        ],
        in_specs=[
            pl.BlockSpec((DP, 1, 192, F), lambda j: (0, j, 0, 0)), *[whole(n) for n in small],
            whole((8, 128)),
        ],
        out_specs=[
            each(D, F), each(D, F), each(F, D), *[whole(n) for n in small], whole((8, EXPERTS)),
        ],
        compiler_params=params,
    )(dw_sum, gq, gk, gv, go, gs)
    return (
        output.reshape(tokens.shape),
        grad_x.astype(BF).reshape(tokens.shape),
        gq,
        gk,
        gv,
        go,
        gr,
        gs[:, 32],
        gs[:, 33],
        g_gate,
        g_up,
        g_down,
    )


def solution(mesh):
    rows, own, both_axes = P("dp", "ep", None), P("ep", None, None), P(("dp", "ep"), None)
    line = P(("dp", "ep"))
    return jax.shard_map(
        per_device,
        mesh=mesh,
        in_specs=(
            rows, rows, P("dp", None), rows, both_axes, both_axes, both_axes, both_axes, both_axes,
            line, line, own, own, own,
        ),
        out_specs=(
            rows, rows, both_axes, both_axes, both_axes, both_axes, both_axes, line, line, own,
            own, own,
        ),
        check_vma=False,
    )
```

```python
import math

import jax
import jax.numpy as jnp
import numpy as np
from jax import lax
from jax.experimental import pallas as pl
from jax.experimental.pallas import tpu as pltpu
from jax.sharding import PartitionSpec as P

MESH = pl.DeviceIdType.MESH
BF = jnp.bfloat16
F32 = jnp.float32
ANY = pl.BlockSpec(memory_space=pl.ANY)
VM = pl.BlockSpec(memory_space=pltpu.VMEM)

DP, EP, CHIPS = 16, 8, 4
D, HD, F = 1024, 64, 512
ROWS, HALF, LEN, SEQS = 256, 128, 1024, 2
EXPERTS, OWN, CAP = 32, 4, 80
SLOTS = EP * CAP
EPS = 1e-6
RES = 0.22
SCORE = 0.015625
LOG2E = 1.4426950408889634
MASKED = -1e30
MIB = 2**20


def nt(a, b):
    return lax.dot_general(a, b, (((1,), (1,)), ((), ())), preferred_element_type=F32)


def nn(a, b):
    return jnp.dot(a, b, preferred_element_type=F32)


def tn(a, b):
    return lax.dot_general(a, b, (((0,), (0,)), ((), ())), preferred_element_type=F32)


def place():
    e = lax.axis_index("ep")
    return lax.axis_index("dp"), e, e // 2, lax.rem(e, 2)


def near(k, n):
    return lax.rem(k + n, 4)


def plane(d, e):
    u, v = d // 4, lax.rem(d, 4)
    up, down = (near(u, 1) * 4 + v, e), (near(u, 3) * 4 + v, e)
    return u, v, up, down, (u * 4 + near(v, 1), e), (u * 4 + near(v, 3), e)


def pair(h):
    return pl.ds(2 * h, 2)


def greet(peers):
    b = pltpu.get_barrier_semaphore()
    for p in peers:
        pl.semaphore_signal(b, inc=1, device_id=p, device_id_type=MESH)
    return lambda: pl.semaphore_wait(b, len(peers))


def ep_peers(d, e):
    return [(d, lax.rem(e + k, EP)) for k in range(1, EP)]


def dp_peers(d, e):
    return [(lax.rem(d + k, DP), e) for k in range(1, DP)]


class Sender:
    def __init__(self, ss, rs):
        self.ss, self.rs, self.n = ss, rs, 0

    def __call__(self, src, dst, dev):
        i = self.n
        self.n += 1
        return pltpu.make_async_remote_copy(
            src, dst, self.ss.at[i], self.rs.at[i], device_id=dev, device_id_type=MESH
        )

    def now(self, src, dst, dev):
        cp = self(src, dst, dev)
        cp.start()
        return cp


class Ring:
    def __init__(self, out, src, d, e, z, c, make):
        right, left = (d, lax.rem(z + 1, CHIPS) * 2 + c), (d, lax.rem(z + 3, CHIPS) * 2 + c)
        part = (d, z * 2 + 1 - c)
        er, el, eo = right[1], left[1], lax.rem(z + 2, CHIPS) * 2 + c
        self.near = [
            [make(src(0), out(e, 0), right), make(src(0), out(e, 0), left)],
            [make(src(1), out(e, 1), left), make(src(1), out(e, 1), right)],
        ]
        self.mate = [make(src(0), out(e, 0), part), make(src(1), out(e, 1), part)]
        self.far = [make(out(el, 0), out(el, 0), right), make(out(er, 1), out(er, 1), left)]
        self.share = [
            make(out(s, h), out(s, h), part)
            for s, h in ((el, 0), (er, 1), (el, 1), (er, 0), (eo, 0), (eo, 1))
        ]

    def start(self, h):
        for cp in self.near[h]:
            cp.start()
        self.mate[h].start()

    def forward(self):
        for h in range(2):
            self.near[h][0].wait_recv()
            self.far[h].start()
            self.share[h].start()
        for h in range(2):
            self.near[1 - h][1].wait_recv()
            self.share[2 + h].start()

    def finish(self):
        for h in range(2):
            self.far[h].wait_recv()
            self.share[4 + h].start()
        for cp in self.near[0] + self.near[1] + self.far:
            cp.wait_send()
        for cp in self.mate + self.share:
            cp.wait()


class Quad:
    def __init__(self, out, me, ahead, behind, make, src=None):
        after, before = lax.rem(me + 1, 4), lax.rem(me + 3, 4)
        mine = lambda h, dev: make(src(h) if src else out(me, h), out(me, h), dev)
        self.near = [
            [mine(0, ahead), mine(0, behind)],
            [mine(1, behind), mine(1, ahead)],
        ]
        self.far = [
            make(out(before, 0), out(before, 0), ahead),
            make(out(after, 1), out(after, 1), behind),
        ]

    def start(self):
        for h in range(2):
            for cp in self.near[h]:
                cp.start()

    def forward(self):
        for h in range(2):
            self.near[h][0].wait_recv()
            self.far[h].start()

    def arrived(self):
        for h in range(2):
            self.near[h][1].wait_recv()
        for h in range(2):
            self.far[h].wait_recv()

    def sent(self):
        for cp in self.near[0] + self.near[1] + self.far:
            cp.wait_send()


def remote_call(body, cid, outs, ins, specs, scratch, sems, out_specs=None, vmem=48, flops=0):
    return pl.pallas_call(
        body,
        name=body.__name__,
        out_shape=outs,
        in_specs=specs,
        out_specs=out_specs if out_specs is not None else [ANY] * len(outs),
        scratch_shapes=[
            *scratch,
            pltpu.SemaphoreType.DMA((24,)),
            pltpu.SemaphoreType.DMA((sems,)),
            pltpu.SemaphoreType.DMA((sems,)),
        ],
        compiler_params=pltpu.CompilerParams(
            collective_id=cid, has_side_effects=True, vmem_limit_bytes=vmem * MIB
        ),
        cost_estimate=pl.CostEstimate(flops=flops, bytes_accessed=20 * MIB, transcendentals=0),
    )(*ins)


def sds(shape, dtype):
    return jax.ShapeDtypeStruct(shape, dtype)


def lanes(shape):
    return lax.broadcasted_iota(jnp.int32, shape, 1)


def turn(v):
    first = lax.rem(lanes(v.shape), HD) < HD // 2
    return jnp.where(first, -pltpu.roll(v, 128 - HD // 2, 1), pltpu.roll(v, HD // 2, 1))


def both(kv):
    low = lanes(kv.shape) < HD
    other = pltpu.roll(kv, HD, 1)
    return jnp.where(low, kv, other).astype(BF), jnp.where(low, other, kv).astype(BF)


def two_heads(v):
    low = lanes(v.shape) < HD
    zero = jnp.zeros_like(v)
    return jnp.concatenate([jnp.where(low, v, zero), jnp.where(low, zero, v)], axis=0)


def spans(i):
    return i * ROWS, min(LEN, i * ROWS + 2 * ROWS)


def before_experts(
    x, rt, w_q, w_k, w_v, wo, wr, ga, gm, cs, sn, ids,
    rall, moe, q_h, kv_h, nrm_h, att_h, lse_h, gt_h, wo_h, mid_h, own_h, at_h, wqkv_h,
    q_o, kv_o, nrm_o, att_o, lse_o, gt_o, wo_o, mid_o, own_o, at_o, wqkv_o,
    xall, wsl, wof, wp, wop, gp, gb, gs, w_s, sm_s, kk_s, vv_s, arr, mo, ls, ss, rs,
):
    d, e, z, c = place()
    u, v, up, down, ahead, behind = plane(d, e)
    pairs = [
        (q_o, q_h), (kv_o, kv_h), (nrm_o, nrm_h), (att_o, att_h), (lse_o, lse_h), (gt_o, gt_h),
        (wo_o, wo_h), (mid_o, mid_h), (own_o, own_h), (at_o, at_h), (wqkv_o, wqkv_h),
    ]
    results = [pltpu.make_async_copy(a, b, ls.at[10 + i]) for i, (a, b) in enumerate(pairs)]
    across = [up, down, (near(u, 2) * 4 + v, e)]
    along = [ahead, behind, (u * 4 + near(v, 2), e)]
    wait = greet(ep_peers(d, e) + across + along)
    q, k, w = w_q[...].astype(F32), w_k[...].astype(F32), w_v[...].astype(F32)
    diagonal = lax.broadcasted_iota(jnp.int32, (8, 8), 0) == lanes((8, 8))
    column = lambda g: jnp.sum(jnp.where(diagonal, g[...].astype(F32), 0.0), axis=1, keepdims=True)
    for t in range(EP):
        kv = [k[:, 64 * t : 64 * t + 64], w[:, 64 * t : 64 * t + 64]]
        row = [q[:, 128 * t : 128 * t + 128], jnp.concatenate(kv, axis=1)]
        wp[t] = jnp.concatenate(row, axis=0).astype(BF)
        wqkv_o[:, 256 * t : 256 * t + 256] = jnp.concatenate(row, axis=1).astype(BF)
    results[10].start()
    w, r = wo[...].astype(F32), wr[...].astype(F32)
    left = jnp.concatenate([w[:, :512], r, jnp.zeros((8, 96), F32)], axis=1)
    right = jnp.concatenate([w[:, 512:], column(ga), column(gm), jnp.zeros((8, 126), F32)], axis=1)
    wop[...] = jnp.concatenate([left, right], axis=0).astype(BF)
    spread = lax.broadcasted_iota(jnp.int32, (8, 128), 1) - 8 * e
    spread = spread == lax.broadcasted_iota(jnp.int32, (8, 128), 0)
    line = jnp.sum(jnp.where(spread, column(ga), 0.0), axis=0, keepdims=True)
    gp[...] = jnp.broadcast_to(line, (8, 128))
    wait()
    make = Sender(ss, rs)
    send = make.now
    own = [
        pltpu.make_async_copy(x, xall.at[e], ls.at[0]),
        pltpu.make_async_copy(wp.at[e], wsl.at[v, u, e], ls.at[1]),
        pltpu.make_async_copy(wop, wof.at[u, v, e], ls.at[2]),
        pltpu.make_async_copy(rt, rall.at[e], ls.at[3]),
        pltpu.make_async_copy(gp, gb.at[e], ls.at[8]),
    ]
    for cp in own:
        cp.start()
    tokens = [
        Ring(lambda s, k: xall.at[s, h, k], lambda k: x.at[h, k], d, e, z, c, make) for h in range(2)
    ]
    moes = [
        Ring(lambda s, k: moe.at[s, h, k], lambda k: mo.at[h, k], d, e, z, c, make) for h in range(2)
    ]
    gains = [send(gp, gb.at[e], p) for p in ep_peers(d, e)]
    first = [send(wp.at[p[1]], wsl.at[v, u, e], p) for p in ep_peers(d, e)]
    first += [send(wop, wof.at[u, v, e], p) for p in ep_peers(d, e)]
    tokens[0].start(0)
    tokens[0].start(1)
    own[1].wait()
    for cp in first[: EP - 1]:
        cp.wait_recv()
    w1 = [send(wsl.at[v, u], wsl.at[v, u], p) for p in across]
    own[4].wait()
    for cp in gains:
        cp.wait_recv()
    line = gb[0]
    for s in range(1, EP):
        line = line + gb[s]
    gs[v, u] = line
    g1 = [send(gs.at[v, u], gs.at[v, u], p) for p in across]
    own[2].wait()
    for cp in first[EP - 1 :]:
        cp.wait_recv()
    mine = pl.ds(c * 4, 4)
    part = (d, z * 2 + 1 - c)
    o1 = [send(wof.at[u, v, mine], wof.at[u, v, mine], p) for p in along]
    tokens[0].forward()
    for cp in w1:
        cp.wait_recv()
    w2 = Quad(lambda i, h: wsl.at[i, pair(h)], v, ahead, behind, make)
    w2.start()
    for cp in g1:
        cp.wait_recv()
    g2 = [send(gs.at[v], gs.at[v], p) for p in along]
    last = []
    for k, cp in zip((1, 3, 2), o1):
        cp.wait_recv()
        t = lax.rem(v + 4 - k, 4)
        last.append(send(wof.at[u, t, mine], wof.at[u, t, mine], part))
    o2 = Quad(lambda i, h: wof.at[i, :, pl.ds(c * 4 + 2 * h, 2)], u, up, down, make)
    o2.start()
    tokens[1].start(0)
    tokens[1].start(1)
    w2.forward()
    tokens[0].finish()
    own[0].wait()
    w2.arrived()
    for cp in g2:
        cp.wait_recv()
    for i in range(DP):
        w = wsl[i % 4, i // 4].astype(F32)
        w = jnp.concatenate([w[:, :8].reshape(64, 128), w[:, 8:].reshape(64, 128)], axis=1)
        w_s[64 * i : 64 * i + 64] = w.astype(BF)
    gain_a = jnp.concatenate([gs[i % 4, i // 4][:1, :64] for i in range(DP)], axis=1)

    def project(h):
        for r in range(4):
            rows = slice(256 * r, 256 * r + 256)
            t = xall[2 * r : 2 * r + 2, h].astype(F32).reshape(256, D)
            factor = lax.rsqrt(jnp.mean(t * t, axis=1, keepdims=True) + EPS)
            n = (t * factor * gain_a).astype(BF)
            nrm_o[h, rows] = n
            pre = nn(n, w_s[...])
            co, si = cs[rows], sn[rows]
            q, kv = pre[:, :128], pre[:, 128:]
            q_o[h, rows] = (q * co + turn(q) * si).astype(BF)
            kv = jnp.where(lanes(kv.shape) < HD, kv * co + turn(kv) * si, kv).astype(BF)
            kv_o[h, rows] = kv
            kk_s[rows], vv_s[rows] = both(kv.astype(F32))

    def attend(h, i):
        ids_k = ids[h : h + 1]
        ids_q = jnp.broadcast_to(ids_k[:, ROWS * i : ROWS * i + ROWS], (128, ROWS)).T[:, :1]
        q2 = two_heads(q_o[h, ROWS * i : ROWS * i + ROWS].astype(F32)).astype(BF)
        own_ids = jnp.concatenate([ids_q, ids_q], axis=0)
        at, end = spans(i)
        parts = []
        if at:
            parts.append((nt(q2, kk_s[:at]) * (SCORE * LOG2E), slice(0, at)))
        t = nt(q2, kk_s[at:end]) * (SCORE * LOG2E)
        parts.append((jnp.where(ids_k[:, at:end] <= own_ids, t, MASKED), slice(at, end)))
        peak = parts[0][0].max(axis=1, keepdims=True)
        for t, _ in parts[1:]:
            peak = jnp.maximum(peak, t.max(axis=1, keepdims=True))
        total, out = 0.0, 0.0
        for t, span in parts:
            p = jnp.exp2(t - peak)
            total = total + p.sum(axis=1, keepdims=True)
            out = out + nn(p.astype(BF), vv_s[span])
        out = out * (1.0 / total)
        lse = jnp.broadcast_to(peak + jnp.log2(total), (2 * ROWS, 128))
        low = lanes((ROWS, 128)) < HD
        att = jnp.where(low, out[:ROWS], out[ROWS:]).astype(BF)
        att_o[2 * i : 2 * i + 2, h] = att.reshape(2, HALF, 128)
        lse_o[h, ROWS * i : ROWS * i + ROWS] = jnp.where(low, lse[:ROWS], lse[ROWS:])

    att_own = [pltpu.make_async_copy(att_o.at[e, h], arr.at[e, h], ls.at[4 + h]) for h in range(2)]
    moe_own = [pltpu.make_async_copy(mo.at[h], moe.at[e, h], ls.at[6 + h]) for h in range(2)]

    def exchange(h):
        att_own[h].start()
        cps = []
        for k in (4, 3, 5, 2, 6, 1, 7):
            t = lax.rem(e + k, EP)
            cps.append(send(att_o.at[t, h], arr.at[e, h], (d, t)))
        return cps

    def branch(h, cps):
        att_own[h].wait()
        for cp in cps:
            cp.wait_recv()
        a = jnp.concatenate([arr[s, h] for s in range(EP)], axis=1)
        at_o[h] = a
        m = xall[e, h].astype(F32).reshape(HALF, D) + RES * nn(a, wo_o[...])
        mid_o[h] = m
        factor = lax.rsqrt(jnp.mean(m * m, axis=1, keepdims=True) + EPS)
        n = (m * factor * gt_o[33:34, :]).astype(BF)
        own_o[h] = n
        mo[h] = n.reshape(2, HALF // 2, D)
        moe_own[h].start()
        moes[h].start(0)
        moes[h].start(1)

    project(0)
    tokens[1].forward()
    attend(0, 0)
    attend(0, 1)
    o2.forward()
    attend(0, 2)
    attend(0, 3)
    x0 = exchange(0)
    tokens[1].finish()
    project(1)
    attend(1, 0)
    attend(1, 1)
    attend(1, 2)
    attend(1, 3)
    x1 = exchange(1)
    for cp in results[:5]:
        cp.start()
    o2.arrived()
    for k in (1, 3, 2):
        t = near(u, k)
        last.append(send(wof.at[t, :, mine], wof.at[t, :, mine], part))
    routes = [send(rt, rall.at[e], p) for p in ep_peers(d, e)]
    for cp in last:
        cp.wait_recv()
    for i in range(4):
        rows = slice(256 * i, 256 * i + 256)
        o = wof[i].astype(F32).reshape(32, 16, 640)
        left, right = o[:, :8].reshape(256, 640), o[:, 8:].reshape(256, 640)
        wo_o[rows, :512] = left[:, :512].astype(BF)
        wo_o[rows, 512:] = right[:, :512].astype(BF)
        sm_s[rows] = jnp.where(lanes((256, 128)) < 32, left[:, 512:], pltpu.roll(right[:, 512:], 32, 1))
    gt_o[...] = sm_s[...].T
    for cp in results[5:7]:
        cp.start()
    branch(0, x0)
    branch(1, x1)
    for cp in results[7:10]:
        cp.start()
    moes[0].forward()
    moes[1].forward()
    moes[0].finish()
    moes[1].finish()
    w2.sent()
    o2.sent()
    for cp in gains + first + w1 + g1 + g2 + o1 + last + x0 + x1:
        cp.wait_send()
    for cp in routes:
        cp.wait()
    own[3].wait()
    for cp in moe_own + results:
        cp.wait()


def routing(rt, logits_t):
    ids = lax.broadcasted_iota(jnp.int32, (EXPERTS, ROWS), 0)
    hit = rt[0:1] == ids
    for k in range(1, 8):
        hit = hit | (rt[k : k + 1] == ids)
    w = jnp.where(hit, logits_t, MASKED)
    w = jnp.where(hit, jnp.exp(w - w.max(axis=0, keepdims=True)), 0.0)
    gates = w / w.sum(axis=0, keepdims=True)
    earlier = lax.broadcasted_iota(jnp.int32, (ROWS, ROWS), 0) < lax.broadcasted_iota(
        jnp.int32, (ROWS, ROWS), 1
    )
    slot = nn(jnp.where(hit, 1.0, 0.0).astype(BF), jnp.where(earlier, 1.0, 0.0).astype(BF))
    return gates, jnp.where(hit, slot, -1.0)


class Reduce:
    def __init__(self, chunk, me, ahead, behind, one, two, three, make):
        at = lambda k: lax.rem(me + k, 4)
        self.one, self.two, self.three = one, two, three
        self.first = [
            make(chunk(at(2), 0), one.at[0], ahead),
            make(chunk(at(2), 1), one.at[1], behind),
        ]
        self.second = [
            make(chunk(at(1), 1), two.at[0], ahead),
            make(chunk(at(3), 0), two.at[1], behind),
        ]
        self.third = [make(one.at[0], three.at[0], ahead), make(one.at[1], three.at[1], behind)]

    def start(self):
        for cp in self.first + self.second:
            cp.start()

    def go_on(self, k, mine, pieces):
        self.first[k].wait_recv()

        def add(i, carry):
            self.one[k, i] = self.one[k, i] + (mine[i] if pieces > 1 else mine[...])
            return carry

        lax.fori_loop(0, pieces, add, 0)
        self.third[k].start()

    def arrived(self, k):
        self.second[1 - k].wait_recv()
        self.third[k].wait_recv()

    def sent(self):
        for cp in self.first + self.second + self.third:
            cp.wait_send()


def close(r, chunk, pieces):
    for k in range(2):
        r.arrived(k)

        def body(i, carry):
            for q in range(2):
                piece = r.two[1 - k, i, q].astype(F32) + r.three[k, i, q].astype(F32)
                chunk[i, 2 * k + q] = (chunk[i, 2 * k + q].astype(F32) + piece).astype(BF)
            return carry

        lax.fori_loop(0, pieces, body, 0)


def experts_weights(
    moe, cot, at, rall, gt, wg, wu, wd, dw_o, eo_h, dg_o, du_o, gg_o, p_h, ca_o, cb_o, at_o,
    eo_o, p_o, cot_s, x_s, y_s, gate_s, a_s, b_s, h_s, dw_s, a1, a2, a3, b1, b2, b3, ls, ss, rs,
):
    step = pl.program_id(0)
    d, e, z, c = place()
    u, v, up, down, ahead, behind = plane(d, e)
    first = e * OWN
    make = Sender(ss, rs)
    cots = Ring(lambda s, k: cot_s.at[s, k], lambda k: cot.at[k], d, e, z, c, make)
    ats = Ring(lambda s, k: at_o.at[s, k], lambda k: at.at[k], d, e, z, c, make)
    ra = Reduce(lambda i, h: dw_s.at[:, i, pair(h), 0], u, up, down, a1, a2, a3, make)
    rb = Reduce(lambda i, h: dw_s.at[:, pair(h), i, 1], v, ahead, behind, b1, b2, b3, make)
    own = pltpu.make_async_copy(cot, cot_s.at[e], ls.at[0])
    own_at = pltpu.make_async_copy(at, at_o.at[e], ls.at[2])
    results = [pltpu.make_async_copy(eo_o, eo_h, ls.at[3]), pltpu.make_async_copy(p_o, p_h, ls.at[4])]
    rows_of = lambda s: pl.ds(pl.multiple_of(s * CAP, 16), CAP)

    @pl.when(step == 0)
    def _():
        load = pltpu.make_async_copy(moe, y_s.at[pl.ds(0, EP * ROWS)], ls.at[1])
        load.start()
        greet(ep_peers(d, e) + [up, down, ahead, behind])()
        cots.start(0)
        cots.start(1)
        own.start()
        own_at.start()
        load.wait()
        router_t = gt[:EXPERTS].astype(BF)
        row = lax.broadcasted_iota(jnp.int32, (EXPERTS, ROWS), 0)
        place_in = lax.broadcasted_iota(jnp.int32, (CAP, ROWS), 0).astype(F32)

        def source(s, carry):
            m = y_s[pl.ds(pl.multiple_of(s * ROWS, ROWS), ROWS)]
            gates, slot = routing(rall[s], nt(router_t, m))
            picks = []
            for i in range(OWN):
                sel = row == first + i
                pick = jnp.sum(jnp.where(sel, slot, 0.0), axis=0, keepdims=True) == place_in
                gate = jnp.sum(jnp.where(sel, gates, 0.0), axis=0, keepdims=True)
                g = jnp.sum(jnp.where(pick, gate, 0.0), axis=1, keepdims=True)
                gate_s[i, rows_of(s)] = jnp.broadcast_to(g, (CAP, 128))
                picks.append(jnp.where(pick, 1.0, 0.0).astype(BF))
            pick = jnp.concatenate(picks, axis=0)
            p_o[s] = pick
            xs = nn(pick, m).astype(BF)
            for i in range(OWN):
                x_s[i, rows_of(s)] = xs[CAP * i : CAP * i + CAP]
            return carry

        lax.fori_loop(0, EP, source, 0)

    @pl.when(step < OWN)
    def _():
        x = x_s[step]
        gate = gate_s[step][:, :1] * RES
        g = nn(x, wg[0])
        u = nn(x, wu[0])
        s = 1.0 / (1.0 + jnp.exp(-g))
        silu = g * s
        a_s[step] = (u * s * (1.0 + g * (1.0 - s))).astype(BF)
        b_s[step] = silu.astype(BF)
        h = silu * u
        h_s[step] = h.astype(BF)
        eo = nn((h * gate).astype(BF), wd[0]).astype(BF)
        for i in range(EP):
            eo_o[i, rows_of(step)] = eo[CAP * i : CAP * i + CAP]

    @pl.when(step == 2)
    def _():
        cots.forward()
        ats.start(0)
        ats.start(1)

    @pl.when(step == OWN)
    def _():
        for cp in results:
            cp.start()
        cots.finish()
        own.wait()

        def source(s, carry):
            ys = nn(p_o[s], cot_s[s].reshape(ROWS, D)).astype(BF)
            for i in range(OWN):
                at = pl.ds(pl.multiple_of(i * SLOTS + s * CAP, 16), CAP)
                y_s[at] = ys[CAP * i : CAP * i + CAP]
            return carry

        lax.fori_loop(0, EP, source, 0)

    def back(j, store):
        x, y = x_s[j], y_s[pl.ds(pl.multiple_of(j * SLOTS, SLOTS), SLOTS)]
        gate = gate_s[j][:, :1] * RES
        dh = nt(y, wd[0])
        h = h_s[j].astype(F32)
        gg_o[0] = jnp.broadcast_to(RES * jnp.sum(h * dh, axis=1, keepdims=True), (SLOTS, 128))
        dh = dh * gate
        dg = (dh * a_s[j].astype(F32)).astype(BF)
        du = (dh * b_s[j].astype(F32)).astype(BF)
        dg_o[0], du_o[0] = dg, du
        w = tn(x, jnp.concatenate([dg, du], axis=1))
        store(0, w[:, :F].astype(BF))
        store(1, w[:, F:].astype(BF))
        w = tn((h * gate).astype(BF), y)
        store(2, jnp.concatenate([w[:, :F], w[:, F:]], axis=0).astype(BF))

    @pl.when(step == OWN)
    def _():
        whole_w = [None] * 3

        def store(i, w):
            whole_w[i] = w

        back(0, store)
        dw_s[0] = jnp.concatenate(whole_w, axis=0).reshape(4, 4, 2, 96, F)
        ra.start()
        rb.start()

    @pl.when(step > OWN)
    def _():
        def store(i, w):
            dw_o[0, D * i : D * i + D] = w

        back(step - OWN, store)

    @pl.when(step == OWN + 1)
    def _():
        ats.forward()
        for k in range(2):
            ra.go_on(k, dw_s.at[0, near(u, 1 + 2 * k), pair(k), 0], 1)
            rb.go_on(k, dw_s.at[0, pair(k), near(v, 1 + 2 * k), 1], 1)

    @pl.when(step == 2 * OWN - 1)
    def _():
        ats.finish()
        own_at.wait()
        for cp in results:
            cp.wait()
        ca_o[0] = dw_s[0, u, :, 0]
        cb_o[0] = dw_s[0, :, v, 1]
        close(ra, ca_o, 1)
        close(rb, cb_o, 1)
        ra.sent()
        rb.sent()


class Combine:
    def __init__(self, term, stage, buf, m1, m2, m3, d, z, c, make):
        right, left = (d, near(z, 1) * 2 + c), (d, near(z, 3) * 2 + c)
        self.term, self.stage, self.buf, self.m1, self.m2, self.m3, self.c = term, stage, buf, m1, m2, m3, c
        self.turns = [near(z, k) * 2 for k in (2, 1, 3, 0)]
        self.mates = [make(stage.at[i], buf.at[i], (d, z * 2 + 1 - c)) for i in range(4)]
        lo, hi = pl.ds(0, HALF), pl.ds(HALF, HALF)
        self.s1 = [make(buf.at[0, lo], m1.at[0], right), make(buf.at[0, hi], m1.at[1], left)]
        self.s2 = [make(buf.at[1, hi], m2.at[0], right), make(buf.at[2, lo], m2.at[1], left)]
        self.s3 = [make(m1.at[0], m3.at[0], right), make(m1.at[1], m3.at[1], left)]

    def begin(self):
        for i, t in enumerate(self.turns):
            self.stage[i] = self.term(t + 1 - self.c).astype(BF)
            self.mates[i].start()

    def add(self, i):
        own = self.term(self.turns[i] + self.c)
        self.mates[i].wait_recv()
        self.buf[i] = (self.buf[i].astype(F32) + own).astype(BF)

    def send(self):
        self.add(0)
        for cp in self.s1:
            cp.start()
        self.add(1)
        self.s2[0].start()
        self.add(2)
        self.s2[1].start()

    def go_on(self):
        for k, i in ((0, 1), (1, 2)):
            self.s1[k].wait_recv()
            self.m1[k] = self.m1[k] + self.buf[i, HALF * k : HALF * k + HALF]
            self.s3[k].start()

    def finish(self, out, columns):
        for k in range(2):
            rows = slice(HALF * k, HALF * k + HALF)
            self.s2[1 - k].wait_recv()
            self.s3[k].wait_recv()
            arrived = self.m2[1 - k].astype(F32) + self.m3[k].astype(F32)
            out[rows, columns] = self.buf[3, rows].astype(F32) + arrived

    def sent(self):
        for cp in self.mates + self.s1 + self.s2 + self.s3:
            cp.wait_send()


def experts_combine(
    eo_h, dg, du, gg_h, picks_h, wg, wu, dw, ca, cb, mg_o, gt_o, sh_o,
    eo, picks, gg, dx_s, gg_s, stage, buf, m1, m2, m3, stage_, buf_, m1_, m2_, m3_,
    a1, a2, a3, amine, ac, b1, b2, b3, bmine, bc, a4, a5, a6, b4, b5, b6, ls, ss, rs,
):
    j = pl.program_id(0)
    d, e, z, c = place()
    u, v, up, down, ahead, behind = plane(d, e)
    make = Sender(ss, rs)
    later = pl.ds(1, OWN - 1)
    deep = lambda h: pl.ds(48 * h, 48)
    ra = Reduce(lambda i, h: dw.at[:, i, pair(h), 0], u, up, down, a1, a2, a3, make)
    rb = Reduce(lambda i, h: dw.at[:, pair(h), i, 1], v, ahead, behind, b1, b2, b3, make)
    qa = Reduce(lambda i, h: ac.at[:, i, deep(h)], v, ahead, behind, a4, a5, a6, make)
    qb = Reduce(lambda i, h: bc.at[:, i, deep(h)], u, up, down, b4, b5, b6, make)
    mix = Combine(lambda s: tn(picks[s], eo[s]), stage, buf, m1, m2, m3, d, z, c, make)
    back = Combine(lambda s: tn(picks[s], dx_s[s]), stage_, buf_, m1_, m2_, m3_, d, z, c, make)
    load = pltpu.make_async_copy
    own = [
        load(dw.at[:, near(u, 1), pair(0), 0], amine.at[0], ls.at[0]),
        load(dw.at[:, near(u, 3), pair(1), 0], amine.at[1], ls.at[1]),
        load(dw.at[:, pair(0), near(v, 1), 1], bmine.at[0], ls.at[2]),
        load(dw.at[:, pair(1), near(v, 3), 1], bmine.at[1], ls.at[3]),
        load(dw.at[:, u, :, 0], ac.at[later], ls.at[4]),
        load(dw.at[:, :, v, 1], bc.at[later], ls.at[5]),
        load(ca, ac.at[pl.ds(0, 1)], ls.at[6]),
        load(cb, bc.at[pl.ds(0, 1)], ls.at[7]),
    ]
    gt_own = load(gg_s.at[e], gt_o.at[e], ls.at[8])
    rows = [make(gg_s.at[p[1]], gt_o.at[e], p) for p in ep_peers(d, e)]

    early = [load(eo_h, eo, ls.at[9]), load(picks_h, picks, ls.at[10]), load(gg_h, gg, ls.at[11])]

    @pl.when(j == 0)
    def _():
        for cp in early:
            cp.start()
        greet(ep_peers(d, e) + [up, down, ahead, behind])()
        ra.start()
        rb.start()
        for cp in own:
            cp.start()
        for cp in early:
            cp.wait()
        mix.begin()

    @pl.when(j == 1)
    def _():
        mix.send()

    dx = (nt(dg[0], wg[0]) + nt(du[0], wu[0])).astype(BF)
    for s in range(EP):
        dx_s[s, pl.ds(pl.multiple_of(j * CAP, 16), CAP)] = dx[CAP * s : CAP * s + CAP]

    @pl.when(j == OWN - 1)
    def _():
        back.begin()
        mix.go_on()
        back.send()
        for cp in own:
            cp.wait()
        for k in range(2):
            ra.go_on(k, amine.at[k], OWN - 1)
            rb.go_on(k, bmine.at[k], OWN - 1)
        mix.add(3)
        for s in range(EP):
            p = picks[s]
            at = pl.ds(pl.multiple_of(s * CAP, 16), CAP)
            lines = [
                jnp.sum(
                    p[CAP * i : CAP * i + CAP].astype(F32) * gg[i, at][:, :1], axis=0, keepdims=True
                )
                for i in range(OWN)
            ]
            gg_s[s] = jnp.concatenate(lines + [jnp.zeros((8 - OWN, ROWS), F32)], axis=0)
        for cp in rows:
            cp.start()
        gt_own.start()
        back.add(3)
        back.go_on()
        mix.finish(mg_o, slice(0, D))
        close(ra, ac.at[later], OWN - 1)
        qa.start()
        close(rb, bc.at[later], OWN - 1)
        qb.start()
        back.finish(mg_o, slice(D, 2 * D))
        for q, chunk, me in ((qa, ac, v), (qb, bc, u)):
            for k in range(2):
                t = near(me, 1 + 2 * k)
                q.first[k].wait_recv()
                q.one[k] = q.one[k] + chunk[:, t, 48 * k : 48 * k + 48]
                q.third[k].start()
        for h, q, chunk, me in ((0, qa, ac, v), (1, qb, bc, u)):
            for k in range(2):
                q.arrived(k)
                mine = chunk[:, me, 48 * k : 48 * k + 48].astype(F32)
                total = mine + q.two[1 - k].astype(F32) + q.three[k].astype(F32)
                sh_o[:, h, 48 * k : 48 * k + 48] = total.astype(BF)
        for r in (ra, rb, qa, qb, mix, back):
            r.sent()
        for cp in rows:
            cp.wait()
        gt_own.wait()


def norm_back(grad, values, factor, gain):
    scaled = grad * gain
    grad_gain = jnp.sum(grad * values * factor, axis=0, keepdims=True)
    mean = jnp.mean(scaled * values, axis=1, keepdims=True)
    return factor * (scaled - values * (factor * factor * mean)), grad_gain


def after_experts(
    mg, gg, rt, moe, mid, cot, gt, wo, gm_o, st_o, da_o, gb_o, da, gb, ls, ss, rs
):
    d, e, z, c = place()
    wait = greet(ep_peers(d, e))
    m = mid[...]
    router_t = gt[:EXPERTS].astype(BF)
    gates, _ = routing(rt, nt(router_t, moe[...]))
    back = gg[...][:, :OWN].reshape(EXPERTS, ROWS)
    both_ = gates * back
    gl = (both_ - gates * jnp.sum(both_, axis=0, keepdims=True)).astype(BF)
    wait()
    make = Sender(ss, rs)
    grad = mg[:, D:] + tn(gl, router_t)
    factor = lax.rsqrt(jnp.mean(m * m, axis=1, keepdims=True) + EPS)
    gm, gain = norm_back(grad, m, factor, gt[33:34])
    gm = cot[...].astype(F32) + gm
    gradient = (RES * gm).astype(BF)
    ga = nt(gradient, wo[...]).astype(BF)
    for t in range(EP):
        da[t] = ga[:, 128 * t : 128 * t + 128]
        gb[t] = gradient[:, 128 * t : 128 * t + 128]
    own = [
        pltpu.make_async_copy(da.at[e], da_o.at[e], ls.at[0]),
        pltpu.make_async_copy(gb.at[e], gb_o.at[e], ls.at[1]),
    ]
    cps = [make.now(da.at[p[1]], da_o.at[e], p) for p in ep_peers(d, e)]
    cps += [make.now(gb.at[p[1]], gb_o.at[e], p) for p in ep_peers(d, e)]
    for cp in own:
        cp.start()
    gm_o[...] = gm
    st_o[...] = jnp.zeros_like(st_o)
    st_o[:EXPERTS] = nn(gl, moe[...])
    st_o[33:34] = gain
    for cp in cps:
        cp.wait()
    for cp in own:
        cp.wait()


def attend_back(q, kv, nrm, att, lse, da, gb, at, cs, sn, ids, dq_o, dw_o, kk_s, vv_s, dk_s, dv_s):
    s = pl.program_id(0)
    kk_s[...], vv_s[...] = both(kv[0].astype(F32))
    dk_s[...] = jnp.zeros_like(dk_s)
    dv_s[...] = jnp.zeros_like(dv_s)
    ids_k = ids[0]
    ids_q = jnp.broadcast_to(ids_k, (128, LEN)).T[:, :1]
    low = lanes((ROWS, 128)) < HD

    def unturn(v, rows):
        return v * cs[rows] - turn(v) * sn[rows]

    dqs = []
    for i in range(4):
        rows = slice(ROWS * i, ROWS * i + ROWS)
        q2 = two_heads(q[0, rows].astype(F32)).astype(BF)
        o = da[2 * i : 2 * i + 2, 0].reshape(ROWS, 128).astype(F32)
        o2f = two_heads(o)
        o2 = o2f.astype(BF)
        a = att[2 * i : 2 * i + 2, 0].reshape(ROWS, 128).astype(F32)
        delta = jnp.sum(o2f * jnp.concatenate([a, a], axis=0), axis=1, keepdims=True)
        l2 = jnp.concatenate([lse[0, rows][:, :1], lse[0, rows][:, HD : HD + 1]], axis=0)
        own = ids_q[rows]
        own = jnp.concatenate([own, own], axis=0)
        at_, end = spans(i)
        dq = 0.0
        for span in ([slice(0, at_)] if at_ else []) + [slice(at_, end)]:
            t = nt(q2, kk_s[span]) * (SCORE * LOG2E) - l2
            if span.start == at_:
                t = jnp.where(ids_k[:, span] <= own, t, MASKED)
            p = jnp.exp2(t)
            gp = nt(o2, vv_s[span])
            ds = (p * (gp - delta)).astype(BF)
            dq = dq + nn(ds, kk_s[span])
            dk_s[span] += tn(ds, q2)
            dv_s[span] += tn(p.astype(BF), o2)
        dq = SCORE * jnp.where(low, dq[:ROWS], dq[ROWS:])
        dqs.append(unturn(dq, rows).astype(BF))
    w = []
    for i in range(4):
        rows = slice(ROWS * i, ROWS * i + ROWS)
        dk, dv = dk_s[rows], dv_s[rows]
        dk = unturn(SCORE * (dk + pltpu.roll(dk, HD, 1)), rows)
        dv = dv + pltpu.roll(dv, HD, 1)
        dkv = jnp.where(low, dk, dv).astype(BF)
        dqkv = jnp.concatenate([dqs[i], dkv], axis=1)
        dq_o[2 * i : 2 * i + 2, 0] = dqkv.reshape(2, HALF, 256)
        w.append(dqkv)
    wqkv = tn(nrm[0], jnp.concatenate(w, axis=0))
    wout = tn(at[:, 0].reshape(LEN, D), gb[:, 0].reshape(LEN, 128))
    w = jnp.concatenate([wqkv, wout], axis=1)

    @pl.when(s == 0)
    def _():
        dw_o[...] = w

    @pl.when(s == 1)
    def _():
        dw_o[...] += w


def finish_weights(
    dq, wf, x, gm, gt, st, dw, gx_o, wq_o, wk_o, wv_o, wo_o, sm_o,
    dq_s, wf_s, pa, pb, a1, a2, a3, b1, b2, b3, ca, cb, a4, a5, a6, b4, b5, b6, s1, r2, ls, ss, rs,
):
    d, e, z, c = place()
    u, v, up, down, ahead, behind = plane(d, e)
    wait = greet(ep_peers(d, e) + [up, down, ahead, behind])
    load = pltpu.make_async_copy
    own = [
        load(wf, wf_s, ls.at[0]),
        load(dq.at[e], dq_s.at[e], ls.at[1]),
    ]
    for cp in own:
        cp.start()
    pa[0] = dw[:, :256].astype(BF).reshape(4, 4, 64, 256)
    wait()
    make = Sender(ss, rs)
    cps = [make.now(dq.at[p[1]], dq_s.at[e], p) for p in ep_peers(d, e)]
    deep = lambda h: pl.ds(32 * h, 32)
    ra = Reduce(lambda i, h: pa.at[:, i, pair(h)], u, up, down, a1, a2, a3, make)
    rb = Reduce(lambda i, h: pb.at[:, pair(h), i], v, ahead, behind, b1, b2, b3, make)
    qa = Reduce(lambda i, h: ca.at[:, i, deep(h)], v, ahead, behind, a4, a5, a6, make)
    qb = Reduce(lambda i, h: cb.at[:, i, deep(h)], u, up, down, b4, b5, b6, make)
    ra.start()
    for k in range(2):
        ra.go_on(k, pa.at[0, near(u, 1 + 2 * k), pair(k)], 1)
    own[0].wait()
    own[1].wait()
    for cp in cps:
        cp.wait_recv()
    grad = 0.0
    for s in range(EP):
        grad = grad + nt(dq_s[s], wf_s[:, 256 * s : 256 * s + 256])
    t = x[...].astype(F32)
    factor = lax.rsqrt(jnp.mean(t * t, axis=1, keepdims=True) + EPS)
    g, gain = norm_back(grad, t, factor, gt[32:33])
    row = lax.broadcasted_iota(jnp.int32, (128, D), 0)
    small = jnp.where(row == 32, gain, st[...]).T
    pb[0] = jnp.concatenate([dw[:, 256:], small], axis=1).astype(BF).reshape(4, 4, 64, 256)
    rb.start()
    gx_o[...] = gm[...] + g
    ca[0] = pa[0, u]
    close(ra, ca, 1)
    qa.start()
    for k in range(2):
        rb.go_on(k, pb.at[0, pair(k), near(v, 1 + 2 * k)], 1)

    def second(q, chunk, me):
        for k in range(2):
            q.first[k].wait_recv()
            q.one[k] = q.one[k] + chunk[:, near(me, 1 + 2 * k), 32 * k : 32 * k + 32]
            q.third[k].start()

    def last(q, chunk, me, columns):
        for k in range(2):
            q.arrived(k)
            mine = chunk[0, me, 32 * k : 32 * k + 32].astype(F32)
            total = mine + q.two[1 - k, 0].astype(F32) + q.three[k, 0].astype(F32)
            s1[4 * k : 4 * k + 4, :, columns] = total.reshape(4, 8, 256)

    second(qa, ca, v)
    cb[0] = pb[0, :, v]
    close(rb, cb, 1)
    qb.start()
    last(qa, ca, v, slice(0, 256))
    second(qb, cb, u)
    last(qb, cb, u, slice(256, 512))
    r2[e] = s1[e]
    more = [make.now(s1.at[p[1]], r2.at[e], p) for p in ep_peers(d, e)]
    for cp in more:
        cp.wait_recv()
    small = r2[0, :, 384:]
    for s in range(1, EP):
        small = small + r2[s, :, 384:]
    sm_o[...] = small
    wq_o[...] = jnp.concatenate([r2[s, :, :128] for s in range(EP)], axis=1)
    wk_o[...] = jnp.concatenate([r2[s, :, 128:192] for s in range(EP)], axis=1)
    wv_o[...] = jnp.concatenate([r2[s, :, 192:256] for s in range(EP)], axis=1)
    wo_o[...] = jnp.concatenate([r2[s, :, 256:384] for s in range(EP)], axis=1)
    for q in (ra, rb, qa, qb):
        q.sent()
    for cp in cps + more:
        cp.wait_send()


def widen(dw, q, k, v, o, sm, g_o, u_o, d_o, q_o, k_o, v_o, o_o, r_o):
    w = dw[...].reshape(3 * D, F).astype(F32)
    g_o[0] = w[:D]
    u_o[0] = w[D : 2 * D]
    d_o[0, :, :F] = w[2 * D : 2 * D + F]
    d_o[0, :, F:] = w[2 * D + F :]

    @pl.when(pl.program_id(0) == 0)
    def _():
        q_o[...], k_o[...], v_o[...], o_o[...] = q[...], k[...], v[...], o[...]
        r_o[...] = sm[:, :EXPERTS]


def tables():
    even = np.arange(0, HD, 2).astype(np.float32)
    frequency = (np.float32(10000.0) ** (-even / np.float32(HD))).astype(np.float32)
    angle = np.arange(LEN, dtype=np.float32)[:, None] * frequency[None, :]
    angle = np.concatenate([angle] * 4, axis=1).astype(np.float64)
    return np.cos(angle).astype(np.float32), np.sin(angle).astype(np.float32)


def per_device(
    tokens, cotangent, block_ids, routes, w_query, w_key, w_value, w_output, w_router,
    gain_attn, gain_moe, expert_gate, expert_up, expert_down,
):
    x = tokens.reshape(ROWS, D)
    cot = cotangent.reshape(ROWS, D)
    rt = routes.reshape(ROWS, 8).T
    cos, sin = tables()
    cos, sin = jnp.asarray(cos), jnp.asarray(sin)
    params = pltpu.CompilerParams(vmem_limit_bytes=60 * MIB)
    once = pl.Buffered(1)

    def whole(shape):
        return pl.BlockSpec(shape, lambda s: (0,) * len(shape), pipeline_mode=once)

    kept = [
        ((SEQS, LEN, 128), BF), ((SEQS, LEN, 128), BF), ((SEQS, LEN, D), BF),
        ((EP, 2, HALF, 128), BF), ((SEQS, LEN, 128), F32), ((128, D), F32), ((D, D), BF),
        ((2, HALF, D), F32), ((2, HALF, D), BF), ((2, HALF, D), BF), ((8, 2 * D), BF),
    ]
    rall, moe, q, kv, nrm, att, lse, gt, wo, mid, moe_own, at_own, w_qkv = remote_call(
        before_experts, 1,
        [
            sds((EP, 8, ROWS), jnp.int32), sds((EP, 2, 2, HALF // 2, D), BF),
            *[sds(*k) for k in kept],
        ],
        [
            tokens.reshape(2, 2, HALF // 2, D), rt, w_query, w_key, w_value, w_output, w_router,
            gain_attn.reshape(1, 8), gain_moe.reshape(1, 8), cos, sin, block_ids,
        ],
        [ANY] + [VM] * 11,
        [
            *[pltpu.VMEM(*k) for k in kept],
            pltpu.VMEM((EP, 2, 2, HALF // 2, D), BF), pltpu.VMEM((4, 4, EP, 16, 128), BF),
            pltpu.VMEM((4, 4, EP, 16, 640), BF), pltpu.VMEM((EP, 16, 128), BF),
            pltpu.VMEM((16, 640), BF), pltpu.VMEM((8, 128), F32), pltpu.VMEM((EP, 8, 128), F32),
            pltpu.VMEM((4, 4, 8, 128), F32), pltpu.VMEM((D, 256), BF), pltpu.VMEM((D, 128), F32),
            pltpu.VMEM((LEN, 128), BF), pltpu.VMEM((LEN, 128), BF),
            pltpu.VMEM((EP, 2, HALF, 128), BF), pltpu.VMEM((2, 2, HALF // 2, D), BF),
        ],
        128,
        vmem=60,
    )
    w_full = lax.all_gather(w_qkv, ("dp", "ep"), axis=0, tiled=True)

    seq = lambda *shape: pl.BlockSpec((1, *shape), lambda s: (s,) + (0,) * len(shape))
    cut = lambda n: pl.BlockSpec((EP, 1, HALF, n), lambda s: (0, s, 0, 0))
    each = lambda *shape: pl.BlockSpec((1, *shape), lambda j: (j,) + (0,) * len(shape))
    fwd = lambda *shape: pl.BlockSpec(
        (1, *shape), lambda j: (jnp.minimum(j, OWN - 1),) + (0,) * len(shape)
    )
    bwd = lambda *shape: pl.BlockSpec(
        (1, *shape), lambda j: (jnp.maximum(j - OWN, 0),) + (0,) * len(shape)
    )
    slots = lambda dtype, n: pltpu.VMEM((OWN, SLOTS, n), dtype)
    rest = pl.BlockSpec((1, 3 * D, F), lambda j: (jnp.maximum(j - OWN - 1, 0), 0, 0))
    both_ways = pl.BlockSpec((1, F, D), lambda j: (lax.rem(j, OWN), 0, 0))
    moved = pltpu.VMEM((2, 1, 2, 96, F), BF)
    dw, eo, dg, du, gg, picks, ca, cb, at_all = pl.pallas_call(
        experts_weights,
        name="experts_weights",
        grid=(2 * OWN,),
        out_shape=[
            sds((OWN - 1, 3 * D, F), BF), sds((EP, OWN * CAP, D), BF), sds((OWN, SLOTS, F), BF),
            sds((OWN, SLOTS, F), BF), sds((OWN, SLOTS, 128), F32), sds((EP, OWN * CAP, ROWS), BF),
            sds((1, 4, 96, F), BF), sds((1, 4, 96, F), BF), sds((EP, 2, HALF, D), BF),
        ],
        in_specs=[
            ANY, ANY, ANY, whole((EP, 8, ROWS)), whole((128, D)), fwd(D, F), fwd(D, F), both_ways,
        ],
        out_specs=[
            rest, ANY, bwd(SLOTS, F), bwd(SLOTS, F), bwd(SLOTS, 128),
            ANY, whole((1, 4, 96, F)), whole((1, 4, 96, F)), ANY,
        ],
        scratch_shapes=[
            pltpu.VMEM((EP, OWN * CAP, D), BF), pltpu.VMEM((EP, OWN * CAP, ROWS), BF),
            pltpu.VMEM((EP, 2, HALF, D), BF), slots(BF, D), pltpu.VMEM((OWN * SLOTS, D), BF),
            slots(F32, 128), slots(BF, F), slots(BF, F), slots(BF, F),
            pltpu.VMEM((1, 4, 4, 2, 96, F), BF), *[moved] * 6, pltpu.SemaphoreType.DMA((5,)),
            pltpu.SemaphoreType.DMA((48,)), pltpu.SemaphoreType.DMA((48,)),
        ],
        compiler_params=pltpu.CompilerParams(
            collective_id=2, has_side_effects=True, vmem_limit_bytes=62 * MIB
        ),
    )(
        moe.reshape(EP * ROWS, D), cotangent.reshape(2, HALF, D), at_own, rall, gt, expert_gate, expert_up,
        expert_down,
    )

    mg, gg_all, shard = pl.pallas_call(
        experts_combine,
        name="experts_combine",
        grid=(OWN,),
        out_shape=[
            sds((ROWS, 2 * D), F32), sds((EP, 8, ROWS), F32), sds((OWN, 2, 96, F), BF),
        ],
        in_specs=[
            ANY, each(SLOTS, F), each(SLOTS, F), ANY, ANY, each(D, F), each(D, F), ANY, ANY, ANY,
        ],
        out_specs=[whole((ROWS, 2 * D)), ANY, whole((OWN, 2, 96, F))],
        scratch_shapes=[
            pltpu.VMEM((EP, OWN * CAP, D), BF), pltpu.VMEM((EP, OWN * CAP, ROWS), BF),
            slots(F32, 128), pltpu.VMEM((EP, OWN * CAP, D), BF), pltpu.VMEM((EP, 8, ROWS), F32),
            *([pltpu.VMEM((4, ROWS, D), BF)] * 2 + [pltpu.VMEM((2, HALF, D), BF)] * 3) * 2,
            *([pltpu.VMEM((2, OWN - 1, 2, 96, F), BF)] * 4 + [pltpu.VMEM((OWN, 4, 96, F), BF)]) * 2,
            *[pltpu.VMEM((2, OWN, 48, F), BF)] * 6,
            pltpu.SemaphoreType.DMA((12,)),
            pltpu.SemaphoreType.DMA((64,)),
            pltpu.SemaphoreType.DMA((64,)),
        ],
        compiler_params=pltpu.CompilerParams(
            collective_id=3, has_side_effects=True, vmem_limit_bytes=62 * MIB
        ),
    )(
        eo, dg, du, gg, picks, expert_gate, expert_up, dw.reshape(OWN - 1, 4, 4, 2, 96, F), ca, cb,
    )
    dw_sum = lax.all_gather(shard.reshape(OWN, 192, F), "dp", axis=0)

    gm, st, da_all, gb_all = remote_call(
        after_experts, 4,
        [
            sds((ROWS, D), F32), sds((128, D), F32), sds((EP, ROWS, 128), BF),
            sds((EP, ROWS, 128), BF),
        ],
        [mg, gg_all, rt, moe_own.reshape(ROWS, D), mid.reshape(ROWS, D), cot, gt, wo],
        [VM] * 8,
        [pltpu.VMEM((EP, ROWS, 128), BF), pltpu.VMEM((EP, ROWS, 128), BF)],
        16,
        [VM] * 2 + [ANY] * 2,
    )
    output = (mid.reshape(ROWS, D) + mg[:, :D]).astype(BF)

    dq, dw_attn = pl.pallas_call(
        attend_back,
        name="attend_back",
        grid=(SEQS,),
        out_shape=[sds((EP, 2, HALF, 256), BF), sds((D, 384), F32)],
        in_specs=[
            seq(LEN, 128), seq(LEN, 128), seq(LEN, D), cut(128), seq(LEN, 128), cut(128),
            cut(128), cut(D), whole((LEN, 128)), whole((LEN, 128)), seq(1, LEN),
        ],
        out_specs=[cut(256), whole((D, 384))],
        scratch_shapes=[
            pltpu.VMEM((LEN, 128), BF), pltpu.VMEM((LEN, 128), BF),
            pltpu.VMEM((LEN, 128), F32), pltpu.VMEM((LEN, 128), F32),
        ],
        compiler_params=params,
    )(
        q, kv, nrm, att, lse, da_all.reshape(EP, 2, HALF, 128), gb_all.reshape(EP, 2, HALF, 128),
        at_all, cos, sin, block_ids.reshape(SEQS, 1, LEN),
    )

    part = lambda *n: [pltpu.VMEM((2, 1, *n), BF)] * 3
    grad_x, gq, gk, gv, go, gs = remote_call(
        finish_weights, 5,
        [
            sds((ROWS, D), F32), sds((8, D), F32), sds((8, 512), F32), sds((8, 512), F32),
            sds((8, D), F32), sds((8, 128), F32),
        ],
        [dq.reshape(EP, ROWS, 256), w_full, x, gm, gt, st, dw_attn],
        [ANY, ANY] + [VM] * 5,
        [
            pltpu.VMEM((EP, ROWS, 256), BF), pltpu.VMEM((D, 2 * D), BF),
            pltpu.VMEM((1, 4, 4, 64, 256), BF), pltpu.VMEM((1, 4, 4, 64, 256), BF),
            *part(2, 64, 256), *part(2, 64, 256), pltpu.VMEM((1, 4, 64, 256), BF),
            pltpu.VMEM((1, 4, 64, 256), BF), *part(32, 256), *part(32, 256),
            pltpu.VMEM((EP, 8, 512), F32), pltpu.VMEM((EP, 8, 512), F32),
        ],
        44,
        [VM] * 6,
    )

    small = [(8, D), (8, 512), (8, 512), (8, D)]
    g_gate, g_up, g_down, gq, gk, gv, go, gr = pl.pallas_call(
        widen,
        name="widen",
        grid=(OWN,),
        out_shape=[
            sds((OWN, D, F), F32), sds((OWN, D, F), F32), sds((OWN, F, D), F32),
            *[sds(n, F32) for n in small], sds((8, EXPERTS), F32),
        ],
        in_specs=[
            pl.BlockSpec((DP, 1, 192, F), lambda j: (0, j, 0, 0)), *[whole(n) for n in small],
            whole((8, 128)),
        ],
        out_specs=[
            each(D, F), each(D, F), each(F, D), *[whole(n) for n in small], whole((8, EXPERTS)),
        ],
        compiler_params=params,
    )(dw_sum, gq, gk, gv, go, gs)
    return (
        output.reshape(tokens.shape),
        grad_x.astype(BF).reshape(tokens.shape),
        gq,
        gk,
        gv,
        go,
        gr,
        gs[:, 32],
        gs[:, 33],
        g_gate,
        g_up,
        g_down,
    )


def solution(mesh):
    rows, own, both_axes = P("dp", "ep", None), P("ep", None, None), P(("dp", "ep"), None)
    line = P(("dp", "ep"))
    return jax.shard_map(
        per_device,
        mesh=mesh,
        in_specs=(
            rows, rows, P("dp", None), rows, both_axes, both_axes, both_axes, both_axes, both_axes,
            line, line, own, own, own,
        ),
        out_specs=(
            rows, rows, both_axes, both_axes, both_axes, both_axes, both_axes, line, line, own,
            own, own,
        ),
        check_vma=False,
    )
```

```python
import math

import jax
import jax.numpy as jnp
import numpy as np
from jax import lax
from jax.experimental import pallas as pl
from jax.experimental.pallas import tpu as pltpu
from jax.sharding import PartitionSpec as P

MESH = pl.DeviceIdType.MESH
BF = jnp.bfloat16
F32 = jnp.float32
ANY = pl.BlockSpec(memory_space=pl.ANY)
VM = pl.BlockSpec(memory_space=pltpu.VMEM)

DP, EP, CHIPS = 16, 8, 4
D, HD, F = 1024, 64, 512
ROWS, HALF, LEN, SEQS = 256, 128, 1024, 2
EXPERTS, OWN, CAP = 32, 4, 80
SLOTS = EP * CAP
EPS = 1e-6
RES = 0.22
SCORE = 0.015625
LOG2E = 1.4426950408889634
MASKED = -1e30
MIB = 2**20


def nt(a, b):
    return lax.dot_general(a, b, (((1,), (1,)), ((), ())), preferred_element_type=F32)


def nn(a, b):
    return jnp.dot(a, b, preferred_element_type=F32)


def tn(a, b):
    return lax.dot_general(a, b, (((0,), (0,)), ((), ())), preferred_element_type=F32)


def place():
    e = lax.axis_index("ep")
    return lax.axis_index("dp"), e, e // 2, lax.rem(e, 2)


def near(k, n):
    return lax.rem(k + n, 4)


def plane(d, e):
    u, v = d // 4, lax.rem(d, 4)
    up, down = (near(u, 1) * 4 + v, e), (near(u, 3) * 4 + v, e)
    return u, v, up, down, (u * 4 + near(v, 1), e), (u * 4 + near(v, 3), e)


def pair(h):
    return pl.ds(2 * h, 2)


def greet(peers):
    b = pltpu.get_barrier_semaphore()
    for p in peers:
        pl.semaphore_signal(b, inc=1, device_id=p, device_id_type=MESH)
    return lambda: pl.semaphore_wait(b, len(peers))


def ep_peers(d, e):
    return [(d, lax.rem(e + k, EP)) for k in range(1, EP)]


def dp_peers(d, e):
    return [(lax.rem(d + k, DP), e) for k in range(1, DP)]


class Sender:
    def __init__(self, ss, rs):
        self.ss, self.rs, self.n = ss, rs, 0

    def __call__(self, src, dst, dev):
        i = self.n
        self.n += 1
        return pltpu.make_async_remote_copy(
            src, dst, self.ss.at[i], self.rs.at[i], device_id=dev, device_id_type=MESH
        )

    def now(self, src, dst, dev):
        cp = self(src, dst, dev)
        cp.start()
        return cp


class Ring:
    def __init__(self, out, src, d, e, z, c, make):
        right, left = (d, lax.rem(z + 1, CHIPS) * 2 + c), (d, lax.rem(z + 3, CHIPS) * 2 + c)
        part = (d, z * 2 + 1 - c)
        er, el, eo = right[1], left[1], lax.rem(z + 2, CHIPS) * 2 + c
        self.near = [
            [make(src(0), out(e, 0), right), make(src(0), out(e, 0), left)],
            [make(src(1), out(e, 1), left), make(src(1), out(e, 1), right)],
        ]
        self.mate = [make(src(0), out(e, 0), part), make(src(1), out(e, 1), part)]
        self.far = [make(out(el, 0), out(el, 0), right), make(out(er, 1), out(er, 1), left)]
        self.share = [
            make(out(s, h), out(s, h), part)
            for s, h in ((el, 0), (er, 1), (el, 1), (er, 0), (eo, 0), (eo, 1))
        ]

    def start(self, h):
        for cp in self.near[h]:
            cp.start()
        self.mate[h].start()

    def forward(self):
        for h in range(2):
            self.near[h][0].wait_recv()
            self.far[h].start()
            self.share[h].start()
        for h in range(2):
            self.near[1 - h][1].wait_recv()
            self.share[2 + h].start()

    def finish(self):
        for h in range(2):
            self.far[h].wait_recv()
            self.share[4 + h].start()
        for cp in self.near[0] + self.near[1] + self.far:
            cp.wait_send()
        for cp in self.mate + self.share:
            cp.wait()


class Quad:
    def __init__(self, out, me, ahead, behind, make, src=None):
        after, before = lax.rem(me + 1, 4), lax.rem(me + 3, 4)
        mine = lambda h, dev: make(src(h) if src else out(me, h), out(me, h), dev)
        self.near = [
            [mine(0, ahead), mine(0, behind)],
            [mine(1, behind), mine(1, ahead)],
        ]
        self.far = [
            make(out(before, 0), out(before, 0), ahead),
            make(out(after, 1), out(after, 1), behind),
        ]

    def start(self):
        for h in range(2):
            for cp in self.near[h]:
                cp.start()

    def forward(self):
        for h in range(2):
            self.near[h][0].wait_recv()
            self.far[h].start()

    def near_arrived(self):
        for h in range(2):
            self.near[h][1].wait_recv()

    def far_arrived(self):
        for h in range(2):
            self.far[h].wait_recv()

    def arrived(self):
        self.near_arrived()
        self.far_arrived()

    def sent(self):
        for cp in self.near[0] + self.near[1] + self.far:
            cp.wait_send()


def remote_call(body, cid, outs, ins, specs, scratch, sems, out_specs=None, vmem=48, flops=0):
    return pl.pallas_call(
        body,
        name=body.__name__,
        out_shape=outs,
        in_specs=specs,
        out_specs=out_specs if out_specs is not None else [ANY] * len(outs),
        scratch_shapes=[
            *scratch,
            pltpu.SemaphoreType.DMA((24,)),
            pltpu.SemaphoreType.DMA((sems,)),
            pltpu.SemaphoreType.DMA((sems,)),
        ],
        compiler_params=pltpu.CompilerParams(
            collective_id=cid, has_side_effects=True, vmem_limit_bytes=vmem * MIB
        ),
        cost_estimate=pl.CostEstimate(flops=flops, bytes_accessed=20 * MIB, transcendentals=0),
    )(*ins)


def sds(shape, dtype):
    return jax.ShapeDtypeStruct(shape, dtype)


def lanes(shape):
    return lax.broadcasted_iota(jnp.int32, shape, 1)


def turn(v):
    first = lax.rem(lanes(v.shape), HD) < HD // 2
    return jnp.where(first, -pltpu.roll(v, 128 - HD // 2, 1), pltpu.roll(v, HD // 2, 1))


def both(kv):
    low = lanes(kv.shape) < HD
    other = pltpu.roll(kv, HD, 1)
    return jnp.where(low, kv, other).astype(BF), jnp.where(low, other, kv).astype(BF)


def two_heads(v):
    low = lanes(v.shape) < HD
    zero = jnp.zeros_like(v)
    return jnp.concatenate([jnp.where(low, v, zero), jnp.where(low, zero, v)], axis=0)


def spans(i):
    return i * ROWS, min(LEN, i * ROWS + 2 * ROWS)


def before_experts(
    x, rt, w_q, w_k, w_v, wo, wr, ga, gm, cs, sn, ids,
    rall, moe, q_h, kv_h, nrm_h, att_h, lse_h, gt_h, wo_h, mid_h, own_h, at_h, wqkv_h,
    q_o, kv_o, nrm_o, att_o, lse_o, gt_o, wo_o, mid_o, own_o, at_o, wqkv_o,
    xall, wsl, wof, wp, wop, gp, gb, gs, w_s, sm_s, kk_s, vv_s, arr, mo, ls, ss, rs,
):
    d, e, z, c = place()
    u, v, up, down, ahead, behind = plane(d, e)
    pairs = [
        (q_o, q_h), (kv_o, kv_h), (nrm_o, nrm_h), (att_o, att_h), (lse_o, lse_h), (gt_o, gt_h),
        (wo_o, wo_h), (mid_o, mid_h), (own_o, own_h), (at_o, at_h), (wqkv_o, wqkv_h),
    ]
    results = [pltpu.make_async_copy(a, b, ls.at[10 + i]) for i, (a, b) in enumerate(pairs)]
    across = [up, down, (near(u, 2) * 4 + v, e)]
    along = [ahead, behind, (u * 4 + near(v, 2), e)]
    wait = greet(ep_peers(d, e) + across + along)
    q, k, w = w_q[...].astype(F32), w_k[...].astype(F32), w_v[...].astype(F32)
    diagonal = lax.broadcasted_iota(jnp.int32, (8, 8), 0) == lanes((8, 8))
    column = lambda g: jnp.sum(jnp.where(diagonal, g[...].astype(F32), 0.0), axis=1, keepdims=True)
    for t in range(EP):
        kv = [k[:, 64 * t : 64 * t + 64], w[:, 64 * t : 64 * t + 64]]
        row = [q[:, 128 * t : 128 * t + 128], jnp.concatenate(kv, axis=1)]
        wp[t] = jnp.concatenate(row, axis=0).astype(BF)
        wqkv_o[:, 256 * t : 256 * t + 256] = jnp.concatenate(row, axis=1).astype(BF)
    results[10].start()
    w, r = wo[...].astype(F32), wr[...].astype(F32)
    left = jnp.concatenate([w[:, :512], r, jnp.zeros((8, 96), F32)], axis=1)
    right = jnp.concatenate([w[:, 512:], column(ga), column(gm), jnp.zeros((8, 126), F32)], axis=1)
    wop[...] = jnp.concatenate([left, right], axis=0).astype(BF)
    spread = lax.broadcasted_iota(jnp.int32, (8, 128), 1) - 8 * e
    spread = spread == lax.broadcasted_iota(jnp.int32, (8, 128), 0)
    line = jnp.sum(jnp.where(spread, column(ga), 0.0), axis=0, keepdims=True)
    gp[...] = jnp.broadcast_to(line, (8, 128))
    wait()
    make = Sender(ss, rs)
    send = make.now
    own = [
        pltpu.make_async_copy(x, xall.at[e], ls.at[0]),
        pltpu.make_async_copy(wp.at[e], wsl.at[v, u, e], ls.at[1]),
        pltpu.make_async_copy(wop, wof.at[u, v, e], ls.at[2]),
        pltpu.make_async_copy(rt, rall.at[e], ls.at[3]),
        pltpu.make_async_copy(gp, gb.at[e], ls.at[8]),
    ]
    for cp in own:
        cp.start()
    tokens = [
        Ring(lambda s, k: xall.at[s, h, k], lambda k: x.at[h, k], d, e, z, c, make) for h in range(2)
    ]
    moes = [
        Ring(lambda s, k: moe.at[s, h, k], lambda k: mo.at[h, k], d, e, z, c, make) for h in range(2)
    ]
    gains = [send(gp, gb.at[e], p) for p in ep_peers(d, e)]
    first = [send(wp.at[p[1]], wsl.at[v, u, e], p) for p in ep_peers(d, e)]
    first += [send(wop, wof.at[u, v, e], p) for p in ep_peers(d, e)]
    tokens[0].start(0)
    tokens[0].start(1)
    own[1].wait()
    for cp in first[: EP - 1]:
        cp.wait_recv()
    w1 = [send(wsl.at[v, u], wsl.at[v, u], p) for p in across]
    own[4].wait()
    for cp in gains:
        cp.wait_recv()
    line = gb[0]
    for s in range(1, EP):
        line = line + gb[s]
    gs[v, u] = line
    g1 = [send(gs.at[v, u], gs.at[v, u], p) for p in across]
    own[2].wait()
    for cp in first[EP - 1 :]:
        cp.wait_recv()
    mine = pl.ds(c * 4, 4)
    part = (d, z * 2 + 1 - c)
    o1 = [send(wof.at[u, v, mine], wof.at[u, v, mine], p) for p in along]
    tokens[0].forward()
    for cp in w1:
        cp.wait_recv()
    w2 = Quad(lambda i, h: wsl.at[i, pair(h)], v, ahead, behind, make)
    w2.start()
    for cp in g1:
        cp.wait_recv()
    g2 = [send(gs.at[v], gs.at[v], p) for p in along]
    last = []
    for k, cp in zip((1, 3, 2), o1):
        cp.wait_recv()
        t = lax.rem(v + 4 - k, 4)
        last.append(send(wof.at[u, t, mine], wof.at[u, t, mine], part))
    o2 = Quad(lambda i, h: wof.at[i, :, pl.ds(c * 4 + 2 * h, 2)], u, up, down, make)
    o2.start()
    tokens[1].start(0)
    tokens[1].start(1)
    w2.forward()
    tokens[0].finish()
    own[0].wait()
    w2.arrived()
    for cp in g2:
        cp.wait_recv()
    for i in range(DP):
        w = wsl[i % 4, i // 4].astype(F32)
        w = jnp.concatenate([w[:, :8].reshape(64, 128), w[:, 8:].reshape(64, 128)], axis=1)
        w_s[64 * i : 64 * i + 64] = w.astype(BF)
    gain_a = jnp.concatenate([gs[i % 4, i // 4][:1, :64] for i in range(DP)], axis=1)

    def project(h):
        for r in range(4):
            rows = slice(256 * r, 256 * r + 256)
            t = xall[2 * r : 2 * r + 2, h].astype(F32).reshape(256, D)
            factor = lax.rsqrt(jnp.mean(t * t, axis=1, keepdims=True) + EPS)
            n = (t * factor * gain_a).astype(BF)
            nrm_o[h, rows] = n
            pre = nn(n, w_s[...])
            co, si = cs[rows], sn[rows]
            q, kv = pre[:, :128], pre[:, 128:]
            q_o[h, rows] = (q * co + turn(q) * si).astype(BF)
            kv = jnp.where(lanes(kv.shape) < HD, kv * co + turn(kv) * si, kv).astype(BF)
            kv_o[h, rows] = kv
            kk_s[rows], vv_s[rows] = both(kv.astype(F32))

    def attend(h, i):
        ids_k = ids[h : h + 1]
        ids_q = jnp.broadcast_to(ids_k[:, ROWS * i : ROWS * i + ROWS], (128, ROWS)).T[:, :1]
        q2 = two_heads(q_o[h, ROWS * i : ROWS * i + ROWS].astype(F32)).astype(BF)
        own_ids = jnp.concatenate([ids_q, ids_q], axis=0)
        at, end = spans(i)
        parts = []
        if at:
            parts.append((nt(q2, kk_s[:at]) * (SCORE * LOG2E), slice(0, at)))
        t = nt(q2, kk_s[at:end]) * (SCORE * LOG2E)
        parts.append((jnp.where(ids_k[:, at:end] <= own_ids, t, MASKED), slice(at, end)))
        peak = parts[0][0].max(axis=1, keepdims=True)
        for t, _ in parts[1:]:
            peak = jnp.maximum(peak, t.max(axis=1, keepdims=True))
        total, out = 0.0, 0.0
        for t, span in parts:
            p = jnp.exp2(t - peak)
            total = total + p.sum(axis=1, keepdims=True)
            out = out + nn(p.astype(BF), vv_s[span])
        out = out * (1.0 / total)
        lse = jnp.broadcast_to(peak + jnp.log2(total), (2 * ROWS, 128))
        low = lanes((ROWS, 128)) < HD
        att = jnp.where(low, out[:ROWS], out[ROWS:]).astype(BF)
        att_o[2 * i : 2 * i + 2, h] = att.reshape(2, HALF, 128)
        lse_o[h, ROWS * i : ROWS * i + ROWS] = jnp.where(low, lse[:ROWS], lse[ROWS:])

    att_own = [pltpu.make_async_copy(att_o.at[e, h], arr.at[e, h], ls.at[4 + h]) for h in range(2)]
    moe_own = [pltpu.make_async_copy(mo.at[h], moe.at[e, h], ls.at[6 + h]) for h in range(2)]

    def exchange(h):
        att_own[h].start()
        cps = []
        for k in (4, 3, 5, 2, 6, 1, 7):
            t = lax.rem(e + k, EP)
            cps.append(send(att_o.at[t, h], arr.at[e, h], (d, t)))
        return cps

    def branch(h, cps):
        att_own[h].wait()
        for cp in cps:
            cp.wait_recv()
        a = jnp.concatenate([arr[s, h] for s in range(EP)], axis=1)
        at_o[h] = a
        m = xall[e, h].astype(F32).reshape(HALF, D) + RES * nn(a, wo_o[...])
        mid_o[h] = m
        factor = lax.rsqrt(jnp.mean(m * m, axis=1, keepdims=True) + EPS)
        n = (m * factor * gt_o[33:34, :]).astype(BF)
        own_o[h] = n
        mo[h] = n.reshape(2, HALF // 2, D)
        moe_own[h].start()
        moes[h].start(0)
        moes[h].start(1)

    project(0)
    tokens[1].forward()
    attend(0, 0)
    attend(0, 1)
    o2.forward()
    attend(0, 2)
    attend(0, 3)
    x0 = exchange(0)
    tokens[1].finish()
    project(1)
    attend(1, 0)
    attend(1, 1)
    attend(1, 2)
    attend(1, 3)
    x1 = exchange(1)
    for cp in results[:5]:
        cp.start()
    o2.arrived()
    for k in (1, 3, 2):
        t = near(u, k)
        last.append(send(wof.at[t, :, mine], wof.at[t, :, mine], part))
    routes = [send(rt, rall.at[e], p) for p in ep_peers(d, e)]
    for cp in last:
        cp.wait_recv()
    for i in range(4):
        rows = slice(256 * i, 256 * i + 256)
        o = wof[i].astype(F32).reshape(32, 16, 640)
        left, right = o[:, :8].reshape(256, 640), o[:, 8:].reshape(256, 640)
        wo_o[rows, :512] = left[:, :512].astype(BF)
        wo_o[rows, 512:] = right[:, :512].astype(BF)
        sm_s[rows] = jnp.where(lanes((256, 128)) < 32, left[:, 512:], pltpu.roll(right[:, 512:], 32, 1))
    gt_o[...] = sm_s[...].T
    for cp in results[5:7]:
        cp.start()
    branch(0, x0)
    branch(1, x1)
    for cp in results[7:10]:
        cp.start()
    moes[0].forward()
    moes[1].forward()
    moes[0].finish()
    moes[1].finish()
    w2.sent()
    o2.sent()
    for cp in gains + first + w1 + g1 + g2 + o1 + last + x0 + x1:
        cp.wait_send()
    for cp in routes:
        cp.wait()
    own[3].wait()
    for cp in moe_own + results:
        cp.wait()


def routing(rt, logits_t):
    ids = lax.broadcasted_iota(jnp.int32, (EXPERTS, ROWS), 0)
    hit = rt[0:1] == ids
    for k in range(1, 8):
        hit = hit | (rt[k : k + 1] == ids)
    w = jnp.where(hit, logits_t, MASKED)
    w = jnp.where(hit, jnp.exp(w - w.max(axis=0, keepdims=True)), 0.0)
    gates = w / w.sum(axis=0, keepdims=True)
    earlier = lax.broadcasted_iota(jnp.int32, (ROWS, ROWS), 0) < lax.broadcasted_iota(
        jnp.int32, (ROWS, ROWS), 1
    )
    slot = nn(jnp.where(hit, 1.0, 0.0).astype(BF), jnp.where(earlier, 1.0, 0.0).astype(BF))
    return gates, jnp.where(hit, slot, -1.0)


class Reduce:
    def __init__(self, chunk, me, ahead, behind, one, two, three, make):
        at = lambda k: lax.rem(me + k, 4)
        self.one, self.two, self.three = one, two, three
        self.first = [
            make(chunk(at(2), 0), one.at[0], ahead),
            make(chunk(at(2), 1), one.at[1], behind),
        ]
        self.second = [
            make(chunk(at(1), 1), two.at[0], ahead),
            make(chunk(at(3), 0), two.at[1], behind),
        ]
        self.third = [make(one.at[0], three.at[0], ahead), make(one.at[1], three.at[1], behind)]

    def start(self):
        for cp in self.first + self.second:
            cp.start()

    def go_on(self, k, mine, pieces):
        self.first[k].wait_recv()

        def add(i, carry):
            self.one[k, i] = self.one[k, i] + (mine[i] if pieces > 1 else mine[...])
            return carry

        lax.fori_loop(0, pieces, add, 0)
        self.third[k].start()

    def arrived(self, k):
        self.second[1 - k].wait_recv()
        self.third[k].wait_recv()

    def sent(self):
        for cp in self.first + self.second + self.third:
            cp.wait_send()


def close(r, chunk, pieces):
    for k in range(2):
        r.arrived(k)

        def body(i, carry):
            for q in range(2):
                piece = r.two[1 - k, i, q].astype(F32) + r.three[k, i, q].astype(F32)
                chunk[i, 2 * k + q] = (chunk[i, 2 * k + q].astype(F32) + piece).astype(BF)
            return carry

        lax.fori_loop(0, pieces, body, 0)


def experts_weights(
    moe, cot, at, rall, gt, wg, wu, wd, dw_o, eo_h, dg_o, du_o, gg_o, p_h, ca_o, cb_o, at_o,
    eo_o, p_o, cot_s, x_s, y_s, gate_s, a_s, b_s, h_s, dw_s, a1, a2, a3, b1, b2, b3, ls, ss, rs,
):
    step = pl.program_id(0)
    d, e, z, c = place()
    u, v, up, down, ahead, behind = plane(d, e)
    first = e * OWN
    make = Sender(ss, rs)
    cots = Ring(lambda s, k: cot_s.at[s, k], lambda k: cot.at[k], d, e, z, c, make)
    ats = Ring(lambda s, k: at_o.at[s, k], lambda k: at.at[k], d, e, z, c, make)
    ra = Reduce(lambda i, h: dw_s.at[:, i, pair(h), 0], u, up, down, a1, a2, a3, make)
    rb = Reduce(lambda i, h: dw_s.at[:, pair(h), i, 1], v, ahead, behind, b1, b2, b3, make)
    own = pltpu.make_async_copy(cot, cot_s.at[e], ls.at[0])
    own_at = pltpu.make_async_copy(at, at_o.at[e], ls.at[2])
    results = [pltpu.make_async_copy(eo_o, eo_h, ls.at[3]), pltpu.make_async_copy(p_o, p_h, ls.at[4])]
    rows_of = lambda s: pl.ds(pl.multiple_of(s * CAP, 16), CAP)

    @pl.when(step == 0)
    def _():
        load = pltpu.make_async_copy(moe, y_s.at[pl.ds(0, EP * ROWS)], ls.at[1])
        load.start()
        greet(ep_peers(d, e) + [up, down, ahead, behind])()
        cots.start(0)
        cots.start(1)
        own.start()
        own_at.start()
        load.wait()
        router_t = gt[:EXPERTS].astype(BF)
        row = lax.broadcasted_iota(jnp.int32, (EXPERTS, ROWS), 0)
        place_in = lax.broadcasted_iota(jnp.int32, (CAP, ROWS), 0).astype(F32)

        def source(s, carry):
            m = y_s[pl.ds(pl.multiple_of(s * ROWS, ROWS), ROWS)]
            gates, slot = routing(rall[s], nt(router_t, m))
            picks = []
            for i in range(OWN):
                sel = row == first + i
                pick = jnp.sum(jnp.where(sel, slot, 0.0), axis=0, keepdims=True) == place_in
                gate = jnp.sum(jnp.where(sel, gates, 0.0), axis=0, keepdims=True)
                g = jnp.sum(jnp.where(pick, gate, 0.0), axis=1, keepdims=True)
                gate_s[i, rows_of(s)] = jnp.broadcast_to(g, (CAP, 128))
                picks.append(jnp.where(pick, 1.0, 0.0).astype(BF))
            pick = jnp.concatenate(picks, axis=0)
            p_o[s] = pick
            xs = nn(pick, m).astype(BF)
            for i in range(OWN):
                x_s[i, rows_of(s)] = xs[CAP * i : CAP * i + CAP]
            return carry

        lax.fori_loop(0, EP, source, 0)

    @pl.when(step < OWN)
    def _():
        x = x_s[step]
        gate = gate_s[step][:, :1] * RES
        g = nn(x, wg[0])
        u = nn(x, wu[0])
        s = 1.0 / (1.0 + jnp.exp(-g))
        silu = g * s
        a_s[step] = (u * s * (1.0 + g * (1.0 - s))).astype(BF)
        b_s[step] = silu.astype(BF)
        h = silu * u
        h_s[step] = h.astype(BF)
        eo = nn((h * gate).astype(BF), wd[0]).astype(BF)
        for i in range(EP):
            eo_o[i, rows_of(step)] = eo[CAP * i : CAP * i + CAP]

    @pl.when(step == 2)
    def _():
        cots.forward()
        ats.start(0)
        ats.start(1)

    @pl.when(step == OWN)
    def _():
        for cp in results:
            cp.start()
        cots.finish()
        own.wait()

        def source(s, carry):
            ys = nn(p_o[s], cot_s[s].reshape(ROWS, D)).astype(BF)
            for i in range(OWN):
                at = pl.ds(pl.multiple_of(i * SLOTS + s * CAP, 16), CAP)
                y_s[at] = ys[CAP * i : CAP * i + CAP]
            return carry

        lax.fori_loop(0, EP, source, 0)

    def back(j, store):
        x, y = x_s[j], y_s[pl.ds(pl.multiple_of(j * SLOTS, SLOTS), SLOTS)]
        gate = gate_s[j][:, :1] * RES
        dh = nt(y, wd[0])
        h = h_s[j].astype(F32)
        gg_o[0] = jnp.broadcast_to(RES * jnp.sum(h * dh, axis=1, keepdims=True), (SLOTS, 128))
        dh = dh * gate
        dg = (dh * a_s[j].astype(F32)).astype(BF)
        du = (dh * b_s[j].astype(F32)).astype(BF)
        dg_o[0], du_o[0] = dg, du
        w = tn(x, jnp.concatenate([dg, du], axis=1))
        store(0, w[:, :F].astype(BF))
        store(1, w[:, F:].astype(BF))
        w = tn((h * gate).astype(BF), y)
        store(2, jnp.concatenate([w[:, :F], w[:, F:]], axis=0).astype(BF))

    @pl.when(step == OWN)
    def _():
        whole_w = [None] * 3

        def store(i, w):
            whole_w[i] = w

        back(0, store)
        dw_s[0] = jnp.concatenate(whole_w, axis=0).reshape(4, 4, 2, 96, F)
        ra.start()
        rb.start()

    @pl.when(step > OWN)
    def _():
        def store(i, w):
            dw_o[0, D * i : D * i + D] = w

        back(step - OWN, store)

    @pl.when(step == OWN + 1)
    def _():
        ats.forward()
        for k in range(2):
            ra.go_on(k, dw_s.at[0, near(u, 1 + 2 * k), pair(k), 0], 1)
            rb.go_on(k, dw_s.at[0, pair(k), near(v, 1 + 2 * k), 1], 1)

    @pl.when(step == 2 * OWN - 1)
    def _():
        ats.finish()
        own_at.wait()
        for cp in results:
            cp.wait()
        ca_o[0] = dw_s[0, u, :, 0]
        cb_o[0] = dw_s[0, :, v, 1]
        close(ra, ca_o, 1)
        close(rb, cb_o, 1)
        ra.sent()
        rb.sent()


class Combine:
    def __init__(self, term, stage, buf, m1, m2, m3, d, z, c, make):
        right, left = (d, near(z, 1) * 2 + c), (d, near(z, 3) * 2 + c)
        self.term, self.stage, self.buf, self.m1, self.m2, self.m3, self.c = term, stage, buf, m1, m2, m3, c
        self.turns = [near(z, k) * 2 for k in (2, 1, 3, 0)]
        self.mates = [make(stage.at[i], buf.at[i], (d, z * 2 + 1 - c)) for i in range(4)]
        lo, hi = pl.ds(0, HALF), pl.ds(HALF, HALF)
        self.s1 = [make(buf.at[0, lo], m1.at[0], right), make(buf.at[0, hi], m1.at[1], left)]
        self.s2 = [make(buf.at[1, hi], m2.at[0], right), make(buf.at[2, lo], m2.at[1], left)]
        self.s3 = [make(m1.at[0], m3.at[0], right), make(m1.at[1], m3.at[1], left)]

    def begin(self):
        for i, t in enumerate(self.turns):
            self.stage[i] = self.term(t + 1 - self.c).astype(BF)
            self.mates[i].start()

    def add(self, i):
        own = self.term(self.turns[i] + self.c)
        self.mates[i].wait_recv()
        self.buf[i] = (self.buf[i].astype(F32) + own).astype(BF)

    def send(self):
        self.add(0)
        for cp in self.s1:
            cp.start()
        self.add(1)
        self.s2[0].start()
        self.add(2)
        self.s2[1].start()

    def go_on(self):
        for k, i in ((0, 1), (1, 2)):
            self.s1[k].wait_recv()
            self.m1[k] = self.m1[k] + self.buf[i, HALF * k : HALF * k + HALF]
            self.s3[k].start()

    def finish(self, out, columns):
        for k in range(2):
            rows = slice(HALF * k, HALF * k + HALF)
            self.s2[1 - k].wait_recv()
            self.s3[k].wait_recv()
            arrived = self.m2[1 - k].astype(F32) + self.m3[k].astype(F32)
            out[rows, columns] = self.buf[3, rows].astype(F32) + arrived

    def sent(self):
        for cp in self.mates + self.s1 + self.s2 + self.s3:
            cp.wait_send()


def experts_combine(
    eo_h, dg, du, gg_h, picks_h, wg, wu, dw, ca, cb, mg_o, gt_o, sh_o,
    eo, picks, gg, dx_s, gg_s, stage, buf, m1, m2, m3, stage_, buf_, m1_, m2_, m3_,
    a1, a2, a3, amine, ac, b1, b2, b3, bmine, bc, a4, a5, a6, b4, b5, b6, ls, ss, rs,
):
    j = pl.program_id(0)
    d, e, z, c = place()
    u, v, up, down, ahead, behind = plane(d, e)
    make = Sender(ss, rs)
    later = pl.ds(1, OWN - 1)
    deep = lambda h: pl.ds(48 * h, 48)
    ra = Reduce(lambda i, h: dw.at[:, i, pair(h), 0], u, up, down, a1, a2, a3, make)
    rb = Reduce(lambda i, h: dw.at[:, pair(h), i, 1], v, ahead, behind, b1, b2, b3, make)
    qa = Reduce(lambda i, h: ac.at[:, i, deep(h)], v, ahead, behind, a4, a5, a6, make)
    qb = Reduce(lambda i, h: bc.at[:, i, deep(h)], u, up, down, b4, b5, b6, make)
    mix = Combine(lambda s: tn(picks[s], eo[s]), stage, buf, m1, m2, m3, d, z, c, make)
    back = Combine(lambda s: tn(picks[s], dx_s[s]), stage_, buf_, m1_, m2_, m3_, d, z, c, make)
    load = pltpu.make_async_copy
    own = [
        load(dw.at[:, near(u, 1), pair(0), 0], amine.at[0], ls.at[0]),
        load(dw.at[:, near(u, 3), pair(1), 0], amine.at[1], ls.at[1]),
        load(dw.at[:, pair(0), near(v, 1), 1], bmine.at[0], ls.at[2]),
        load(dw.at[:, pair(1), near(v, 3), 1], bmine.at[1], ls.at[3]),
        load(dw.at[:, u, :, 0], ac.at[later], ls.at[4]),
        load(dw.at[:, :, v, 1], bc.at[later], ls.at[5]),
        load(ca, ac.at[pl.ds(0, 1)], ls.at[6]),
        load(cb, bc.at[pl.ds(0, 1)], ls.at[7]),
    ]
    gt_own = load(gg_s.at[e], gt_o.at[e], ls.at[8])
    rows = [make(gg_s.at[p[1]], gt_o.at[e], p) for p in ep_peers(d, e)]

    early = [load(eo_h, eo, ls.at[9]), load(picks_h, picks, ls.at[10]), load(gg_h, gg, ls.at[11])]

    @pl.when(j == 0)
    def _():
        for cp in early:
            cp.start()
        greet(ep_peers(d, e) + [up, down, ahead, behind])()
        ra.start()
        rb.start()
        for cp in own:
            cp.start()
        for cp in early:
            cp.wait()
        mix.begin()

    @pl.when(j == 1)
    def _():
        mix.send()

    dx = (nt(dg[0], wg[0]) + nt(du[0], wu[0])).astype(BF)
    for s in range(EP):
        dx_s[s, pl.ds(pl.multiple_of(j * CAP, 16), CAP)] = dx[CAP * s : CAP * s + CAP]

    @pl.when(j == OWN - 1)
    def _():
        back.begin()
        mix.go_on()
        back.send()
        for cp in own:
            cp.wait()
        for k in range(2):
            ra.go_on(k, amine.at[k], OWN - 1)
            rb.go_on(k, bmine.at[k], OWN - 1)
        mix.add(3)
        for s in range(EP):
            p = picks[s]
            at = pl.ds(pl.multiple_of(s * CAP, 16), CAP)
            lines = [
                jnp.sum(
                    p[CAP * i : CAP * i + CAP].astype(F32) * gg[i, at][:, :1], axis=0, keepdims=True
                )
                for i in range(OWN)
            ]
            gg_s[s] = jnp.concatenate(lines + [jnp.zeros((8 - OWN, ROWS), F32)], axis=0)
        for cp in rows:
            cp.start()
        gt_own.start()
        back.add(3)
        back.go_on()
        mix.finish(mg_o, slice(0, D))
        close(ra, ac.at[later], OWN - 1)
        qa.start()
        close(rb, bc.at[later], OWN - 1)
        qb.start()
        back.finish(mg_o, slice(D, 2 * D))
        for q, chunk, me in ((qa, ac, v), (qb, bc, u)):
            for k in range(2):
                t = near(me, 1 + 2 * k)
                q.first[k].wait_recv()
                q.one[k] = q.one[k] + chunk[:, t, 48 * k : 48 * k + 48]
                q.third[k].start()
        for h, q, chunk, me in ((0, qa, ac, v), (1, qb, bc, u)):
            for k in range(2):
                q.arrived(k)
                mine = chunk[:, me, 48 * k : 48 * k + 48].astype(F32)
                total = mine + q.two[1 - k].astype(F32) + q.three[k].astype(F32)
                sh_o[:, h, 48 * k : 48 * k + 48] = total.astype(BF)
        for r in (ra, rb, qa, qb, mix, back):
            r.sent()
        for cp in rows:
            cp.wait()
        gt_own.wait()


def norm_back(grad, values, factor, gain):
    scaled = grad * gain
    grad_gain = jnp.sum(grad * values * factor, axis=0, keepdims=True)
    mean = jnp.mean(scaled * values, axis=1, keepdims=True)
    return factor * (scaled - values * (factor * factor * mean)), grad_gain


def tail(
    mg_h, mid_h, wo_h, wf_h, q_h, kv_h, nrm_h, att_h, lse_h, at_h, sh, gg, rt, moe, cot, gt, x, cs, sn, ids,
    ag, out_o, gx_o, wq_o, wk_o, wv_o, wo_o, sm_o,
    mg, mid, wo, wf, q_s, kv_s, nrm, att, lse, at, da, gb, da_s, gb_s, dq, dq_s, kk_s, vv_s, dk_s, dv_s,
    gm, dw, pa, pb, ra, rb, ta, tb, qa, qb, s1, r2, ls, ss, rs,
):
    d, e, z, c = place()
    u, v, up, down, ahead, behind = plane(d, e)
    across = [up, down, (near(u, 2) * 4 + v, e)]
    along = [ahead, behind, (u * 4 + near(v, 2), e)]
    wait = greet(ep_peers(d, e) + across + along)
    pairs = [
        (mg_h, mg), (mid_h, mid), (wo_h, wo), (q_h, q_s), (kv_h, kv_s), (att_h, att), (lse_h, lse),
        (nrm_h, nrm), (at_h, at), (wf_h, wf), (sh, ag.at[u, v]),
    ]
    loads = [pltpu.make_async_copy(a, b, ls.at[i]) for i, (a, b) in enumerate(pairs)]
    for cp in loads:
        cp.start()
    router_t = gt[:EXPERTS].astype(BF)
    gates, _ = routing(rt, nt(router_t, moe[...]))
    back = gg[...][:, :OWN].reshape(EXPERTS, ROWS)
    both_ = gates * back
    gl = (both_ - gates * jnp.sum(both_, axis=0, keepdims=True)).astype(BF)
    wait()
    make = Sender(ss, rs)
    low_half = lambda k: pl.ds(48 * k, 48)
    own_a, own_b = (lambda k: sh.at[:, 0, low_half(k)]), (lambda k: sh.at[:, 1, low_half(k)])

    def piece(fixed, along_u, half, src=None):
        if along_u:
            out = lambda i, k: ag.at[i, fixed, :, half, low_half(k)]
            return Quad(out, u, up, down, make, src)
        out = lambda i, k: ag.at[fixed, i, :, half, low_half(k)]
        return Quad(out, v, ahead, behind, make, src)

    one = [piece(u, False, 0, own_a), piece(v, True, 1, own_b)]
    two = [
        [piece(near(v, k), True, 0, None if k else own_a), piece(near(u, k), False, 1, None if k else own_b)]
        for k in range(4)
    ]
    for r in one + two[0]:
        r.start()
    loads[0].wait()
    loads[1].wait()
    loads[2].wait()
    m = mid[...]
    grad = mg[:, D:] + tn(gl, router_t)
    factor = lax.rsqrt(jnp.mean(m * m, axis=1, keepdims=True) + EPS)
    t, gain_m = norm_back(grad, m, factor, gt[33:34])
    t = cot[...].astype(F32) + t
    gm[...] = t
    gradient = (RES * t).astype(BF)
    ga = nt(gradient, wo[...]).astype(BF)
    for i in range(EP):
        da[i] = ga[:, 128 * i : 128 * i + 128].reshape(2, HALF, 128)
        gb[i] = gradient[:, 128 * i : 128 * i + 128].reshape(2, HALF, 128)
    own = [
        pltpu.make_async_copy(da.at[e], da_s.at[e], ls.at[11]),
        pltpu.make_async_copy(gb.at[e], gb_s.at[e], ls.at[12]),
    ]
    for cp in own:
        cp.start()
    da_c = [make.now(da.at[p[1]], da_s.at[e], p) for p in ep_peers(d, e)]
    gb_c = [make.now(gb.at[p[1]], gb_s.at[e], p) for p in ep_peers(d, e)]
    router = nn(gl, moe[...])
    out_o[...] = (m + mg[:, :D]).astype(BF)
    for r in one:
        r.forward()
    for r in one:
        r.near_arrived()
    for r in two[1] + two[3]:
        r.start()
    for cp in loads[3:9]:
        cp.wait()
    for cp in own:
        cp.wait()
    for cp in da_c + gb_c:
        cp.wait_recv()
    low = lanes((ROWS, 128)) < HD

    def unturn(w, rows):
        return w * cs[rows] - turn(w) * sn[rows]

    def attend_back(s):
        kk_s[...], vv_s[...] = both(kv_s[s].astype(F32))
        dk_s[...] = jnp.zeros_like(dk_s)
        dv_s[...] = jnp.zeros_like(dv_s)
        ids_k = ids[s : s + 1]
        dqs = []
        for i in range(4):
            rows = slice(ROWS * i, ROWS * i + ROWS)
            q2 = two_heads(q_s[s, rows].astype(F32)).astype(BF)
            o2f = two_heads(da_s[2 * i : 2 * i + 2, s].reshape(ROWS, 128).astype(F32))
            o2 = o2f.astype(BF)
            a = att[2 * i : 2 * i + 2, s].reshape(ROWS, 128).astype(F32)
            delta = jnp.sum(o2f * jnp.concatenate([a, a], axis=0), axis=1, keepdims=True)
            l2 = jnp.concatenate([lse[s, rows][:, :1], lse[s, rows][:, HD : HD + 1]], axis=0)
            ids_q = jnp.broadcast_to(ids_k[:, rows], (128, ROWS)).T[:, :1]
            ids_q = jnp.concatenate([ids_q, ids_q], axis=0)
            start, end = spans(i)
            grad_q = 0.0
            for span in ([slice(0, start)] if start else []) + [slice(start, end)]:
                w = nt(q2, kk_s[span]) * (SCORE * LOG2E) - l2
                if span.start == start:
                    w = jnp.where(ids_k[:, span] <= ids_q, w, MASKED)
                p = jnp.exp2(w)
                gp = nt(o2, vv_s[span])
                ds = (p * (gp - delta)).astype(BF)
                grad_q = grad_q + nn(ds, kk_s[span])
                dk_s[span] += tn(ds, q2)
                dv_s[span] += tn(p.astype(BF), o2)
            grad_q = SCORE * jnp.where(low, grad_q[:ROWS], grad_q[ROWS:])
            dqs.append(unturn(grad_q, rows).astype(BF))
        grads = []
        for i in range(4):
            rows = slice(ROWS * i, ROWS * i + ROWS)
            dk, dv = dk_s[rows], dv_s[rows]
            dk = unturn(SCORE * (dk + pltpu.roll(dk, HD, 1)), rows)
            dv = dv + pltpu.roll(dv, HD, 1)
            dqkv = jnp.concatenate([dqs[i], jnp.where(low, dk, dv).astype(BF)], axis=1)
            dq[2 * i : 2 * i + 2, s] = dqkv.reshape(2, HALF, 256)
            grads.append(dqkv)
        dq_own[s].start()
        cps = [make.now(dq.at[p[1], s], dq_s.at[e, s], p) for p in ep_peers(d, e)]
        wqkv = tn(nrm[s], jnp.concatenate(grads, axis=0))
        wout = tn(at[:, s].reshape(LEN, D), gb_s[:, s].reshape(LEN, 128))
        w = jnp.concatenate([wqkv, wout], axis=1)
        if s == 0:
            dw[...] = w
        else:
            dw[...] += w
        return cps

    dq_own = [pltpu.make_async_copy(dq.at[e, s], dq_s.at[e, s], ls.at[13 + s]) for s in range(2)]
    dq_c = [attend_back(0)]
    for r in two[0]:
        r.forward()
    dq_c.append(attend_back(1))
    pa[...] = dw[:, :256].astype(BF).reshape(4, 4, 64, 256)
    a_first = [make.now(pa.at[p[0] // 4], ra.at[i], p) for i, p in enumerate(across)]
    for r in one:
        r.far_arrived()
    for r in two[2]:
        r.start()
    loads[9].wait()
    gain_a = 0.0
    for s in range(2):
        rows = slice(HALF * s, HALF * s + HALF)
        dq_own[s].wait()
        for cp in dq_c[s]:
            cp.wait_recv()
        grad = 0.0
        for i in range(EP):
            grad = grad + nt(dq_s[i, s], wf[:, 256 * i : 256 * i + 256])
        t = x[rows].astype(F32)
        factor = lax.rsqrt(jnp.mean(t * t, axis=1, keepdims=True) + EPS)
        g, gain = norm_back(grad, t, factor, gt[32:33])
        gx_o[rows] = (gm[rows] + g).astype(BF)
        gain_a = gain_a + gain
    lines = [router, gain_a, gain_m, jnp.zeros((128 - EXPERTS - 2, D), F32)]
    small = jnp.concatenate(lines, axis=0).T
    pb[...] = jnp.concatenate([dw[:, 256:], small], axis=1).astype(BF).reshape(4, 4, 64, 256)
    b_first = [make.now(pb.at[:, lax.rem(p[0], 4)], rb.at[i], p) for i, p in enumerate(along)]
    for r in two[1] + two[3]:
        r.forward()

    def total(mine, arrived, cps):
        for cp in cps:
            cp.wait_recv()
        return mine.astype(F32) + arrived[0].astype(F32) + arrived[1].astype(F32) + arrived[2].astype(F32)

    ta[...] = total(pa[u], ra, a_first).astype(BF)
    a_second = [make.now(ta.at[lax.rem(p[0], 4)], qa.at[i], p) for i, p in enumerate(along)]
    tb[...] = total(pb[:, v], rb, b_first).astype(BF)
    b_second = [make.now(tb.at[p[0] // 4], qb.at[i], p) for i, p in enumerate(across)]
    for r in two[2]:
        r.forward()
    s1[:, :, :256] = total(ta[v], qa, a_second).reshape(EP, 8, 256)
    s1[:, :, 256:] = total(tb[u], qb, b_second).reshape(EP, 8, 256)
    r2[e] = s1[e]
    more = [make.now(s1.at[p[1]], r2.at[e], p) for p in ep_peers(d, e)]
    for cp in more:
        cp.wait_recv()
    small = r2[0, :, 384:]
    for s in range(1, EP):
        small = small + r2[s, :, 384:]
    sm_o[...] = small
    wq_o[...] = jnp.concatenate([r2[s, :, :128] for s in range(EP)], axis=1)
    wk_o[...] = jnp.concatenate([r2[s, :, 128:192] for s in range(EP)], axis=1)
    wv_o[...] = jnp.concatenate([r2[s, :, 192:256] for s in range(EP)], axis=1)
    wo_o[...] = jnp.concatenate([r2[s, :, 256:384] for s in range(EP)], axis=1)
    for group in two:
        for r in group:
            r.arrived()
    for r in one + two[0] + two[1] + two[2] + two[3]:
        r.sent()
    for cp in da_c + gb_c + dq_c[0] + dq_c[1] + a_first + b_first + a_second + b_second + more:
        cp.wait_send()
    loads[10].wait()


def widen(dw, out, gx, q, k, v, o, sm, g_o, u_o, d_o, out_o, gx_o, q_o, k_o, v_o, o_o, r_o, ga_o, gm_o):
    w = dw[...].reshape(3 * D, F).astype(F32)
    g_o[0] = w[:D]
    u_o[0] = w[D : 2 * D]
    d_o[0, :, :F] = w[2 * D : 2 * D + F]
    d_o[0, :, F:] = w[2 * D + F :]
    out_o[...], gx_o[...] = out[...], gx[...]

    @pl.when(pl.program_id(0) == 0)
    def _():
        q_o[...], k_o[...], v_o[...], o_o[...] = q[...], k[...], v[...], o[...]
        r_o[...] = sm[:, :EXPERTS]
        diagonal = lax.broadcasted_iota(jnp.int32, (8, 8), 0) == lanes((8, 8))
        for i, ref in ((32, ga_o), (33, gm_o)):
            ref[...] = jnp.sum(jnp.where(diagonal, sm[:, i : i + 1], 0.0), axis=0, keepdims=True)


def tables():
    even = np.arange(0, HD, 2).astype(np.float32)
    frequency = (np.float32(10000.0) ** (-even / np.float32(HD))).astype(np.float32)
    angle = np.arange(LEN, dtype=np.float32)[:, None] * frequency[None, :]
    angle = np.concatenate([angle] * 4, axis=1).astype(np.float64)
    return np.cos(angle).astype(np.float32), np.sin(angle).astype(np.float32)


def per_device(
    tokens, cotangent, block_ids, routes, w_query, w_key, w_value, w_output, w_router,
    gain_attn, gain_moe, expert_gate, expert_up, expert_down,
):
    x = tokens.reshape(ROWS, D)
    cot = cotangent.reshape(ROWS, D)
    rt = routes.reshape(ROWS, 8).T
    cos, sin = tables()
    cos, sin = jnp.asarray(cos), jnp.asarray(sin)
    params = pltpu.CompilerParams(vmem_limit_bytes=60 * MIB)
    once = pl.Buffered(1)

    def whole(shape):
        return pl.BlockSpec(shape, lambda s: (0,) * len(shape), pipeline_mode=once)

    kept = [
        ((SEQS, LEN, 128), BF), ((SEQS, LEN, 128), BF), ((SEQS, LEN, D), BF),
        ((EP, 2, HALF, 128), BF), ((SEQS, LEN, 128), F32), ((128, D), F32), ((D, D), BF),
        ((2, HALF, D), F32), ((2, HALF, D), BF), ((2, HALF, D), BF), ((8, 2 * D), BF),
    ]
    rall, moe, q, kv, nrm, att, lse, gt, wo, mid, moe_own, at_own, w_qkv = remote_call(
        before_experts, 1,
        [
            sds((EP, 8, ROWS), jnp.int32), sds((EP, 2, 2, HALF // 2, D), BF),
            *[sds(*k) for k in kept],
        ],
        [
            tokens.reshape(2, 2, HALF // 2, D), rt, w_query, w_key, w_value, w_output, w_router,
            gain_attn.reshape(1, 8), gain_moe.reshape(1, 8), cos, sin, block_ids,
        ],
        [ANY] + [VM] * 11,
        [
            *[pltpu.VMEM(*k) for k in kept],
            pltpu.VMEM((EP, 2, 2, HALF // 2, D), BF), pltpu.VMEM((4, 4, EP, 16, 128), BF),
            pltpu.VMEM((4, 4, EP, 16, 640), BF), pltpu.VMEM((EP, 16, 128), BF),
            pltpu.VMEM((16, 640), BF), pltpu.VMEM((8, 128), F32), pltpu.VMEM((EP, 8, 128), F32),
            pltpu.VMEM((4, 4, 8, 128), F32), pltpu.VMEM((D, 256), BF), pltpu.VMEM((D, 128), F32),
            pltpu.VMEM((LEN, 128), BF), pltpu.VMEM((LEN, 128), BF),
            pltpu.VMEM((EP, 2, HALF, 128), BF), pltpu.VMEM((2, 2, HALF // 2, D), BF),
        ],
        128,
        vmem=60,
    )
    w_full = lax.all_gather(w_qkv, ("dp", "ep"), axis=0, tiled=True)

    each = lambda *shape: pl.BlockSpec((1, *shape), lambda j: (j,) + (0,) * len(shape))
    fwd = lambda *shape: pl.BlockSpec(
        (1, *shape), lambda j: (jnp.minimum(j, OWN - 1),) + (0,) * len(shape)
    )
    bwd = lambda *shape: pl.BlockSpec(
        (1, *shape), lambda j: (jnp.maximum(j - OWN, 0),) + (0,) * len(shape)
    )
    slots = lambda dtype, n: pltpu.VMEM((OWN, SLOTS, n), dtype)
    rest = pl.BlockSpec((1, 3 * D, F), lambda j: (jnp.maximum(j - OWN - 1, 0), 0, 0))
    both_ways = pl.BlockSpec((1, F, D), lambda j: (lax.rem(j, OWN), 0, 0))
    moved = pltpu.VMEM((2, 1, 2, 96, F), BF)
    dw, eo, dg, du, gg, picks, ca, cb, at_all = pl.pallas_call(
        experts_weights,
        name="experts_weights",
        grid=(2 * OWN,),
        out_shape=[
            sds((OWN - 1, 3 * D, F), BF), sds((EP, OWN * CAP, D), BF), sds((OWN, SLOTS, F), BF),
            sds((OWN, SLOTS, F), BF), sds((OWN, SLOTS, 128), F32), sds((EP, OWN * CAP, ROWS), BF),
            sds((1, 4, 96, F), BF), sds((1, 4, 96, F), BF), sds((EP, 2, HALF, D), BF),
        ],
        in_specs=[
            ANY, ANY, ANY, whole((EP, 8, ROWS)), whole((128, D)), fwd(D, F), fwd(D, F), both_ways,
        ],
        out_specs=[
            rest, ANY, bwd(SLOTS, F), bwd(SLOTS, F), bwd(SLOTS, 128),
            ANY, whole((1, 4, 96, F)), whole((1, 4, 96, F)), ANY,
        ],
        scratch_shapes=[
            pltpu.VMEM((EP, OWN * CAP, D), BF), pltpu.VMEM((EP, OWN * CAP, ROWS), BF),
            pltpu.VMEM((EP, 2, HALF, D), BF), slots(BF, D), pltpu.VMEM((OWN * SLOTS, D), BF),
            slots(F32, 128), slots(BF, F), slots(BF, F), slots(BF, F),
            pltpu.VMEM((1, 4, 4, 2, 96, F), BF), *[moved] * 6, pltpu.SemaphoreType.DMA((5,)),
            pltpu.SemaphoreType.DMA((48,)), pltpu.SemaphoreType.DMA((48,)),
        ],
        compiler_params=pltpu.CompilerParams(
            collective_id=2, has_side_effects=True, vmem_limit_bytes=62 * MIB
        ),
    )(
        moe.reshape(EP * ROWS, D), cotangent.reshape(2, HALF, D), at_own, rall, gt, expert_gate, expert_up,
        expert_down,
    )

    mg, gg_all, shard = pl.pallas_call(
        experts_combine,
        name="experts_combine",
        grid=(OWN,),
        out_shape=[
            sds((ROWS, 2 * D), F32), sds((EP, 8, ROWS), F32), sds((OWN, 2, 96, F), BF),
        ],
        in_specs=[
            ANY, each(SLOTS, F), each(SLOTS, F), ANY, ANY, each(D, F), each(D, F), ANY, ANY, ANY,
        ],
        out_specs=[whole((ROWS, 2 * D)), ANY, whole((OWN, 2, 96, F))],
        scratch_shapes=[
            pltpu.VMEM((EP, OWN * CAP, D), BF), pltpu.VMEM((EP, OWN * CAP, ROWS), BF),
            slots(F32, 128), pltpu.VMEM((EP, OWN * CAP, D), BF), pltpu.VMEM((EP, 8, ROWS), F32),
            *([pltpu.VMEM((4, ROWS, D), BF)] * 2 + [pltpu.VMEM((2, HALF, D), BF)] * 3) * 2,
            *([pltpu.VMEM((2, OWN - 1, 2, 96, F), BF)] * 4 + [pltpu.VMEM((OWN, 4, 96, F), BF)]) * 2,
            *[pltpu.VMEM((2, OWN, 48, F), BF)] * 6,
            pltpu.SemaphoreType.DMA((12,)),
            pltpu.SemaphoreType.DMA((64,)),
            pltpu.SemaphoreType.DMA((64,)),
        ],
        compiler_params=pltpu.CompilerParams(
            collective_id=3, has_side_effects=True, vmem_limit_bytes=62 * MIB
        ),
    )(
        eo, dg, du, gg, picks, expert_gate, expert_up, dw.reshape(OWN - 1, 4, 4, 2, 96, F), ca, cb,
    )
    heads = pltpu.VMEM((EP, 2, HALF, 128), BF)
    blocks = pltpu.VMEM((4, 4, 64, 256), BF)
    arriving = pltpu.VMEM((3, 4, 64, 256), BF)
    column = pltpu.VMEM((4, 64, 256), BF)
    dw_sum, output, grad_x, gq, gk, gv, go, gs = remote_call(
        tail, 4,
        [
            sds((4, 4, OWN, 2, 96, F), BF), sds((ROWS, D), BF), sds((ROWS, D), BF), sds((8, D), F32),
            sds((8, 512), F32), sds((8, 512), F32), sds((8, D), F32), sds((8, 128), F32),
        ],
        [
            mg, mid.reshape(ROWS, D), wo, w_full, q, kv, nrm, att, lse, at_all, shard, gg_all, rt,
            moe_own.reshape(ROWS, D), cot, gt, x, cos, sin, block_ids,
        ],
        [ANY] * 11 + [VM] * 9,
        [
            pltpu.VMEM((ROWS, 2 * D), F32), pltpu.VMEM((ROWS, D), F32), pltpu.VMEM((D, D), BF),
            pltpu.VMEM((D, 2 * D), BF), pltpu.VMEM((SEQS, LEN, 128), BF),
            pltpu.VMEM((SEQS, LEN, 128), BF), pltpu.VMEM((SEQS, LEN, D), BF), heads,
            pltpu.VMEM((SEQS, LEN, 128), F32), pltpu.VMEM((EP, 2, HALF, D), BF), *[heads] * 4,
            pltpu.VMEM((EP, 2, HALF, 256), BF), pltpu.VMEM((EP, 2, HALF, 256), BF),
            pltpu.VMEM((LEN, 128), BF), pltpu.VMEM((LEN, 128), BF), pltpu.VMEM((LEN, 128), F32),
            pltpu.VMEM((LEN, 128), F32), pltpu.VMEM((ROWS, D), F32), pltpu.VMEM((D, 384), F32),
            blocks, blocks, arriving, arriving, column, column, pltpu.VMEM((3, 64, 256), BF),
            pltpu.VMEM((3, 64, 256), BF),
            pltpu.VMEM((EP, 8, 512), F32), pltpu.VMEM((EP, 8, 512), F32),
        ],
        128,
        [ANY] + [VM] * 7,
        vmem=60,
    )

    small = [(8, D), (8, 512), (8, 512), (8, D)]
    rows = pl.BlockSpec((ROWS // OWN, D), lambda j: (j, 0))
    g_gate, g_up, g_down, output, grad_x, gq, gk, gv, go, gr, g_attn, g_moe = pl.pallas_call(
        widen,
        name="widen",
        grid=(OWN,),
        out_shape=[
            sds((OWN, D, F), F32), sds((OWN, D, F), F32), sds((OWN, F, D), F32),
            sds((ROWS, D), BF), sds((ROWS, D), BF), *[sds(n, F32) for n in small],
            sds((8, EXPERTS), F32), sds((1, 8), F32), sds((1, 8), F32),
        ],
        in_specs=[
            pl.BlockSpec((DP, 1, 192, F), lambda j: (0, j, 0, 0)), rows, rows,
            *[whole(n) for n in small], whole((8, 128)),
        ],
        out_specs=[
            each(D, F), each(D, F), each(F, D), rows, rows, *[whole(n) for n in small],
            whole((8, EXPERTS)), whole((1, 8)), whole((1, 8)),
        ],
        compiler_params=params,
    )(dw_sum.reshape(DP, OWN, 192, F), output, grad_x, gq, gk, gv, go, gs)
    return (
        output.reshape(tokens.shape),
        grad_x.reshape(tokens.shape),
        gq,
        gk,
        gv,
        go,
        gr,
        g_attn.reshape(8),
        g_moe.reshape(8),
        g_gate,
        g_up,
        g_down,
    )


def solution(mesh):
    rows, own, both_axes = P("dp", "ep", None), P("ep", None, None), P(("dp", "ep"), None)
    line = P(("dp", "ep"))
    return jax.shard_map(
        per_device,
        mesh=mesh,
        in_specs=(
            rows, rows, P("dp", None), rows, both_axes, both_axes, both_axes, both_axes, both_axes,
            line, line, own, own, own,
        ),
        out_specs=(
            rows, rows, both_axes, both_axes, both_axes, both_axes, both_axes, line, line, own,
            own, own,
        ),
        check_vma=False,
    )
```

```python
import math

import jax
import jax.numpy as jnp
import numpy as np
from jax import lax
from jax.experimental import pallas as pl
from jax.experimental.pallas import tpu as pltpu
from jax.sharding import PartitionSpec as P

MESH = pl.DeviceIdType.MESH
BF = jnp.bfloat16
F32 = jnp.float32
ANY = pl.BlockSpec(memory_space=pl.ANY)
VM = pl.BlockSpec(memory_space=pltpu.VMEM)

DP, EP, CHIPS = 16, 8, 4
D, HD, F = 1024, 64, 512
ROWS, HALF, LEN, SEQS = 256, 128, 1024, 2
EXPERTS, OWN, CAP = 32, 4, 80
SLOTS = EP * CAP
EPS = 1e-6
RES = 0.22
SCORE = 0.015625
LOG2E = 1.4426950408889634
MASKED = -1e30
MIB = 2**20


def nt(a, b):
    return lax.dot_general(a, b, (((1,), (1,)), ((), ())), preferred_element_type=F32)


def nn(a, b):
    return jnp.dot(a, b, preferred_element_type=F32)


def tn(a, b):
    return lax.dot_general(a, b, (((0,), (0,)), ((), ())), preferred_element_type=F32)


def place():
    e = lax.axis_index("ep")
    return lax.axis_index("dp"), e, e // 2, lax.rem(e, 2)


def near(k, n):
    return lax.rem(k + n, 4)


def plane(d, e):
    u, v = d // 4, lax.rem(d, 4)
    up, down = (near(u, 1) * 4 + v, e), (near(u, 3) * 4 + v, e)
    return u, v, up, down, (u * 4 + near(v, 1), e), (u * 4 + near(v, 3), e)


def pair(h):
    return pl.ds(2 * h, 2)


def greet(peers):
    b = pltpu.get_barrier_semaphore()
    for p in peers:
        pl.semaphore_signal(b, inc=1, device_id=p, device_id_type=MESH)
    return lambda: pl.semaphore_wait(b, len(peers))


def ep_peers(d, e):
    return [(d, lax.rem(e + k, EP)) for k in range(1, EP)]


def dp_peers(d, e):
    return [(lax.rem(d + k, DP), e) for k in range(1, DP)]


class Sender:
    def __init__(self, ss, rs):
        self.ss, self.rs, self.n = ss, rs, 0

    def __call__(self, src, dst, dev):
        i = self.n
        self.n += 1
        return pltpu.make_async_remote_copy(
            src, dst, self.ss.at[i], self.rs.at[i], device_id=dev, device_id_type=MESH
        )

    def now(self, src, dst, dev):
        cp = self(src, dst, dev)
        cp.start()
        return cp


class Ring:
    def __init__(self, out, src, d, e, z, c, make):
        right, left = (d, lax.rem(z + 1, CHIPS) * 2 + c), (d, lax.rem(z + 3, CHIPS) * 2 + c)
        part = (d, z * 2 + 1 - c)
        er, el, eo = right[1], left[1], lax.rem(z + 2, CHIPS) * 2 + c
        self.near = [
            [make(src(0), out(e, 0), right), make(src(0), out(e, 0), left)],
            [make(src(1), out(e, 1), left), make(src(1), out(e, 1), right)],
        ]
        self.mate = [make(src(0), out(e, 0), part), make(src(1), out(e, 1), part)]
        self.far = [make(out(el, 0), out(el, 0), right), make(out(er, 1), out(er, 1), left)]
        self.share = [
            make(out(s, h), out(s, h), part)
            for s, h in ((el, 0), (er, 1), (el, 1), (er, 0), (eo, 0), (eo, 1))
        ]

    def start(self, h):
        for cp in self.near[h]:
            cp.start()
        self.mate[h].start()

    def forward(self):
        for h in range(2):
            self.near[h][0].wait_recv()
            self.far[h].start()
            self.share[h].start()
        for h in range(2):
            self.near[1 - h][1].wait_recv()
            self.share[2 + h].start()

    def finish(self):
        for h in range(2):
            self.far[h].wait_recv()
            self.share[4 + h].start()
        for cp in self.near[0] + self.near[1] + self.far:
            cp.wait_send()
        for cp in self.mate + self.share:
            cp.wait()


class Quad:
    def __init__(self, out, me, ahead, behind, make, src=None):
        after, before = lax.rem(me + 1, 4), lax.rem(me + 3, 4)
        mine = lambda h, dev: make(src(h) if src else out(me, h), out(me, h), dev)
        self.near = [
            [mine(0, ahead), mine(0, behind)],
            [mine(1, behind), mine(1, ahead)],
        ]
        self.far = [
            make(out(before, 0), out(before, 0), ahead),
            make(out(after, 1), out(after, 1), behind),
        ]

    def start(self):
        for h in range(2):
            for cp in self.near[h]:
                cp.start()

    def forward(self):
        for h in range(2):
            self.near[h][0].wait_recv()
            self.far[h].start()

    def near_arrived(self):
        for h in range(2):
            self.near[h][1].wait_recv()

    def far_arrived(self):
        for h in range(2):
            self.far[h].wait_recv()

    def arrived(self):
        self.near_arrived()
        self.far_arrived()

    def sent(self):
        for cp in self.near[0] + self.near[1] + self.far:
            cp.wait_send()


def remote_call(body, cid, outs, ins, specs, scratch, sems, out_specs=None, vmem=48, flops=0):
    return pl.pallas_call(
        body,
        name=body.__name__,
        out_shape=outs,
        in_specs=specs,
        out_specs=out_specs if out_specs is not None else [ANY] * len(outs),
        scratch_shapes=[
            *scratch,
            pltpu.SemaphoreType.DMA((24,)),
            pltpu.SemaphoreType.DMA((sems,)),
            pltpu.SemaphoreType.DMA((sems,)),
        ],
        compiler_params=pltpu.CompilerParams(
            collective_id=cid, has_side_effects=True, vmem_limit_bytes=vmem * MIB
        ),
        cost_estimate=pl.CostEstimate(flops=flops, bytes_accessed=20 * MIB, transcendentals=0),
    )(*ins)


def sds(shape, dtype):
    return jax.ShapeDtypeStruct(shape, dtype)


def lanes(shape):
    return lax.broadcasted_iota(jnp.int32, shape, 1)


def turn(v):
    first = lax.rem(lanes(v.shape), HD) < HD // 2
    return jnp.where(first, -pltpu.roll(v, 128 - HD // 2, 1), pltpu.roll(v, HD // 2, 1))


def both(kv):
    low = lanes(kv.shape) < HD
    other = pltpu.roll(kv, HD, 1)
    return jnp.where(low, kv, other).astype(BF), jnp.where(low, other, kv).astype(BF)


def two_heads(v):
    low = lanes(v.shape) < HD
    zero = jnp.zeros_like(v)
    return jnp.concatenate([jnp.where(low, v, zero), jnp.where(low, zero, v)], axis=0)


def spans(i):
    return i * ROWS, min(LEN, i * ROWS + 2 * ROWS)


def before_experts(
    x, rt, w_q, w_k, w_v, wo, wr, ga, gm, cs, sn, ids, cot,
    rall, moe, cot_o, q_h, kv_h, nrm_h, att_h, lse_h, gt_h, wo_h, mid_h, own_h, at_h, ws_h,
    q_o, kv_o, nrm_o, att_o, lse_o, gt_o, wo_o, mid_o, own_o, at_o, w_s,
    xall, wsl, wof, wp, wop, gp, gb, gs, sm_s, kk_s, vv_s, arr, mo, ls, ss, rs,
):
    d, e, z, c = place()
    u, v, up, down, ahead, behind = plane(d, e)
    pairs = [
        (q_o, q_h), (kv_o, kv_h), (nrm_o, nrm_h), (att_o, att_h), (lse_o, lse_h), (gt_o, gt_h),
        (wo_o, wo_h), (mid_o, mid_h), (own_o, own_h), (at_o, at_h), (w_s, ws_h),
    ]
    results = [pltpu.make_async_copy(a, b, ls.at[10 + i]) for i, (a, b) in enumerate(pairs)]
    across = [up, down, (near(u, 2) * 4 + v, e)]
    along = [ahead, behind, (u * 4 + near(v, 2), e)]
    wait = greet(ep_peers(d, e) + across + along)
    q, k, w = w_q[...].astype(F32), w_k[...].astype(F32), w_v[...].astype(F32)
    diagonal = lax.broadcasted_iota(jnp.int32, (8, 8), 0) == lanes((8, 8))
    column = lambda g: jnp.sum(jnp.where(diagonal, g[...].astype(F32), 0.0), axis=1, keepdims=True)
    for t in range(EP):
        kv = [k[:, 64 * t : 64 * t + 64], w[:, 64 * t : 64 * t + 64]]
        row = [q[:, 128 * t : 128 * t + 128], jnp.concatenate(kv, axis=1)]
        wp[t] = jnp.concatenate(row, axis=0).astype(BF)
    w, r = wo[...].astype(F32), wr[...].astype(F32)
    left = jnp.concatenate([w[:, :512], r, jnp.zeros((8, 96), F32)], axis=1)
    right = jnp.concatenate([w[:, 512:], column(ga), column(gm), jnp.zeros((8, 126), F32)], axis=1)
    wop[...] = jnp.concatenate([left, right], axis=0).astype(BF)
    spread = lax.broadcasted_iota(jnp.int32, (8, 128), 1) - 8 * e
    spread = spread == lax.broadcasted_iota(jnp.int32, (8, 128), 0)
    line = jnp.sum(jnp.where(spread, column(ga), 0.0), axis=0, keepdims=True)
    gp[...] = jnp.broadcast_to(line, (8, 128))
    wait()
    make = Sender(ss, rs)
    send = make.now
    own = [
        pltpu.make_async_copy(x, xall.at[e], ls.at[0]),
        pltpu.make_async_copy(wp.at[e], wsl.at[v, u, e], ls.at[1]),
        pltpu.make_async_copy(wop, wof.at[u, v, e], ls.at[2]),
        pltpu.make_async_copy(rt, rall.at[e], ls.at[3]),
        pltpu.make_async_copy(gp, gb.at[e], ls.at[8]),
        pltpu.make_async_copy(cot.at[0], cot_o.at[e], ls.at[9]),
    ]
    for cp in own:
        cp.start()
    tokens = [
        Ring(lambda s, k: xall.at[s, h, k], lambda k: x.at[h, k], d, e, z, c, make) for h in range(2)
    ]
    moes = [
        Ring(lambda s, k: moe.at[s, h, k], lambda k: mo.at[h, k], d, e, z, c, make) for h in range(2)
    ]
    gains = [send(gp, gb.at[e], p) for p in ep_peers(d, e)]
    first = [send(wp.at[p[1]], wsl.at[v, u, e], p) for p in ep_peers(d, e)]
    first += [send(wop, wof.at[u, v, e], p) for p in ep_peers(d, e)]
    tokens[0].start(0)
    tokens[0].start(1)
    own[1].wait()
    for cp in first[: EP - 1]:
        cp.wait_recv()
    w1 = [send(wsl.at[v, u], wsl.at[v, u], p) for p in across]
    own[4].wait()
    for cp in gains:
        cp.wait_recv()
    line = gb[0]
    for s in range(1, EP):
        line = line + gb[s]
    gs[v, u] = line
    g1 = [send(gs.at[v, u], gs.at[v, u], p) for p in across]
    own[2].wait()
    for cp in first[EP - 1 :]:
        cp.wait_recv()
    mine = pl.ds(c * 4, 4)
    part = (d, z * 2 + 1 - c)
    o1 = [send(wof.at[u, v, mine], wof.at[u, v, mine], p) for p in along]
    tokens[0].forward()
    for cp in w1:
        cp.wait_recv()
    w2 = Quad(lambda i, h: wsl.at[i, pair(h)], v, ahead, behind, make)
    w2.start()
    for cp in g1:
        cp.wait_recv()
    g2 = [send(gs.at[v], gs.at[v], p) for p in along]
    last = []
    for k, cp in zip((1, 3, 2), o1):
        cp.wait_recv()
        t = lax.rem(v + 4 - k, 4)
        last.append(send(wof.at[u, t, mine], wof.at[u, t, mine], part))
    o2 = Quad(lambda i, h: wof.at[i, :, pl.ds(c * 4 + 2 * h, 2)], u, up, down, make)
    o2.start()
    tokens[1].start(0)
    tokens[1].start(1)
    w2.forward()
    tokens[0].finish()
    own[0].wait()
    w2.arrived()
    for cp in g2:
        cp.wait_recv()
    for i in range(DP):
        w = wsl[i % 4, i // 4].astype(F32)
        w = jnp.concatenate([w[:, :8].reshape(64, 128), w[:, 8:].reshape(64, 128)], axis=1)
        w_s[64 * i : 64 * i + 64] = w.astype(BF)
    results[10].start()
    gain_a = jnp.concatenate([gs[i % 4, i // 4][:1, :64] for i in range(DP)], axis=1)

    def project(h):
        for r in range(4):
            rows = slice(256 * r, 256 * r + 256)
            t = xall[2 * r : 2 * r + 2, h].astype(F32).reshape(256, D)
            factor = lax.rsqrt(jnp.mean(t * t, axis=1, keepdims=True) + EPS)
            n = (t * factor * gain_a).astype(BF)
            nrm_o[h, rows] = n
            pre = nn(n, w_s[...])
            co, si = cs[rows], sn[rows]
            q, kv = pre[:, :128], pre[:, 128:]
            q_o[h, rows] = (q * co + turn(q) * si).astype(BF)
            kv = jnp.where(lanes(kv.shape) < HD, kv * co + turn(kv) * si, kv).astype(BF)
            kv_o[h, rows] = kv
            kk_s[rows], vv_s[rows] = both(kv.astype(F32))

    def attend(h, i):
        ids_k = ids[h : h + 1]
        ids_q = jnp.broadcast_to(ids_k[:, ROWS * i : ROWS * i + ROWS], (128, ROWS)).T[:, :1]
        q2 = two_heads(q_o[h, ROWS * i : ROWS * i + ROWS].astype(F32)).astype(BF)
        own_ids = jnp.concatenate([ids_q, ids_q], axis=0)
        at, end = spans(i)
        parts = []
        if at:
            parts.append((nt(q2, kk_s[:at]) * (SCORE * LOG2E), slice(0, at)))
        t = nt(q2, kk_s[at:end]) * (SCORE * LOG2E)
        parts.append((jnp.where(ids_k[:, at:end] <= own_ids, t, MASKED), slice(at, end)))
        peak = parts[0][0].max(axis=1, keepdims=True)
        for t, _ in parts[1:]:
            peak = jnp.maximum(peak, t.max(axis=1, keepdims=True))
        total, out = 0.0, 0.0
        for t, span in parts:
            p = jnp.exp2(t - peak)
            total = total + p.sum(axis=1, keepdims=True)
            out = out + nn(p.astype(BF), vv_s[span])
        out = out * (1.0 / total)
        lse = jnp.broadcast_to(peak + jnp.log2(total), (2 * ROWS, 128))
        low = lanes((ROWS, 128)) < HD
        att = jnp.where(low, out[:ROWS], out[ROWS:]).astype(BF)
        att_o[2 * i : 2 * i + 2, h] = att.reshape(2, HALF, 128)
        lse_o[h, ROWS * i : ROWS * i + ROWS] = jnp.where(low, lse[:ROWS], lse[ROWS:])

    att_own = [pltpu.make_async_copy(att_o.at[e, h], arr.at[e, h], ls.at[4 + h]) for h in range(2)]
    moe_own = [pltpu.make_async_copy(mo.at[h], moe.at[e, h], ls.at[6 + h]) for h in range(2)]

    def exchange(h):
        att_own[h].start()
        cps = []
        for k in (4, 3, 5, 2, 6, 1, 7):
            t = lax.rem(e + k, EP)
            cps.append(send(att_o.at[t, h], arr.at[e, h], (d, t)))
        return cps

    def branch(h, cps):
        att_own[h].wait()
        for cp in cps:
            cp.wait_recv()
        a = jnp.concatenate([arr[s, h] for s in range(EP)], axis=1)
        at_o[h] = a
        m = xall[e, h].astype(F32).reshape(HALF, D) + RES * nn(a, wo_o[...])
        mid_o[h] = m
        factor = lax.rsqrt(jnp.mean(m * m, axis=1, keepdims=True) + EPS)
        n = (m * factor * gt_o[33:34, :]).astype(BF)
        own_o[h] = n
        mo[h] = n.reshape(2, HALF // 2, D)
        moe_own[h].start()
        moes[h].start(0)
        moes[h].start(1)

    project(0)
    tokens[1].forward()
    attend(0, 0)
    attend(0, 1)
    o2.forward()
    attend(0, 2)
    attend(0, 3)
    x0 = exchange(0)
    up_z, down_z = near(z, 1) * 2 + c, near(z, 3) * 2 + c
    cots = [send(cot.at[0], cot_o.at[e], (d, t)) for t in (up_z, down_z, z * 2 + 1 - c)]
    tokens[1].finish()
    project(1)
    attend(1, 0)
    attend(1, 1)
    attend(1, 2)
    attend(1, 3)
    x1 = exchange(1)
    for cp in results[:5]:
        cp.start()
    o2.arrived()
    for k in (1, 3, 2):
        t = near(u, k)
        last.append(send(wof.at[t, :, mine], wof.at[t, :, mine], part))
    routes = [send(rt, rall.at[e], p) for p in ep_peers(d, e)]
    for cp in last:
        cp.wait_recv()
    for i in range(4):
        rows = slice(256 * i, 256 * i + 256)
        o = wof[i].astype(F32).reshape(32, 16, 640)
        left, right = o[:, :8].reshape(256, 640), o[:, 8:].reshape(256, 640)
        wo_o[rows, :512] = left[:, :512].astype(BF)
        wo_o[rows, 512:] = right[:, :512].astype(BF)
        sm_s[rows] = jnp.where(lanes((256, 128)) < 32, left[:, 512:], pltpu.roll(right[:, 512:], 32, 1))
    gt_o[...] = sm_s[...].T
    for cp in results[5:7]:
        cp.start()
    branch(0, x0)
    branch(1, x1)
    for cp in results[7:10]:
        cp.start()
    moes[0].forward()
    moes[1].forward()
    for cp, t in zip(cots[:2], (down_z, up_z)):
        cp.wait_recv()
        cots.append(send(cot_o.at[t], cot_o.at[t], part))
    moes[0].finish()
    moes[1].finish()
    w2.sent()
    o2.sent()
    for cp in gains + first + w1 + g1 + g2 + o1 + last + x0 + x1:
        cp.wait_send()
    for cp in routes:
        cp.wait()
    own[3].wait()
    own[5].wait()
    for cp in cots[:2]:
        cp.wait_send()
    for cp in cots[2:] + moe_own + results:
        cp.wait()


def routing(rt, logits_t):
    ids = lax.broadcasted_iota(jnp.int32, (EXPERTS, ROWS), 0)
    hit = rt[0:1] == ids
    for k in range(1, 8):
        hit = hit | (rt[k : k + 1] == ids)
    w = jnp.where(hit, logits_t, MASKED)
    w = jnp.where(hit, jnp.exp(w - w.max(axis=0, keepdims=True)), 0.0)
    gates = w / w.sum(axis=0, keepdims=True)
    earlier = lax.broadcasted_iota(jnp.int32, (ROWS, ROWS), 0) < lax.broadcasted_iota(
        jnp.int32, (ROWS, ROWS), 1
    )
    slot = nn(jnp.where(hit, 1.0, 0.0).astype(BF), jnp.where(earlier, 1.0, 0.0).astype(BF))
    return gates, jnp.where(hit, slot, -1.0)


class Reduce:
    def __init__(self, chunk, me, ahead, behind, one, two, three, make):
        at = lambda k: lax.rem(me + k, 4)
        self.one, self.two, self.three = one, two, three
        self.first = [
            make(chunk(at(2), 0), one.at[0], ahead),
            make(chunk(at(2), 1), one.at[1], behind),
        ]
        self.second = [
            make(chunk(at(1), 1), two.at[0], ahead),
            make(chunk(at(3), 0), two.at[1], behind),
        ]
        self.third = [make(one.at[0], three.at[0], ahead), make(one.at[1], three.at[1], behind)]

    def start(self):
        for cp in self.first + self.second:
            cp.start()

    def go_on(self, k, mine, pieces):
        self.first[k].wait_recv()

        def add(i, carry):
            self.one[k, i] = self.one[k, i] + (mine[i] if pieces > 1 else mine[...])
            return carry

        lax.fori_loop(0, pieces, add, 0)
        self.third[k].start()

    def arrived(self, k):
        self.second[1 - k].wait_recv()
        self.third[k].wait_recv()

    def sent(self):
        for cp in self.first + self.second + self.third:
            cp.wait_send()


def close(r, chunk, pieces):
    for k in range(2):
        r.arrived(k)

        def body(i, carry):
            for q in range(2):
                piece = r.two[1 - k, i, q].astype(F32) + r.three[k, i, q].astype(F32)
                chunk[i, 2 * k + q] = (chunk[i, 2 * k + q].astype(F32) + piece).astype(BF)
            return carry

        lax.fori_loop(0, pieces, body, 0)


def experts_weights(
    moe, cot, cot_h, w_own, rall, gt, wg, wu, wd, dw_o, eo_h, dg_o, du_o, gg_o, p_h, ca_o, cb_o, w_o,
    eo_o, p_o, cot_s, x_s, y_s, gate_s, a_s, b_s, h_s, dw_s, a1, a2, a3, b1, b2, b3, ls, ss, rs,
):
    step = pl.program_id(0)
    d, e, z, c = place()
    u, v, up, down, ahead, behind = plane(d, e)
    first = e * OWN
    make = Sender(ss, rs)
    right, left, other = near(z, 1) * 2 + c, near(z, 3) * 2 + c, z * 2 + 1 - c
    far = near(z, 2) * 2 + c
    near_c = [make(cot.at[1], cot_s.at[e, 1], (d, t)) for t in (left, right, other)]
    far_c = [
        make(cot_h.at[left], cot_s.at[left, 0], (d, right)),
        make(cot_s.at[right, 1], cot_s.at[right, 1], (d, left)),
    ]
    share = [
        make(cot_s.at[t, k], cot_s.at[t, k], (d, other)) for t, k in ((right, 1), (left, 1), (far, 0), (far, 1))
    ]
    ra = Reduce(lambda i, h: dw_s.at[:, i, pair(h), 0], u, up, down, a1, a2, a3, make)
    rb = Reduce(lambda i, h: dw_s.at[:, pair(h), i, 1], v, ahead, behind, b1, b2, b3, make)
    slices = Ring(lambda s, k: w_o.at[s, k], lambda k: w_own.at[k], d, e, z, c, make)
    own_w = pltpu.make_async_copy(w_own, w_o.at[e], ls.at[2])
    two = lambda k: pl.ds(near(z, k) * 2, 2)
    own = [pltpu.make_async_copy(cot_h.at[two(k)], cot_s.at[two(k), 0], ls.at[7 + i]) for i, k in enumerate((0, 1, 3))]
    own.append(pltpu.make_async_copy(cot.at[1], cot_s.at[e, 1], ls.at[5]))
    results = [pltpu.make_async_copy(eo_o, eo_h, ls.at[3]), pltpu.make_async_copy(p_o, p_h, ls.at[4])]
    rows_of = lambda s: pl.ds(pl.multiple_of(s * CAP, 16), CAP)

    @pl.when(step == 0)
    def _():
        load = pltpu.make_async_copy(moe, y_s.at[pl.ds(0, EP * ROWS)], ls.at[6])
        load.start()
        greet(ep_peers(d, e) + [up, down, ahead, behind])()
        for cp in near_c + far_c[:1] + own:
            cp.start()
        load.wait()
        router_t = gt[:EXPERTS].astype(BF)
        row = lax.broadcasted_iota(jnp.int32, (EXPERTS, ROWS), 0)
        place_in = lax.broadcasted_iota(jnp.int32, (CAP, ROWS), 0).astype(F32)

        def source(s, carry):
            m = y_s[pl.ds(pl.multiple_of(s * ROWS, ROWS), ROWS)]
            gates, slot = routing(rall[s], nt(router_t, m))
            picks = []
            for i in range(OWN):
                sel = row == first + i
                pick = jnp.sum(jnp.where(sel, slot, 0.0), axis=0, keepdims=True) == place_in
                gate = jnp.sum(jnp.where(sel, gates, 0.0), axis=0, keepdims=True)
                g = jnp.sum(jnp.where(pick, gate, 0.0), axis=1, keepdims=True)
                gate_s[i, rows_of(s)] = jnp.broadcast_to(g, (CAP, 128))
                picks.append(jnp.where(pick, 1.0, 0.0).astype(BF))
            pick = jnp.concatenate(picks, axis=0)
            p_o[s] = pick
            xs = nn(pick, m).astype(BF)
            for i in range(OWN):
                x_s[i, rows_of(s)] = xs[CAP * i : CAP * i + CAP]
            return carry

        lax.fori_loop(0, EP, source, 0)

    @pl.when(step < OWN)
    def _():
        x = x_s[step]
        gate = gate_s[step][:, :1] * RES
        g = nn(x, wg[0])
        u = nn(x, wu[0])
        s = 1.0 / (1.0 + jnp.exp(-g))
        silu = g * s
        a_s[step] = (u * s * (1.0 + g * (1.0 - s))).astype(BF)
        b_s[step] = silu.astype(BF)
        h = silu * u
        h_s[step] = h.astype(BF)
        eo = nn((h * gate).astype(BF), wd[0]).astype(BF)
        for i in range(EP):
            eo_o[i, rows_of(step)] = eo[CAP * i : CAP * i + CAP]

    @pl.when(step == 2)
    def _():
        near_c[0].wait_recv()
        far_c[1].start()
        share[0].start()
        near_c[1].wait_recv()
        share[1].start()
        far_c[0].wait_recv()
        share[2].start()
        slices.start(0)
        slices.start(1)
        own_w.start()

    @pl.when(step == OWN)
    def _():
        for cp in results:
            cp.start()
        far_c[1].wait_recv()
        share[3].start()
        for cp in own + share + near_c[2:]:
            cp.wait()
        for cp in near_c[:2] + far_c:
            cp.wait_send()

        def source(s, carry):
            ys = nn(p_o[s], cot_s[s].reshape(ROWS, D)).astype(BF)
            for i in range(OWN):
                at = pl.ds(pl.multiple_of(i * SLOTS + s * CAP, 16), CAP)
                y_s[at] = ys[CAP * i : CAP * i + CAP]
            return carry

        lax.fori_loop(0, EP, source, 0)

    def back(j, store):
        x, y = x_s[j], y_s[pl.ds(pl.multiple_of(j * SLOTS, SLOTS), SLOTS)]
        gate = gate_s[j][:, :1] * RES
        dh = nt(y, wd[0])
        h = h_s[j].astype(F32)
        gg_o[0] = jnp.broadcast_to(RES * jnp.sum(h * dh, axis=1, keepdims=True), (SLOTS, 128))
        dh = dh * gate
        dg = (dh * a_s[j].astype(F32)).astype(BF)
        du = (dh * b_s[j].astype(F32)).astype(BF)
        dg_o[0], du_o[0] = dg, du
        w = tn(x, jnp.concatenate([dg, du], axis=1))
        store(0, w[:, :F].astype(BF))
        store(1, w[:, F:].astype(BF))
        w = tn((h * gate).astype(BF), y)
        store(2, jnp.concatenate([w[:, :F], w[:, F:]], axis=0).astype(BF))

    @pl.when(step == OWN)
    def _():
        whole_w = [None] * 3

        def store(i, w):
            whole_w[i] = w

        back(0, store)
        dw_s[0] = jnp.concatenate(whole_w, axis=0).reshape(4, 4, 2, 96, F)
        ra.start()
        rb.start()

    @pl.when(step > OWN)
    def _():
        def store(i, w):
            dw_o[0, D * i : D * i + D] = w

        back(step - OWN, store)

    @pl.when(step == OWN + 1)
    def _():
        slices.forward()
        for k in range(2):
            ra.go_on(k, dw_s.at[0, near(u, 1 + 2 * k), pair(k), 0], 1)
            rb.go_on(k, dw_s.at[0, pair(k), near(v, 1 + 2 * k), 1], 1)

    @pl.when(step == 2 * OWN - 1)
    def _():
        for cp in results:
            cp.wait()
        slices.finish()
        own_w.wait()
        ca_o[0] = dw_s[0, u, :, 0]
        cb_o[0] = dw_s[0, :, v, 1]
        close(ra, ca_o, 1)
        close(rb, cb_o, 1)
        ra.sent()
        rb.sent()


class Combine:
    def __init__(self, term, stage, buf, m1, m2, m3, d, z, c, make):
        right, left = (d, near(z, 1) * 2 + c), (d, near(z, 3) * 2 + c)
        self.term, self.stage, self.buf, self.m1, self.m2, self.m3, self.c = term, stage, buf, m1, m2, m3, c
        self.turns = [near(z, k) * 2 for k in (2, 1, 3, 0)]
        self.mates = [make(stage.at[i], buf.at[i], (d, z * 2 + 1 - c)) for i in range(4)]
        lo, hi = pl.ds(0, HALF), pl.ds(HALF, HALF)
        self.s1 = [make(buf.at[0, lo], m1.at[0], right), make(buf.at[0, hi], m1.at[1], left)]
        self.s2 = [make(buf.at[1, hi], m2.at[0], right), make(buf.at[2, lo], m2.at[1], left)]
        self.s3 = [make(m1.at[0], m3.at[0], right), make(m1.at[1], m3.at[1], left)]

    def begin(self):
        for i, t in enumerate(self.turns):
            self.stage[i] = self.term(t + 1 - self.c).astype(BF)
            self.mates[i].start()

    def add(self, i):
        own = self.term(self.turns[i] + self.c)
        self.mates[i].wait_recv()
        self.buf[i] = (self.buf[i].astype(F32) + own).astype(BF)

    def send(self):
        self.add(0)
        for cp in self.s1:
            cp.start()
        self.add(1)
        self.s2[0].start()
        self.add(2)
        self.s2[1].start()

    def go_on(self):
        for k, i in ((0, 1), (1, 2)):
            self.s1[k].wait_recv()
            self.m1[k] = self.m1[k] + self.buf[i, HALF * k : HALF * k + HALF]
            self.s3[k].start()

    def finish(self, out, columns):
        for k in range(2):
            rows = slice(HALF * k, HALF * k + HALF)
            self.s2[1 - k].wait_recv()
            self.s3[k].wait_recv()
            arrived = self.m2[1 - k].astype(F32) + self.m3[k].astype(F32)
            out[rows, columns] = self.buf[3, rows].astype(F32) + arrived

    def sent(self):
        for cp in self.mates + self.s1 + self.s2 + self.s3:
            cp.wait_send()


def experts_combine(
    eo_h, dg, du, gg_h, picks_h, wg, wu, dw, ca, cb, mg_o, gt_o, sh_o,
    eo, picks, gg, dx_s, gg_s, stage, buf, m1, m2, m3, stage_, buf_, m1_, m2_, m3_,
    a1, a2, a3, amine, ac, b1, b2, b3, bmine, bc, a4, a5, a6, b4, b5, b6, ls, ss, rs,
):
    j = pl.program_id(0)
    d, e, z, c = place()
    u, v, up, down, ahead, behind = plane(d, e)
    make = Sender(ss, rs)
    later = pl.ds(1, OWN - 1)
    deep = lambda h: pl.ds(48 * h, 48)
    ra = Reduce(lambda i, h: dw.at[:, i, pair(h), 0], u, up, down, a1, a2, a3, make)
    rb = Reduce(lambda i, h: dw.at[:, pair(h), i, 1], v, ahead, behind, b1, b2, b3, make)
    qa = Reduce(lambda i, h: ac.at[:, i, deep(h)], v, ahead, behind, a4, a5, a6, make)
    qb = Reduce(lambda i, h: bc.at[:, i, deep(h)], u, up, down, b4, b5, b6, make)
    mix = Combine(lambda s: tn(picks[s], eo[s]), stage, buf, m1, m2, m3, d, z, c, make)
    back = Combine(lambda s: tn(picks[s], dx_s[s]), stage_, buf_, m1_, m2_, m3_, d, z, c, make)
    load = pltpu.make_async_copy
    own = [
        load(dw.at[:, near(u, 1), pair(0), 0], amine.at[0], ls.at[0]),
        load(dw.at[:, near(u, 3), pair(1), 0], amine.at[1], ls.at[1]),
        load(dw.at[:, pair(0), near(v, 1), 1], bmine.at[0], ls.at[2]),
        load(dw.at[:, pair(1), near(v, 3), 1], bmine.at[1], ls.at[3]),
        load(dw.at[:, u, :, 0], ac.at[later], ls.at[4]),
        load(dw.at[:, :, v, 1], bc.at[later], ls.at[5]),
        load(ca, ac.at[pl.ds(0, 1)], ls.at[6]),
        load(cb, bc.at[pl.ds(0, 1)], ls.at[7]),
    ]
    gt_own = load(gg_s.at[e], gt_o.at[e], ls.at[8])
    rows = [make(gg_s.at[p[1]], gt_o.at[e], p) for p in ep_peers(d, e)]

    early = [load(eo_h, eo, ls.at[9]), load(picks_h, picks, ls.at[10]), load(gg_h, gg, ls.at[11])]

    @pl.when(j == 0)
    def _():
        for cp in early:
            cp.start()
        greet(ep_peers(d, e) + [up, down, ahead, behind])()
        ra.start()
        rb.start()
        for cp in own:
            cp.start()
        for cp in early:
            cp.wait()
        mix.begin()

    @pl.when(j == 1)
    def _():
        mix.send()

    dx = (nt(dg[0], wg[0]) + nt(du[0], wu[0])).astype(BF)
    for s in range(EP):
        dx_s[s, pl.ds(pl.multiple_of(j * CAP, 16), CAP)] = dx[CAP * s : CAP * s + CAP]

    @pl.when(j == OWN - 1)
    def _():
        back.begin()
        mix.go_on()
        back.send()
        for cp in own:
            cp.wait()
        for k in range(2):
            ra.go_on(k, amine.at[k], OWN - 1)
            rb.go_on(k, bmine.at[k], OWN - 1)
        mix.add(3)
        for s in range(EP):
            p = picks[s]
            at = pl.ds(pl.multiple_of(s * CAP, 16), CAP)
            lines = [
                jnp.sum(
                    p[CAP * i : CAP * i + CAP].astype(F32) * gg[i, at][:, :1], axis=0, keepdims=True
                )
                for i in range(OWN)
            ]
            gg_s[s] = jnp.concatenate(lines + [jnp.zeros((8 - OWN, ROWS), F32)], axis=0)
        for cp in rows:
            cp.start()
        gt_own.start()
        back.add(3)
        back.go_on()
        mix.finish(mg_o, slice(0, D))
        close(ra, ac.at[later], OWN - 1)
        qa.start()
        close(rb, bc.at[later], OWN - 1)
        qb.start()
        back.finish(mg_o, slice(D, 2 * D))
        for q, chunk, me in ((qa, ac, v), (qb, bc, u)):
            for k in range(2):
                t = near(me, 1 + 2 * k)
                q.first[k].wait_recv()
                q.one[k] = q.one[k] + chunk[:, t, 48 * k : 48 * k + 48]
                q.third[k].start()
        for h, q, chunk, me in ((0, qa, ac, v), (1, qb, bc, u)):
            for k in range(2):
                q.arrived(k)
                mine = chunk[:, me, 48 * k : 48 * k + 48].astype(F32)
                total = mine + q.two[1 - k].astype(F32) + q.three[k].astype(F32)
                sh_o[:, h, 48 * k : 48 * k + 48] = total.astype(BF)
        for r in (ra, rb, qa, qb, mix, back):
            r.sent()
        for cp in rows:
            cp.wait()
        gt_own.wait()


def norm_back(grad, values, factor, gain):
    scaled = grad * gain
    grad_gain = jnp.sum(grad * values * factor, axis=0, keepdims=True)
    mean = jnp.mean(scaled * values, axis=1, keepdims=True)
    return factor * (scaled - values * (factor * factor * mean)), grad_gain


def tail(
    mg_h, mid_h, wo_h, wf_h, q_h, kv_h, nrm_h, att_h, lse_h, at_h, sh, gg, rt, moe, cot, gt, x, cs, sn, ids,
    ag, out_o, gx_o, wq_o, wk_o, wv_o, wo_o, sm_o,
    mg, mid, wo, wf, q_s, kv_s, nrm, att, lse, at, da, gb, da_s, gb_s, dq, dq_s, kk_s, vv_s, dk_s, dv_s,
    gm, dw, pa, pb, ra, rb, ta, tb, qa, qb, s1, r2, ls, ss, rs,
):
    d, e, z, c = place()
    u, v, up, down, ahead, behind = plane(d, e)
    across = [up, down, (near(u, 2) * 4 + v, e)]
    along = [ahead, behind, (u * 4 + near(v, 2), e)]
    wait = greet(ep_peers(d, e) + across + along)
    pairs = [
        (mg_h, mg), (mid_h, mid), (wo_h, wo), (q_h, q_s), (kv_h, kv_s), (att_h, att), (lse_h, lse),
        (nrm_h, nrm), (at_h, at.at[e]), (wf_h, wf), (sh, ag.at[u, v]),
    ]
    loads = [pltpu.make_async_copy(a, b, ls.at[i]) for i, (a, b) in enumerate(pairs)]
    for cp in loads:
        cp.start()
    wait()
    make = Sender(ss, rs)
    low_half = lambda k: pl.ds(48 * k, 48)
    own_a, own_b = (lambda k: sh.at[:, 0, low_half(k)]), (lambda k: sh.at[:, 1, low_half(k)])

    def piece(fixed, along_u, half, src=None):
        if along_u:
            out = lambda i, k: ag.at[i, fixed, :, half, low_half(k)]
            return Quad(out, u, up, down, make, src)
        out = lambda i, k: ag.at[fixed, i, :, half, low_half(k)]
        return Quad(out, v, ahead, behind, make, src)

    one = [piece(u, False, 0, own_a), piece(v, True, 1, own_b)]
    two = [
        [piece(near(v, k), True, 0, None if k else own_a), piece(near(u, k), False, 1, None if k else own_b)]
        for k in range(4)
    ]
    for r in one + two[0]:
        r.start()
    router_t = gt[:EXPERTS].astype(BF)
    gates, _ = routing(rt, nt(router_t, moe[...]))
    back = gg[...][:, :OWN].reshape(EXPERTS, ROWS)
    both_ = gates * back
    gl = (both_ - gates * jnp.sum(both_, axis=0, keepdims=True)).astype(BF)
    loads[0].wait()
    loads[1].wait()
    loads[2].wait()
    m = mid[...]
    grad = mg[:, D:] + tn(gl, router_t)
    factor = lax.rsqrt(jnp.mean(m * m, axis=1, keepdims=True) + EPS)
    t, gain_m = norm_back(grad, m, factor, gt[33:34])
    t = cot[...].astype(F32) + t
    gm[...] = t
    gradient = (RES * t).astype(BF)
    ga = nt(gradient, wo[...]).astype(BF)
    for i in range(EP):
        da[i] = ga[:, 128 * i : 128 * i + 128].reshape(2, HALF, 128)
        gb[i] = gradient[:, 128 * i : 128 * i + 128].reshape(2, HALF, 128)
    own = [
        pltpu.make_async_copy(da.at[e], da_s.at[e], ls.at[11]),
        pltpu.make_async_copy(gb.at[e], gb_s.at[e], ls.at[12]),
    ]
    for cp in own:
        cp.start()
    da_c = [make.now(da.at[p[1]], da_s.at[e], p) for p in ep_peers(d, e)]
    gb_c = [make.now(gb.at[p[1]], gb_s.at[e], p) for p in ep_peers(d, e)]
    ats = Ring(lambda s, k: at.at[s, k], lambda k: at_h.at[k], d, e, z, c, make)
    ats.start(0)
    ats.start(1)
    router = nn(gl, moe[...])
    out_o[...] = (m + mg[:, :D]).astype(BF)
    for r in one:
        r.forward()
    for r in one:
        r.near_arrived()
    for r in two[1] + two[3]:
        r.start()
    for cp in loads[3:9]:
        cp.wait()
    for cp in own:
        cp.wait()
    for cp in da_c + gb_c:
        cp.wait_recv()
    low = lanes((ROWS, 128)) < HD

    def unturn(w, rows):
        return w * cs[rows] - turn(w) * sn[rows]

    def attend_back(s):
        kk_s[...], vv_s[...] = both(kv_s[s].astype(F32))
        dk_s[...] = jnp.zeros_like(dk_s)
        dv_s[...] = jnp.zeros_like(dv_s)
        ids_k = ids[s : s + 1]
        dqs = []
        for i in range(4):
            rows = slice(ROWS * i, ROWS * i + ROWS)
            q2 = two_heads(q_s[s, rows].astype(F32)).astype(BF)
            o2f = two_heads(da_s[2 * i : 2 * i + 2, s].reshape(ROWS, 128).astype(F32))
            o2 = o2f.astype(BF)
            a = att[2 * i : 2 * i + 2, s].reshape(ROWS, 128).astype(F32)
            delta = jnp.sum(o2f * jnp.concatenate([a, a], axis=0), axis=1, keepdims=True)
            l2 = jnp.concatenate([lse[s, rows][:, :1], lse[s, rows][:, HD : HD + 1]], axis=0)
            ids_q = jnp.broadcast_to(ids_k[:, rows], (128, ROWS)).T[:, :1]
            ids_q = jnp.concatenate([ids_q, ids_q], axis=0)
            start, end = spans(i)
            grad_q = 0.0
            for span in ([slice(0, start)] if start else []) + [slice(start, end)]:
                w = nt(q2, kk_s[span]) * (SCORE * LOG2E) - l2
                if span.start == start:
                    w = jnp.where(ids_k[:, span] <= ids_q, w, MASKED)
                p = jnp.exp2(w)
                gp = nt(o2, vv_s[span])
                ds = (p * (gp - delta)).astype(BF)
                grad_q = grad_q + nn(ds, kk_s[span])
                dk_s[span] += tn(ds, q2)
                dv_s[span] += tn(p.astype(BF), o2)
            grad_q = SCORE * jnp.where(low, grad_q[:ROWS], grad_q[ROWS:])
            dqs.append(unturn(grad_q, rows).astype(BF))
        grads = []
        for i in range(4):
            rows = slice(ROWS * i, ROWS * i + ROWS)
            dk, dv = dk_s[rows], dv_s[rows]
            dk = unturn(SCORE * (dk + pltpu.roll(dk, HD, 1)), rows)
            dv = dv + pltpu.roll(dv, HD, 1)
            dqkv = jnp.concatenate([dqs[i], jnp.where(low, dk, dv).astype(BF)], axis=1)
            dq[2 * i : 2 * i + 2, s] = dqkv.reshape(2, HALF, 256)
            grads.append(dqkv)
        dq_own[s].start()
        cps = [make.now(dq.at[p[1], s], dq_s.at[e, s], p) for p in ep_peers(d, e)]
        wqkv = tn(nrm[s], jnp.concatenate(grads, axis=0))
        if s == 0:
            dw[:, :256] = wqkv
        else:
            dw[:, :256] += wqkv
        return cps

    dq_own = [pltpu.make_async_copy(dq.at[e, s], dq_s.at[e, s], ls.at[13 + s]) for s in range(2)]
    dq_c = [attend_back(0)]
    ats.forward()
    for r in two[0]:
        r.forward()
    dq_c.append(attend_back(1))
    pa[...] = dw[:, :256].astype(BF).reshape(4, 4, 64, 256)
    a_first = [make.now(pa.at[p[0] // 4], ra.at[i], p) for i, p in enumerate(across)]
    for r in one:
        r.far_arrived()
    for r in two[2]:
        r.start()
    loads[9].wait()
    gain_a = 0.0
    for s in range(2):
        rows = slice(HALF * s, HALF * s + HALF)
        dq_own[s].wait()
        for cp in dq_c[s]:
            cp.wait_recv()
        grad = 0.0
        for i in range(EP):
            grad = grad + nt(dq_s[i, s], wf[i].reshape(D, 256))
        t = x[rows].astype(F32)
        factor = lax.rsqrt(jnp.mean(t * t, axis=1, keepdims=True) + EPS)
        g, gain = norm_back(grad, t, factor, gt[32:33])
        gx_o[rows] = (gm[rows] + g).astype(BF)
        gain_a = gain_a + gain
    ats.finish()
    wout = 0.0
    for s in range(2):
        wout = wout + tn(at[:, s].reshape(LEN, D), gb_s[:, s].reshape(LEN, 128))
    dw[:, 256:] = wout
    lines = [router, gain_a, gain_m, jnp.zeros((128 - EXPERTS - 2, D), F32)]
    small = jnp.concatenate(lines, axis=0).T
    pb[...] = jnp.concatenate([dw[:, 256:], small], axis=1).astype(BF).reshape(4, 4, 64, 256)
    b_first = [make.now(pb.at[:, lax.rem(p[0], 4)], rb.at[i], p) for i, p in enumerate(along)]
    for r in two[1] + two[3]:
        r.forward()

    def total(mine, arrived, cps):
        for cp in cps:
            cp.wait_recv()
        return mine.astype(F32) + arrived[0].astype(F32) + arrived[1].astype(F32) + arrived[2].astype(F32)

    ta[...] = total(pa[u], ra, a_first).astype(BF)
    a_second = [make.now(ta.at[lax.rem(p[0], 4)], qa.at[i], p) for i, p in enumerate(along)]
    tb[...] = total(pb[:, v], rb, b_first).astype(BF)
    b_second = [make.now(tb.at[p[0] // 4], qb.at[i], p) for i, p in enumerate(across)]
    for r in two[2]:
        r.forward()
    s1[:, :, :256] = total(ta[v], qa, a_second).reshape(EP, 8, 256)
    s1[:, :, 256:] = total(tb[u], qb, b_second).reshape(EP, 8, 256)
    r2[e] = s1[e]
    more = [make.now(s1.at[p[1]], r2.at[e], p) for p in ep_peers(d, e)]
    for cp in more:
        cp.wait_recv()
    small = r2[0, :, 384:]
    for s in range(1, EP):
        small = small + r2[s, :, 384:]
    sm_o[...] = small
    wq_o[...] = jnp.concatenate([r2[s, :, :128] for s in range(EP)], axis=1)
    wk_o[...] = jnp.concatenate([r2[s, :, 128:192] for s in range(EP)], axis=1)
    wv_o[...] = jnp.concatenate([r2[s, :, 192:256] for s in range(EP)], axis=1)
    wo_o[...] = jnp.concatenate([r2[s, :, 256:384] for s in range(EP)], axis=1)
    for group in two:
        for r in group:
            r.arrived()
    for r in one + two[0] + two[1] + two[2] + two[3]:
        r.sent()
    for cp in da_c + gb_c + dq_c[0] + dq_c[1] + a_first + b_first + a_second + b_second + more:
        cp.wait_send()
    loads[10].wait()


def widen(dw, out, gx, q, k, v, o, sm, g_o, u_o, d_o, out_o, gx_o, q_o, k_o, v_o, o_o, r_o, ga_o, gm_o):
    w = dw[...].reshape(3 * D, F).astype(F32)
    g_o[0] = w[:D]
    u_o[0] = w[D : 2 * D]
    d_o[0, :, :F] = w[2 * D : 2 * D + F]
    d_o[0, :, F:] = w[2 * D + F :]
    out_o[...], gx_o[...] = out[...], gx[...]

    @pl.when(pl.program_id(0) == 0)
    def _():
        q_o[...], k_o[...], v_o[...], o_o[...] = q[...], k[...], v[...], o[...]
        r_o[...] = sm[:, :EXPERTS]
        diagonal = lax.broadcasted_iota(jnp.int32, (8, 8), 0) == lanes((8, 8))
        for i, ref in ((32, ga_o), (33, gm_o)):
            ref[...] = jnp.sum(jnp.where(diagonal, sm[:, i : i + 1], 0.0), axis=0, keepdims=True)


def tables():
    even = np.arange(0, HD, 2).astype(np.float32)
    frequency = (np.float32(10000.0) ** (-even / np.float32(HD))).astype(np.float32)
    angle = np.arange(LEN, dtype=np.float32)[:, None] * frequency[None, :]
    angle = np.concatenate([angle] * 4, axis=1).astype(np.float64)
    return np.cos(angle).astype(np.float32), np.sin(angle).astype(np.float32)


def per_device(
    tokens, cotangent, block_ids, routes, w_query, w_key, w_value, w_output, w_router,
    gain_attn, gain_moe, expert_gate, expert_up, expert_down,
):
    x = tokens.reshape(ROWS, D)
    cot = cotangent.reshape(ROWS, D)
    rt = routes.reshape(ROWS, 8).T
    cos, sin = tables()
    cos, sin = jnp.asarray(cos), jnp.asarray(sin)
    params = pltpu.CompilerParams(vmem_limit_bytes=60 * MIB)
    once = pl.Buffered(1)

    def whole(shape):
        return pl.BlockSpec(shape, lambda s: (0,) * len(shape), pipeline_mode=once)

    kept = [
        ((SEQS, LEN, 128), BF), ((SEQS, LEN, 128), BF), ((SEQS, LEN, D), BF),
        ((EP, 2, HALF, 128), BF), ((SEQS, LEN, 128), F32), ((128, D), F32), ((D, D), BF),
        ((2, HALF, D), F32), ((2, HALF, D), BF), ((2, HALF, D), BF), ((D, 256), BF),
    ]
    rall, moe, cot_half, q, kv, nrm, att, lse, gt, wo, mid, moe_own, at_own, w_own = remote_call(
        before_experts, 1,
        [
            sds((EP, 8, ROWS), jnp.int32), sds((EP, 2, 2, HALF // 2, D), BF),
            sds((EP, HALF, D), BF), *[sds(*k) for k in kept],
        ],
        [
            tokens.reshape(2, 2, HALF // 2, D), rt, w_query, w_key, w_value, w_output, w_router,
            gain_attn.reshape(1, 8), gain_moe.reshape(1, 8), cos, sin, block_ids,
            cotangent.reshape(2, HALF, D),
        ],
        [ANY] + [VM] * 11 + [ANY],
        [
            *[pltpu.VMEM(*k) for k in kept],
            pltpu.VMEM((EP, 2, 2, HALF // 2, D), BF), pltpu.VMEM((4, 4, EP, 16, 128), BF),
            pltpu.VMEM((4, 4, EP, 16, 640), BF), pltpu.VMEM((EP, 16, 128), BF),
            pltpu.VMEM((16, 640), BF), pltpu.VMEM((8, 128), F32), pltpu.VMEM((EP, 8, 128), F32),
            pltpu.VMEM((4, 4, 8, 128), F32), pltpu.VMEM((D, 128), F32),
            pltpu.VMEM((LEN, 128), BF), pltpu.VMEM((LEN, 128), BF),
            pltpu.VMEM((EP, 2, HALF, 128), BF), pltpu.VMEM((2, 2, HALF // 2, D), BF),
        ],
        136,
        vmem=60,
    )

    each = lambda *shape: pl.BlockSpec((1, *shape), lambda j: (j,) + (0,) * len(shape))
    fwd = lambda *shape: pl.BlockSpec(
        (1, *shape), lambda j: (jnp.minimum(j, OWN - 1),) + (0,) * len(shape)
    )
    bwd = lambda *shape: pl.BlockSpec(
        (1, *shape), lambda j: (jnp.maximum(j - OWN, 0),) + (0,) * len(shape)
    )
    slots = lambda dtype, n: pltpu.VMEM((OWN, SLOTS, n), dtype)
    rest = pl.BlockSpec((1, 3 * D, F), lambda j: (jnp.maximum(j - OWN - 1, 0), 0, 0))
    both_ways = pl.BlockSpec((1, F, D), lambda j: (lax.rem(j, OWN), 0, 0))
    moved = pltpu.VMEM((2, 1, 2, 96, F), BF)
    dw, eo, dg, du, gg, picks, ca, cb, w_all = pl.pallas_call(
        experts_weights,
        name="experts_weights",
        grid=(2 * OWN,),
        out_shape=[
            sds((OWN - 1, 3 * D, F), BF), sds((EP, OWN * CAP, D), BF), sds((OWN, SLOTS, F), BF),
            sds((OWN, SLOTS, F), BF), sds((OWN, SLOTS, 128), F32), sds((EP, OWN * CAP, ROWS), BF),
            sds((1, 4, 96, F), BF), sds((1, 4, 96, F), BF), sds((EP, 2, D // 2, 256), BF),
        ],
        in_specs=[
            ANY, ANY, ANY, ANY, whole((EP, 8, ROWS)), whole((128, D)), fwd(D, F), fwd(D, F), both_ways,
        ],
        out_specs=[
            rest, ANY, bwd(SLOTS, F), bwd(SLOTS, F), bwd(SLOTS, 128),
            ANY, whole((1, 4, 96, F)), whole((1, 4, 96, F)), ANY,
        ],
        scratch_shapes=[
            pltpu.VMEM((EP, OWN * CAP, D), BF), pltpu.VMEM((EP, OWN * CAP, ROWS), BF),
            pltpu.VMEM((EP, 2, HALF, D), BF), slots(BF, D), pltpu.VMEM((OWN * SLOTS, D), BF),
            slots(F32, 128), slots(BF, F), slots(BF, F), slots(BF, F),
            pltpu.VMEM((1, 4, 4, 2, 96, F), BF), *[moved] * 6, pltpu.SemaphoreType.DMA((10,)),
            pltpu.SemaphoreType.DMA((48,)), pltpu.SemaphoreType.DMA((48,)),
        ],
        compiler_params=pltpu.CompilerParams(
            collective_id=2, has_side_effects=True, vmem_limit_bytes=62 * MIB
        ),
    )(
        moe.reshape(EP * ROWS, D), cotangent.reshape(2, HALF, D), cot_half, w_own.reshape(2, D // 2, 256),
        rall, gt, expert_gate, expert_up,
        expert_down,
    )

    mg, gg_all, shard = pl.pallas_call(
        experts_combine,
        name="experts_combine",
        grid=(OWN,),
        out_shape=[
            sds((ROWS, 2 * D), F32), sds((EP, 8, ROWS), F32), sds((OWN, 2, 96, F), BF),
        ],
        in_specs=[
            ANY, each(SLOTS, F), each(SLOTS, F), ANY, ANY, each(D, F), each(D, F), ANY, ANY, ANY,
        ],
        out_specs=[whole((ROWS, 2 * D)), ANY, whole((OWN, 2, 96, F))],
        scratch_shapes=[
            pltpu.VMEM((EP, OWN * CAP, D), BF), pltpu.VMEM((EP, OWN * CAP, ROWS), BF),
            slots(F32, 128), pltpu.VMEM((EP, OWN * CAP, D), BF), pltpu.VMEM((EP, 8, ROWS), F32),
            *([pltpu.VMEM((4, ROWS, D), BF)] * 2 + [pltpu.VMEM((2, HALF, D), BF)] * 3) * 2,
            *([pltpu.VMEM((2, OWN - 1, 2, 96, F), BF)] * 4 + [pltpu.VMEM((OWN, 4, 96, F), BF)]) * 2,
            *[pltpu.VMEM((2, OWN, 48, F), BF)] * 6,
            pltpu.SemaphoreType.DMA((12,)),
            pltpu.SemaphoreType.DMA((64,)),
            pltpu.SemaphoreType.DMA((64,)),
        ],
        compiler_params=pltpu.CompilerParams(
            collective_id=3, has_side_effects=True, vmem_limit_bytes=62 * MIB
        ),
    )(
        eo, dg, du, gg, picks, expert_gate, expert_up, dw.reshape(OWN - 1, 4, 4, 2, 96, F), ca, cb,
    )
    heads = pltpu.VMEM((EP, 2, HALF, 128), BF)
    blocks = pltpu.VMEM((4, 4, 64, 256), BF)
    arriving = pltpu.VMEM((3, 4, 64, 256), BF)
    column = pltpu.VMEM((4, 64, 256), BF)
    dw_sum, output, grad_x, gq, gk, gv, go, gs = remote_call(
        tail, 4,
        [
            sds((4, 4, OWN, 2, 96, F), BF), sds((ROWS, D), BF), sds((ROWS, D), BF), sds((8, D), F32),
            sds((8, 512), F32), sds((8, 512), F32), sds((8, D), F32), sds((8, 128), F32),
        ],
        [
            mg, mid.reshape(ROWS, D), wo, w_all, q, kv, nrm, att, lse, at_own, shard, gg_all, rt,
            moe_own.reshape(ROWS, D), cot, gt, x, cos, sin, block_ids,
        ],
        [ANY] * 11 + [VM] * 9,
        [
            pltpu.VMEM((ROWS, 2 * D), F32), pltpu.VMEM((ROWS, D), F32), pltpu.VMEM((D, D), BF),
            pltpu.VMEM((EP, 2, D // 2, 256), BF), pltpu.VMEM((SEQS, LEN, 128), BF),
            pltpu.VMEM((SEQS, LEN, 128), BF), pltpu.VMEM((SEQS, LEN, D), BF), heads,
            pltpu.VMEM((SEQS, LEN, 128), F32), pltpu.VMEM((EP, 2, HALF, D), BF), *[heads] * 4,
            pltpu.VMEM((EP, 2, HALF, 256), BF), pltpu.VMEM((EP, 2, HALF, 256), BF),
            pltpu.VMEM((LEN, 128), BF), pltpu.VMEM((LEN, 128), BF), pltpu.VMEM((LEN, 128), F32),
            pltpu.VMEM((LEN, 128), F32), pltpu.VMEM((ROWS, D), F32), pltpu.VMEM((D, 384), F32),
            blocks, blocks, arriving, arriving, column, column, pltpu.VMEM((3, 64, 256), BF),
            pltpu.VMEM((3, 64, 256), BF),
            pltpu.VMEM((EP, 8, 512), F32), pltpu.VMEM((EP, 8, 512), F32),
        ],
        160,
        [ANY] + [VM] * 7,
        vmem=60,
    )

    small = [(8, D), (8, 512), (8, 512), (8, D)]
    rows = pl.BlockSpec((ROWS // OWN, D), lambda j: (j, 0))
    g_gate, g_up, g_down, output, grad_x, gq, gk, gv, go, gr, g_attn, g_moe = pl.pallas_call(
        widen,
        name="widen",
        grid=(OWN,),
        out_shape=[
            sds((OWN, D, F), F32), sds((OWN, D, F), F32), sds((OWN, F, D), F32),
            sds((ROWS, D), BF), sds((ROWS, D), BF), *[sds(n, F32) for n in small],
            sds((8, EXPERTS), F32), sds((1, 8), F32), sds((1, 8), F32),
        ],
        in_specs=[
            pl.BlockSpec((DP, 1, 192, F), lambda j: (0, j, 0, 0)), rows, rows,
            *[whole(n) for n in small], whole((8, 128)),
        ],
        out_specs=[
            each(D, F), each(D, F), each(F, D), rows, rows, *[whole(n) for n in small],
            whole((8, EXPERTS)), whole((1, 8)), whole((1, 8)),
        ],
        compiler_params=params,
    )(dw_sum.reshape(DP, OWN, 192, F), output, grad_x, gq, gk, gv, go, gs)
    return (
        output.reshape(tokens.shape),
        grad_x.reshape(tokens.shape),
        gq,
        gk,
        gv,
        go,
        gr,
        g_attn.reshape(8),
        g_moe.reshape(8),
        g_gate,
        g_up,
        g_down,
    )


def solution(mesh):
    rows, own, both_axes = P("dp", "ep", None), P("ep", None, None), P(("dp", "ep"), None)
    line = P(("dp", "ep"))
    return jax.shard_map(
        per_device,
        mesh=mesh,
        in_specs=(
            rows, rows, P("dp", None), rows, both_axes, both_axes, both_axes, both_axes, both_axes,
            line, line, own, own, own,
        ),
        out_specs=(
            rows, rows, both_axes, both_axes, both_axes, both_axes, both_axes, line, line, own,
            own, own,
        ),
        check_vma=False,
    )
```

```python
import math

import jax
import jax.numpy as jnp
import numpy as np
from jax import lax
from jax.experimental import pallas as pl
from jax.experimental.pallas import tpu as pltpu
from jax.sharding import PartitionSpec as P

MESH = pl.DeviceIdType.MESH
BF = jnp.bfloat16
F32 = jnp.float32
ANY = pl.BlockSpec(memory_space=pl.ANY)
VM = pl.BlockSpec(memory_space=pltpu.VMEM)

DP, EP, CHIPS = 16, 8, 4
D, HD, F = 1024, 64, 512
ROWS, HALF, LEN, SEQS = 256, 128, 1024, 2
EXPERTS, OWN, CAP = 32, 4, 80
SLOTS = EP * CAP
EPS = 1e-6
RES = 0.22
SCORE = 0.015625
LOG2E = 1.4426950408889634
MASKED = -1e30
MIB = 2**20


def nt(a, b):
    return lax.dot_general(a, b, (((1,), (1,)), ((), ())), preferred_element_type=F32)


def nn(a, b):
    return jnp.dot(a, b, preferred_element_type=F32)


def tn(a, b):
    return lax.dot_general(a, b, (((0,), (0,)), ((), ())), preferred_element_type=F32)


def place():
    e = lax.axis_index("ep")
    return lax.axis_index("dp"), e, e // 2, lax.rem(e, 2)


def near(k, n):
    return lax.rem(k + n, 4)


def plane(d, e):
    u, v = d // 4, lax.rem(d, 4)
    up, down = (near(u, 1) * 4 + v, e), (near(u, 3) * 4 + v, e)
    return u, v, up, down, (u * 4 + near(v, 1), e), (u * 4 + near(v, 3), e)


def pair(h):
    return pl.ds(2 * h, 2)


def greet(peers):
    b = pltpu.get_barrier_semaphore()
    for p in peers:
        pl.semaphore_signal(b, inc=1, device_id=p, device_id_type=MESH)
    return lambda: pl.semaphore_wait(b, len(peers))


def ep_peers(d, e):
    return [(d, lax.rem(e + k, EP)) for k in range(1, EP)]


def dp_peers(d, e):
    return [(lax.rem(d + k, DP), e) for k in range(1, DP)]


class Sender:
    def __init__(self, ss, rs):
        self.ss, self.rs, self.n = ss, rs, 0

    def __call__(self, src, dst, dev):
        i = self.n
        self.n += 1
        return pltpu.make_async_remote_copy(
            src, dst, self.ss.at[i], self.rs.at[i], device_id=dev, device_id_type=MESH
        )

    def now(self, src, dst, dev):
        cp = self(src, dst, dev)
        cp.start()
        return cp


class Ring:
    def __init__(self, out, src, d, e, z, c, make):
        right, left = (d, lax.rem(z + 1, CHIPS) * 2 + c), (d, lax.rem(z + 3, CHIPS) * 2 + c)
        part = (d, z * 2 + 1 - c)
        er, el, eo = right[1], left[1], lax.rem(z + 2, CHIPS) * 2 + c
        self.near = [
            [make(src(0), out(e, 0), right), make(src(0), out(e, 0), left)],
            [make(src(1), out(e, 1), left), make(src(1), out(e, 1), right)],
        ]
        self.mate = [make(src(0), out(e, 0), part), make(src(1), out(e, 1), part)]
        self.far = [make(out(el, 0), out(el, 0), right), make(out(er, 1), out(er, 1), left)]
        self.share = [
            make(out(s, h), out(s, h), part)
            for s, h in ((el, 0), (er, 1), (el, 1), (er, 0), (eo, 0), (eo, 1))
        ]

    def start(self, h):
        for cp in self.near[h]:
            cp.start()
        self.mate[h].start()

    def forward(self):
        for h in range(2):
            self.near[h][0].wait_recv()
            self.far[h].start()
            self.share[h].start()
        for h in range(2):
            self.near[1 - h][1].wait_recv()
            self.share[2 + h].start()

    def finish(self):
        for h in range(2):
            self.far[h].wait_recv()
            self.share[4 + h].start()
        for cp in self.near[0] + self.near[1] + self.far:
            cp.wait_send()
        for cp in self.mate + self.share:
            cp.wait()


class Quad:
    def __init__(self, out, me, ahead, behind, make, src=None):
        after, before = lax.rem(me + 1, 4), lax.rem(me + 3, 4)
        mine = lambda h, dev: make(src(h) if src else out(me, h), out(me, h), dev)
        self.near = [
            [mine(0, ahead), mine(0, behind)],
            [mine(1, behind), mine(1, ahead)],
        ]
        self.far = [
            make(out(before, 0), out(before, 0), ahead),
            make(out(after, 1), out(after, 1), behind),
        ]

    def start(self):
        for h in range(2):
            for cp in self.near[h]:
                cp.start()

    def forward(self):
        for h in range(2):
            self.near[h][0].wait_recv()
            self.far[h].start()

    def near_arrived(self):
        for h in range(2):
            self.near[h][1].wait_recv()

    def far_arrived(self):
        for h in range(2):
            self.far[h].wait_recv()

    def arrived(self):
        self.near_arrived()
        self.far_arrived()

    def sent(self):
        for cp in self.near[0] + self.near[1] + self.far:
            cp.wait_send()


def remote_call(body, cid, outs, ins, specs, scratch, sems, out_specs=None, vmem=48, flops=0):
    return pl.pallas_call(
        body,
        name=body.__name__,
        out_shape=outs,
        in_specs=specs,
        out_specs=out_specs if out_specs is not None else [ANY] * len(outs),
        scratch_shapes=[
            *scratch,
            pltpu.SemaphoreType.DMA((24,)),
            pltpu.SemaphoreType.DMA((sems,)),
            pltpu.SemaphoreType.DMA((sems,)),
        ],
        compiler_params=pltpu.CompilerParams(
            collective_id=cid, has_side_effects=True, vmem_limit_bytes=vmem * MIB
        ),
        cost_estimate=pl.CostEstimate(flops=flops, bytes_accessed=20 * MIB, transcendentals=0),
    )(*ins)


def sds(shape, dtype):
    return jax.ShapeDtypeStruct(shape, dtype)


def lanes(shape):
    return lax.broadcasted_iota(jnp.int32, shape, 1)


def turn(v):
    first = lax.rem(lanes(v.shape), HD) < HD // 2
    return jnp.where(first, -pltpu.roll(v, 128 - HD // 2, 1), pltpu.roll(v, HD // 2, 1))


def both(kv):
    low = lanes(kv.shape) < HD
    other = pltpu.roll(kv, HD, 1)
    return jnp.where(low, kv, other).astype(BF), jnp.where(low, other, kv).astype(BF)


def two_heads(v):
    low = lanes(v.shape) < HD
    zero = jnp.zeros_like(v)
    return jnp.concatenate([jnp.where(low, v, zero), jnp.where(low, zero, v)], axis=0)


def spans(i):
    return i * ROWS, min(LEN, i * ROWS + 2 * ROWS)


def before_experts(
    x, rt, w_q, w_k, w_v, wo, wr, ga, gm, cs, sn, ids, cot,
    rall, moe, cot_o, q_h, kv_h, nrm_h, att_h, lse_h, gt_h, wo_h, mid_h, own_h, at_h, ws_h,
    q_o, kv_o, nrm_o, att_o, lse_o, gt_o, wo_o, mid_o, own_o, at_o, w_s,
    xall, wsl, wof, wp, wop, gp, gb, gs, sm_s, kk_s, vv_s, arr, mo, ls, ss, rs,
):
    d, e, z, c = place()
    u, v, up, down, ahead, behind = plane(d, e)
    pairs = [
        (q_o, q_h), (kv_o, kv_h), (nrm_o, nrm_h), (att_o, att_h), (lse_o, lse_h), (gt_o, gt_h),
        (wo_o, wo_h), (mid_o, mid_h), (own_o, own_h), (at_o, at_h), (w_s, ws_h),
    ]
    results = [pltpu.make_async_copy(a, b, ls.at[10 + i]) for i, (a, b) in enumerate(pairs)]
    across = [up, down, (near(u, 2) * 4 + v, e)]
    along = [ahead, behind, (u * 4 + near(v, 2), e)]
    wait = greet(ep_peers(d, e) + across + along)
    q, k, w = w_q[...].astype(F32), w_k[...].astype(F32), w_v[...].astype(F32)
    diagonal = lax.broadcasted_iota(jnp.int32, (8, 8), 0) == lanes((8, 8))
    column = lambda g: jnp.sum(jnp.where(diagonal, g[...].astype(F32), 0.0), axis=1, keepdims=True)
    for t in range(EP):
        kv = [k[:, 64 * t : 64 * t + 64], w[:, 64 * t : 64 * t + 64]]
        row = [q[:, 128 * t : 128 * t + 128], jnp.concatenate(kv, axis=1)]
        wp[t] = jnp.concatenate(row, axis=0).astype(BF)
    w, r = wo[...].astype(F32), wr[...].astype(F32)
    left = jnp.concatenate([w[:, :512], r, jnp.zeros((8, 96), F32)], axis=1)
    right = jnp.concatenate([w[:, 512:], column(ga), column(gm), jnp.zeros((8, 126), F32)], axis=1)
    wop[...] = jnp.concatenate([left, right], axis=0).astype(BF)
    spread = lax.broadcasted_iota(jnp.int32, (8, 128), 1) - 8 * e
    spread = spread == lax.broadcasted_iota(jnp.int32, (8, 128), 0)
    line = jnp.sum(jnp.where(spread, column(ga), 0.0), axis=0, keepdims=True)
    gp[...] = jnp.broadcast_to(line, (8, 128))
    wait()
    make = Sender(ss, rs)
    send = make.now
    own = [
        pltpu.make_async_copy(x, xall.at[e], ls.at[0]),
        pltpu.make_async_copy(wp.at[e], wsl.at[v, u, e], ls.at[1]),
        pltpu.make_async_copy(wop, wof.at[u, v, e], ls.at[2]),
        pltpu.make_async_copy(rt, rall.at[e], ls.at[3]),
        pltpu.make_async_copy(gp, gb.at[e], ls.at[8]),
        pltpu.make_async_copy(cot.at[0], cot_o.at[e], ls.at[9]),
    ]
    for cp in own:
        cp.start()
    tokens = [
        Ring(lambda s, k: xall.at[s, h, k], lambda k: x.at[h, k], d, e, z, c, make) for h in range(2)
    ]
    moes = [
        Ring(lambda s, k: moe.at[s, h, k], lambda k: mo.at[h, k], d, e, z, c, make) for h in range(2)
    ]
    gains = [send(gp, gb.at[e], p) for p in ep_peers(d, e)]
    first = [send(wp.at[p[1]], wsl.at[v, u, e], p) for p in ep_peers(d, e)]
    first += [send(wop, wof.at[u, v, e], p) for p in ep_peers(d, e)]
    tokens[0].start(0)
    tokens[0].start(1)
    own[1].wait()
    for cp in first[: EP - 1]:
        cp.wait_recv()
    w1 = [send(wsl.at[v, u], wsl.at[v, u], p) for p in across]
    own[4].wait()
    for cp in gains:
        cp.wait_recv()
    line = gb[0]
    for s in range(1, EP):
        line = line + gb[s]
    gs[v, u] = line
    g1 = [send(gs.at[v, u], gs.at[v, u], p) for p in across]
    own[2].wait()
    for cp in first[EP - 1 :]:
        cp.wait_recv()
    mine = pl.ds(c * 4, 4)
    part = (d, z * 2 + 1 - c)
    o1 = [send(wof.at[u, v, mine], wof.at[u, v, mine], p) for p in along]
    tokens[0].forward()
    for cp in w1:
        cp.wait_recv()
    w2 = Quad(lambda i, h: wsl.at[i, pair(h)], v, ahead, behind, make)
    w2.start()
    for cp in g1:
        cp.wait_recv()
    g2 = [send(gs.at[v], gs.at[v], p) for p in along]
    last = []
    for k, cp in zip((1, 3, 2), o1):
        cp.wait_recv()
        t = lax.rem(v + 4 - k, 4)
        last.append(send(wof.at[u, t, mine], wof.at[u, t, mine], part))
    o2 = Quad(lambda i, h: wof.at[i, :, pl.ds(c * 4 + 2 * h, 2)], u, up, down, make)
    o2.start()
    tokens[1].start(0)
    tokens[1].start(1)
    w2.forward()
    tokens[0].finish()
    own[0].wait()
    w2.arrived()
    for cp in g2:
        cp.wait_recv()
    for i in range(DP):
        w = wsl[i % 4, i // 4].astype(F32)
        w = jnp.concatenate([w[:, :8].reshape(64, 128), w[:, 8:].reshape(64, 128)], axis=1)
        w_s[64 * i : 64 * i + 64] = w.astype(BF)
    results[10].start()
    gain_a = jnp.concatenate([gs[i % 4, i // 4][:1, :64] for i in range(DP)], axis=1)

    def project(h):
        for r in range(4):
            rows = slice(256 * r, 256 * r + 256)
            t = xall[2 * r : 2 * r + 2, h].astype(F32).reshape(256, D)
            factor = lax.rsqrt(jnp.mean(t * t, axis=1, keepdims=True) + EPS)
            n = (t * factor * gain_a).astype(BF)
            nrm_o[h, rows] = n
            pre = nn(n, w_s[...])
            co, si = cs[rows], sn[rows]
            q, kv = pre[:, :128], pre[:, 128:]
            q_o[h, rows] = (q * co + turn(q) * si).astype(BF)
            kv = jnp.where(lanes(kv.shape) < HD, kv * co + turn(kv) * si, kv).astype(BF)
            kv_o[h, rows] = kv
            kk_s[rows], vv_s[rows] = both(kv.astype(F32))

    def attend(h, i):
        ids_k = ids[h : h + 1]
        ids_q = jnp.broadcast_to(ids_k[:, ROWS * i : ROWS * i + ROWS], (128, ROWS)).T[:, :1]
        q2 = two_heads(q_o[h, ROWS * i : ROWS * i + ROWS].astype(F32)).astype(BF)
        own_ids = jnp.concatenate([ids_q, ids_q], axis=0)
        at, end = spans(i)
        parts = []
        if at:
            parts.append((nt(q2, kk_s[:at]) * (SCORE * LOG2E), slice(0, at)))
        t = nt(q2, kk_s[at:end]) * (SCORE * LOG2E)
        parts.append((jnp.where(ids_k[:, at:end] <= own_ids, t, MASKED), slice(at, end)))
        peak = parts[0][0].max(axis=1, keepdims=True)
        for t, _ in parts[1:]:
            peak = jnp.maximum(peak, t.max(axis=1, keepdims=True))
        total, out = 0.0, 0.0
        for t, span in parts:
            p = jnp.exp2(t - peak)
            total = total + p.sum(axis=1, keepdims=True)
            out = out + nn(p.astype(BF), vv_s[span])
        out = out * (1.0 / total)
        lse = jnp.broadcast_to(peak + jnp.log2(total), (2 * ROWS, 128))
        low = lanes((ROWS, 128)) < HD
        att = jnp.where(low, out[:ROWS], out[ROWS:]).astype(BF)
        att_o[2 * i : 2 * i + 2, h] = att.reshape(2, HALF, 128)
        lse_o[h, ROWS * i : ROWS * i + ROWS] = jnp.where(low, lse[:ROWS], lse[ROWS:])

    att_own = [pltpu.make_async_copy(att_o.at[e, h], arr.at[e, h], ls.at[4 + h]) for h in range(2)]
    moe_own = [pltpu.make_async_copy(mo.at[h], moe.at[e, h], ls.at[6 + h]) for h in range(2)]

    def exchange(h):
        att_own[h].start()
        cps = []
        for k in (4, 3, 5, 2, 6, 1, 7):
            t = lax.rem(e + k, EP)
            cps.append(send(att_o.at[t, h], arr.at[e, h], (d, t)))
        return cps

    def branch(h, cps):
        att_own[h].wait()
        for cp in cps:
            cp.wait_recv()
        a = jnp.concatenate([arr[s, h] for s in range(EP)], axis=1)
        at_o[h] = a
        m = xall[e, h].astype(F32).reshape(HALF, D) + RES * nn(a, wo_o[...])
        mid_o[h] = m
        factor = lax.rsqrt(jnp.mean(m * m, axis=1, keepdims=True) + EPS)
        n = (m * factor * gt_o[33:34, :]).astype(BF)
        own_o[h] = n
        mo[h] = n.reshape(2, HALF // 2, D)
        moe_own[h].start()
        moes[h].start(0)
        moes[h].start(1)

    project(0)
    tokens[1].forward()
    attend(0, 0)
    attend(0, 1)
    o2.forward()
    attend(0, 2)
    attend(0, 3)
    x0 = exchange(0)
    up_z, down_z = near(z, 1) * 2 + c, near(z, 3) * 2 + c
    cots = [send(cot.at[0], cot_o.at[e], (d, t)) for t in (up_z, down_z, z * 2 + 1 - c)]
    tokens[1].finish()
    project(1)
    attend(1, 0)
    attend(1, 1)
    attend(1, 2)
    attend(1, 3)
    x1 = exchange(1)
    for cp in results[:5]:
        cp.start()
    o2.arrived()
    for k in (1, 3, 2):
        t = near(u, k)
        last.append(send(wof.at[t, :, mine], wof.at[t, :, mine], part))
    routes = [send(rt, rall.at[e], p) for p in ep_peers(d, e)]
    for cp in last:
        cp.wait_recv()
    for i in range(4):
        rows = slice(256 * i, 256 * i + 256)
        o = wof[i].astype(F32).reshape(32, 16, 640)
        left, right = o[:, :8].reshape(256, 640), o[:, 8:].reshape(256, 640)
        wo_o[rows, :512] = left[:, :512].astype(BF)
        wo_o[rows, 512:] = right[:, :512].astype(BF)
        sm_s[rows] = jnp.where(lanes((256, 128)) < 32, left[:, 512:], pltpu.roll(right[:, 512:], 32, 1))
    gt_o[...] = sm_s[...].T
    for cp in results[5:7]:
        cp.start()
    branch(0, x0)
    branch(1, x1)
    for cp in results[7:10]:
        cp.start()
    moes[0].forward()
    moes[1].forward()
    for cp, t in zip(cots[:2], (down_z, up_z)):
        cp.wait_recv()
        cots.append(send(cot_o.at[t], cot_o.at[t], part))
    moes[0].finish()
    moes[1].finish()
    w2.sent()
    o2.sent()
    for cp in gains + first + w1 + g1 + g2 + o1 + last + x0 + x1:
        cp.wait_send()
    for cp in routes:
        cp.wait()
    own[3].wait()
    own[5].wait()
    for cp in cots[:2]:
        cp.wait_send()
    for cp in cots[2:] + moe_own + results:
        cp.wait()


def routing(rt, logits_t):
    ids = lax.broadcasted_iota(jnp.int32, (EXPERTS, ROWS), 0)
    hit = rt[0:1] == ids
    for k in range(1, 8):
        hit = hit | (rt[k : k + 1] == ids)
    w = jnp.where(hit, logits_t, MASKED)
    w = jnp.where(hit, jnp.exp(w - w.max(axis=0, keepdims=True)), 0.0)
    gates = w / w.sum(axis=0, keepdims=True)
    earlier = lax.broadcasted_iota(jnp.int32, (ROWS, ROWS), 0) < lax.broadcasted_iota(
        jnp.int32, (ROWS, ROWS), 1
    )
    slot = nn(jnp.where(hit, 1.0, 0.0).astype(BF), jnp.where(earlier, 1.0, 0.0).astype(BF))
    return gates, jnp.where(hit, slot, -1.0)


class Reduce:
    def __init__(self, chunk, me, ahead, behind, one, two, three, make):
        at = lambda k: lax.rem(me + k, 4)
        self.one, self.two, self.three = one, two, three
        self.first = [
            make(chunk(at(2), 0), one.at[0], ahead),
            make(chunk(at(2), 1), one.at[1], behind),
        ]
        self.second = [
            make(chunk(at(1), 1), two.at[0], ahead),
            make(chunk(at(3), 0), two.at[1], behind),
        ]
        self.third = [make(one.at[0], three.at[0], ahead), make(one.at[1], three.at[1], behind)]

    def start(self):
        for cp in self.first + self.second:
            cp.start()

    def go_on(self, k, mine, pieces):
        self.first[k].wait_recv()

        def add(i, carry):
            self.one[k, i] = self.one[k, i] + (mine[i] if pieces > 1 else mine[...])
            return carry

        lax.fori_loop(0, pieces, add, 0)
        self.third[k].start()

    def arrived(self, k):
        self.second[1 - k].wait_recv()
        self.third[k].wait_recv()

    def sent(self):
        for cp in self.first + self.second + self.third:
            cp.wait_send()


def close(r, chunk, pieces):
    for k in range(2):
        r.arrived(k)

        def body(i, carry):
            for q in range(2):
                piece = r.two[1 - k, i, q].astype(F32) + r.three[k, i, q].astype(F32)
                chunk[i, 2 * k + q] = (chunk[i, 2 * k + q].astype(F32) + piece).astype(BF)
            return carry

        lax.fori_loop(0, pieces, body, 0)


def experts_weights(
    moe, cot, cot_h, w_own, rall, gt, wg, wu, wd, dw_o, eo_h, dg_o, du_o, gg_o, p_h, ca_o, cb_o, w_o,
    eo_o, p_o, cot_s, x_s, y_s, gate_s, a_s, b_s, h_s, dw_s, a1, a2, a3, b1, b2, b3, ls, ss, rs,
):
    step = pl.program_id(0)
    d, e, z, c = place()
    u, v, up, down, ahead, behind = plane(d, e)
    first = e * OWN
    make = Sender(ss, rs)
    right, left, other = near(z, 1) * 2 + c, near(z, 3) * 2 + c, z * 2 + 1 - c
    far = near(z, 2) * 2 + c
    near_c = [make(cot.at[1], cot_s.at[e, 1], (d, t)) for t in (left, right, other)]
    far_c = [
        make(cot_h.at[left], cot_s.at[left, 0], (d, right)),
        make(cot_s.at[right, 1], cot_s.at[right, 1], (d, left)),
    ]
    share = [
        make(cot_s.at[t, k], cot_s.at[t, k], (d, other)) for t, k in ((right, 1), (left, 1), (far, 0), (far, 1))
    ]
    ra = Reduce(lambda i, h: dw_s.at[:, i, pair(h), 0], u, up, down, a1, a2, a3, make)
    rb = Reduce(lambda i, h: dw_s.at[:, pair(h), i, 1], v, ahead, behind, b1, b2, b3, make)
    slices = Ring(lambda s, k: w_o.at[s, k], lambda k: w_own.at[k], d, e, z, c, make)
    own_w = pltpu.make_async_copy(w_own, w_o.at[e], ls.at[2])
    two = lambda k: pl.ds(near(z, k) * 2, 2)
    own = [pltpu.make_async_copy(cot_h.at[two(k)], cot_s.at[two(k), 0], ls.at[7 + i]) for i, k in enumerate((0, 1, 3))]
    own.append(pltpu.make_async_copy(cot.at[1], cot_s.at[e, 1], ls.at[5]))
    results = [pltpu.make_async_copy(eo_o, eo_h, ls.at[3]), pltpu.make_async_copy(p_o, p_h, ls.at[4])]
    rows_of = lambda s: pl.ds(pl.multiple_of(s * CAP, 16), CAP)

    @pl.when(step == 0)
    def _():
        load = pltpu.make_async_copy(moe, y_s.at[pl.ds(0, EP * ROWS)], ls.at[6])
        load.start()
        greet(ep_peers(d, e) + [up, down, ahead, behind])()
        for cp in near_c + far_c[:1] + own:
            cp.start()
        load.wait()
        router_t = gt[:EXPERTS].astype(BF)
        row = lax.broadcasted_iota(jnp.int32, (EXPERTS, ROWS), 0)
        place_in = lax.broadcasted_iota(jnp.int32, (CAP, ROWS), 0).astype(F32)

        def source(s, carry):
            m = y_s[pl.ds(pl.multiple_of(s * ROWS, ROWS), ROWS)]
            gates, slot = routing(rall[s], nt(router_t, m))
            picks = []
            for i in range(OWN):
                sel = row == first + i
                pick = jnp.sum(jnp.where(sel, slot, 0.0), axis=0, keepdims=True) == place_in
                gate = jnp.sum(jnp.where(sel, gates, 0.0), axis=0, keepdims=True)
                g = jnp.sum(jnp.where(pick, gate, 0.0), axis=1, keepdims=True)
                gate_s[i, rows_of(s)] = jnp.broadcast_to(g, (CAP, 128))
                picks.append(jnp.where(pick, 1.0, 0.0).astype(BF))
            pick = jnp.concatenate(picks, axis=0)
            p_o[s] = pick
            xs = nn(pick, m).astype(BF)
            for i in range(OWN):
                x_s[i, rows_of(s)] = xs[CAP * i : CAP * i + CAP]
            return carry

        lax.fori_loop(0, EP, source, 0)

    @pl.when(step < OWN)
    def _():
        x = x_s[step]
        gate = gate_s[step][:, :1] * RES
        g = nn(x, wg[0])
        u = nn(x, wu[0])
        s = 1.0 / (1.0 + jnp.exp(-g))
        silu = g * s
        a_s[step] = (u * s * (1.0 + g * (1.0 - s))).astype(BF)
        b_s[step] = silu.astype(BF)
        h = silu * u
        h_s[step] = h.astype(BF)
        eo = nn((h * gate).astype(BF), wd[0]).astype(BF)
        for i in range(EP):
            eo_o[i, rows_of(step)] = eo[CAP * i : CAP * i + CAP]

    @pl.when(step == 2)
    def _():
        near_c[0].wait_recv()
        far_c[1].start()
        share[0].start()
        near_c[1].wait_recv()
        share[1].start()
        far_c[0].wait_recv()
        share[2].start()
        slices.start(0)
        slices.start(1)
        own_w.start()

    @pl.when(step == OWN)
    def _():
        for cp in results:
            cp.start()
        far_c[1].wait_recv()
        share[3].start()
        for cp in own + share + near_c[2:]:
            cp.wait()
        for cp in near_c[:2] + far_c:
            cp.wait_send()

        def source(s, carry):
            ys = nn(p_o[s], cot_s[s].reshape(ROWS, D)).astype(BF)
            for i in range(OWN):
                at = pl.ds(pl.multiple_of(i * SLOTS + s * CAP, 16), CAP)
                y_s[at] = ys[CAP * i : CAP * i + CAP]
            return carry

        lax.fori_loop(0, EP, source, 0)

    def back(j, store):
        x, y = x_s[j], y_s[pl.ds(pl.multiple_of(j * SLOTS, SLOTS), SLOTS)]
        gate = gate_s[j][:, :1] * RES
        dh = nt(y, wd[0])
        h = h_s[j].astype(F32)
        gg_o[0] = jnp.broadcast_to(RES * jnp.sum(h * dh, axis=1, keepdims=True), (SLOTS, 128))
        dh = dh * gate
        dg = (dh * a_s[j].astype(F32)).astype(BF)
        du = (dh * b_s[j].astype(F32)).astype(BF)
        dg_o[0], du_o[0] = dg, du
        w = tn(x, jnp.concatenate([dg, du], axis=1))
        store(0, w[:, :F].astype(BF))
        store(1, w[:, F:].astype(BF))
        w = tn((h * gate).astype(BF), y)
        store(2, jnp.concatenate([w[:, :F], w[:, F:]], axis=0).astype(BF))

    @pl.when(step == OWN)
    def _():
        whole_w = [None] * 3

        def store(i, w):
            whole_w[i] = w

        back(0, store)
        dw_s[0] = jnp.concatenate(whole_w, axis=0).reshape(4, 4, 2, 96, F)
        ra.start()
        rb.start()

    @pl.when(step > OWN)
    def _():
        def store(i, w):
            dw_o[0, D * i : D * i + D] = w

        back(step - OWN, store)

    @pl.when(step == OWN + 1)
    def _():
        slices.forward()
        for k in range(2):
            ra.go_on(k, dw_s.at[0, near(u, 1 + 2 * k), pair(k), 0], 1)
            rb.go_on(k, dw_s.at[0, pair(k), near(v, 1 + 2 * k), 1], 1)

    @pl.when(step == 2 * OWN - 1)
    def _():
        for cp in results:
            cp.wait()
        slices.finish()
        own_w.wait()
        ca_o[0] = dw_s[0, u, :, 0]
        cb_o[0] = dw_s[0, :, v, 1]
        close(ra, ca_o, 1)
        close(rb, cb_o, 1)
        ra.sent()
        rb.sent()


class Combine:
    def __init__(self, term, stage, buf, m1, m2, m3, d, z, c, make):
        right, left = (d, near(z, 1) * 2 + c), (d, near(z, 3) * 2 + c)
        self.term, self.stage, self.buf, self.m1, self.m2, self.m3, self.c = term, stage, buf, m1, m2, m3, c
        self.turns = [near(z, k) * 2 for k in (2, 1, 3, 0)]
        self.mates = [make(stage.at[i], buf.at[i], (d, z * 2 + 1 - c)) for i in range(4)]
        lo, hi = pl.ds(0, HALF), pl.ds(HALF, HALF)
        self.s1 = [make(buf.at[0, lo], m1.at[0], right), make(buf.at[0, hi], m1.at[1], left)]
        self.s2 = [make(buf.at[1, hi], m2.at[0], right), make(buf.at[2, lo], m2.at[1], left)]
        self.s3 = [make(m1.at[0], m3.at[0], right), make(m1.at[1], m3.at[1], left)]

    def begin(self):
        for i, t in enumerate(self.turns):
            self.stage[i] = self.term(t + 1 - self.c).astype(BF)
            self.mates[i].start()

    def add(self, i):
        own = self.term(self.turns[i] + self.c)
        self.mates[i].wait_recv()
        self.buf[i] = (self.buf[i].astype(F32) + own).astype(BF)

    def send(self):
        self.add(0)
        for cp in self.s1:
            cp.start()
        self.add(1)
        self.s2[0].start()
        self.add(2)
        self.s2[1].start()

    def go_on(self):
        for k, i in ((0, 1), (1, 2)):
            self.s1[k].wait_recv()
            self.m1[k] = self.m1[k] + self.buf[i, HALF * k : HALF * k + HALF]
            self.s3[k].start()

    def finish(self, out, columns):
        for k in range(2):
            rows = slice(HALF * k, HALF * k + HALF)
            self.s2[1 - k].wait_recv()
            self.s3[k].wait_recv()
            arrived = self.m2[1 - k].astype(F32) + self.m3[k].astype(F32)
            out[rows, columns] = self.buf[3, rows].astype(F32) + arrived

    def sent(self):
        for cp in self.mates + self.s1 + self.s2 + self.s3:
            cp.wait_send()


def experts_combine(
    eo_h, dg, du, gg_h, picks_h, wg, wu, dw, ca, cb, mg_h, gt_o, sh_o,
    mg_o, eo, picks, gg, dx_s, gg_s, stage, buf, m1, m2, m3, stage_, buf_, m1_, m2_, m3_,
    a1, a2, a3, amine, ac, b1, b2, b3, bmine, bc, a4, a5, a6, b4, b5, b6, ls, ss, rs,
):
    j = pl.program_id(0)
    d, e, z, c = place()
    u, v, up, down, ahead, behind = plane(d, e)
    make = Sender(ss, rs)
    later = pl.ds(1, OWN - 1)
    deep = lambda h: pl.ds(48 * h, 48)
    ra = Reduce(lambda i, h: dw.at[:, i, pair(h), 0], u, up, down, a1, a2, a3, make)
    rb = Reduce(lambda i, h: dw.at[:, pair(h), i, 1], v, ahead, behind, b1, b2, b3, make)
    qa = Reduce(lambda i, h: ac.at[:, i, deep(h)], v, ahead, behind, a4, a5, a6, make)
    qb = Reduce(lambda i, h: bc.at[:, i, deep(h)], u, up, down, b4, b5, b6, make)
    mix = Combine(lambda s: tn(picks[s], eo[s]), stage, buf, m1, m2, m3, d, z, c, make)
    back = Combine(lambda s: tn(picks[s], dx_s[s]), stage_, buf_, m1_, m2_, m3_, d, z, c, make)
    load = pltpu.make_async_copy
    own = [
        load(dw.at[:, near(u, 1), pair(0), 0], amine.at[0], ls.at[0]),
        load(dw.at[:, near(u, 3), pair(1), 0], amine.at[1], ls.at[1]),
        load(dw.at[:, pair(0), near(v, 1), 1], bmine.at[0], ls.at[2]),
        load(dw.at[:, pair(1), near(v, 3), 1], bmine.at[1], ls.at[3]),
        load(dw.at[:, u, :, 0], ac.at[later], ls.at[4]),
        load(dw.at[:, :, v, 1], bc.at[later], ls.at[5]),
        load(ca, ac.at[pl.ds(0, 1)], ls.at[6]),
        load(cb, bc.at[pl.ds(0, 1)], ls.at[7]),
    ]
    gt_own = load(gg_s.at[e], gt_o.at[e], ls.at[8])
    rows = [make(gg_s.at[p[1]], gt_o.at[e], p) for p in ep_peers(d, e)]

    sums = [load(mg_o.at[:, pl.ds(D * i, D)], mg_h.at[:, pl.ds(D * i, D)], ls.at[12 + i]) for i in range(2)]
    early = [load(eo_h, eo, ls.at[9]), load(picks_h, picks, ls.at[10]), load(gg_h, gg, ls.at[11])]

    @pl.when(j == 0)
    def _():
        for cp in early:
            cp.start()
        greet(ep_peers(d, e) + [up, down, ahead, behind])()
        ra.start()
        rb.start()
        for cp in own:
            cp.start()
        for cp in early:
            cp.wait()
        mix.begin()

    @pl.when(j == 1)
    def _():
        mix.send()

    dx = (nt(dg[0], wg[0]) + nt(du[0], wu[0])).astype(BF)
    for s in range(EP):
        dx_s[s, pl.ds(pl.multiple_of(j * CAP, 16), CAP)] = dx[CAP * s : CAP * s + CAP]

    @pl.when(j == OWN - 1)
    def _():
        back.begin()
        mix.go_on()
        back.send()
        for cp in own:
            cp.wait()
        for k in range(2):
            ra.go_on(k, amine.at[k], OWN - 1)
            rb.go_on(k, bmine.at[k], OWN - 1)
        mix.add(3)
        for s in range(EP):
            p = picks[s]
            at = pl.ds(pl.multiple_of(s * CAP, 16), CAP)
            lines = [
                jnp.sum(
                    p[CAP * i : CAP * i + CAP].astype(F32) * gg[i, at][:, :1], axis=0, keepdims=True
                )
                for i in range(OWN)
            ]
            gg_s[s] = jnp.concatenate(lines + [jnp.zeros((8 - OWN, ROWS), F32)], axis=0)
        for cp in rows:
            cp.start()
        gt_own.start()
        back.add(3)
        back.go_on()
        mix.finish(mg_o, slice(0, D))
        sums[0].start()
        close(ra, ac.at[later], OWN - 1)
        qa.start()
        close(rb, bc.at[later], OWN - 1)
        qb.start()
        back.finish(mg_o, slice(D, 2 * D))
        sums[1].start()
        for q, chunk, me in ((qa, ac, v), (qb, bc, u)):
            for k in range(2):
                t = near(me, 1 + 2 * k)
                q.first[k].wait_recv()
                q.one[k] = q.one[k] + chunk[:, t, 48 * k : 48 * k + 48]
                q.third[k].start()
        for h, q, chunk, me in ((0, qa, ac, v), (1, qb, bc, u)):
            for k in range(2):
                q.arrived(k)
                mine = chunk[:, me, 48 * k : 48 * k + 48].astype(F32)
                total = mine + q.two[1 - k].astype(F32) + q.three[k].astype(F32)
                sh_o[:, h, 48 * k : 48 * k + 48] = total.astype(BF)
        for r in (ra, rb, qa, qb, mix, back):
            r.sent()
        for cp in rows:
            cp.wait()
        gt_own.wait()
        for cp in sums:
            cp.wait()


def norm_back(grad, values, factor, gain):
    scaled = grad * gain
    grad_gain = jnp.sum(grad * values * factor, axis=0, keepdims=True)
    mean = jnp.mean(scaled * values, axis=1, keepdims=True)
    return factor * (scaled - values * (factor * factor * mean)), grad_gain


def tail(
    mg_h, mid_h, wo_h, wf_h, q_h, kv_h, nrm_h, att_h, lse_h, at_h, sh, moe_h, cot_h, gt_h, x_h, cs_h, sn_h,
    gg, rt, ids, ag, out_h, gx_h, wq_o, wk_o, wv_o, wo_o, sm_o,
    out_o, gx_o, moe, cot, gt, x, cs, sn, mg, mid, wo, wf, q_s, kv_s, nrm, att, lse, at, da, gb, da_s, gb_s, dq, dq_s, kk_s, vv_s, dk_s, dv_s,
    gm, dw, pa, pb, ra, rb, ta, tb, qa, qb, s1, r2, ls, ss, rs,
):
    d, e, z, c = place()
    u, v, up, down, ahead, behind = plane(d, e)
    across = [up, down, (near(u, 2) * 4 + v, e)]
    along = [ahead, behind, (u * 4 + near(v, 2), e)]
    wait = greet(ep_peers(d, e) + across + along)
    pairs = [
        (mg_h, mg), (mid_h, mid), (wo_h, wo), (q_h, q_s), (kv_h, kv_s), (att_h, att), (lse_h, lse),
        (nrm_h, nrm), (at_h, at.at[e]), (wf_h, wf), (sh, ag.at[u, v]),
    ]
    loads = [pltpu.make_async_copy(a, b, ls.at[i]) for i, (a, b) in enumerate(pairs)]
    pairs = [(gt_h, gt), (moe_h, moe), (cot_h, cot), (x_h, x), (cs_h, cs), (sn_h, sn)]
    more_loads = [pltpu.make_async_copy(a, b, ls.at[15 + i]) for i, (a, b) in enumerate(pairs)]
    results = [pltpu.make_async_copy(out_o, out_h, ls.at[21]), pltpu.make_async_copy(gx_o, gx_h, ls.at[22])]
    for cp in more_loads[:3] + loads + more_loads[3:]:
        cp.start()
    wait()
    make = Sender(ss, rs)
    low_half = lambda k: pl.ds(48 * k, 48)
    own_a, own_b = (lambda k: sh.at[:, 0, low_half(k)]), (lambda k: sh.at[:, 1, low_half(k)])

    def piece(fixed, along_u, half, src=None):
        if along_u:
            out = lambda i, k: ag.at[i, fixed, :, half, low_half(k)]
            return Quad(out, u, up, down, make, src)
        out = lambda i, k: ag.at[fixed, i, :, half, low_half(k)]
        return Quad(out, v, ahead, behind, make, src)

    one = [piece(u, False, 0, own_a), piece(v, True, 1, own_b)]
    two = [
        [piece(near(v, k), True, 0, None if k else own_a), piece(near(u, k), False, 1, None if k else own_b)]
        for k in range(4)
    ]
    for r in one + two[0]:
        r.start()
    for cp in more_loads[:3]:
        cp.wait()
    router_t = gt[:EXPERTS].astype(BF)
    gates, _ = routing(rt, nt(router_t, moe[...]))
    back = gg[...][:, :OWN].reshape(EXPERTS, ROWS)
    both_ = gates * back
    gl = (both_ - gates * jnp.sum(both_, axis=0, keepdims=True)).astype(BF)
    loads[0].wait()
    loads[1].wait()
    loads[2].wait()
    m = mid[...]
    grad = mg[:, D:] + tn(gl, router_t)
    factor = lax.rsqrt(jnp.mean(m * m, axis=1, keepdims=True) + EPS)
    t, gain_m = norm_back(grad, m, factor, gt[33:34])
    t = cot[...].astype(F32) + t
    gm[...] = t
    gradient = (RES * t).astype(BF)
    ga = nt(gradient, wo[...]).astype(BF)
    for i in range(EP):
        da[i] = ga[:, 128 * i : 128 * i + 128].reshape(2, HALF, 128)
        gb[i] = gradient[:, 128 * i : 128 * i + 128].reshape(2, HALF, 128)
    own = [
        pltpu.make_async_copy(da.at[e], da_s.at[e], ls.at[11]),
        pltpu.make_async_copy(gb.at[e], gb_s.at[e], ls.at[12]),
    ]
    for cp in own:
        cp.start()
    da_c = [make.now(da.at[p[1]], da_s.at[e], p) for p in ep_peers(d, e)]
    gb_c = [make.now(gb.at[p[1]], gb_s.at[e], p) for p in ep_peers(d, e)]
    ats = Ring(lambda s, k: at.at[s, k], lambda k: at_h.at[k], d, e, z, c, make)
    ats.start(0)
    ats.start(1)
    router = nn(gl, moe[...])
    out_o[...] = (m + mg[:, :D]).astype(BF)
    results[0].start()
    for r in one:
        r.forward()
    for r in one:
        r.near_arrived()
    for r in two[1] + two[3]:
        r.start()
    for cp in loads[3:9] + more_loads[3:]:
        cp.wait()
    for cp in own:
        cp.wait()
    for cp in da_c + gb_c:
        cp.wait_recv()
    low = lanes((ROWS, 128)) < HD

    def unturn(w, rows):
        return w * cs[rows] - turn(w) * sn[rows]

    def attend_back(s):
        kk_s[...], vv_s[...] = both(kv_s[s].astype(F32))
        dk_s[...] = jnp.zeros_like(dk_s)
        dv_s[...] = jnp.zeros_like(dv_s)
        ids_k = ids[s : s + 1]
        dqs = []
        for i in range(4):
            rows = slice(ROWS * i, ROWS * i + ROWS)
            q2 = two_heads(q_s[s, rows].astype(F32)).astype(BF)
            o2f = two_heads(da_s[2 * i : 2 * i + 2, s].reshape(ROWS, 128).astype(F32))
            o2 = o2f.astype(BF)
            a = att[2 * i : 2 * i + 2, s].reshape(ROWS, 128).astype(F32)
            delta = jnp.sum(o2f * jnp.concatenate([a, a], axis=0), axis=1, keepdims=True)
            l2 = jnp.concatenate([lse[s, rows][:, :1], lse[s, rows][:, HD : HD + 1]], axis=0)
            ids_q = jnp.broadcast_to(ids_k[:, rows], (128, ROWS)).T[:, :1]
            ids_q = jnp.concatenate([ids_q, ids_q], axis=0)
            start, end = spans(i)
            grad_q = 0.0
            for span in ([slice(0, start)] if start else []) + [slice(start, end)]:
                w = nt(q2, kk_s[span]) * (SCORE * LOG2E) - l2
                if span.start == start:
                    w = jnp.where(ids_k[:, span] <= ids_q, w, MASKED)
                p = jnp.exp2(w)
                gp = nt(o2, vv_s[span])
                ds = (p * (gp - delta)).astype(BF)
                grad_q = grad_q + nn(ds, kk_s[span])
                dk_s[span] += tn(ds, q2)
                dv_s[span] += tn(p.astype(BF), o2)
            grad_q = SCORE * jnp.where(low, grad_q[:ROWS], grad_q[ROWS:])
            dqs.append(unturn(grad_q, rows).astype(BF))
        grads = []
        for i in range(4):
            rows = slice(ROWS * i, ROWS * i + ROWS)
            dk, dv = dk_s[rows], dv_s[rows]
            dk = unturn(SCORE * (dk + pltpu.roll(dk, HD, 1)), rows)
            dv = dv + pltpu.roll(dv, HD, 1)
            dqkv = jnp.concatenate([dqs[i], jnp.where(low, dk, dv).astype(BF)], axis=1)
            dq[2 * i : 2 * i + 2, s] = dqkv.reshape(2, HALF, 256)
            grads.append(dqkv)
        dq_own[s].start()
        cps = [make.now(dq.at[p[1], s], dq_s.at[e, s], p) for p in ep_peers(d, e)]
        wqkv = tn(nrm[s], jnp.concatenate(grads, axis=0))
        if s == 0:
            dw[:, :256] = wqkv
        else:
            dw[:, :256] += wqkv
        return cps

    dq_own = [pltpu.make_async_copy(dq.at[e, s], dq_s.at[e, s], ls.at[13 + s]) for s in range(2)]
    dq_c = [attend_back(0)]
    ats.forward()
    for r in two[0]:
        r.forward()
    dq_c.append(attend_back(1))
    pa[...] = dw[:, :256].astype(BF).reshape(4, 4, 64, 256)
    a_first = [make.now(pa.at[p[0] // 4], ra.at[i], p) for i, p in enumerate(across)]
    for r in one:
        r.far_arrived()
    for r in two[2]:
        r.start()
    loads[9].wait()
    gain_a = 0.0
    for s in range(2):
        rows = slice(HALF * s, HALF * s + HALF)
        dq_own[s].wait()
        for cp in dq_c[s]:
            cp.wait_recv()
        grad = 0.0
        for i in range(EP):
            grad = grad + nt(dq_s[i, s], wf[i].reshape(D, 256))
        t = x[rows].astype(F32)
        factor = lax.rsqrt(jnp.mean(t * t, axis=1, keepdims=True) + EPS)
        g, gain = norm_back(grad, t, factor, gt[32:33])
        gx_o[rows] = (gm[rows] + g).astype(BF)
        gain_a = gain_a + gain
    results[1].start()
    ats.finish()
    wout = 0.0
    for s in range(2):
        wout = wout + tn(at[:, s].reshape(LEN, D), gb_s[:, s].reshape(LEN, 128))
    dw[:, 256:] = wout
    lines = [router, gain_a, gain_m, jnp.zeros((128 - EXPERTS - 2, D), F32)]
    small = jnp.concatenate(lines, axis=0).T
    pb[...] = jnp.concatenate([dw[:, 256:], small], axis=1).astype(BF).reshape(4, 4, 64, 256)
    b_first = [make.now(pb.at[:, lax.rem(p[0], 4)], rb.at[i], p) for i, p in enumerate(along)]
    for r in two[1] + two[3]:
        r.forward()

    def total(mine, arrived, cps):
        for cp in cps:
            cp.wait_recv()
        return mine.astype(F32) + arrived[0].astype(F32) + arrived[1].astype(F32) + arrived[2].astype(F32)

    ta[...] = total(pa[u], ra, a_first).astype(BF)
    a_second = [make.now(ta.at[lax.rem(p[0], 4)], qa.at[i], p) for i, p in enumerate(along)]
    tb[...] = total(pb[:, v], rb, b_first).astype(BF)
    b_second = [make.now(tb.at[p[0] // 4], qb.at[i], p) for i, p in enumerate(across)]
    for r in two[2]:
        r.forward()
    s1[:, :, :256] = total(ta[v], qa, a_second).reshape(EP, 8, 256)
    s1[:, :, 256:] = total(tb[u], qb, b_second).reshape(EP, 8, 256)
    r2[e] = s1[e]
    more = [make.now(s1.at[p[1]], r2.at[e], p) for p in ep_peers(d, e)]
    for cp in more:
        cp.wait_recv()
    small = r2[0, :, 384:]
    for s in range(1, EP):
        small = small + r2[s, :, 384:]
    sm_o[...] = small
    wq_o[...] = jnp.concatenate([r2[s, :, :128] for s in range(EP)], axis=1)
    wk_o[...] = jnp.concatenate([r2[s, :, 128:192] for s in range(EP)], axis=1)
    wv_o[...] = jnp.concatenate([r2[s, :, 192:256] for s in range(EP)], axis=1)
    wo_o[...] = jnp.concatenate([r2[s, :, 256:384] for s in range(EP)], axis=1)
    for group in two:
        for r in group:
            r.arrived()
    for r in one + two[0] + two[1] + two[2] + two[3]:
        r.sent()
    for cp in da_c + gb_c + dq_c[0] + dq_c[1] + a_first + b_first + a_second + b_second + more:
        cp.wait_send()
    loads[10].wait()
    for cp in results:
        cp.wait()


def widen(dw, out, gx, q, k, v, o, sm, g_o, u_o, d_o, out_o, gx_o, q_o, k_o, v_o, o_o, r_o, ga_o, gm_o):
    w = dw[...].reshape(3 * D, F).astype(F32)
    g_o[0] = w[:D]
    u_o[0] = w[D : 2 * D]
    d_o[0, :, :F] = w[2 * D : 2 * D + F]
    d_o[0, :, F:] = w[2 * D + F :]
    out_o[...], gx_o[...] = out[...], gx[...]

    @pl.when(pl.program_id(0) == 0)
    def _():
        q_o[...], k_o[...], v_o[...], o_o[...] = q[...], k[...], v[...], o[...]
        r_o[...] = sm[:, :EXPERTS]
        diagonal = lax.broadcasted_iota(jnp.int32, (8, 8), 0) == lanes((8, 8))
        for i, ref in ((32, ga_o), (33, gm_o)):
            ref[...] = jnp.sum(jnp.where(diagonal, sm[:, i : i + 1], 0.0), axis=0, keepdims=True)


def tables():
    even = np.arange(0, HD, 2).astype(np.float32)
    frequency = (np.float32(10000.0) ** (-even / np.float32(HD))).astype(np.float32)
    angle = np.arange(LEN, dtype=np.float32)[:, None] * frequency[None, :]
    angle = np.concatenate([angle] * 4, axis=1).astype(np.float64)
    return np.cos(angle).astype(np.float32), np.sin(angle).astype(np.float32)


def per_device(
    tokens, cotangent, block_ids, routes, w_query, w_key, w_value, w_output, w_router,
    gain_attn, gain_moe, expert_gate, expert_up, expert_down,
):
    x = tokens.reshape(ROWS, D)
    cot = cotangent.reshape(ROWS, D)
    rt = routes.reshape(ROWS, 8).T
    cos, sin = tables()
    cos, sin = jnp.asarray(cos), jnp.asarray(sin)
    params = pltpu.CompilerParams(vmem_limit_bytes=60 * MIB)
    once = pl.Buffered(1)

    def whole(shape):
        return pl.BlockSpec(shape, lambda s: (0,) * len(shape), pipeline_mode=once)

    kept = [
        ((SEQS, LEN, 128), BF), ((SEQS, LEN, 128), BF), ((SEQS, LEN, D), BF),
        ((EP, 2, HALF, 128), BF), ((SEQS, LEN, 128), F32), ((128, D), F32), ((D, D), BF),
        ((2, HALF, D), F32), ((2, HALF, D), BF), ((2, HALF, D), BF), ((D, 256), BF),
    ]
    rall, moe, cot_half, q, kv, nrm, att, lse, gt, wo, mid, moe_own, at_own, w_own = remote_call(
        before_experts, 1,
        [
            sds((EP, 8, ROWS), jnp.int32), sds((EP, 2, 2, HALF // 2, D), BF),
            sds((EP, HALF, D), BF), *[sds(*k) for k in kept],
        ],
        [
            tokens.reshape(2, 2, HALF // 2, D), rt, w_query, w_key, w_value, w_output, w_router,
            gain_attn.reshape(1, 8), gain_moe.reshape(1, 8), cos, sin, block_ids,
            cotangent.reshape(2, HALF, D),
        ],
        [ANY] + [VM] * 11 + [ANY],
        [
            *[pltpu.VMEM(*k) for k in kept],
            pltpu.VMEM((EP, 2, 2, HALF // 2, D), BF), pltpu.VMEM((4, 4, EP, 16, 128), BF),
            pltpu.VMEM((4, 4, EP, 16, 640), BF), pltpu.VMEM((EP, 16, 128), BF),
            pltpu.VMEM((16, 640), BF), pltpu.VMEM((8, 128), F32), pltpu.VMEM((EP, 8, 128), F32),
            pltpu.VMEM((4, 4, 8, 128), F32), pltpu.VMEM((D, 128), F32),
            pltpu.VMEM((LEN, 128), BF), pltpu.VMEM((LEN, 128), BF),
            pltpu.VMEM((EP, 2, HALF, 128), BF), pltpu.VMEM((2, 2, HALF // 2, D), BF),
        ],
        136,
        vmem=60,
    )

    each = lambda *shape: pl.BlockSpec((1, *shape), lambda j: (j,) + (0,) * len(shape))
    fwd = lambda *shape: pl.BlockSpec(
        (1, *shape), lambda j: (jnp.minimum(j, OWN - 1),) + (0,) * len(shape)
    )
    bwd = lambda *shape: pl.BlockSpec(
        (1, *shape), lambda j: (jnp.maximum(j - OWN, 0),) + (0,) * len(shape)
    )
    slots = lambda dtype, n: pltpu.VMEM((OWN, SLOTS, n), dtype)
    rest = pl.BlockSpec((1, 3 * D, F), lambda j: (jnp.maximum(j - OWN - 1, 0), 0, 0))
    both_ways = pl.BlockSpec((1, F, D), lambda j: (lax.rem(j, OWN), 0, 0))
    moved = pltpu.VMEM((2, 1, 2, 96, F), BF)
    dw, eo, dg, du, gg, picks, ca, cb, w_all = pl.pallas_call(
        experts_weights,
        name="experts_weights",
        grid=(2 * OWN,),
        out_shape=[
            sds((OWN - 1, 3 * D, F), BF), sds((EP, OWN * CAP, D), BF), sds((OWN, SLOTS, F), BF),
            sds((OWN, SLOTS, F), BF), sds((OWN, SLOTS, 128), F32), sds((EP, OWN * CAP, ROWS), BF),
            sds((1, 4, 96, F), BF), sds((1, 4, 96, F), BF), sds((EP, 2, D // 2, 256), BF),
        ],
        in_specs=[
            ANY, ANY, ANY, ANY, whole((EP, 8, ROWS)), whole((128, D)), fwd(D, F), fwd(D, F), both_ways,
        ],
        out_specs=[
            rest, ANY, bwd(SLOTS, F), bwd(SLOTS, F), bwd(SLOTS, 128),
            ANY, whole((1, 4, 96, F)), whole((1, 4, 96, F)), ANY,
        ],
        scratch_shapes=[
            pltpu.VMEM((EP, OWN * CAP, D), BF), pltpu.VMEM((EP, OWN * CAP, ROWS), BF),
            pltpu.VMEM((EP, 2, HALF, D), BF), slots(BF, D), pltpu.VMEM((OWN * SLOTS, D), BF),
            slots(F32, 128), slots(BF, F), slots(BF, F), slots(BF, F),
            pltpu.VMEM((1, 4, 4, 2, 96, F), BF), *[moved] * 6, pltpu.SemaphoreType.DMA((10,)),
            pltpu.SemaphoreType.DMA((48,)), pltpu.SemaphoreType.DMA((48,)),
        ],
        compiler_params=pltpu.CompilerParams(
            collective_id=2, has_side_effects=True, vmem_limit_bytes=62 * MIB
        ),
    )(
        moe.reshape(EP * ROWS, D), cotangent.reshape(2, HALF, D), cot_half, w_own.reshape(2, D // 2, 256),
        rall, gt, expert_gate, expert_up,
        expert_down,
    )

    mg, gg_all, shard = pl.pallas_call(
        experts_combine,
        name="experts_combine",
        grid=(OWN,),
        out_shape=[
            sds((ROWS, 2 * D), F32), sds((EP, 8, ROWS), F32), sds((OWN, 2, 96, F), BF),
        ],
        in_specs=[
            ANY, each(SLOTS, F), each(SLOTS, F), ANY, ANY, each(D, F), each(D, F), ANY, ANY, ANY,
        ],
        out_specs=[ANY, ANY, whole((OWN, 2, 96, F))],
        scratch_shapes=[
            pltpu.VMEM((ROWS, 2 * D), F32),
            pltpu.VMEM((EP, OWN * CAP, D), BF), pltpu.VMEM((EP, OWN * CAP, ROWS), BF),
            slots(F32, 128), pltpu.VMEM((EP, OWN * CAP, D), BF), pltpu.VMEM((EP, 8, ROWS), F32),
            *([pltpu.VMEM((4, ROWS, D), BF)] * 2 + [pltpu.VMEM((2, HALF, D), BF)] * 3) * 2,
            *([pltpu.VMEM((2, OWN - 1, 2, 96, F), BF)] * 4 + [pltpu.VMEM((OWN, 4, 96, F), BF)]) * 2,
            *[pltpu.VMEM((2, OWN, 48, F), BF)] * 6,
            pltpu.SemaphoreType.DMA((14,)),
            pltpu.SemaphoreType.DMA((64,)),
            pltpu.SemaphoreType.DMA((64,)),
        ],
        compiler_params=pltpu.CompilerParams(
            collective_id=3, has_side_effects=True, vmem_limit_bytes=62 * MIB
        ),
    )(
        eo, dg, du, gg, picks, expert_gate, expert_up, dw.reshape(OWN - 1, 4, 4, 2, 96, F), ca, cb,
    )
    heads = pltpu.VMEM((EP, 2, HALF, 128), BF)
    blocks = pltpu.VMEM((4, 4, 64, 256), BF)
    arriving = pltpu.VMEM((3, 4, 64, 256), BF)
    column = pltpu.VMEM((4, 64, 256), BF)
    dw_sum, output, grad_x, gq, gk, gv, go, gs = remote_call(
        tail, 4,
        [
            sds((4, 4, OWN, 2, 96, F), BF), sds((ROWS, D), BF), sds((ROWS, D), BF), sds((8, D), F32),
            sds((8, 512), F32), sds((8, 512), F32), sds((8, D), F32), sds((8, 128), F32),
        ],
        [
            mg, mid.reshape(ROWS, D), wo, w_all, q, kv, nrm, att, lse, at_own, shard,
            moe_own.reshape(ROWS, D), cot, gt, x, cos, sin, gg_all, rt, block_ids,
        ],
        [ANY] * 17 + [VM] * 3,
        [
            *[pltpu.VMEM((ROWS, D), BF)] * 4, pltpu.VMEM((128, D), F32), pltpu.VMEM((ROWS, D), BF),
            pltpu.VMEM((LEN, 128), F32), pltpu.VMEM((LEN, 128), F32),
            pltpu.VMEM((ROWS, 2 * D), F32), pltpu.VMEM((ROWS, D), F32), pltpu.VMEM((D, D), BF),
            pltpu.VMEM((EP, 2, D // 2, 256), BF), pltpu.VMEM((SEQS, LEN, 128), BF),
            pltpu.VMEM((SEQS, LEN, 128), BF), pltpu.VMEM((SEQS, LEN, D), BF), heads,
            pltpu.VMEM((SEQS, LEN, 128), F32), pltpu.VMEM((EP, 2, HALF, D), BF), *[heads] * 4,
            pltpu.VMEM((EP, 2, HALF, 256), BF), pltpu.VMEM((EP, 2, HALF, 256), BF),
            pltpu.VMEM((LEN, 128), BF), pltpu.VMEM((LEN, 128), BF), pltpu.VMEM((LEN, 128), F32),
            pltpu.VMEM((LEN, 128), F32), pltpu.VMEM((ROWS, D), F32), pltpu.VMEM((D, 384), F32),
            blocks, blocks, arriving, arriving, column, column, pltpu.VMEM((3, 64, 256), BF),
            pltpu.VMEM((3, 64, 256), BF),
            pltpu.VMEM((EP, 8, 512), F32), pltpu.VMEM((EP, 8, 512), F32),
        ],
        160,
        [ANY] * 3 + [VM] * 5,
        vmem=60,
    )

    small = [(8, D), (8, 512), (8, 512), (8, D)]
    rows = pl.BlockSpec((ROWS // OWN, D), lambda j: (j, 0))
    g_gate, g_up, g_down, output, grad_x, gq, gk, gv, go, gr, g_attn, g_moe = pl.pallas_call(
        widen,
        name="widen",
        grid=(OWN,),
        out_shape=[
            sds((OWN, D, F), F32), sds((OWN, D, F), F32), sds((OWN, F, D), F32),
            sds((ROWS, D), BF), sds((ROWS, D), BF), *[sds(n, F32) for n in small],
            sds((8, EXPERTS), F32), sds((1, 8), F32), sds((1, 8), F32),
        ],
        in_specs=[
            pl.BlockSpec((DP, 1, 192, F), lambda j: (0, j, 0, 0)), rows, rows,
            *[whole(n) for n in small], whole((8, 128)),
        ],
        out_specs=[
            each(D, F), each(D, F), each(F, D), rows, rows, *[whole(n) for n in small],
            whole((8, EXPERTS)), whole((1, 8)), whole((1, 8)),
        ],
        compiler_params=params,
    )(dw_sum.reshape(DP, OWN, 192, F), output, grad_x, gq, gk, gv, go, gs)
    return (
        output.reshape(tokens.shape),
        grad_x.reshape(tokens.shape),
        gq,
        gk,
        gv,
        go,
        gr,
        g_attn.reshape(8),
        g_moe.reshape(8),
        g_gate,
        g_up,
        g_down,
    )


def solution(mesh):
    rows, own, both_axes = P("dp", "ep", None), P("ep", None, None), P(("dp", "ep"), None)
    line = P(("dp", "ep"))
    return jax.shard_map(
        per_device,
        mesh=mesh,
        in_specs=(
            rows, rows, P("dp", None), rows, both_axes, both_axes, both_axes, both_axes, both_axes,
            line, line, own, own, own,
        ),
        out_specs=(
            rows, rows, both_axes, both_axes, both_axes, both_axes, both_axes, line, line, own,
            own, own,
        ),
        check_vma=False,
    )
```
